32 devices in a mesh: dev: 32 (over z, y, x, core).
Axes of the slice: x: 2, y: 2, z: 4, core: 2. Of those that a mesh axis runs over, the one named last changes fastest.
Arguments:
- tokens: bfloat16 [2, 8192, 1152], P(None, 'dev'), may hold values from -6 to 6
- counts: int32 [2], replicated, may hold values from 6 to 11, as said below
- qkv_weight: bfloat16 [3981312], P('dev'), may hold values from -0.25 to 0.25
- out_weight: bfloat16 [1327104], P('dev'), may hold values from -0.75 to 0.75
- up_weight: bfloat16 [4958208], P('dev'), may hold values from -0.1875 to 0.1875
- down_weight: bfloat16 [4958208], P('dev'), may hold values from -0.09375 to 0.09375
- vectors: bfloat16 [13536], P('dev'), may hold values from -1.5 to 1.75, as said below
- cotangent: bfloat16 [2, 8192, 1152], P(None, 'dev'), may hold values from -6 to 6
Outputs:
- result: bfloat16 [2, 8192, 1152], P(None, 'dev')
- input_grad: bfloat16 [2, 8192, 1152], P(None, 'dev')
- qkv_grad: float32 [3981312], P('dev')
- out_grad: float32 [1327104], P('dev')
- up_grad: float32 [4958208], P('dev')
- down_grad: float32 [4958208], P('dev')
- vector_grad: float32 [13536], P('dev')
The draws below stay inside these ranges and needn't reach their ends.
Inputs may be any that keep to these rules, and one draw needn't show every extreme that they name: counts[m] whole images of 729 tokens fill micro-batch m from slot 0; one micro-batch in every draw holds 11 images. `vectors`: gains near one and biases spread around zero, in the order given in the reference program.
All inputs are finite; a program needn't handle non-finite values.
Results may differ from the reference program's by a relative error of at most 0.013.
The reference program's roundings to bfloat16 on the way count: a program that leaves them out, or rounds other values in their place, can miss the bound.
Values may be sent and summed in bfloat16 or wider, within the bound.
A program may use at most 384 MiB of HBM per device.

```python
from functools import partial
import jax
import jax.numpy as jnp
from jax import lax

D = 1152
HEADS = 16
FF = 4304
IMG_LEN = 729
NMB = 2
MB_TOK = 8192
CAP = 11
VEC = 13536


def draw_counts(key, part):
    key = jax.random.fold_in(key, 11)
    first_key, second_key = jax.random.split(key)
    fewest = (CAP + 1) // 2
    drawn = jax.random.randint(first_key, (NMB,), fewest, CAP + 1)
    chosen = jax.random.randint(second_key, (), 0, NMB)
    return jnp.where(jnp.arange(NMB) == chosen, CAP, drawn).astype(jnp.int32)


def draw_vectors(key, part):
    key = jax.random.fold_in(key, 5)
    position = jnp.arange(VEC)
    segment = position // D
    noise = jnp.clip(jax.random.normal(key, (VEC,), jnp.float32), -3.0, 3.0)
    is_gain = jnp.logical_or(segment == 0, segment == 5)
    values = jnp.where(is_gain, 1.0 + 0.25 * noise, 0.5 * noise)
    return values.astype(jnp.bfloat16)


def level_of(stream_key, shape, shards, low, top_value):
    level, own = 1.0, jax.random.fold_in(stream_key, 6)
    for dim, shards_of in shards:
        steps = jnp.exp(jax.random.uniform(jax.random.fold_in(own, dim), (shards_of,), jnp.float32, low / len(shards), top_value / len(shards)))
        level = level * jnp.repeat(steps, shape[dim] // shards_of).reshape([-1 if axis == dim else 1 for axis in range(len(shape))])
    return level


def gaussian(rng, shape, scale, limit, cuts=(), held_as=jnp.bfloat16):
    entries = jax.random.normal(rng, shape, jnp.float32) * scale
    if len(cuts) > 0:
        entries = level_of(rng, shape, cuts, -0.22, 0.18) * entries
    return jnp.clip(entries, min=-limit, max=limit).astype(held_as)


def setup_inputs(seed: int = 0) -> dict:
    streams_of = jax.random.split(jax.random.key(seed), 9)
    return {
        "tokens": gaussian(streams_of[0], (NMB, MB_TOK, D), 1.0, 6.0, ((1, 32),)),
        "counts": draw_counts(jax.random.fold_in(streams_of[8], 71), 0),
        "qkv_weight": gaussian(streams_of[2], (3 * D * D,), (D // 2) ** -0.5, 0.25, ((0, 32),)),
        "out_weight": gaussian(streams_of[3], (D * D,), (D // 16) ** -0.5, 0.75, ((0, 32),)),
        "up_weight": gaussian(streams_of[4], (D * FF,), D ** -0.5, 0.1875, ((0, 32),)),
        "down_weight": gaussian(streams_of[5], (FF * D,), FF ** -0.5, 0.09375, ((0, 32),)),
        "vectors": draw_vectors(jax.random.fold_in(streams_of[8], 71), 0),
        "cotangent": gaussian(streams_of[7], (NMB, MB_TOK, D), 1.0, 6.0, ((1, 32),)),
    }


@jax.custom_vjp
def low(v):
    return lax.optimization_barrier(v.astype(jnp.bfloat16)).astype(jnp.float32)

@jax.custom_vjp
def low_back(v):
    return v

def low_keep(v):
    return (low(v), None)

def low_pass(kept, grad):
    return (grad,)

def back_keep(v):
    return (v, None)

def back_low(kept, grad):
    return (low(grad),)
low.defvjp(low_keep, low_pass)
low_back.defvjp(back_keep, back_low)

def matmul(left, right):
    return jnp.dot(left, right, precision=lax.Precision.HIGHEST, preferred_element_type=jnp.float32)

def layer_norm(values, gain, bias):
    centered = values - lax.optimization_barrier(jnp.mean(values, axis=-1, keepdims=True))
    inverse = lax.rsqrt(lax.optimization_barrier(jnp.mean(centered * centered, axis=-1, keepdims=True)) + 1e-06)
    return centered * inverse * gain + bias

def image_attention(query, keys, values, image_count):
    total_rows = query.shape[0]
    head_dim = D // HEADS
    images = -(-total_rows // IMG_LEN)
    extra_rows = images * IMG_LEN - total_rows

    def by_image(array):
        return jnp.pad(array, ((0, extra_rows), (0, 0))).reshape(images, IMG_LEN, HEADS, head_dim)
    live_images = jnp.arange(images, dtype=jnp.int32) < image_count

    def one_image(packed):
        query_img, keys_img, values_img, live = packed
        raw_scores = low_back(jnp.einsum('qhd,khd->hqk', query_img, keys_img, precision=lax.Precision.HIGHEST))
        scores = raw_scores * head_dim ** (-0.5)
        visible = jnp.logical_or(live, jnp.eye(IMG_LEN, dtype=bool))
        scores = jnp.where(visible[None], scores, -1e+30)
        probabilities = low(jax.nn.softmax(scores, axis=-1))
        return jnp.einsum('hqk,khd->qhd', probabilities, values_img, precision=lax.Precision.HIGHEST)
    attended = lax.map(jax.checkpoint(one_image), (by_image(query), by_image(keys), by_image(values), live_images))
    return attended.reshape(images * IMG_LEN, D)[:total_rows]

def forward(inputs, qkv_w, out_w, up_w, down_w, packed, image_count):
    pieces = [packed[segment * D:(segment + 1) * D] for segment in range(8)]
    up_bias = packed[8 * D:8 * D + FF]
    hidden_one = low(layer_norm(inputs, pieces[0], pieces[1]))
    projected = matmul(hidden_one, qkv_w)
    query = low_back(low(projected[:, :D] + pieces[2]))
    keys = low_back(low(projected[:, D:2 * D]))
    values = low_back(low(projected[:, 2 * D:] + pieces[3]))
    attended = low_back(low(image_attention(query, keys, values, image_count)))
    middle = inputs + low_back(matmul(attended, out_w) + pieces[4])
    hidden_two = low(layer_norm(middle, pieces[5], pieces[6]))
    upper = low_back(matmul(hidden_two, up_w) + up_bias)
    active = low(jax.nn.gelu(upper, approximate=True))
    return middle + (matmul(active, down_w) + pieces[7])

def reference(tokens, counts, qkv_weight, out_weight, up_weight, down_weight, vectors, cotangent):
    params = (qkv_weight.astype(jnp.float32).reshape(D, 3 * D), out_weight.astype(jnp.float32).reshape(D, D), up_weight.astype(jnp.float32).reshape(D, FF), down_weight.astype(jnp.float32).reshape(FF, D), vectors.astype(jnp.float32))
    results, grad_inputs = ([], [])
    totals = [jnp.zeros_like(param) for param in params]
    for batch_index in range(NMB):
        layer = partial(forward, image_count=counts[batch_index])
        output, pullback = jax.vjp(layer, tokens[batch_index].astype(jnp.float32), *params)
        grads = pullback(cotangent[batch_index].astype(jnp.float32))
        results.append(output.astype(jnp.bfloat16))
        grad_inputs.append(grads[0].astype(jnp.bfloat16))
        totals = [earlier + current for earlier, current in zip(totals, grads[1:])]
    return (jnp.stack(results), jnp.stack(grad_inputs), totals[0].reshape(-1), totals[1].reshape(-1), totals[2].reshape(-1), totals[3].reshape(-1), totals[4])
```

```python
from functools import partial

import jax
import jax.numpy as jnp
from jax import lax
from jax.experimental import pallas as pl
from jax.experimental.pallas import tpu as pltpu
from jax.sharding import PartitionSpec as P

D = 1152
HEADS = 16
FF = 4304
IMG_LEN = 729


heads_per_block = 4
EPSILON = 1e-06
MASKED = -1e30


def passed_along(block, axis, distance):
    devices = range(lax.axis_size(axis))
    route = [(i - distance, i) for i in devices if i - distance in devices]
    return lax.ppermute(block, axis, route)


def layer_stats(values):
    centered = values - jnp.mean(values, axis=-1, keepdims=True)
    inverse = lax.rsqrt(jnp.mean(centered * centered, axis=-1, keepdims=True) + EPSILON)
    return (centered * inverse, inverse)


def layer_back(grad_output, normed, inverse, gain):
    scaled = grad_output * gain
    return inverse * (
        scaled
        - jnp.mean(scaled, axis=-1, keepdims=True)
        - normed * jnp.mean(scaled * normed, axis=-1, keepdims=True)
    )


def image_of(positions, image_count):
    return jnp.where(positions < image_count * IMG_LEN, positions // IMG_LEN, -positions - 1)


def reach_sizes(shard_rows):
    rim_rows = IMG_LEN - 1
    reach_count = (rim_rows + shard_rows - 1) // shard_rows
    return [
        min(shard_rows, rim_rows - (distance - 1) * shard_rows)
        for distance in range(1, reach_count + 1)
    ]


def widen(key_value, shard_rows):
    edge_sizes = reach_sizes(shard_rows)
    arrived = {}
    for distance, amount in enumerate(edge_sizes, start=1):
        for direction in (1, -1):
            sent_rows = key_value[shard_rows - amount :] if direction > 0 else key_value[:amount]
            arrived[distance, direction] = passed_along(sent_rows, "dev", direction * distance)
    before = [arrived[distance, 1] for distance in range(len(edge_sizes), 0, -1)]
    after = [arrived[distance, -1] for distance in range(1, len(edge_sizes) + 1)]
    return jnp.concatenate(before + [key_value] + after, axis=0)


def return_edges(grad_extended, shard_rows):
    edge_sizes = reach_sizes(shard_rows)
    rim_rows = IMG_LEN - 1
    combined = grad_extended[rim_rows : rim_rows + shard_rows]
    for distance, amount in enumerate(edge_sizes, start=1):
        for direction in (1, -1):
            if direction > 0:
                begin_row = rim_rows - sum(edge_sizes[:distance])
            else:
                begin_row = rim_rows + shard_rows + sum(edge_sizes[: distance - 1])
            arrived = passed_along(
                grad_extended[begin_row : begin_row + amount].astype(jnp.bfloat16),
                "dev",
                -direction * distance,
            ).astype(jnp.float32)
            if direction > 0:
                combined = combined.at[shard_rows - amount :].add(arrived)
            else:
                combined = combined.at[:amount].add(arrived)
    return combined


def key_window(device_index, shard_rows, image_count):
    span_rows = ((shard_rows + IMG_LEN - 2) // IMG_LEN + 1) * IMG_LEN
    shard_start = device_index * shard_rows
    window_start = shard_start // IMG_LEN * IMG_LEN
    offset_rows = window_start - shard_start + IMG_LEN - 1
    query_images = image_of(shard_start + jnp.arange(shard_rows, dtype=jnp.int32), image_count)
    key_images = image_of(window_start + jnp.arange(span_rows, dtype=jnp.int32), image_count)
    return (span_rows, offset_rows, query_images[:, None] == key_images[None, :])


def head_slices(query, window_kv, block_index):
    head_dim = D // HEADS
    block_width = heads_per_block * head_dim
    first_column = block_index * block_width
    query_block = query[:, first_column : first_column + block_width].reshape(
        query.shape[0], heads_per_block, head_dim
    )
    key_block = window_kv[:, first_column : first_column + block_width].reshape(
        window_kv.shape[0], heads_per_block, head_dim
    )
    value_block = window_kv[:, D + first_column : D + first_column + block_width].reshape(
        window_kv.shape[0], heads_per_block, head_dim
    )
    return (query_block, key_block, value_block, first_column, block_width)


def attend(query, window_kv, visible):
    score_scale = (D // HEADS) ** (-0.5)
    outputs, log_sums = ([], [])
    for block_index in range(HEADS // heads_per_block):
        query_block, key_block, value_block, first_column, block_width = head_slices(
            query, window_kv, block_index
        )
        raw_scores = jnp.einsum(
            "qhd,khd->hqk", query_block, key_block, preferred_element_type=jnp.float32
        )
        scores = jnp.where(visible[None], raw_scores * score_scale, MASKED)
        largest = jnp.max(scores, axis=-1, keepdims=True)
        exponent = jnp.exp(scores - largest)
        row_totals = jnp.sum(exponent, axis=-1, keepdims=True)
        probabilities = (exponent / row_totals).astype(jnp.bfloat16)
        log_sums.append(largest + jnp.log(row_totals))
        attended = jnp.einsum(
            "hqk,khd->qhd", probabilities, value_block, preferred_element_type=jnp.float32
        )
        outputs.append(attended.reshape(query.shape[0], block_width))
    return (jnp.concatenate(outputs, axis=1), log_sums)


def attend_back(query, window_kv, visible, log_sums, grad_attended):
    score_scale = (D // HEADS) ** (-0.5)
    grad_queries, grad_keys, grad_values = ([], [], [])
    for block_index in range(HEADS // heads_per_block):
        query_block, key_block, value_block, first_column, block_width = head_slices(
            query, window_kv, block_index
        )
        grad_block = grad_attended[:, first_column : first_column + block_width].reshape(
            query.shape[0], heads_per_block, block_width // heads_per_block
        )
        raw_scores = jnp.einsum(
            "qhd,khd->hqk", query_block, key_block, preferred_element_type=jnp.float32
        )
        scores = jnp.where(visible[None], raw_scores * score_scale, MASKED)
        probabilities = jnp.exp(scores - log_sums[block_index])
        grad_values.append(
            jnp.einsum(
                "hqk,qhd->khd",
                probabilities.astype(jnp.bfloat16),
                grad_block,
                preferred_element_type=jnp.float32,
            ).reshape(window_kv.shape[0], block_width)
        )
        grad_probs = jnp.einsum(
            "qhd,khd->hqk", grad_block, value_block, preferred_element_type=jnp.float32
        )
        inner = jnp.sum(probabilities * grad_probs, axis=-1, keepdims=True)
        grad_raw = (probabilities * (grad_probs - inner) * score_scale).astype(jnp.bfloat16)
        grad_queries.append(
            jnp.einsum(
                "hqk,khd->qhd", grad_raw, key_block, preferred_element_type=jnp.float32
            ).reshape(query.shape[0], block_width)
        )
        grad_keys.append(
            jnp.einsum(
                "hqk,qhd->khd", grad_raw, query_block, preferred_element_type=jnp.float32
            ).reshape(window_kv.shape[0], block_width)
        )
    return (jnp.concatenate(grad_queries, axis=1), jnp.concatenate(grad_keys + grad_values, axis=1))


def unpack(gathered):
    qkv_flat, out_flat, up_flat, down_flat, packed = gathered
    packed = packed.astype(jnp.float32)
    pieces = [packed[segment * D : (segment + 1) * D] for segment in range(8)]
    up_bias = packed[8 * D : 8 * D + FF]
    return (
        qkv_flat.reshape(D, 3 * D),
        out_flat.reshape(D, D),
        up_flat.reshape(D, FF),
        down_flat.reshape(FF, D),
        pieces,
        up_bias,
    )


def forward_batch(tokens_batch, image_count, weights, device_index):
    qkv_w, out_w, up_w, down_w, pieces, up_bias = weights
    shard_rows = tokens_batch.shape[0]
    rim_rows = IMG_LEN - 1
    inputs = tokens_batch.astype(jnp.float32)
    normed_one, inverse_one = layer_stats(inputs)
    hidden_one = (normed_one * pieces[0] + pieces[1]).astype(jnp.bfloat16)
    projected = jnp.dot(hidden_one, qkv_w, preferred_element_type=jnp.float32)
    query = (projected[:, :D] + pieces[2]).astype(jnp.bfloat16)
    key_value = jnp.concatenate(
        [projected[:, D : 2 * D], projected[:, 2 * D :] + pieces[3]], axis=1
    ).astype(jnp.bfloat16)
    extended = widen(key_value, shard_rows)
    span_rows, offset_rows, visible = key_window(device_index, shard_rows, image_count)
    padded = jnp.pad(extended, ((0, rim_rows + span_rows - extended.shape[0]), (0, 0)))
    window_kv = lax.dynamic_slice_in_dim(padded, offset_rows, span_rows, 0)
    attended, log_sums = attend(query, window_kv, visible)
    attended_low = attended.astype(jnp.bfloat16)
    middle = inputs + (jnp.dot(attended_low, out_w, preferred_element_type=jnp.float32) + pieces[4])
    normed_two, inverse_two = layer_stats(middle)
    hidden_two = (normed_two * pieces[5] + pieces[6]).astype(jnp.bfloat16)
    upper = jnp.dot(hidden_two, up_w, preferred_element_type=jnp.float32) + up_bias
    active = jax.nn.gelu(upper, approximate=True).astype(jnp.bfloat16)
    output = middle + (jnp.dot(active, down_w, preferred_element_type=jnp.float32) + pieces[7])
    saved = (
        normed_one,
        inverse_one,
        hidden_one,
        query,
        window_kv,
        offset_rows,
        visible,
        log_sums,
        attended_low,
        normed_two,
        inverse_two,
        hidden_two,
        upper,
        active,
    )
    return (output.astype(jnp.bfloat16), saved)


def backward_batch(grad_output, saved, weights, vector_length):
    qkv_w, out_w, up_w, down_w, pieces, up_bias = weights
    (
        normed_one,
        inverse_one,
        hidden_one,
        query,
        window_kv,
        offset_rows,
        visible,
        log_sums,
        attended_low,
        normed_two,
        inverse_two,
        hidden_two,
        upper,
        active,
    ) = saved
    shard_rows = query.shape[0]
    span_rows = window_kv.shape[0]
    rim_rows = IMG_LEN - 1
    grad_wide = grad_output.astype(jnp.float32)
    grad_down = jnp.einsum("tf,td->fd", active, grad_output, preferred_element_type=jnp.float32)
    grad_down_bias = jnp.sum(grad_wide, axis=0)
    grad_active = jnp.einsum("td,fd->tf", grad_output, down_w, preferred_element_type=jnp.float32)
    gelu_back = jax.vjp(partial(jax.nn.gelu, approximate=True), upper)[1]
    grad_upper = gelu_back(grad_active)[0].astype(jnp.bfloat16)
    grad_up = jnp.einsum("td,tf->df", hidden_two, grad_upper, preferred_element_type=jnp.float32)
    grad_up_bias = jnp.sum(grad_upper.astype(jnp.float32), axis=0)
    grad_hidden_two = jnp.einsum("tf,df->td", grad_upper, up_w, preferred_element_type=jnp.float32)
    grad_gain_two = jnp.sum(grad_hidden_two * normed_two, axis=0)
    grad_bias_two = jnp.sum(grad_hidden_two, axis=0)
    grad_middle = grad_wide + layer_back(grad_hidden_two, normed_two, inverse_two, pieces[5])
    grad_branch = grad_middle.astype(jnp.bfloat16)
    grad_out = jnp.einsum(
        "td,te->de", attended_low, grad_branch, preferred_element_type=jnp.float32
    )
    grad_out_bias = jnp.sum(grad_branch.astype(jnp.float32), axis=0)
    grad_attended = jnp.einsum(
        "te,de->td", grad_branch, out_w, preferred_element_type=jnp.float32
    ).astype(jnp.bfloat16)
    grad_query, grad_window = attend_back(query, window_kv, visible, log_sums, grad_attended)
    grad_padded = lax.dynamic_update_slice_in_dim(
        jnp.zeros((rim_rows + span_rows, 2 * D), jnp.float32), grad_window, offset_rows, 0
    )
    grad_kv = return_edges(grad_padded[: shard_rows + 2 * rim_rows], shard_rows)
    grad_query_low = grad_query.astype(jnp.bfloat16)
    grad_kv_low = grad_kv.astype(jnp.bfloat16)
    grad_projected = jnp.concatenate([grad_query_low, grad_kv_low], axis=1)
    grad_qkv = jnp.einsum(
        "td,te->de", hidden_one, grad_projected, preferred_element_type=jnp.float32
    )
    grad_query_bias = jnp.sum(grad_query_low.astype(jnp.float32), axis=0)
    grad_value_bias = jnp.sum(grad_kv_low[:, D:].astype(jnp.float32), axis=0)
    grad_hidden_one = jnp.einsum(
        "te,de->td", grad_projected, qkv_w, preferred_element_type=jnp.float32
    )
    grad_gain_one = jnp.sum(grad_hidden_one * normed_one, axis=0)
    grad_bias_one = jnp.sum(grad_hidden_one, axis=0)
    grad_input = grad_middle + layer_back(grad_hidden_one, normed_one, inverse_one, pieces[0])
    vector_grad = jnp.concatenate(
        [
            grad_gain_one,
            grad_bias_one,
            grad_query_bias,
            grad_value_bias,
            grad_out_bias,
            grad_gain_two,
            grad_bias_two,
            grad_down_bias,
            grad_up_bias,
            jnp.zeros((vector_length - 8 * D - FF,), jnp.float32),
        ]
    )
    flat_grads = (
        grad_qkv.reshape(-1),
        grad_out.reshape(-1),
        grad_up.reshape(-1),
        grad_down.reshape(-1),
        vector_grad,
    )
    return (grad_input.astype(jnp.bfloat16), flat_grads)


def generic_local(tokens, counts, qkv_weight, out_weight, up_weight, down_weight, vectors, cotangent):
    device_index = lax.axis_index("dev")
    vector_length = vectors.shape[0] * lax.axis_size("dev")
    gathered = (
        lax.all_gather(qkv_weight, "dev", axis=0, tiled=True),
        lax.all_gather(out_weight, "dev", axis=0, tiled=True),
        lax.all_gather(up_weight, "dev", axis=0, tiled=True),
        lax.all_gather(down_weight, "dev", axis=0, tiled=True),
        lax.all_gather(vectors, "dev", axis=0, tiled=True),
    )
    weights = unpack(gathered)
    results, kept_state = ([], [])
    for batch_index in range(tokens.shape[0]):
        output, saved = forward_batch(
            tokens[batch_index], counts[batch_index], weights, device_index
        )
        results.append(output)
        kept_state.append(saved)
    weights = unpack(
        (
            lax.all_gather(qkv_weight, "dev", axis=0, tiled=True),
            lax.all_gather(out_weight, "dev", axis=0, tiled=True),
            lax.all_gather(up_weight, "dev", axis=0, tiled=True),
            lax.all_gather(down_weight, "dev", axis=0, tiled=True),
            lax.all_gather(vectors, "dev", axis=0, tiled=True),
        )
    )
    grad_inputs = []
    totals = None
    for batch_index in range(tokens.shape[0]):
        grad_input, flat_grads = backward_batch(
            cotangent[batch_index], kept_state[batch_index], weights, vector_length
        )
        grad_inputs.append(grad_input)
        totals = (
            flat_grads
            if totals is None
            else tuple((earlier + current for earlier, current in zip(totals, flat_grads)))
        )
    totals = lax.psum_scatter(totals, "dev", scatter_dimension=0, tiled=True)
    return (
        jnp.stack(results),
        jnp.stack(grad_inputs),
        totals[0],
        totals[1],
        totals[2],
        totals[3],
        totals[4],
    )


CHIPS = 16
HEAD = D // HEADS
HALF = D // 2
CORE_HEADS = HEADS // 2
ROWS = D // CHIPS
UNIT = FF // CHIPS
UNIT_HALF = 136
FFH = CHIPS * UNIT_HALF
SHARD = 256
CHIP_ROWS = 2 * SHARD
WINDOW = 1536
TILE = 128
ONE_IMAGE = 768
SCALE = HEAD**-0.5


def route(target):
    return [(i, target(i)) for i in range(2 * CHIPS)]


def swap(block):
    return lax.ppermute(block, "dev", route(lambda i: i ^ 1))


def by_core(core, first, second):
    return jnp.where(core == 0, first, second)


def joined(core, mine, theirs, axis):
    return by_core(
        core,
        jnp.concatenate([mine, theirs], axis=axis),
        jnp.concatenate([theirs, mine], axis=axis),
    )


def needed_shards(chip):
    start = chip * CHIP_ROWS
    first = start // IMG_LEN * IMG_LEN
    last = ((start + CHIP_ROWS - 1) // IMG_LEN + 1) * IMG_LEN - 1
    return range(first // SHARD, min(last // SHARD, 2 * CHIPS - 1) + 1)


def halo_routes(offsets):
    pairs = []
    for device in range(2 * CHIPS):
        wanted = device // 2 * 2 + offsets[device % 2]
        if wanted in needed_shards(device // 2):
            pairs.append((wanted // 2 * 2 + device % 2, device))
    return pairs


def chip_routes(distance):
    pairs = []
    for device in range(2 * CHIPS):
        chip = device // 2 + distance
        if abs(distance) == 1:
            wanted = {2 * chip, 2 * chip + 1}
        else:
            wanted = {2 * chip + 1} if distance < 0 else {2 * chip}
        if 0 <= chip < CHIPS and wanted & set(needed_shards(device // 2)):
            pairs.append((2 * chip + device % 2, device))
    return pairs


def head_lanes(head):
    first = head * HEAD
    low = first // 128 * 128
    high = min((first + HEAD + 127) // 128 * 128, HALF)
    return low, high, first - low


def head_mask(head):
    low, high, skip = head_lanes(head)
    lanes = lax.broadcasted_iota(jnp.int32, (1, high - low), 1)
    return (lanes >= skip) & (lanes < skip + HEAD)


NT = (((1,), (1,)), ((), ()))
NN = (((1,), (0,)), ((), ()))


def mm(left, right, dims):
    return lax.dot_general(left, right, dims, preferred_element_type=jnp.float32)


def window_of(chip):
    start = chip * CHIP_ROWS
    image = start // IMG_LEN * IMG_LEN
    offset = (3 * SHARD + image - start) // 16 * 16
    return start - 3 * SHARD + offset, 3 * SHARD - offset


def tile_geometry(origin, shift, tile):
    row = pl.multiple_of(shift + TILE * tile, 16)
    position = origin + row
    first = position // IMG_LEN
    last = (position + TILE - 1) // IMG_LEN
    start = pl.multiple_of((first * IMG_LEN - origin) // 16 * 16, 16)
    return row, position, first == last, start


def image_ids(position, shape, axis, live):
    at = position + lax.broadcasted_iota(jnp.int32, shape, axis)
    return jnp.where(at < live, at // IMG_LEN, -at - 1)


def attend_tile(origin, shift, batch, tile, live, q_ref, k_ref, v_ref, att_ref, lse_ref, acc):
    row, position, single, begin = tile_geometry(origin, shift, tile)
    out = pl.ds(pl.multiple_of(tile * TILE, TILE), TILE)
    acc[...] = jnp.zeros_like(acc)

    def run(start, length):
        visible = image_ids(position, (TILE, 1), 0, live) == image_ids(
            origin + start, (1, length), 1, live
        )
        stats = jnp.zeros((TILE, 128), jnp.float32)
        lane = lax.broadcasted_iota(jnp.int32, (TILE, 128), 1)
        for head in range(CORE_HEADS):
            low, high, _ = head_lanes(head)
            mask = head_mask(head)
            query = jnp.where(mask, q_ref[batch, pl.ds(row, TILE), low:high], 0)
            keys = k_ref[batch, pl.ds(start, length), low:high]
            scores = jnp.where(visible, mm(query, keys, NT) * SCALE, MASKED)
            largest = jnp.max(scores, axis=1, keepdims=True)
            exponent = jnp.exp(scores - largest)
            total = jnp.sum(exponent, axis=1, keepdims=True)
            probs = (exponent * (1.0 / total)).astype(jnp.bfloat16)
            part = mm(probs, v_ref[batch, pl.ds(start, length), low:high], NN)
            acc[:, low:high] += jnp.where(mask, part, 0.0)
            stats = jnp.where(lane == head, largest + jnp.log(total), stats)
        lse_ref[batch, out] = stats
        att_ref[batch, out] = acc[...].astype(jnp.bfloat16)

    @pl.when(single)
    def _():
        run(begin, ONE_IMAGE)

    @pl.when(jnp.logical_not(single))
    def _():
        run(0, WINDOW)


class Scatter:
    def __init__(self, place, grad_ref, total_ref, split, scratch):
        self.core, self.x, self.y, self.z = place
        self.grad_ref, self.total_ref, self.split = grad_ref, total_ref, split
        (self.half_x, self.half_y, self.sum_x, self.sum_y, self.whole_x, self.whole_y, self.line, self.from_z) = scratch[:8]
        (self.half_out, self.half_in, self.pair_out, self.pair_in, self.z_out, self.z_in) = scratch[8:]

    @staticmethod
    def scratch(shape, split):
        rows, columns = shape[1:]
        dma = pltpu.SemaphoreType.DMA
        block = lambda count, width: pltpu.VMEM((count, rows, width), jnp.bfloat16)
        return (
            [block(4, split), block(4, columns - split)]
            + [block(4, columns) for _ in range(4)]
            + [block(3, columns), block(3, columns)]
            + [dma((2, 4)), dma((2, 4)), dma((2, 4)), dma((2, 4)), dma((3,)), dma((3,))]
        )

    COUNT = 14

    def unit(self, at_x, at_y, turn):
        at_z = (self.z + 1 + turn) % 4
        return self.grad_ref.at[(at_z * 2 + at_y) * 2 + at_x]

    def remote(self, source, target_ref, send_sem, recv_sem, device):
        return pltpu.make_async_remote_copy(
            src_ref=source,
            dst_ref=target_ref,
            send_sem=send_sem,
            recv_sem=recv_sem,
            device_id=device,
            device_id_type=MESH_ID,
        )

    def half(self, turn, axis):
        diagonal = self.unit(1 - self.x, 1 - self.y, turn)
        columns = self.grad_ref.shape[2]
        source = diagonal.at[:, pl.ds(0, self.split) if axis == 0 else pl.ds(self.split, columns - self.split)]
        device = (peer(1 - self.x, self.y, self.z, self.core), peer(self.x, 1 - self.y, self.z, self.core))[axis]
        target = (self.half_x, self.half_y)[axis].at[turn]
        return self.remote(source, target, self.half_out.at[axis, turn], self.half_in.at[axis, turn], device)

    def whole(self, turn, axis):
        device = (peer(1 - self.x, self.y, self.z, self.core), peer(self.x, 1 - self.y, self.z, self.core))[axis]
        source, target = ((self.sum_x, self.whole_x), (self.sum_y, self.whole_y))[axis]
        return self.remote(
            source.at[turn], target.at[turn], self.pair_out.at[axis, turn], self.pair_in.at[axis, turn], device
        )

    def along(self, turn):
        device = peer(self.x, self.y, (self.z + 1 + turn) % 4, self.core)
        return self.remote(self.line.at[turn], self.from_z.at[turn], self.z_out.at[turn], self.z_in.at[turn], device)

    def begin(self, turn):
        self.half(turn, 0).start()
        self.half(turn, 1).start()

    def pair(self, turn):
        split = self.split
        wide = lambda value: value.astype(jnp.float32)
        self.half(turn, 0).wait_recv()
        grad = self.unit(self.x, 1 - self.y, turn)
        self.sum_y[turn, :, :split] = (wide(grad[:, :split]) + wide(self.half_x[turn])).astype(jnp.bfloat16)
        self.sum_y[turn, :, split:] = grad[:, split:]
        self.whole(turn, 1).start()
        self.half(turn, 1).wait_recv()
        grad = self.unit(1 - self.x, self.y, turn)
        self.sum_x[turn, :, :split] = grad[:, :split]
        self.sum_x[turn, :, split:] = (wide(grad[:, split:]) + wide(self.half_y[turn])).astype(jnp.bfloat16)
        self.whole(turn, 0).start()

    def join(self, turn):
        wide = lambda value: value.astype(jnp.float32)
        self.whole(turn, 0).wait_recv()
        self.whole(turn, 1).wait_recv()
        total = wide(self.unit(self.x, self.y, turn)[...]) + (wide(self.whole_x[turn]) + wide(self.whole_y[turn]))

        @pl.when(turn < 3)
        def _():
            self.line[turn] = total.astype(jnp.bfloat16)
            self.along(turn).start()

        @pl.when(turn == 3)
        def _():
            self.total_ref[...] = total

    def total(self, turn):
        self.along(turn).wait_recv()
        self.total_ref[...] += self.from_z[turn].astype(jnp.float32)

    def finish(self):
        def pairs(turn, carry):
            for axis in range(2):
                self.half(turn, axis).wait_send()
                self.whole(turn, axis).wait_send()
            return carry

        def lines(turn, carry):
            self.along(turn).wait_send()
            return carry

        lax.fori_loop(0, 4, pairs, 0)
        lax.fori_loop(0, 3, lines, 0)


def each_turn(action, count=4):
    def body(turn, carry):
        action(turn)
        return carry

    lax.fori_loop(0, count, body, 0)


def scatter_kernel(split, grad_ref, total_ref, *scratch):
    place = position_of()
    greet_line(*place)
    scatter = Scatter(place, grad_ref, total_ref, split, scratch)
    each_turn(scatter.begin)
    each_turn(scatter.pair)
    each_turn(scatter.join)
    each_turn(scatter.total, 3)
    scatter.finish()


def scatter_units(grad, split, collective_id):
    vmem = pl.BlockSpec(memory_space=pltpu.VMEM)
    return pl.pallas_call(
        partial(scatter_kernel, split),
        out_shape=jax.ShapeDtypeStruct(grad.shape[1:], jnp.float32),
        in_specs=[vmem],
        out_specs=vmem,
        scratch_shapes=Scatter.scratch(grad.shape, split),
        compiler_params=pltpu.CompilerParams(
            collective_id=collective_id, has_side_effects=True, vmem_limit_bytes=48 * 1024 * 1024
        ),
        cost_estimate=pl.CostEstimate(flops=0, bytes_accessed=150 * 10**6, transcendentals=0),
        name="scatter_units",
    )(grad)


def attend_back_tile(
    origin, shift, batch, tile, live,
    q_ref, k_ref, v_ref, g_ref, st_ref, stt_ref, dq_ref, dk_ref, dv_ref, dq_acc, dk_acc, dv_acc,
):
    row, position, single, begin = tile_geometry(origin, shift, tile)
    out = pl.ds(pl.multiple_of(tile * TILE, TILE), TILE)
    dq_acc[...] = jnp.zeros_like(dq_acc)
    dk_acc[...] = jnp.zeros_like(dk_acc)
    dv_acc[...] = jnp.zeros_like(dv_acc)

    def run(start, length):
        visible = image_ids(position, (TILE, 1), 0, live) == image_ids(
            origin + start, (1, length), 1, live
        )
        stats = st_ref[batch, pl.ds(row, TILE), :]
        if length == WINDOW:
            stats_t = stt_ref[batch]
        else:
            lead = pl.multiple_of(start // 128 * 128, 128)
            stats_t = stt_ref[batch, :, pl.ds(lead, length + 128)]
            stats_t = pltpu.roll(stats_t, length + 128 - (start - lead), 1)[:, :length]
        own, wide = pl.ds(row, TILE), pl.ds(start, length)
        for head in range(CORE_HEADS):
            low, high, _ = head_lanes(head)
            mask = head_mask(head)
            keys = k_ref[batch, wide, low:high]
            query = jnp.where(mask, q_ref[batch, own, low:high], 0)
            grad = jnp.where(mask, g_ref[batch, own, low:high], 0)
            lse = stats[:, head : head + 1]
            delta = stats[:, CORE_HEADS + head : CORE_HEADS + head + 1]
            probs = jnp.where(visible, jnp.exp(mm(query, keys, NT) * SCALE - lse), 0.0)
            grad_probs = mm(grad, v_ref[batch, wide, low:high], NT)
            grad_raw = (probs * (grad_probs - delta) * SCALE).astype(jnp.bfloat16)
            dq_acc[:, low:high] += jnp.where(mask, mm(grad_raw, keys, NN), 0.0)
            queries = q_ref[batch, wide, low:high]
            grads = g_ref[batch, wide, low:high]
            own_keys = jnp.where(mask, k_ref[batch, own, low:high], 0)
            own_values = jnp.where(mask, v_ref[batch, own, low:high], 0)
            lse_row = stats_t[head : head + 1]
            delta_row = stats_t[CORE_HEADS + head : CORE_HEADS + head + 1]
            probs_t = jnp.where(visible, jnp.exp(mm(own_keys, queries, NT) * SCALE - lse_row), 0.0)
            dv_acc[:, low:high] += jnp.where(
                mask, mm(probs_t.astype(jnp.bfloat16), grads, NN), 0.0
            )
            grad_probs_t = mm(own_values, grads, NT)
            grad_raw_t = (probs_t * (grad_probs_t - delta_row) * SCALE).astype(jnp.bfloat16)
            dk_acc[:, low:high] += jnp.where(mask, mm(grad_raw_t, queries, NN), 0.0)
        dq_ref[batch, out] = dq_acc[...].astype(jnp.bfloat16)
        dk_ref[batch, out] = dk_acc[...].astype(jnp.bfloat16)
        dv_ref[batch, out] = dv_acc[...].astype(jnp.bfloat16)

    @pl.when(single)
    def _():
        run(begin, ONE_IMAGE)

    @pl.when(jnp.logical_not(single))
    def _():
        run(0, WINDOW)


BACK_SPLITS = (640, 1152, 256)


def attend_scatter_kernel(
    counts, q_ref, k_ref, v_ref, g_ref, st_ref, stt_ref, down_ref, up_ref, out_ref,
    dq_ref, dk_ref, dv_ref, down_total, up_total, out_total, dq_acc, dk_acc, dv_acc, *scratch
):
    place = position_of()
    core, x, y, z = place
    chip = (z * 2 + y) * 2 + x
    greet_line(*place)
    count = Scatter.COUNT
    down, up, out = [
        Scatter(place, grad, total, split, scratch[n * count : (n + 1) * count])
        for n, (grad, total, split) in enumerate(
            zip((down_ref, up_ref, out_ref), (down_total, up_total, out_total), BACK_SPLITS)
        )
    ]
    each_turn(down.begin)
    tiles = CHIP_ROWS // TILE
    origin, shift = window_of(chip)
    work = {
        0: [(down.pair, 0, 1)],
        1: [(down.pair, 1, 3)],
        2: [(down.pair, 3, 4), (up.begin, 0, 4)],
        3: [(down.join, 0, 1)],
        4: [(down.join, 1, 2), (up.pair, 0, 1), (out.begin, 0, 4)],
        5: [(down.join, 2, 3), (up.pair, 1, 2)],
        6: [(down.join, 3, 4), (up.pair, 2, 4)],
        7: [(out.pair, 0, 4), (down.total, 0, 3)],
    }

    def loop(action, first, last):
        def body(turn, carry):
            action(turn)
            return carry

        lax.fori_loop(first, last, body, 0)

    def attend(index, carry):
        batch, tile = index // tiles, index % tiles
        attend_back_tile(
            origin, shift, batch, tile, counts[batch] * IMG_LEN,
            q_ref, k_ref, v_ref, g_ref, st_ref, stt_ref, dq_ref, dk_ref, dv_ref, dq_acc, dk_acc, dv_acc,
        )
        for at, actions in work.items():
            @pl.when(index == at)
            def _():
                for action, first, last in actions:
                    loop(action, first, last)
        return carry

    lax.fori_loop(0, q_ref.shape[0] * tiles, attend, 0)
    each_turn(up.join)
    each_turn(out.join)
    each_turn(up.total, 3)
    each_turn(out.total, 3)
    for scatter in (down, up, out):
        scatter.finish()


def attend_and_scatter(counts, query, keys, values, grads, stats, down, up, out, collective_id):
    batches = query.shape[0]
    vmem = pl.BlockSpec(memory_space=pltpu.VMEM)
    rows = jax.ShapeDtypeStruct((batches, CHIP_ROWS, HALF), jnp.bfloat16)
    parts = (down, up, out)
    return pl.pallas_call(
        attend_scatter_kernel,
        out_shape=[rows] * 3 + [jax.ShapeDtypeStruct(g.shape[1:], jnp.float32) for g in parts],
        in_specs=[pl.BlockSpec(memory_space=pltpu.SMEM)] + [vmem] * 9,
        out_specs=[vmem] * 6,
        scratch_shapes=[pltpu.VMEM((TILE, HALF), jnp.float32)] * 3
        + sum([Scatter.scratch(g.shape, split) for g, split in zip(parts, BACK_SPLITS)], []),
        compiler_params=pltpu.CompilerParams(
            collective_id=collective_id, has_side_effects=True, vmem_limit_bytes=60 * 1024 * 1024
        ),
        cost_estimate=pl.CostEstimate(flops=0, bytes_accessed=300 * 10**6, transcendentals=0),
        name="attend_and_scatter",
    )(
        counts, query, keys, values, grads,
        jnp.concatenate(stats, axis=-1),
        jnp.concatenate([s.swapaxes(1, 2) for s in stats], axis=1),
        *parts,
    )


def split_bf16(value, count):
    parts = []
    for _ in range(count):
        part = lax.reduce_precision(value, 8, 7)
        parts.append(part.astype(jnp.bfloat16))
        value = value - part
    return parts


def chip_unit(core, low, high):
    theirs = swap(by_core(core, high, low))
    return joined(core, by_core(core, low, high), theirs, 0)


def peer(x, y, z, core):
    return (((z * 2 + y) * 2 + x) * 2 + core,)


MESH_ID = pl.DeviceIdType.MESH


def position_of():
    device = lax.axis_index("dev")
    return device % 2, device // 2 % 2, device // 4 % 2, device // 8


def greet_line(core, x, y, z):
    barrier = pltpu.get_barrier_semaphore()
    targets = [peer(1 - x, y, z, core), peer(x, 1 - y, z, core)]
    targets += [peer(x, y, (z + step) % 4, core) for step in (1, 2, 3)]
    for target in targets:
        pl.semaphore_signal(barrier, inc=1, device_id=target, device_id_type=MESH_ID)
    pl.semaphore_wait(barrier, len(targets))


def greet(core, x, y, z, partner):
    barrier = pltpu.get_barrier_semaphore()
    targets = [peer(1 - x, y, z, core), peer(x, 1 - y, z, core)]
    if partner:
        targets.append(peer(x, y, z, 1 - core))
    for target in targets:
        pl.semaphore_signal(barrier, inc=1, device_id=target, device_id_type=MESH_ID)
    for side, there in ((-1, z > 0), (1, z < 3)):
        @pl.when(there)
        def _():
            pl.semaphore_signal(
                barrier, inc=1, device_id=peer(x, y, z + side, core), device_id_type=MESH_ID
            )
    ends = jnp.logical_or(z == 0, z == 3).astype(jnp.int32)
    pl.semaphore_wait(barrier, len(targets) + 2 - ends)


class Gather:
    def __init__(self, place, unit_ref, full_ref, other_ref, split, sems):
        self.core, self.x, self.y, self.z = place
        self.unit_ref, self.full_ref, self.other_ref, self.split = unit_ref, full_ref, other_ref, split
        (
            self.z_out,
            self.z_in,
            self.pair_out,
            self.pair_in,
            self.half_out,
            self.half_in,
            self.chain_out,
            self.chain_in,
            self.own_sem,
        ) = sems[:9]
        if other_ref is not None:
            self.swap_out, self.swap_in = sems[9:]
        self.sides = ((-1, self.z > 0), (1, self.z < 3))
        self.x_peer = peer(1 - self.x, self.y, self.z, self.core)
        self.y_peer = peer(self.x, 1 - self.y, self.z, self.core)

    @staticmethod
    def scratch(partner):
        dma = pltpu.SemaphoreType.DMA
        shapes = [(2, 4), (4,), (2, 4), (2, 4), (2, 4), (2, 4), (2, 4), (4,)]
        return [dma(shape) for shape in shapes] + [dma] + ([dma((CHIPS,))] * 2 if partner else [])

    def unit_index(self, at_x, at_y, at_z):
        return (at_z * 2 + at_y) * 2 + at_x

    def slot(self, at_x, at_y, at_z):
        return self.full_ref.at[self.unit_index(at_x, at_y, at_z)]

    def column(self, turn, at_z):
        at_x, at_y = [(self.x, self.y), (self.x, 1 - self.y), (1 - self.x, self.y), (1 - self.x, 1 - self.y)][turn]
        return self.slot(at_x, at_y, at_z)

    def copy(self, block, send_sem, recv_sem, target, source=None):
        return pltpu.make_async_remote_copy(
            src_ref=block if source is None else source,
            dst_ref=block,
            send_sem=send_sem,
            recv_sem=recv_sem,
            device_id=target,
            device_id_type=MESH_ID,
        )

    def along(self, at_z, side, source=None):
        index = 0 if side < 0 else 1
        target = peer(self.x, self.y, self.z + side, self.core)
        return self.copy(self.column(0, at_z), self.z_out.at[index, at_z], self.z_in.at[at_z], target, source)

    def chain(self, at_z, side):
        index = 0 if side < 0 else 1
        target = peer(self.x, self.y, self.z + side, self.core)
        return self.copy(self.column(3, at_z), self.chain_out.at[index, at_z], self.chain_in.at[at_z], target)

    def whole(self, at_z, axis, source=None):
        target = (self.x_peer, self.y_peer)[axis]
        return self.copy(self.column(0, at_z), self.pair_out.at[axis, at_z], self.pair_in.at[axis, at_z], target, source)

    def part(self, block, axis):
        width = self.full_ref.shape[2]
        return block.at[:, pl.ds(0, self.split) if axis == 0 else pl.ds(self.split, width - self.split)]

    def half(self, at_z, axis):
        block = self.part(self.column(1 + axis, at_z), axis)
        target = (self.x_peer, self.y_peer)[axis]
        return self.copy(block, self.half_out.at[axis, at_z], self.half_in.at[axis, at_z], target)

    def half_arrival(self, at_z, axis):
        block = self.part(self.column(3, at_z), axis)
        return self.copy(block, self.half_out.at[axis, at_z], self.half_in.at[axis, at_z], self.x_peer)

    def by_halves(self, at_z):
        near = jnp.logical_and(jnp.abs(at_z - self.z) == 1, jnp.logical_or(at_z == 1, at_z == 2))
        return jnp.logical_or(at_z == self.z, near)

    def trade(self, turn, at_z, source=None):
        at_x, at_y = [(self.x, self.y), (self.x, 1 - self.y), (1 - self.x, self.y), (1 - self.x, 1 - self.y)][turn]
        index = self.unit_index(at_x, at_y, at_z)
        block = self.full_ref.at[index] if source is None else source
        return pltpu.make_async_remote_copy(
            src_ref=block,
            dst_ref=self.other_ref.at[index],
            send_sem=self.swap_out.at[index],
            recv_sem=self.swap_in.at[index],
            device_id=peer(self.x, self.y, self.z, 1 - self.core),
            device_id_type=MESH_ID,
        )

    def share(self, turn, at_z, source=None):
        if self.other_ref is not None:
            self.trade(turn, at_z, source).start()

    def each(self, distance, action):
        if distance == 0:
            action(self.z, 0)
            return
        for side in (-1, 1):
            at_z = self.z + side * distance
            @pl.when(jnp.logical_and(at_z >= 0, at_z <= 3))
            def _():
                action(at_z, side)

    def onwards(self, side, action):
        for to, there in self.sides:
            if side == 0 or to == -side:
                @pl.when(there)
                def _():
                    action(to)

    def arrive(self, at_z, side):
        source = None
        if side == 0:
            source = self.unit_ref
            pltpu.make_async_copy(self.unit_ref, self.column(0, at_z), self.own_sem).start()
        else:
            self.along(at_z, side).wait_recv()
        self.onwards(side, lambda to: self.along(at_z, to, source).start())
        self.whole(at_z, 0, source).start()
        self.whole(at_z, 1, source).start()
        self.share(0, at_z, source)

    def cross(self, at_z, side):
        for axis in (1, 0):
            arrived = self.column(2 - axis, at_z)
            self.copy(arrived, self.pair_out.at[axis, at_z], self.pair_in.at[axis, at_z], self.x_peer).wait_recv()
            @pl.when(self.by_halves(at_z))
            def _():
                self.half(at_z, 1 - axis).start()
            self.share(2 - axis, at_z)

    def far_chain(self, at_z, side):
        return jnp.logical_or(at_z == 0, at_z == 3) if side == 0 else True

    def diagonal(self, at_z, side):
        halves = self.by_halves(at_z)
        @pl.when(halves)
        def _():
            self.half_arrival(at_z, 0).wait_recv()
            self.half_arrival(at_z, 1).wait_recv()
        if side != 0:
            @pl.when(jnp.logical_not(halves))
            def _():
                self.chain(at_z, side).wait_recv()
        @pl.when(self.far_chain(at_z, side))
        def _():
            self.onwards(side, lambda to: self.chain(at_z, to).start())
        self.share(3, at_z)

    def steps(self):
        order = [
            (0, self.arrive),
            (1, self.arrive),
            (0, self.cross),
            (2, self.arrive),
            (0, self.diagonal),
            (1, self.cross),
            (3, self.arrive),
            (1, self.diagonal),
            (2, self.cross),
            (2, self.diagonal),
            (3, self.cross),
            (3, self.diagonal),
        ]
        return [partial(self.each, distance, action) for distance, action in order]

    def settle(self, at_z, side):
        self.onwards(side, lambda to: self.along(at_z, to).wait_send())
        @pl.when(self.far_chain(at_z, side))
        def _():
            self.onwards(side, lambda to: self.chain(at_z, to).wait_send())
        for axis in range(2):
            self.whole(at_z, axis).wait_send()
            @pl.when(self.by_halves(at_z))
            def _():
                self.half(at_z, axis).wait_send()

    def finish(self):
        for distance in range(4):
            self.each(distance, self.settle)
        pltpu.make_async_copy(self.unit_ref, self.column(0, self.z), self.own_sem).wait()
        if self.other_ref is not None:
            def traded(at_z, carry):
                for turn in range(4):
                    self.trade(turn, at_z).wait()
                return carry

            lax.fori_loop(0, 4, traded, 0)


def gather_kernel(split, unit_ref, full_ref, *sems):
    place = position_of()
    greet(*place, False)
    gather = Gather(place, unit_ref, full_ref, None, split, sems)
    for step in gather.steps():
        step()
    gather.finish()


def gather_units(unit, collective_id):
    rows, columns = unit.shape
    return pl.pallas_call(
        partial(gather_kernel, columns // 2),
        out_shape=jax.ShapeDtypeStruct((CHIPS, rows, columns), unit.dtype),
        in_specs=[pl.BlockSpec(memory_space=pltpu.VMEM)],
        out_specs=pl.BlockSpec(memory_space=pl.ANY),
        scratch_shapes=Gather.scratch(False),
        compiler_params=pltpu.CompilerParams(collective_id=collective_id, has_side_effects=True),
        cost_estimate=pl.CostEstimate(flops=0, bytes_accessed=150 * 10**6, transcendentals=0),
        name="gather_units",
    )(unit)


def attend_gather_kernel(
    splits, counts, q_ref, k_ref, v_ref, up_unit, down_unit,
    att_ref, lse_ref, up_ref, up_other, down_ref, down_other, acc, *sems
):
    place = position_of()
    core, x, y, z = place
    chip = (z * 2 + y) * 2 + x
    greet(*place, True)
    half = len(sems) // 2
    gathers = [
        Gather(place, up_unit, up_ref, up_other, splits[0], sems[:half]),
        Gather(place, down_unit, down_ref, down_other, splits[1], sems[half:]),
    ]
    steps = [g.steps() for g in gathers]

    def advance(index):
        for s in steps:
            s[index]()

    tiles = CHIP_ROWS // TILE
    advance(0)
    origin, shift = window_of(chip)

    def attend(index, carry):
        batch, tile = index // tiles, index % tiles
        attend_tile(
            origin, shift, batch, tile, counts[batch] * IMG_LEN, q_ref, k_ref, v_ref, att_ref, lse_ref, acc
        )
        for at, first, last in ((3, 1, 3), (6, 3, 5)):
            @pl.when(index == at)
            def _():
                for step in range(first, last):
                    advance(step)
        return carry

    lax.fori_loop(0, q_ref.shape[0] * tiles, attend, 0)
    for step in range(5, len(steps[0])):
        advance(step)
    for g in gathers:
        g.finish()


def attend_and_gather(counts, query, keys, values, up_unit, down_unit, collective_id):
    batches = query.shape[0]
    full = lambda unit: jax.ShapeDtypeStruct((CHIPS,) + unit.shape, unit.dtype)
    vmem, hbm = pl.BlockSpec(memory_space=pltpu.VMEM), pl.BlockSpec(memory_space=pl.ANY)
    outs = pl.pallas_call(
        partial(attend_gather_kernel, (1152, 640)),
        out_shape=[
            jax.ShapeDtypeStruct((batches, CHIP_ROWS, HALF), jnp.bfloat16),
            jax.ShapeDtypeStruct((batches, CHIP_ROWS, 128), jnp.float32),
            full(up_unit),
            full(up_unit),
            full(down_unit),
            full(down_unit),
        ],
        in_specs=[pl.BlockSpec(memory_space=pltpu.SMEM)] + [vmem] * 5,
        out_specs=[vmem] * 2 + [hbm] * 4,
        scratch_shapes=[pltpu.VMEM((TILE, HALF), jnp.float32)] + Gather.scratch(True) * 2,
        compiler_params=pltpu.CompilerParams(
            collective_id=collective_id, has_side_effects=True, vmem_limit_bytes=48 * 1024 * 1024
        ),
        cost_estimate=pl.CostEstimate(flops=0, bytes_accessed=250 * 10**6, transcendentals=0),
        name="attend_and_gather",
    )(counts, query, keys, values, up_unit, down_unit)
    return list(outs[:2]) + [w.reshape(-1, w.shape[2]) for w in outs[2:]]


def vector_kernel(sent_ref, total_ref, arrived, send_sems, recv_sems):
    device = lax.axis_index("dev")
    devices = 2 * CHIPS
    mesh_id = pl.DeviceIdType.MESH
    barrier = pltpu.get_barrier_semaphore()

    def greet(step, carry):
        pl.semaphore_signal(
            barrier, inc=1, device_id=(lax.rem(device + step, devices),), device_id_type=mesh_id
        )
        return carry

    lax.fori_loop(1, devices, greet, 0)
    pl.semaphore_wait(barrier, devices - 1)

    def copy(step):
        target = lax.rem(device + step, devices)
        return pltpu.make_async_remote_copy(
            src_ref=sent_ref.at[target],
            dst_ref=arrived.at[step],
            send_sem=send_sems.at[step],
            recv_sem=recv_sems.at[step],
            device_id=(target,),
            device_id_type=mesh_id,
        )

    def start(step, carry):
        copy(step).start()
        return carry

    lax.fori_loop(1, devices, start, 0)

    def add(step, total):
        copy(step).wait()
        return total + arrived[step]

    total_ref[...] = lax.fori_loop(1, devices, add, sent_ref[device])


def scatter_vector(vector, share, collective_id):
    rows = jnp.pad(vector.reshape(2 * CHIPS, share), ((0, 0), (0, 1024 - share)))
    dma = pltpu.SemaphoreType.DMA
    total = pl.pallas_call(
        vector_kernel,
        out_shape=jax.ShapeDtypeStruct((8, 128), jnp.float32),
        in_specs=[pl.BlockSpec(memory_space=pltpu.VMEM)],
        out_specs=pl.BlockSpec(memory_space=pltpu.VMEM),
        scratch_shapes=[
            pltpu.VMEM((2 * CHIPS, 8, 128), jnp.float32),
            dma((2 * CHIPS,)),
            dma((2 * CHIPS,)),
        ],
        compiler_params=pltpu.CompilerParams(collective_id=collective_id, has_side_effects=True),
        cost_estimate=pl.CostEstimate(flops=0, bytes_accessed=20 * 10**6, transcendentals=0),
        name="scatter_vector",
    )(rows.reshape(2 * CHIPS, 8, 128))
    return total.reshape(-1)[:share]


def held_back(value, *others):
    return lax.optimization_barrier((value,) + others)[0]


def topo_local(tokens, counts, qkv_weight, out_weight, up_weight, down_weight, vectors, cotangent):
    device = lax.axis_index("dev")
    core, chip = device % 2, device // 2
    batches = tokens.shape[0]
    share = vectors.shape[0]
    own_rows = batches * SHARD

    qkv36 = qkv_weight.reshape(ROWS // 2, 3 * D)
    out36 = out_weight.reshape(ROWS // 2, D)
    sides = [
        jnp.concatenate(
            [qkv36[:, s * HALF + j * D :][:, :HALF] for j in range(3)] + [out36[:, s * HALF :][:, :HALF]],
            axis=1,
        )
        for s in range(2)
    ]
    up36 = up_weight.reshape(ROWS // 2, CHIPS, UNIT)
    up_low = up36[:, :, :UNIT_HALF].reshape(ROWS // 2, FFH)
    up_high = jnp.pad(up36[:, :, UNIT_HALF:], ((0, 0), (0, 0), (0, 2 * UNIT_HALF - UNIT))).reshape(
        ROWS // 2, FFH
    )
    spill = UNIT_HALF * D - down_weight.shape[0]
    borrowed = lax.ppermute(
        down_weight[:spill], "dev", [(i + 1, i) for i in range(0, 2 * CHIPS, 2)]
    )
    down_unit = by_core(
        core,
        jnp.concatenate([down_weight, borrowed]),
        jnp.concatenate([down_weight[spill:], jnp.zeros((2 * spill,), jnp.bfloat16)]),
    ).reshape(UNIT_HALF, D)
    first_unit = chip_unit(
        core,
        jnp.concatenate([sides[0], up_low], axis=1),
        jnp.concatenate([sides[1], up_high], axis=1),
    )
    shares = jnp.pad(vectors, (0, 512 - share)).reshape(1, 512)
    shares = joined(core, shares, swap(shares), 0).reshape(1, 1024)
    extra = jnp.pad(shares, ((0, 7), (0, 4 * HALF - 1024)))
    full = gather_units(jnp.concatenate([first_unit[:, : 4 * HALF], extra], axis=0), 1)
    attention_w = full[:, :ROWS]
    query_w, key_w, value_w, out_mine = [
        attention_w[:, :, j * HALF : (j + 1) * HALF].reshape(D, HALF) for j in range(4)
    ]
    out_theirs = swap(out_mine)
    packed = full[:, ROWS, :1024].reshape(2 * CHIPS, 512)[:, :share].reshape(-1).astype(jnp.float32)
    pieces = [packed[segment * D : (segment + 1) * D] for segment in range(8)]
    bias_units = packed[8 * D : 8 * D + FF].reshape(CHIPS, UNIT)
    bias_low = bias_units[:, :UNIT_HALF].reshape(-1)
    bias_high = jnp.pad(bias_units[:, UNIT_HALF:], ((0, 0), (0, 2 * UNIT_HALF - UNIT))).reshape(-1)
    up_bias_mine = by_core(core, bias_low, bias_high)
    up_bias_theirs = by_core(core, bias_high, bias_low)
    half_of = lambda vector: lax.dynamic_slice_in_dim(vector, core * HALF, HALF, 0)

    chip_start = chip * CHIP_ROWS
    origin, shift = window_of(chip)
    window_offset = 3 * SHARD - shift
    meta = jnp.stack(
        [origin, shift] + [counts[m] * IMG_LEN for m in range(batches)]
    ).astype(jnp.int32)
    arrived = [
        lax.ppermute(tokens, "dev", halo_routes(offsets)) for offsets in ((-2, -1), (2, 3), (4, -3))
    ]
    shards = jnp.stack(arrived + [tokens])
    others = swap(shards)
    low, high = by_core(core, shards, others), by_core(core, others, shards)
    filler = jnp.zeros((batches, SHARD, D), jnp.bfloat16)
    extended = jnp.concatenate(
        [high[2], low[0], high[0], low[3], high[3], low[1], high[1], low[2], filler], axis=1
    )
    window = lax.dynamic_slice_in_dim(extended, window_offset, WINDOW, 1)
    window_normed = layer_stats(window.astype(jnp.float32))[0]
    hidden_one = (window_normed * pieces[0] + pieces[1]).astype(jnp.bfloat16)
    project = lambda w: jnp.dot(
        hidden_one.reshape(-1, D), w, preferred_element_type=jnp.float32
    ).reshape(batches, WINDOW, HALF)
    query = (project(query_w) + half_of(pieces[2])).astype(jnp.bfloat16)
    keys = project(key_w).astype(jnp.bfloat16)
    values = (project(value_w) + half_of(pieces[3])).astype(jnp.bfloat16)
    attended, log_sums, up_mine, up_theirs, down_mine, down_theirs = attend_and_gather(
        counts, query, keys, values, first_unit[:, 4 * HALF :], down_unit, 3
    )
    attended_chip = joined(core, attended, swap(attended), 2)
    attended_own = lax.dynamic_slice_in_dim(attended_chip, core * SHARD, SHARD, 1).reshape(own_rows, D)

    def dot(left, right):
        return jnp.dot(left, right, preferred_element_type=jnp.float32)

    def dot_nt(left, right):
        return lax.dot_general(left, right, NT, preferred_element_type=jnp.float32)

    def dot_tn(left, right):
        return lax.dot_general(left, right, (((0,), (0,)), ((), ())), preferred_element_type=jnp.float32)

    inputs = tokens.reshape(own_rows, D).astype(jnp.float32)
    branch = joined(core, dot(attended_own, out_mine), dot(attended_own, out_theirs), 1)
    middle = inputs + (branch + pieces[4])
    normed_two, inverse_two = layer_stats(middle)
    hidden_two = (normed_two * pieces[5] + pieces[6]).astype(jnp.bfloat16)
    upper_mine = dot(hidden_two, up_mine) + up_bias_mine
    upper_theirs = dot(hidden_two, up_theirs) + up_bias_theirs
    gelu = partial(jax.nn.gelu, approximate=True)
    active_mine = gelu(upper_mine).astype(jnp.bfloat16)
    active_theirs = gelu(upper_theirs).astype(jnp.bfloat16)
    result = middle + ((dot(active_mine, down_mine) + dot(active_theirs, down_theirs)) + pieces[7])

    grad_output = cotangent.reshape(own_rows, D)
    grad_wide = grad_output.astype(jnp.float32)
    pair = lambda mine, theirs: jnp.concatenate([mine, swap(theirs)], axis=0)
    grad_down = dot_tn(pair(active_mine, active_theirs), pair(grad_output, grad_output))
    grad_down = grad_down.astype(jnp.bfloat16)
    grad_upper_mine = jax.vjp(gelu, upper_mine)[1](dot_nt(grad_output, down_mine))[0].astype(jnp.bfloat16)
    grad_upper_theirs = jax.vjp(gelu, upper_theirs)[1](dot_nt(grad_output, down_theirs))[0].astype(
        jnp.bfloat16
    )
    grad_up = dot_tn(pair(hidden_two, hidden_two), pair(grad_upper_mine, grad_upper_theirs))
    grad_up = grad_up.astype(jnp.bfloat16)
    grad_hidden_two = dot_nt(grad_upper_mine, up_mine) + dot_nt(grad_upper_theirs, up_theirs)
    grad_middle = grad_wide + layer_back(grad_hidden_two, normed_two, inverse_two, pieces[5])
    grad_branch = grad_middle.astype(jnp.bfloat16)
    branch_low, branch_high = grad_branch[:, :HALF], grad_branch[:, HALF:]
    branch_mine = by_core(core, branch_low, branch_high)
    branch_theirs = by_core(core, branch_high, branch_low)
    grad_attended = (dot_nt(branch_mine, out_mine) + dot_nt(branch_theirs, out_theirs)).astype(jnp.bfloat16)
    chip_order = lambda mine, theirs: joined(
        core, mine.reshape(batches, SHARD, HALF), theirs.reshape(batches, SHARD, HALF), 1
    )
    grad_low, grad_high = grad_attended[:, :HALF], grad_attended[:, HALF:]
    grad_heads = chip_order(
        by_core(core, grad_low, grad_high), swap(by_core(core, grad_high, grad_low))
    )
    branch_chip = chip_order(branch_mine, swap(branch_theirs)).reshape(-1, HALF)
    by_head = lambda rows: rows.astype(jnp.float32).reshape(batches, CHIP_ROWS, CORE_HEADS, HEAD)
    delta = jnp.sum(by_head(grad_heads) * by_head(attended), axis=-1)
    sent = jnp.concatenate(
        [grad_heads] + split_bf16(log_sums[..., :CORE_HEADS], 3) + split_bf16(delta, 3)
        + [jnp.zeros((batches, CHIP_ROWS, 16), jnp.bfloat16)],
        axis=-1,
    )
    before = lax.ppermute(sent, "dev", chip_routes(-1))
    after = lax.ppermute(sent, "dev", chip_routes(1))
    far_before = lax.ppermute(sent[:, SHARD:], "dev", chip_routes(-2))
    far_after = lax.ppermute(sent[:, :SHARD], "dev", chip_routes(2))
    grad_extended = jnp.concatenate(
        [far_before, before, sent, after, far_after, jnp.zeros_like(far_after)], axis=1
    )
    grad_window = lax.dynamic_slice_in_dim(grad_extended, window_offset, WINDOW, 1)
    decoded = grad_window[..., HALF : HALF + 48].astype(jnp.float32).reshape(batches, WINDOW, 2, 3, CORE_HEADS)
    decoded = decoded[..., 0, :] + (decoded[..., 1, :] + decoded[..., 2, :])
    flat = lambda block: block.reshape(batches * CHIP_ROWS, -1)
    grad_out = dot_tn(flat(attended_chip), branch_chip).astype(jnp.bfloat16)
    grad_query, grad_keys, grad_values, down_total, up_total, out_total = attend_and_scatter(
        counts, query, keys, values, grad_window[..., :HALF], [decoded[:, :, 0], decoded[:, :, 1]],
        grad_down.reshape(CHIPS, UNIT_HALF, D), grad_up.reshape(CHIPS, ROWS, FFH), grad_out.reshape(CHIPS, ROWS, HALF), 4,
    )
    hidden_chip = flat(lax.dynamic_slice_in_dim(hidden_one, meta[1], CHIP_ROWS, 1))
    grad_query, grad_keys, grad_values = flat(grad_query), flat(grad_keys), flat(grad_values)
    grad_attention = jnp.concatenate(
        [dot_tn(hidden_chip, g).astype(jnp.bfloat16) for g in (grad_query, grad_keys, grad_values)], axis=1
    )
    attention_total = scatter_units(grad_attention.reshape(CHIPS, ROWS, 3 * HALF), 896, 5)
    attention_total = jnp.concatenate([attention_total, out_total], axis=1)
    grad_partial = (
        dot_nt(grad_query, query_w) + dot_nt(grad_keys, key_w) + dot_nt(grad_values, value_w)
    ).reshape(batches, 2, SHARD, D)
    grad_hidden_one = lax.dynamic_index_in_dim(grad_partial, core, 1, keepdims=False) + swap(
        lax.dynamic_index_in_dim(grad_partial, 1 - core, 1, keepdims=False)
    )
    grad_hidden_one = grad_hidden_one.reshape(own_rows, D)
    normed_one, inverse_one = layer_stats(inputs)
    grad_input = grad_middle + layer_back(grad_hidden_one, normed_one, inverse_one, pieces[0])

    sums = lambda values: jnp.sum(values.astype(jnp.float32), axis=0)
    at_heads = lambda vector: lax.dynamic_update_slice_in_dim(
        jnp.zeros((D,), jnp.float32), vector, core * HALF, 0
    )
    bias_mine, bias_theirs = sums(grad_upper_mine), sums(grad_upper_theirs)
    bias_low = by_core(core, bias_mine, bias_theirs).reshape(CHIPS, UNIT_HALF)
    bias_high = by_core(core, bias_theirs, bias_mine).reshape(CHIPS, UNIT_HALF)
    grad_up_bias = jnp.concatenate([bias_low, bias_high[:, : UNIT - UNIT_HALF]], axis=1).reshape(-1)
    vector_grad = jnp.concatenate(
        [
            sums(grad_hidden_one * normed_one),
            sums(grad_hidden_one),
            at_heads(sums(grad_query)),
            at_heads(sums(grad_values)),
            sums(grad_branch),
            sums(grad_hidden_two * normed_two),
            sums(grad_hidden_two),
            sums(grad_wide),
            grad_up_bias,
            jnp.zeros((32 * share - 8 * D - FF,), jnp.float32),
        ]
    )
    vector_grad = scatter_vector(vector_grad, share, 2)

    half_rows = ROWS // 2

    def whole_rows(total):
        kept = by_core(core, total[:half_rows], total[half_rows:])
        theirs = swap(by_core(core, total[half_rows:], total[:half_rows]))
        return by_core(core, kept, theirs), by_core(core, theirs, kept)

    low, high = whole_rows(attention_total)
    columns = [
        jnp.concatenate([low[:, j * HALF : (j + 1) * HALF], high[:, j * HALF : (j + 1) * HALF]], axis=1)
        for j in range(4)
    ]
    qkv_grad = jnp.concatenate(columns[:3], axis=1).reshape(-1)
    out_grad = columns[3].reshape(-1)
    low, high = whole_rows(up_total)
    up_grad = jnp.concatenate(
        [
            low.reshape(half_rows, CHIPS, UNIT_HALF),
            high.reshape(half_rows, CHIPS, UNIT_HALF)[:, :, : UNIT - UNIT_HALF],
        ],
        axis=2,
    ).reshape(-1)
    down_flat = down_total.reshape(-1)
    returned = lax.ppermute(
        down_flat[down_flat.shape[0] - spill :], "dev", [(i, i + 1) for i in range(0, 2 * CHIPS, 2)]
    )
    down_grad = by_core(
        core,
        down_flat[: down_weight.shape[0]],
        jnp.concatenate([returned, down_flat[: down_weight.shape[0] - spill]]),
    )
    return (
        result.astype(jnp.bfloat16).reshape(tokens.shape),
        grad_input.astype(jnp.bfloat16).reshape(tokens.shape),
        qkv_grad,
        out_grad,
        up_grad,
        down_grad,
        vector_grad,
    )


def solution(mesh):
    local = topo_local if mesh.shape["dev"] == 32 else generic_local
    return jax.shard_map(
        local,
        mesh=mesh,
        in_specs=(
            P(None, "dev", None),
            P(),
            P("dev"),
            P("dev"),
            P("dev"),
            P("dev"),
            P("dev"),
            P(None, "dev", None),
        ),
        out_specs=(
            P(None, "dev", None),
            P(None, "dev", None),
            P("dev"),
            P("dev"),
            P("dev"),
            P("dev"),
            P("dev"),
        ),
        check_vma=False,
    )
```

```python
from functools import partial

import jax
import jax.numpy as jnp
from jax import lax
from jax.experimental import pallas as pl
from jax.experimental.pallas import tpu as pltpu
from jax.sharding import PartitionSpec as P

D = 1152
HEADS = 16
FF = 4304
IMG_LEN = 729


heads_per_block = 4
EPSILON = 1e-06
MASKED = -1e30


def passed_along(block, axis, distance):
    devices = range(lax.axis_size(axis))
    route = [(i - distance, i) for i in devices if i - distance in devices]
    return lax.ppermute(block, axis, route)


def layer_stats(values):
    centered = values - jnp.mean(values, axis=-1, keepdims=True)
    inverse = lax.rsqrt(jnp.mean(centered * centered, axis=-1, keepdims=True) + EPSILON)
    return (centered * inverse, inverse)


def layer_back(grad_output, normed, inverse, gain):
    scaled = grad_output * gain
    return inverse * (
        scaled
        - jnp.mean(scaled, axis=-1, keepdims=True)
        - normed * jnp.mean(scaled * normed, axis=-1, keepdims=True)
    )


def image_of(positions, image_count):
    return jnp.where(positions < image_count * IMG_LEN, positions // IMG_LEN, -positions - 1)


def reach_sizes(shard_rows):
    rim_rows = IMG_LEN - 1
    reach_count = (rim_rows + shard_rows - 1) // shard_rows
    return [
        min(shard_rows, rim_rows - (distance - 1) * shard_rows)
        for distance in range(1, reach_count + 1)
    ]


def widen(key_value, shard_rows):
    edge_sizes = reach_sizes(shard_rows)
    arrived = {}
    for distance, amount in enumerate(edge_sizes, start=1):
        for direction in (1, -1):
            sent_rows = key_value[shard_rows - amount :] if direction > 0 else key_value[:amount]
            arrived[distance, direction] = passed_along(sent_rows, "dev", direction * distance)
    before = [arrived[distance, 1] for distance in range(len(edge_sizes), 0, -1)]
    after = [arrived[distance, -1] for distance in range(1, len(edge_sizes) + 1)]
    return jnp.concatenate(before + [key_value] + after, axis=0)


def return_edges(grad_extended, shard_rows):
    edge_sizes = reach_sizes(shard_rows)
    rim_rows = IMG_LEN - 1
    combined = grad_extended[rim_rows : rim_rows + shard_rows]
    for distance, amount in enumerate(edge_sizes, start=1):
        for direction in (1, -1):
            if direction > 0:
                begin_row = rim_rows - sum(edge_sizes[:distance])
            else:
                begin_row = rim_rows + shard_rows + sum(edge_sizes[: distance - 1])
            arrived = passed_along(
                grad_extended[begin_row : begin_row + amount].astype(jnp.bfloat16),
                "dev",
                -direction * distance,
            ).astype(jnp.float32)
            if direction > 0:
                combined = combined.at[shard_rows - amount :].add(arrived)
            else:
                combined = combined.at[:amount].add(arrived)
    return combined


def key_window(device_index, shard_rows, image_count):
    span_rows = ((shard_rows + IMG_LEN - 2) // IMG_LEN + 1) * IMG_LEN
    shard_start = device_index * shard_rows
    window_start = shard_start // IMG_LEN * IMG_LEN
    offset_rows = window_start - shard_start + IMG_LEN - 1
    query_images = image_of(shard_start + jnp.arange(shard_rows, dtype=jnp.int32), image_count)
    key_images = image_of(window_start + jnp.arange(span_rows, dtype=jnp.int32), image_count)
    return (span_rows, offset_rows, query_images[:, None] == key_images[None, :])


def head_slices(query, window_kv, block_index):
    head_dim = D // HEADS
    block_width = heads_per_block * head_dim
    first_column = block_index * block_width
    query_block = query[:, first_column : first_column + block_width].reshape(
        query.shape[0], heads_per_block, head_dim
    )
    key_block = window_kv[:, first_column : first_column + block_width].reshape(
        window_kv.shape[0], heads_per_block, head_dim
    )
    value_block = window_kv[:, D + first_column : D + first_column + block_width].reshape(
        window_kv.shape[0], heads_per_block, head_dim
    )
    return (query_block, key_block, value_block, first_column, block_width)


def attend(query, window_kv, visible):
    score_scale = (D // HEADS) ** (-0.5)
    outputs, log_sums = ([], [])
    for block_index in range(HEADS // heads_per_block):
        query_block, key_block, value_block, first_column, block_width = head_slices(
            query, window_kv, block_index
        )
        raw_scores = jnp.einsum(
            "qhd,khd->hqk", query_block, key_block, preferred_element_type=jnp.float32
        )
        scores = jnp.where(visible[None], raw_scores * score_scale, MASKED)
        largest = jnp.max(scores, axis=-1, keepdims=True)
        exponent = jnp.exp(scores - largest)
        row_totals = jnp.sum(exponent, axis=-1, keepdims=True)
        probabilities = (exponent / row_totals).astype(jnp.bfloat16)
        log_sums.append(largest + jnp.log(row_totals))
        attended = jnp.einsum(
            "hqk,khd->qhd", probabilities, value_block, preferred_element_type=jnp.float32
        )
        outputs.append(attended.reshape(query.shape[0], block_width))
    return (jnp.concatenate(outputs, axis=1), log_sums)


def attend_back(query, window_kv, visible, log_sums, grad_attended):
    score_scale = (D // HEADS) ** (-0.5)
    grad_queries, grad_keys, grad_values = ([], [], [])
    for block_index in range(HEADS // heads_per_block):
        query_block, key_block, value_block, first_column, block_width = head_slices(
            query, window_kv, block_index
        )
        grad_block = grad_attended[:, first_column : first_column + block_width].reshape(
            query.shape[0], heads_per_block, block_width // heads_per_block
        )
        raw_scores = jnp.einsum(
            "qhd,khd->hqk", query_block, key_block, preferred_element_type=jnp.float32
        )
        scores = jnp.where(visible[None], raw_scores * score_scale, MASKED)
        probabilities = jnp.exp(scores - log_sums[block_index])
        grad_values.append(
            jnp.einsum(
                "hqk,qhd->khd",
                probabilities.astype(jnp.bfloat16),
                grad_block,
                preferred_element_type=jnp.float32,
            ).reshape(window_kv.shape[0], block_width)
        )
        grad_probs = jnp.einsum(
            "qhd,khd->hqk", grad_block, value_block, preferred_element_type=jnp.float32
        )
        inner = jnp.sum(probabilities * grad_probs, axis=-1, keepdims=True)
        grad_raw = (probabilities * (grad_probs - inner) * score_scale).astype(jnp.bfloat16)
        grad_queries.append(
            jnp.einsum(
                "hqk,khd->qhd", grad_raw, key_block, preferred_element_type=jnp.float32
            ).reshape(query.shape[0], block_width)
        )
        grad_keys.append(
            jnp.einsum(
                "hqk,qhd->khd", grad_raw, query_block, preferred_element_type=jnp.float32
            ).reshape(window_kv.shape[0], block_width)
        )
    return (jnp.concatenate(grad_queries, axis=1), jnp.concatenate(grad_keys + grad_values, axis=1))


def unpack(gathered):
    qkv_flat, out_flat, up_flat, down_flat, packed = gathered
    packed = packed.astype(jnp.float32)
    pieces = [packed[segment * D : (segment + 1) * D] for segment in range(8)]
    up_bias = packed[8 * D : 8 * D + FF]
    return (
        qkv_flat.reshape(D, 3 * D),
        out_flat.reshape(D, D),
        up_flat.reshape(D, FF),
        down_flat.reshape(FF, D),
        pieces,
        up_bias,
    )


def forward_batch(tokens_batch, image_count, weights, device_index):
    qkv_w, out_w, up_w, down_w, pieces, up_bias = weights
    shard_rows = tokens_batch.shape[0]
    rim_rows = IMG_LEN - 1
    inputs = tokens_batch.astype(jnp.float32)
    normed_one, inverse_one = layer_stats(inputs)
    hidden_one = (normed_one * pieces[0] + pieces[1]).astype(jnp.bfloat16)
    projected = jnp.dot(hidden_one, qkv_w, preferred_element_type=jnp.float32)
    query = (projected[:, :D] + pieces[2]).astype(jnp.bfloat16)
    key_value = jnp.concatenate(
        [projected[:, D : 2 * D], projected[:, 2 * D :] + pieces[3]], axis=1
    ).astype(jnp.bfloat16)
    extended = widen(key_value, shard_rows)
    span_rows, offset_rows, visible = key_window(device_index, shard_rows, image_count)
    padded = jnp.pad(extended, ((0, rim_rows + span_rows - extended.shape[0]), (0, 0)))
    window_kv = lax.dynamic_slice_in_dim(padded, offset_rows, span_rows, 0)
    attended, log_sums = attend(query, window_kv, visible)
    attended_low = attended.astype(jnp.bfloat16)
    middle = inputs + (jnp.dot(attended_low, out_w, preferred_element_type=jnp.float32) + pieces[4])
    normed_two, inverse_two = layer_stats(middle)
    hidden_two = (normed_two * pieces[5] + pieces[6]).astype(jnp.bfloat16)
    upper = jnp.dot(hidden_two, up_w, preferred_element_type=jnp.float32) + up_bias
    active = jax.nn.gelu(upper, approximate=True).astype(jnp.bfloat16)
    output = middle + (jnp.dot(active, down_w, preferred_element_type=jnp.float32) + pieces[7])
    saved = (
        normed_one,
        inverse_one,
        hidden_one,
        query,
        window_kv,
        offset_rows,
        visible,
        log_sums,
        attended_low,
        normed_two,
        inverse_two,
        hidden_two,
        upper,
        active,
    )
    return (output.astype(jnp.bfloat16), saved)


def backward_batch(grad_output, saved, weights, vector_length):
    qkv_w, out_w, up_w, down_w, pieces, up_bias = weights
    (
        normed_one,
        inverse_one,
        hidden_one,
        query,
        window_kv,
        offset_rows,
        visible,
        log_sums,
        attended_low,
        normed_two,
        inverse_two,
        hidden_two,
        upper,
        active,
    ) = saved
    shard_rows = query.shape[0]
    span_rows = window_kv.shape[0]
    rim_rows = IMG_LEN - 1
    grad_wide = grad_output.astype(jnp.float32)
    grad_down = jnp.einsum("tf,td->fd", active, grad_output, preferred_element_type=jnp.float32)
    grad_down_bias = jnp.sum(grad_wide, axis=0)
    grad_active = jnp.einsum("td,fd->tf", grad_output, down_w, preferred_element_type=jnp.float32)
    gelu_back = jax.vjp(partial(jax.nn.gelu, approximate=True), upper)[1]
    grad_upper = gelu_back(grad_active)[0].astype(jnp.bfloat16)
    grad_up = jnp.einsum("td,tf->df", hidden_two, grad_upper, preferred_element_type=jnp.float32)
    grad_up_bias = jnp.sum(grad_upper.astype(jnp.float32), axis=0)
    grad_hidden_two = jnp.einsum("tf,df->td", grad_upper, up_w, preferred_element_type=jnp.float32)
    grad_gain_two = jnp.sum(grad_hidden_two * normed_two, axis=0)
    grad_bias_two = jnp.sum(grad_hidden_two, axis=0)
    grad_middle = grad_wide + layer_back(grad_hidden_two, normed_two, inverse_two, pieces[5])
    grad_branch = grad_middle.astype(jnp.bfloat16)
    grad_out = jnp.einsum(
        "td,te->de", attended_low, grad_branch, preferred_element_type=jnp.float32
    )
    grad_out_bias = jnp.sum(grad_branch.astype(jnp.float32), axis=0)
    grad_attended = jnp.einsum(
        "te,de->td", grad_branch, out_w, preferred_element_type=jnp.float32
    ).astype(jnp.bfloat16)
    grad_query, grad_window = attend_back(query, window_kv, visible, log_sums, grad_attended)
    grad_padded = lax.dynamic_update_slice_in_dim(
        jnp.zeros((rim_rows + span_rows, 2 * D), jnp.float32), grad_window, offset_rows, 0
    )
    grad_kv = return_edges(grad_padded[: shard_rows + 2 * rim_rows], shard_rows)
    grad_query_low = grad_query.astype(jnp.bfloat16)
    grad_kv_low = grad_kv.astype(jnp.bfloat16)
    grad_projected = jnp.concatenate([grad_query_low, grad_kv_low], axis=1)
    grad_qkv = jnp.einsum(
        "td,te->de", hidden_one, grad_projected, preferred_element_type=jnp.float32
    )
    grad_query_bias = jnp.sum(grad_query_low.astype(jnp.float32), axis=0)
    grad_value_bias = jnp.sum(grad_kv_low[:, D:].astype(jnp.float32), axis=0)
    grad_hidden_one = jnp.einsum(
        "te,de->td", grad_projected, qkv_w, preferred_element_type=jnp.float32
    )
    grad_gain_one = jnp.sum(grad_hidden_one * normed_one, axis=0)
    grad_bias_one = jnp.sum(grad_hidden_one, axis=0)
    grad_input = grad_middle + layer_back(grad_hidden_one, normed_one, inverse_one, pieces[0])
    vector_grad = jnp.concatenate(
        [
            grad_gain_one,
            grad_bias_one,
            grad_query_bias,
            grad_value_bias,
            grad_out_bias,
            grad_gain_two,
            grad_bias_two,
            grad_down_bias,
            grad_up_bias,
            jnp.zeros((vector_length - 8 * D - FF,), jnp.float32),
        ]
    )
    flat_grads = (
        grad_qkv.reshape(-1),
        grad_out.reshape(-1),
        grad_up.reshape(-1),
        grad_down.reshape(-1),
        vector_grad,
    )
    return (grad_input.astype(jnp.bfloat16), flat_grads)


def generic_local(tokens, counts, qkv_weight, out_weight, up_weight, down_weight, vectors, cotangent):
    device_index = lax.axis_index("dev")
    vector_length = vectors.shape[0] * lax.axis_size("dev")
    gathered = (
        lax.all_gather(qkv_weight, "dev", axis=0, tiled=True),
        lax.all_gather(out_weight, "dev", axis=0, tiled=True),
        lax.all_gather(up_weight, "dev", axis=0, tiled=True),
        lax.all_gather(down_weight, "dev", axis=0, tiled=True),
        lax.all_gather(vectors, "dev", axis=0, tiled=True),
    )
    weights = unpack(gathered)
    results, kept_state = ([], [])
    for batch_index in range(tokens.shape[0]):
        output, saved = forward_batch(
            tokens[batch_index], counts[batch_index], weights, device_index
        )
        results.append(output)
        kept_state.append(saved)
    weights = unpack(
        (
            lax.all_gather(qkv_weight, "dev", axis=0, tiled=True),
            lax.all_gather(out_weight, "dev", axis=0, tiled=True),
            lax.all_gather(up_weight, "dev", axis=0, tiled=True),
            lax.all_gather(down_weight, "dev", axis=0, tiled=True),
            lax.all_gather(vectors, "dev", axis=0, tiled=True),
        )
    )
    grad_inputs = []
    totals = None
    for batch_index in range(tokens.shape[0]):
        grad_input, flat_grads = backward_batch(
            cotangent[batch_index], kept_state[batch_index], weights, vector_length
        )
        grad_inputs.append(grad_input)
        totals = (
            flat_grads
            if totals is None
            else tuple((earlier + current for earlier, current in zip(totals, flat_grads)))
        )
    totals = lax.psum_scatter(totals, "dev", scatter_dimension=0, tiled=True)
    return (
        jnp.stack(results),
        jnp.stack(grad_inputs),
        totals[0],
        totals[1],
        totals[2],
        totals[3],
        totals[4],
    )


CHIPS = 16
HEAD = D // HEADS
HALF = D // 2
CORE_HEADS = HEADS // 2
ROWS = D // CHIPS
UNIT = FF // CHIPS
UNIT_HALF = 136
FFH = CHIPS * UNIT_HALF
SHARD = 256
CHIP_ROWS = 2 * SHARD
TILE = 128
CHUNK = 16
SPAN = 768
SPAN_CHUNKS = SPAN // CHUNK
SHARD_CHUNKS = SHARD // CHUNK
SPAN_DEVICES = 4
TOKENS = 2 * CHIPS * SHARD
SCALE = HEAD**-0.5


def route(target):
    return [(i, target(i)) for i in range(2 * CHIPS)]


def swap(block):
    return lax.ppermute(block, "dev", route(lambda i: i ^ 1))


def by_core(core, first, second):
    return jnp.where(core == 0, first, second)


def joined(core, mine, theirs, axis):
    return by_core(
        core,
        jnp.concatenate([mine, theirs], axis=axis),
        jnp.concatenate([theirs, mine], axis=axis),
    )


def head_lanes(head):
    first = head * HEAD
    low = first // 128 * 128
    high = min((first + HEAD + 127) // 128 * 128, HALF)
    return low, high, first - low


def head_mask(head):
    low, high, skip = head_lanes(head)
    lanes = lax.broadcasted_iota(jnp.int32, (1, high - low), 1)
    return (lanes >= skip) & (lanes < skip + HEAD)


NT = (((1,), (1,)), ((), ()))
NN = (((1,), (0,)), ((), ()))
TN = (((0,), (0,)), ((), ()))


def mm(left, right, dims):
    return lax.dot_general(left, right, dims, preferred_element_type=jnp.float32)


def image_of_chip(chip):
    image = (CHIP_ROWS * chip + IMG_LEN // 2) // IMG_LEN
    has = owner_of_image(image) == chip
    first = image * IMG_LEN // CHUNK
    last = jnp.minimum((image * IMG_LEN + IMG_LEN - 1) // CHUNK, TOKENS // CHUNK - 1)
    return image, has, first, jnp.where(has, last - first + 1, 0)


def owner_of_image(image):
    return jnp.minimum((image * IMG_LEN + IMG_LEN // 2) // CHIP_ROWS, CHIPS - 1)


def in_image(image, has, first, rows, axis):
    shape = (rows, 1) if axis == 0 else (1, rows)
    at = first * CHUNK + lax.broadcasted_iota(jnp.int32, shape, axis)
    there = (at >= image * IMG_LEN) & (at < jnp.minimum((image + 1) * IMG_LEN, TOKENS))
    return there & has


def diagonal_tile(tile):
    row = tile * TILE + lax.broadcasted_iota(jnp.int32, (TILE, SPAN), 0)
    return row == lax.broadcasted_iota(jnp.int32, (TILE, SPAN), 1)


def attend_tile(image, has, first, batch, tile, live, q_ref, k_ref, v_ref, att_ref, lse_ref, acc):
    rows = pl.ds(pl.multiple_of(tile * TILE, TILE), TILE)
    visible = in_image(image, has, first, SPAN, 1) & (live | diagonal_tile(tile))
    stats = jnp.zeros((TILE, 128), jnp.float32)
    lane = lax.broadcasted_iota(jnp.int32, (TILE, 128), 1)
    acc[...] = jnp.zeros_like(acc)
    for head in range(CORE_HEADS):
        low, high, _ = head_lanes(head)
        mask = head_mask(head)
        query = jnp.where(mask, q_ref[batch, rows, low:high], 0)
        scores = jnp.where(visible, mm(query, k_ref[batch, :, low:high], NT) * SCALE, MASKED)
        largest = jnp.max(scores, axis=1, keepdims=True)
        exponent = jnp.exp(scores - largest)
        total = jnp.sum(exponent, axis=1, keepdims=True)
        probs = (exponent * (1.0 / total)).astype(jnp.bfloat16)
        part = mm(probs, v_ref[batch, :, low:high], NN)
        acc[:, low:high] += jnp.where(mask, part, 0.0)
        stats = jnp.where(lane == head, largest + jnp.log(total), stats)
    lse_ref[batch, rows] = stats
    att_ref[batch, rows] = acc[...].astype(jnp.bfloat16)


class Scatter:
    def __init__(self, place, grad_ref, total_ref, split, scratch):
        self.core, self.x, self.y, self.z = place
        self.grad_ref, self.total_ref, self.split = grad_ref, total_ref, split
        (self.half_x, self.half_y, self.whole_x, self.whole_y, self.from_z) = scratch[:5]
        (self.half_out, self.half_in, self.pair_out, self.pair_in, self.z_out, self.z_in) = scratch[5:]

    @staticmethod
    def scratch(shape, split):
        rows, columns = shape[1:]
        dma = pltpu.SemaphoreType.DMA
        block = lambda count, width: pltpu.VMEM((count, rows, width), jnp.bfloat16)
        return (
            [block(4, split), block(4, columns - split)]
            + [block(4, columns), block(4, columns), block(3, columns)]
            + [dma((2, 4)), dma((2, 4)), dma((2, 4)), dma((2, 4)), dma((3,)), dma((3,))]
        )

    COUNT = 11

    def unit(self, at_x, at_y, turn):
        at_z = (self.z + 1 + turn) % 4
        return self.grad_ref.at[(at_z * 2 + at_y) * 2 + at_x]

    def remote(self, source, target_ref, send_sem, recv_sem, device):
        return pltpu.make_async_remote_copy(
            src_ref=source,
            dst_ref=target_ref,
            send_sem=send_sem,
            recv_sem=recv_sem,
            device_id=device,
            device_id_type=MESH_ID,
        )

    def half(self, turn, axis):
        diagonal = self.unit(1 - self.x, 1 - self.y, turn)
        columns = self.grad_ref.shape[2]
        source = diagonal.at[:, pl.ds(0, self.split) if axis == 0 else pl.ds(self.split, columns - self.split)]
        device = (peer(1 - self.x, self.y, self.z, self.core), peer(self.x, 1 - self.y, self.z, self.core))[axis]
        target = (self.half_x, self.half_y)[axis].at[turn]
        return self.remote(source, target, self.half_out.at[axis, turn], self.half_in.at[axis, turn], device)

    def whole(self, turn, axis):
        device = (peer(1 - self.x, self.y, self.z, self.core), peer(self.x, 1 - self.y, self.z, self.core))[axis]
        source = (self.unit(1 - self.x, self.y, turn), self.unit(self.x, 1 - self.y, turn))[axis]
        target = (self.whole_x, self.whole_y)[axis]
        return self.remote(
            source, target.at[turn], self.pair_out.at[axis, turn], self.pair_in.at[axis, turn], device
        )

    def along(self, turn):
        device = peer(self.x, self.y, (self.z + 1 + turn) % 4, self.core)
        return self.remote(self.unit(self.x, self.y, turn), self.from_z.at[turn], self.z_out.at[turn], self.z_in.at[turn], device)

    def begin(self, turn):
        self.half(turn, 0).start()
        self.half(turn, 1).start()

    def pair(self, turn):
        split = self.split
        wide = lambda value: value.astype(jnp.float32)
        self.half(turn, 0).wait_recv()
        grad = self.unit(self.x, 1 - self.y, turn)
        grad[:, :split] = (wide(grad[:, :split]) + wide(self.half_x[turn])).astype(jnp.bfloat16)
        self.whole(turn, 1).start()
        self.half(turn, 1).wait_recv()
        grad = self.unit(1 - self.x, self.y, turn)
        grad[:, split:] = (wide(grad[:, split:]) + wide(self.half_y[turn])).astype(jnp.bfloat16)
        self.whole(turn, 0).start()

    def join(self, turn):
        wide = lambda value: value.astype(jnp.float32)
        self.whole(turn, 0).wait_recv()
        self.whole(turn, 1).wait_recv()
        own = self.unit(self.x, self.y, turn)
        total = wide(own[...]) + (wide(self.whole_x[turn]) + wide(self.whole_y[turn]))

        @pl.when(turn < 3)
        def _():
            own[...] = total.astype(jnp.bfloat16)
            self.along(turn).start()

        @pl.when(turn == 3)
        def _():
            self.total_ref[...] = total

    def total(self, turn):
        self.along(turn).wait_recv()
        self.total_ref[...] += self.from_z[turn].astype(jnp.float32)

    def finish(self):
        def pairs(turn, carry):
            for axis in range(2):
                self.half(turn, axis).wait_send()
                self.whole(turn, axis).wait_send()
            return carry

        def lines(turn, carry):
            self.along(turn).wait_send()
            return carry

        lax.fori_loop(0, 4, pairs, 0)
        lax.fori_loop(0, 3, lines, 0)


def each_turn(action, count=4):
    def body(turn, carry):
        action(turn)
        return carry

    lax.fori_loop(0, count, body, 0)


def attend_back_tile(
    image, has, first, batch, tile, live,
    q_ref, k_ref, v_ref, g_ref, stt_ref, dq_acc, dk_acc, dv_acc,
):
    rows = pl.ds(pl.multiple_of(tile * TILE, TILE), TILE)
    queries_there = in_image(image, has, first, SPAN, 1)
    at = first * CHUNK + tile * TILE + lax.broadcasted_iota(jnp.int32, (TILE, 1), 0)
    keys_there = (at >= image * IMG_LEN) & (at < jnp.minimum((image + 1) * IMG_LEN, TOKENS)) & has
    visible = queries_there & keys_there & (live | diagonal_tile(tile))
    dk_acc[...] = jnp.zeros_like(dk_acc)
    dv_acc[...] = jnp.zeros_like(dv_acc)

    @pl.when(tile == 0)
    def _():
        dq_acc[...] = jnp.zeros_like(dq_acc)

    for head in range(CORE_HEADS):
        low, high, _ = head_lanes(head)
        mask = head_mask(head)
        keys = jnp.where(mask, k_ref[batch, rows, low:high], 0)
        values = jnp.where(mask, v_ref[batch, rows, low:high], 0)
        queries = q_ref[batch, :, low:high]
        grads = g_ref[batch, :, low:high]
        lse = stt_ref[batch, head : head + 1]
        delta = stt_ref[batch, CORE_HEADS + head : CORE_HEADS + head + 1]
        probs = jnp.where(visible, jnp.exp(mm(keys, queries, NT) * SCALE - lse), 0.0)
        dv_acc[:, low:high] += jnp.where(mask, mm(probs.astype(jnp.bfloat16), grads, NN), 0.0)
        grad_probs = mm(values, grads, NT)
        grad_raw = (probs * (grad_probs - delta) * SCALE).astype(jnp.bfloat16)
        dk_acc[:, low:high] += jnp.where(mask, mm(grad_raw, queries, NN), 0.0)
        dq_acc[:, low:high] += mm(grad_raw, keys, TN)
    k_ref[batch, rows] = dk_acc[...].astype(jnp.bfloat16)
    v_ref[batch, rows] = dv_acc[...].astype(jnp.bfloat16)

    @pl.when(tile == SPAN // TILE - 1)
    def _():
        q_ref[batch] = dq_acc[:, :HALF].astype(jnp.bfloat16)


BACK_SPLITS = (640, 1152, 256, 896)


class Rows:
    def __init__(self, place):
        core, x, y, z = place
        self.core = core
        self.chip = (z * 2 + y) * 2 + x
        self.device = self.chip * 2 + core
        self.image, self.has, self.first, self.count = image_of_chip(self.chip)
        start = self.device * SHARD
        images = [start // IMG_LEN, (start + SHARD - 1) // IMG_LEN]
        self.parts = []
        for part, image in enumerate(images):
            low = jnp.maximum(image * IMG_LEN - start, 0) // CHUNK
            high = jnp.minimum((image + 1) * IMG_LEN - 1 - start, SHARD - 1) // CHUNK + 1
            if part == 1:
                high = jnp.where(images[1] == images[0], low, high)
            self.parts.append((owner_of_image(image), image * IMG_LEN // CHUNK, low, high))

    def peers(self):
        holders = [
            ((self.first // SHARD_CHUNKS + n,), self.holds(n)) for n in range(SPAN_DEVICES)
        ]
        images = [
            ((owner * 2 + side,), jnp.logical_and(high > low, owner * 2 + side != self.device))
            for owner, _, low, high in self.parts
            for side in range(2)
        ]
        return holders + images

    def holds(self, n):
        device = self.first // SHARD_CHUNKS + n
        last = (self.first + self.count - 1) // SHARD_CHUNKS
        there = jnp.logical_and(self.count > 0, device <= last)
        return jnp.logical_and(there, device != self.device)

    @staticmethod
    def scratch():
        dma = pltpu.SemaphoreType.DMA
        return [dma((2, 2, SHARD_CHUNKS)), dma((SPAN_CHUNKS,))]

    def span_rows(self, ref, chunk):
        return ref.at[:, pl.ds(pl.multiple_of(chunk * CHUNK, CHUNK), CHUNK)]

    def chunk_rows(self, ref, chunk):
        return ref.at[pl.ds(pl.multiple_of(chunk * CHUNK, CHUNK), CHUNK)]

    def each_own(self, action):
        for part, (owner, first, low, high) in enumerate(self.parts):
            for side in range(2):
                def body(chunk, carry):
                    action(part, side, chunk, owner * 2 + side, self.device * SHARD_CHUNKS + chunk - first)
                    return carry

                lax.fori_loop(low, high, body, 0)

    def each_span(self, action):
        def body(chunk, carry):
            at = self.first + chunk
            device = at // SHARD_CHUNKS
            part = jnp.where(device * SHARD // IMG_LEN == self.image, 0, 1)
            action(chunk, device, at % SHARD_CHUNKS, part)
            return carry

        lax.fori_loop(0, self.count, body, 0)

    def elsewhere(self, device, action, here):
        @pl.when(device != self.device)
        def _():
            action()

        if here is not None:
            @pl.when(device == self.device)
            def _():
                here()

    def to_images(self, sources, span_ref, sems):
        token_sems, span_sems = sems

        def start(part, side, chunk, device, at):
            source, target = self.span_rows(sources[side], chunk), self.span_rows(span_ref, at)
            copy = remote(source, target, token_sems.at[part, side, chunk], span_sems.at[at], (device,))
            self.elsewhere(device, copy.start, pltpu.make_async_copy(source, target, span_sems.at[at]).start)

        self.each_own(start)

    def images_arrived(self, sources, span_ref, sems):
        token_sems, span_sems = sems

        def wait(chunk, device, at, part):
            block = self.span_rows(span_ref, chunk)
            span_sem = span_sems.at[chunk]
            copy = remote(block, block, token_sems.at[0, 0, 0], span_sem, (device,))
            local = pltpu.make_async_copy(self.span_rows(sources[0], at), block, span_sem)
            self.elsewhere(device, copy.wait_recv, local.wait)

        def sent(part, side, chunk, device, at):
            source = self.span_rows(sources[side], chunk)
            copy = remote(source, source, token_sems.at[part, side, chunk], span_sems.at[0], (device,))
            self.elsewhere(device, copy.wait_send, None)

        self.each_span(wait)
        self.each_own(sent)

    def to_both(self, own_ref, span_ref, sems):
        token_sems, span_sems, _, _ = sems

        def start(part, side, chunk, device, at):
            source, target = self.span_rows(own_ref, chunk), self.span_rows(span_ref, at)
            copy = remote(source, target, token_sems.at[part, 0, chunk], span_sems.at[at], (device,))

            def here():
                target[...] = source[...]

            @pl.when(side == self.core)
            def _():
                self.elsewhere(device, copy.start, here)

        self.each_own(start)

    def trade(self, span_ref, chunk, sems):
        block = self.span_rows(span_ref, chunk)
        return remote(block, block, sems[2].at[chunk], sems[3].at[chunk], (self.chip * 2 + 1 - self.core,))

    def relay(self, span_ref, sems):
        token_sems, span_sems, _, _ = sems

        def pass_on(chunk, device, at, part):
            block = self.span_rows(span_ref, chunk)
            copy = remote(block, block, token_sems.at[0, 0, 0], span_sems.at[chunk], (device,))

            @pl.when(device % 2 == self.core)
            def _():
                self.elsewhere(device, copy.wait_recv, None)
                self.trade(span_ref, chunk, sems).start()

        self.each_span(pass_on)

    def both_arrived(self, own_ref, span_ref, sems):
        token_sems, span_sems, _, _ = sems

        def traded(chunk, device, at, part):
            @pl.when(device % 2 == self.core)
            def _():
                self.trade(span_ref, chunk, sems).wait_send()

            @pl.when(device % 2 != self.core)
            def _():
                self.trade(span_ref, chunk, sems).wait_recv()

        def sent(part, side, chunk, device, at):
            source = self.span_rows(own_ref, chunk)
            copy = remote(source, source, token_sems.at[part, 0, chunk], span_sems.at[0], (device,))

            @pl.when(side == self.core)
            def _():
                self.elsewhere(device, copy.wait_send, None)

        self.each_span(traded)
        self.each_own(sent)

    def batch_to_tokens(self, span_ref, landing, sems):
        token_sems, span_sems = sems

        def start(chunk, device, at, part):
            source, target = self.chunk_rows(span_ref, chunk), self.chunk_rows(landing.at[part, self.core], at)
            token_sem = token_sems.at[part, self.core, at]
            copy = remote(source, target, span_sems.at[chunk], token_sem, (device,))
            self.elsewhere(device, copy.start, pltpu.make_async_copy(source, target, token_sem).start)

        self.each_span(start)

    def batches_arrived(self, span_ref, landing, sems):
        token_sems, span_sems = sems

        def wait(part, side, chunk, device, at):
            source, target = self.chunk_rows(span_ref, at), self.chunk_rows(landing.at[part, side], chunk)
            token_sem = token_sems.at[part, side, chunk]
            copy = remote(target, target, span_sems.at[0], token_sem, (device,))
            self.elsewhere(device, copy.wait_recv, pltpu.make_async_copy(source, target, token_sem).wait)

        def sent(chunk, device, at, part):
            block = self.chunk_rows(span_ref, chunk)
            copy = remote(block, block, span_sems.at[chunk], token_sems.at[0, 0, 0], (device,))
            self.elsewhere(device, copy.wait_send, None)

        self.each_own(wait)
        self.each_span(sent)

    def to_tokens(self, span_ref, landing, sems):
        token_sems, span_sems = sems

        def start(chunk, device, at, part):
            source = self.span_rows(span_ref, chunk)
            target = self.span_rows(landing.at[part, self.core], at)
            copy = remote(source, target, span_sems.at[chunk], token_sems.at[part, self.core, at], (device,))

            def here():
                target[...] = source[...]

            self.elsewhere(device, copy.start, here)

        self.each_span(start)

    def tokens_arrived(self, span_ref, landing, sems):
        token_sems, span_sems = sems

        def wait(part, side, chunk, device, at):
            block = self.span_rows(landing.at[part, side], chunk)
            copy = remote(block, block, span_sems.at[0], token_sems.at[part, side, chunk], (device,))
            self.elsewhere(device, copy.wait_recv, None)

        def sent(chunk, device, at, part):
            block = self.span_rows(span_ref, chunk)
            copy = remote(block, block, span_sems.at[chunk], token_sems.at[0, 0, 0], (device,))
            self.elsewhere(device, copy.wait_send, None)

        self.each_own(wait)
        self.each_span(sent)


def backward_kernel(
    counts, q_in, k_in, v_in, hidden_in, weight_in, att_ref, lse_ref, low_ref, high_ref, down_in, up_in, out_in,
    dq_out, dk_out, dv_out, landing, down_total, up_total, out_total, qkv_total,
    q_ref, k_ref, v_ref, hidden, weight, arrived, down_ref, up_ref, out_ref, qkv_ref,
    dq_acc, dk_acc, dv_acc, span, stt_ref, load_sems, token_sems, span_sems, back_token_sems, back_span_sems,
    swap_out, swap_in, *scratch
):
    place = position_of()
    rows = Rows(place)
    pairs = [
        (down_in, down_ref), (q_in, q_ref), (k_in, k_ref), (v_in, v_ref), (up_in, up_ref), (hidden_in, hidden), (out_in, out_ref), (weight_in, weight)
    ]
    loads = [pltpu.make_async_copy(a, b, load_sems.at[n]) for n, (a, b) in enumerate(pairs)]
    for load in loads:
        load.start()
    greet(pair_peers(*place) + line_peers(*place) + [(partner_of(*place), True)] + rows.peers())
    sems, sources = (token_sems, span_sems), (low_ref, high_ref)
    rows.to_images(sources, span, sems)
    count = Scatter.COUNT
    down, up, out, qkv = [
        Scatter(place, grad, total, split, scratch[n * count : (n + 1) * count])
        for n, (grad, total, split) in enumerate(
            zip((down_ref, up_ref, out_ref, qkv_ref), (down_total, up_total, out_total, qkv_total), BACK_SPLITS)
        )
    ]
    loads[0].wait()
    each_turn(down.begin)
    for load in loads[1:]:
        load.wait()
    rows.images_arrived(sources, span, sems)
    batches = q_ref.shape[0]

    def prepare(batch, carry):
        there = in_image(rows.image, rows.has, rows.first, SPAN, 0)
        grads = jnp.where(there, span[batch], 0)
        span[batch] = grads
        lane = lax.broadcasted_iota(jnp.int32, (SPAN, 128), 1)
        stats = jnp.where(lane < CORE_HEADS, lse_ref[batch], 0.0)
        for head in range(CORE_HEADS):
            low, high, _ = head_lanes(head)
            product = grads[:, low:high].astype(jnp.float32) * att_ref[batch, :, low:high].astype(jnp.float32)
            total = jnp.sum(jnp.where(head_mask(head), product, 0.0), axis=1, keepdims=True)
            stats = jnp.where(lane == CORE_HEADS + head, total, stats)
        stt_ref[batch] = stats.T[: 2 * CORE_HEADS]
        return carry

    lax.fori_loop(0, batches, prepare, 0)
    tiles = SPAN // TILE
    work = {
        0: [(down.pair, 0, 2)],
        1: [(down.pair, 2, 3)],
        2: [(down.pair, 3, 4), (up.begin, 0, 2)],
        4: [(down.join, 0, 1), (up.begin, 2, 4)],
        6: [(down.join, 1, 2)],
        8: [(down.join, 2, 3), (up.pair, 0, 1)],
        10: [(down.join, 3, 4), (up.pair, 1, 2)],
        11: [(up.pair, 2, 3), (out.begin, 0, 4)],
    }

    def loop(action, first, last):
        def body(turn, carry):
            action(turn)
            return carry

        lax.fori_loop(first, last, body, 0)

    def attend(index, carry):
        batch, tile = index // tiles, index % tiles
        attend_back_tile(
            rows.image, rows.has, rows.first, batch, tile, rows.image < counts[batch],
            q_ref, k_ref, v_ref, span, stt_ref, dq_acc, dk_acc, dv_acc,
        )
        for at, actions in work.items():
            @pl.when(index == at)
            def _():
                for action, first, last in actions:
                    loop(action, first, last)
        return carry

    lax.fori_loop(0, batches * tiles, attend, 0)
    stores = [
        pltpu.make_async_copy(a, b, load_sems.at[n]) for n, (a, b) in enumerate([(q_ref, dq_out), (k_ref, dk_out), (v_ref, dv_out)])
    ]
    for store in stores:
        store.start()

    def weight_grad(first, end, grads):
        for half in range(2):
            units = slice(half * CHIPS // 2, (half + 1) * CHIPS // 2)
            for batch in range(batches):
                part = mm(hidden[batch, :, half * HALF : (half + 1) * HALF], grads(batch), TN)
                if batch == 0:
                    dq_acc[:HALF, : end - first] = part
                else:
                    dq_acc[:HALF, : end - first] += part
            total = dq_acc[:HALF, : end - first].reshape(CHIPS // 2, ROWS, end - first)
            qkv_ref[units, :, first:end] = total.astype(jnp.bfloat16)

    weight_grad(0, 640, lambda batch: jnp.concatenate([q_ref[batch], k_ref[batch, :, :64]], axis=1))
    weight_grad(640, D, lambda batch: k_ref[batch, :, 64:])
    loop(up.pair, 3, 4)
    loop(up.join, 0, 1)
    weight_grad(D, 3 * HALF, lambda batch: v_ref[batch])
    each_turn(qkv.begin)

    def token_grad(batch, others):
        def block(index, carry):
            here = pl.ds(pl.multiple_of(index * TILE, TILE), TILE)
            grads = jnp.concatenate([ref[batch, here] for ref in (q_ref, k_ref, v_ref)], axis=1)
            total = mm(grads, weight[...], NT)
            if others is not None:
                total = total + others[here].astype(jnp.float32)
            hidden[batch, here] = total.astype(jnp.bfloat16)
            return carry

        lax.fori_loop(0, SPAN // TILE, block, 0)

    core = place[0]
    token_grad(1 - core, None)
    trade = remote(hidden.at[1 - core], arrived, swap_out, swap_in, partner_of(*place))
    trade.start()
    loop(up.join, 1, 2)
    trade.wait_recv()
    token_grad(core, arrived)
    back_sems = (back_token_sems, back_span_sems)
    rows.batch_to_tokens(hidden.at[core], landing, back_sems)
    each_turn(out.pair)
    loop(up.join, 2, 4)
    each_turn(out.join)
    each_turn(qkv.pair)
    each_turn(down.total, 3)
    each_turn(qkv.join)
    each_turn(up.total, 3)
    each_turn(out.total, 3)
    each_turn(qkv.total, 3)
    trade.wait_send()
    rows.batches_arrived(hidden.at[core], landing, back_sems)
    for store in stores:
        store.wait()
    for scatter in (down, up, out, qkv):
        scatter.finish()


def backward(counts, query, keys, values, hidden, weight, attended, lse, low, high, down, up, out, collective_id):
    batches = query.shape[0]
    vmem, hbm = pl.BlockSpec(memory_space=pltpu.VMEM), pl.BlockSpec(memory_space=pl.ANY)
    rows = jax.ShapeDtypeStruct((batches, SPAN, HALF), jnp.bfloat16)
    qkv_shape = (CHIPS, ROWS, 3 * HALF)
    shapes = [g.shape for g in (down, up, out)] + [qkv_shape]
    held = lambda *shape: pltpu.VMEM(shape, jnp.bfloat16)
    return pl.pallas_call(
        backward_kernel,
        out_shape=[rows] * 3
        + [jax.ShapeDtypeStruct((2, batches, SHARD, D), jnp.bfloat16)]
        + [jax.ShapeDtypeStruct(shape[1:], jnp.float32) for shape in shapes],
        in_specs=[pl.BlockSpec(memory_space=pltpu.SMEM)] + [hbm] * 5 + [vmem] * 2 + [hbm] * 5,
        out_specs=[hbm] * 4 + [vmem] * 4,
        scratch_shapes=[held(batches, SPAN, HALF)] * 3
        + [held(batches, SPAN, D), held(D, 3 * HALF), held(SPAN, D)]
        + [held(*shape) for shape in shapes]
        + [
            pltpu.VMEM((SPAN, HALF + 64), jnp.float32),
            pltpu.VMEM((TILE, HALF), jnp.float32),
            pltpu.VMEM((TILE, HALF), jnp.float32),
            held(batches, SPAN, HALF),
            pltpu.VMEM((batches, 2 * CORE_HEADS, SPAN), jnp.float32),
            pltpu.SemaphoreType.DMA((8,)),
        ]
        + Rows.scratch() * 2
        + [pltpu.SemaphoreType.DMA] * 2
        + sum([Scatter.scratch(shape, split) for shape, split in zip(shapes, BACK_SPLITS)], []),
        compiler_params=pltpu.CompilerParams(
            collective_id=collective_id, has_side_effects=True, vmem_limit_bytes=60 * 1024 * 1024
        ),
        cost_estimate=pl.CostEstimate(flops=0, bytes_accessed=500 * 10**6, transcendentals=0),
        name="backward",
    )(counts, query, keys, values, hidden, weight, attended, lse, low, high, down, up, out)


def chip_unit(core, low, high):
    theirs = swap(by_core(core, high, low))
    return joined(core, by_core(core, low, high), theirs, 0)


def peer(x, y, z, core):
    return (((z * 2 + y) * 2 + x) * 2 + core,)


MESH_ID = pl.DeviceIdType.MESH


def position_of():
    device = lax.axis_index("dev")
    return device % 2, device // 2 % 2, device // 4 % 2, device // 8


def greet(targets):
    barrier = pltpu.get_barrier_semaphore()
    count = 0
    for target, there in targets:
        if there is True:
            pl.semaphore_signal(barrier, inc=1, device_id=target, device_id_type=MESH_ID)
            count = count + 1
        else:
            @pl.when(there)
            def _():
                pl.semaphore_signal(barrier, inc=1, device_id=target, device_id_type=MESH_ID)
            count = count + there.astype(jnp.int32)
    pl.semaphore_wait(barrier, count)


def pair_peers(core, x, y, z):
    return [(peer(1 - x, y, z, core), True), (peer(x, 1 - y, z, core), True)]


def next_peers(core, x, y, z):
    return [(peer(x, y, z - 1, core), z > 0), (peer(x, y, z + 1, core), z < 3)]


def line_peers(core, x, y, z):
    return [(peer(x, y, (z + step) % 4, core), True) for step in (1, 2, 3)]


def partner_of(core, x, y, z):
    return peer(x, y, z, 1 - core)


class Gather:
    def __init__(self, place, unit_ref, full_ref, other_ref, split, sems):
        self.core, self.x, self.y, self.z = place
        self.unit_ref, self.full_ref, self.other_ref, self.split = unit_ref, full_ref, other_ref, split
        (
            self.z_out,
            self.z_in,
            self.pair_out,
            self.pair_in,
            self.half_out,
            self.half_in,
            self.chain_out,
            self.chain_in,
            self.own_sem,
        ) = sems[:9]
        if other_ref is not None:
            self.swap_out, self.swap_in = sems[9:]
        self.sides = ((-1, self.z > 0), (1, self.z < 3))
        self.x_peer = peer(1 - self.x, self.y, self.z, self.core)
        self.y_peer = peer(self.x, 1 - self.y, self.z, self.core)

    @staticmethod
    def scratch(partner):
        dma = pltpu.SemaphoreType.DMA
        shapes = [(2, 4), (4,), (2, 4), (2, 4), (2, 4), (2, 4), (2, 4), (4,)]
        return [dma(shape) for shape in shapes] + [dma] + ([dma((CHIPS,))] * 2 if partner else [])

    def unit_index(self, at_x, at_y, at_z):
        return (at_z * 2 + at_y) * 2 + at_x

    def slot(self, at_x, at_y, at_z):
        return self.full_ref.at[self.unit_index(at_x, at_y, at_z)]

    def column(self, turn, at_z):
        at_x, at_y = [(self.x, self.y), (self.x, 1 - self.y), (1 - self.x, self.y), (1 - self.x, 1 - self.y)][turn]
        return self.slot(at_x, at_y, at_z)

    def copy(self, block, send_sem, recv_sem, target, source=None):
        return pltpu.make_async_remote_copy(
            src_ref=block if source is None else source,
            dst_ref=block,
            send_sem=send_sem,
            recv_sem=recv_sem,
            device_id=target,
            device_id_type=MESH_ID,
        )

    def along(self, at_z, side, source=None):
        index = 0 if side < 0 else 1
        target = peer(self.x, self.y, self.z + side, self.core)
        return self.copy(self.column(0, at_z), self.z_out.at[index, at_z], self.z_in.at[at_z], target, source)

    def chain(self, at_z, side):
        index = 0 if side < 0 else 1
        target = peer(self.x, self.y, self.z + side, self.core)
        return self.copy(self.column(3, at_z), self.chain_out.at[index, at_z], self.chain_in.at[at_z], target)

    def whole(self, at_z, axis, source=None):
        target = (self.x_peer, self.y_peer)[axis]
        return self.copy(self.column(0, at_z), self.pair_out.at[axis, at_z], self.pair_in.at[axis, at_z], target, source)

    def part(self, block, axis):
        width = self.full_ref.shape[2]
        return block.at[:, pl.ds(0, self.split) if axis == 0 else pl.ds(self.split, width - self.split)]

    def half(self, at_z, axis):
        block = self.part(self.column(1 + axis, at_z), axis)
        target = (self.x_peer, self.y_peer)[axis]
        return self.copy(block, self.half_out.at[axis, at_z], self.half_in.at[axis, at_z], target)

    def half_arrival(self, at_z, axis):
        block = self.part(self.column(3, at_z), axis)
        return self.copy(block, self.half_out.at[axis, at_z], self.half_in.at[axis, at_z], self.x_peer)

    def by_halves(self, at_z):
        near = jnp.logical_and(jnp.abs(at_z - self.z) == 1, jnp.logical_or(at_z == 1, at_z == 2))
        return jnp.logical_or(at_z == self.z, near)

    def trade(self, turn, at_z, source=None):
        at_x, at_y = [(self.x, self.y), (self.x, 1 - self.y), (1 - self.x, self.y), (1 - self.x, 1 - self.y)][turn]
        index = self.unit_index(at_x, at_y, at_z)
        block = self.full_ref.at[index] if source is None else source
        width = self.other_ref.shape[2]
        if width < self.full_ref.shape[2]:
            block = block.at[:, pl.ds(0, width)]
        return pltpu.make_async_remote_copy(
            src_ref=block,
            dst_ref=self.other_ref.at[index],
            send_sem=self.swap_out.at[index],
            recv_sem=self.swap_in.at[index],
            device_id=peer(self.x, self.y, self.z, 1 - self.core),
            device_id_type=MESH_ID,
        )

    def share(self, turn, at_z, source=None):
        if self.other_ref is not None:
            self.trade(turn, at_z, source).start()

    def each(self, distance, action):
        if distance == 0:
            action(self.z, 0)
            return
        for side in (-1, 1):
            at_z = self.z + side * distance
            @pl.when(jnp.logical_and(at_z >= 0, at_z <= 3))
            def _():
                action(at_z, side)

    def onwards(self, side, action):
        for to, there in self.sides:
            if side == 0 or to == -side:
                @pl.when(there)
                def _():
                    action(to)

    def arrive(self, at_z, side):
        source = None
        if side == 0:
            source = self.unit_ref
            pltpu.make_async_copy(self.unit_ref, self.column(0, at_z), self.own_sem).start()
        else:
            self.along(at_z, side).wait_recv()
        self.onwards(side, lambda to: self.along(at_z, to, source).start())
        self.whole(at_z, 0, source).start()
        self.whole(at_z, 1, source).start()
        self.share(0, at_z, source)

    def cross(self, at_z, side):
        for axis in (1, 0):
            arrived = self.column(2 - axis, at_z)
            self.copy(arrived, self.pair_out.at[axis, at_z], self.pair_in.at[axis, at_z], self.x_peer).wait_recv()
            @pl.when(self.by_halves(at_z))
            def _():
                self.half(at_z, 1 - axis).start()
            self.share(2 - axis, at_z)

    def far_chain(self, at_z, side):
        return jnp.logical_or(at_z == 0, at_z == 3) if side == 0 else True

    def diagonal(self, at_z, side):
        halves = self.by_halves(at_z)
        @pl.when(halves)
        def _():
            self.half_arrival(at_z, 0).wait_recv()
            self.half_arrival(at_z, 1).wait_recv()
        if side != 0:
            @pl.when(jnp.logical_not(halves))
            def _():
                self.chain(at_z, side).wait_recv()
        @pl.when(self.far_chain(at_z, side))
        def _():
            self.onwards(side, lambda to: self.chain(at_z, to).start())
        self.share(3, at_z)

    def steps(self):
        order = [
            (0, self.arrive),
            (1, self.arrive),
            (0, self.cross),
            (2, self.arrive),
            (0, self.diagonal),
            (1, self.cross),
            (3, self.arrive),
            (1, self.diagonal),
            (2, self.cross),
            (2, self.diagonal),
            (3, self.cross),
            (3, self.diagonal),
        ]
        return [partial(self.each, distance, action) for distance, action in order]

    def settle(self, at_z, side):
        self.onwards(side, lambda to: self.along(at_z, to).wait_send())
        @pl.when(self.far_chain(at_z, side))
        def _():
            self.onwards(side, lambda to: self.chain(at_z, to).wait_send())
        for axis in range(2):
            self.whole(at_z, axis).wait_send()
            @pl.when(self.by_halves(at_z))
            def _():
                self.half(at_z, axis).wait_send()

    def own_ready(self):
        pltpu.make_async_copy(self.unit_ref, self.column(0, self.z), self.own_sem).wait()

    def finish(self):
        for distance in range(4):
            self.each(distance, self.settle)
        if self.other_ref is not None:
            def traded(at_z, carry):
                for turn in range(4):
                    self.trade(turn, at_z).wait()
                return carry

            lax.fori_loop(0, 4, traded, 0)


def remote(source, target, send_sem, recv_sem, device):
    return pltpu.make_async_remote_copy(
        src_ref=source,
        dst_ref=target,
        send_sem=send_sem,
        recv_sem=recv_sem,
        device_id=device,
        device_id_type=MESH_ID,
    )


PADDED = 80
WIDE = CHIPS * PADDED
SHARE = 423


def vector_part(full_ref, start, length, width):
    lane = lax.broadcasted_iota(jnp.int32, (1, width), 1)
    total = jnp.zeros((1, width), jnp.float32)
    for device in range(start // SHARE, (start + length - 1) // SHARE + 1):
        base = 512 * (device % 2)
        tile = full_ref[device // 2, PADDED - 16 :, base : base + 512].astype(jnp.float32)
        row = tile[ROWS - PADDED + 16 : ROWS - PADDED + 17]
        if width > 512:
            row = jnp.concatenate([row, jnp.zeros((1, width - 512), jnp.float32)], axis=1)
        shift = device * SHARE - start
        row = pltpu.roll(row, shift % width, 1) if shift % width else row
        first, last = max(shift, 0), min(shift + SHARE, length)
        total = total + jnp.where((lane >= first) & (lane < last), row, 0.0)
    return total


PROJECT_STEPS = ((0, 0, 1, 2), (1, 0, 2, 3), (2, 1, 1, 2), (3, 0, 3, 4), (4, 0, 4, 6), (5, 1, 2, 3))
ATTEND_STEPS = ((2, 0, 6, 8), (5, 1, 3, 4), (8, 0, 8, 10), (11, 1, 4, 6))
LAST_STEPS = ((0, 10, 12), (1, 6, 12))


def forward_kernel(
    splits, counts, unit, up_unit, down_unit, tokens_ref, pad_ref,
    q_ref, k_ref, v_ref, hidden_ref, att_ref, lse_ref, landing, full_ref, full_other, up_ref, up_other, down_ref, down_other,
    span, padded, acc, token_sems, span_sems, trade_out, trade_in, back_token_sems, back_span_sems, *sems
):
    place = position_of()
    rows = Rows(place)
    greet(pair_peers(*place) + next_peers(*place) + [(partner_of(*place), True)] + rows.peers())
    more = len(Gather.scratch(True))
    first = Gather(place, unit, full_ref, full_other, splits[0], sems[:more])
    second = Gather(place, up_unit, up_ref, up_other, splits[1], sems[more : 2 * more])
    third = Gather(place, down_unit, down_ref, down_other, splits[2], sems[2 * more :])
    one, two, three = first.steps(), second.steps(), third.steps()
    row_sems = (token_sems, span_sems, trade_out, trade_in)

    def run(steps, start, stop):
        for step in steps[start:stop]:
            step()

    run(one, 0, 1)
    rows.to_both(tokens_ref, span, row_sems)
    run(one, 1, 3)
    rows.relay(span, row_sems)
    run(one, 3, 6)
    run(two, 0, 1)
    run(three, 0, 1)
    rows.both_arrived(tokens_ref, span, row_sems)
    run(one, 6, len(one))
    first.own_ready()
    batches = tokens_ref.shape[0]
    gain, bias = vector_part(full_ref, 0, D, WIDE)[:, :D], vector_part(full_ref, D, D, WIDE)[:, :D]
    core = place[0]
    half = lambda start: jnp.where(
        core == 0, vector_part(full_ref, start, HALF, 1024), vector_part(full_ref, start + HALF, HALF, 1024)
    )[:, :HALF]
    query_bias, value_bias = half(2 * D), half(3 * D)
    block = 256

    def between(table, index):
        for at, steps, start, stop in table:
            @pl.when(index == at)
            def _():
                run((two, three)[steps], start, stop)

    def project(index, carry):
        batch, at = index // (SPAN // block), index % (SPAN // block)
        here = pl.ds(pl.multiple_of(at * block, block), block)
        token = rows.first * CHUNK + at * block + lax.broadcasted_iota(jnp.int32, (block, 1), 0)
        there = (token >= rows.image * IMG_LEN) & (token < jnp.minimum((rows.image + 1) * IMG_LEN, TOKENS)) & rows.has
        value = jnp.where(there, span[batch, here], 0).astype(jnp.float32)
        centered = value - jnp.mean(value, axis=1, keepdims=True)
        inverse = lax.rsqrt(jnp.mean(centered * centered, axis=1, keepdims=True) + EPSILON)
        hidden = (centered * inverse * gain + bias).astype(jnp.bfloat16)
        hidden_ref[batch, here] = hidden
        padded[...] = mm(hidden, pad_ref[...], NN).astype(jnp.bfloat16)
        wide = mm(padded[...], full_ref[:, :, HALF - 64 : D].reshape(WIDE, HALF + 64), NN)[:, 64:]
        q_ref[batch, here] = (wide + query_bias).astype(jnp.bfloat16)
        wide = mm(padded[...], full_ref[:, :, D:].reshape(WIDE, D), NN)
        k_ref[batch, here] = wide[:, :HALF].astype(jnp.bfloat16)
        v_ref[batch, here] = (wide[:, HALF:] + value_bias).astype(jnp.bfloat16)
        between(PROJECT_STEPS, index)
        return carry

    lax.fori_loop(0, batches * (SPAN // block), project, 0)
    tiles = SPAN // TILE

    def attend(index, carry):
        batch, tile = index // tiles, index % tiles
        attend_tile(
            rows.image, rows.has, rows.first, batch, tile, rows.image < counts[batch],
            q_ref, k_ref, v_ref, att_ref, lse_ref, acc,
        )
        between(ATTEND_STEPS, index)
        return carry

    lax.fori_loop(0, batches * tiles, attend, 0)
    back_sems = (back_token_sems, back_span_sems)
    rows.to_tokens(att_ref, landing, back_sems)
    for steps, start, stop in LAST_STEPS:
        run((two, three)[steps], start, stop)
    rows.tokens_arrived(att_ref, landing, back_sems)
    second.own_ready()
    third.own_ready()
    for gather in (first, second, third):
        gather.finish()


def forward(counts, unit, up_unit, down_unit, tokens, collective_id):
    batches = tokens.shape[0]
    full = lambda unit: jax.ShapeDtypeStruct((CHIPS,) + unit.shape, unit.dtype)
    low = lambda *shape: jax.ShapeDtypeStruct(shape, jnp.bfloat16)
    vmem, hbm = pl.BlockSpec(memory_space=pltpu.VMEM), pl.BlockSpec(memory_space=pl.ANY)
    dma = pltpu.SemaphoreType.DMA
    feature, lane = jnp.arange(D)[:, None], jnp.arange(WIDE)[None]
    pad = (feature // ROWS * PADDED + feature % ROWS == lane).astype(jnp.bfloat16)
    outs = pl.pallas_call(
        partial(forward_kernel, (1152, 1152, 640)),
        out_shape=[low(batches, SPAN, HALF)] * 3
        + [
            low(batches, SPAN, D),
            low(batches, SPAN, HALF),
            jax.ShapeDtypeStruct((batches, SPAN, 128), jnp.float32),
            low(2, 2, batches, SHARD, HALF),
            full(unit),
            low(CHIPS, PADDED, HALF + 64),
            full(up_unit),
            full(up_unit),
            full(down_unit),
            full(down_unit),
        ],
        in_specs=[pl.BlockSpec(memory_space=pltpu.SMEM)] + [vmem] * 5,
        out_specs=[vmem] * 8 + [hbm] * 5,
        scratch_shapes=[
            pltpu.VMEM((batches, SPAN, D), jnp.bfloat16),
            pltpu.VMEM((256, WIDE), jnp.bfloat16),
            pltpu.VMEM((TILE, HALF), jnp.float32),
        ]
        + Rows.scratch()
        + [dma((SPAN_CHUNKS,)), dma((SPAN_CHUNKS,))]
        + Rows.scratch()
        + Gather.scratch(True) * 3,
        compiler_params=pltpu.CompilerParams(
            collective_id=collective_id, has_side_effects=True, vmem_limit_bytes=60 * 1024 * 1024
        ),
        cost_estimate=pl.CostEstimate(flops=0, bytes_accessed=500 * 10**6, transcendentals=0),
        name="forward",
    )(counts, unit, up_unit, down_unit, tokens, pad)
    return list(outs[:9]) + [w.reshape(-1, w.shape[2]) for w in outs[9:]]


def vector_kernel(sent_ref, total_ref, arrived, send_sems, recv_sems):
    device = lax.axis_index("dev")
    devices = 2 * CHIPS
    mesh_id = pl.DeviceIdType.MESH
    barrier = pltpu.get_barrier_semaphore()

    def greet(step, carry):
        pl.semaphore_signal(
            barrier, inc=1, device_id=(lax.rem(device + step, devices),), device_id_type=mesh_id
        )
        return carry

    lax.fori_loop(1, devices, greet, 0)
    pl.semaphore_wait(barrier, devices - 1)

    def copy(step):
        target = lax.rem(device + step, devices)
        return pltpu.make_async_remote_copy(
            src_ref=sent_ref.at[target],
            dst_ref=arrived.at[step],
            send_sem=send_sems.at[step],
            recv_sem=recv_sems.at[step],
            device_id=(target,),
            device_id_type=mesh_id,
        )

    def start(step, carry):
        copy(step).start()
        return carry

    lax.fori_loop(1, devices, start, 0)

    def add(step, total):
        copy(step).wait()
        return total + arrived[step]

    total_ref[...] = lax.fori_loop(1, devices, add, sent_ref[device])


def scatter_vector(vector, share, collective_id):
    rows = jnp.pad(vector.reshape(2 * CHIPS, share), ((0, 0), (0, 1024 - share)))
    dma = pltpu.SemaphoreType.DMA
    total = pl.pallas_call(
        vector_kernel,
        out_shape=jax.ShapeDtypeStruct((8, 128), jnp.float32),
        in_specs=[pl.BlockSpec(memory_space=pltpu.VMEM)],
        out_specs=pl.BlockSpec(memory_space=pltpu.VMEM),
        scratch_shapes=[
            pltpu.VMEM((2 * CHIPS, 8, 128), jnp.float32),
            dma((2 * CHIPS,)),
            dma((2 * CHIPS,)),
        ],
        compiler_params=pltpu.CompilerParams(collective_id=collective_id, has_side_effects=True),
        cost_estimate=pl.CostEstimate(flops=0, bytes_accessed=20 * 10**6, transcendentals=0),
        name="scatter_vector",
    )(rows.reshape(2 * CHIPS, 8, 128))
    return total.reshape(-1)[:share]


def later_image(device):
    start = device * SHARD
    at = start + lax.broadcasted_iota(jnp.int32, (SHARD, 1), 0)
    return at >= (start // IMG_LEN + 1) * IMG_LEN


MLP_ROWS = SHARD
GELU_A, GELU_B = 0.7978845608028654, 0.044715


def mlp_kernel(
    x_ref, landing, g_ref, wo_a, wo_b, up_a, up_b, down_a, down_b, vec_ref, bias_ref,
    att_low, att_high, result_ref, act_a, act_b, gu_a, gu_b, h2_ref, gb_a, gb_b, gm_ref, go_a, go_b, sums_ref, bias_sums_ref,
    up_w, down_w, slope, sems,
):
    loads = [
        pltpu.make_async_copy(source, target, sems.at[n])
        for n, (source, target) in enumerate(
            [(up_a, up_w.at[0]), (up_b, up_w.at[1]), (down_a, down_w.at[0]), (down_b, down_w.at[1])]
        )
    ]
    for load in loads:
        load.start()
    sums_ref[...] = jnp.zeros_like(sums_ref)
    bias_sums_ref[...] = jnp.zeros_like(bias_sums_ref)
    acts, grads_up = (act_a, act_b), (gu_a, gu_b)
    device = lax.axis_index("dev")
    core = device % 2
    later = later_image(device)
    mean = lambda value: jnp.mean(value, axis=1, keepdims=True)

    def tile(index, carry):
        rows = pl.ds(pl.multiple_of(index * MLP_ROWS, MLP_ROWS), MLP_ROWS)

        def ready(load):
            @pl.when(index == 0)
            def _():
                load.wait()

        atts = [jnp.where(later, landing[1, side, index], landing[0, side, index]) for side in range(2)]
        att_low[rows], att_high[rows] = atts
        sides = [mm(atts[0], wo[:HALF], NN) + mm(atts[1], wo[HALF:], NN) for wo in (wo_a, wo_b)]
        branch = jnp.where(core == 0, jnp.concatenate(sides, axis=1), jnp.concatenate(sides[::-1], axis=1))
        middle = x_ref[rows].astype(jnp.float32) + (branch + vec_ref[0:1])
        centered = middle - mean(middle)
        inverse = lax.rsqrt(mean(centered * centered) + EPSILON)
        normed = centered * inverse
        gain = vec_ref[1:2]
        hidden = (normed * gain + vec_ref[2:3]).astype(jnp.bfloat16)
        h2_ref[rows] = hidden
        for half in range(2):
            ready(loads[half])
            upper = mm(hidden, up_w[half], NN) + bias_ref[half : half + 1]
            square = upper * upper
            tanh = jnp.tanh(GELU_A * (upper + GELU_B * (square * upper)))
            acts[half][rows] = (0.5 * upper * (1.0 + tanh)).astype(jnp.bfloat16)
            slope[half] = 0.5 * (1.0 + tanh) + (0.5 * GELU_A) * upper * (1.0 - tanh * tanh) * (
                1.0 + (3.0 * GELU_B) * square
            )
        for half in range(2):
            ready(loads[2 + half])
        lower = mm(act_a[rows], down_w[0], NN) + mm(act_b[rows], down_w[1], NN)
        result_ref[rows] = (middle + (lower + vec_ref[3:4])).astype(jnp.bfloat16)
        grad = g_ref[rows]
        for half in range(2):
            grad_upper = (mm(grad, down_w[half], NT) * slope[half]).astype(jnp.bfloat16)
            grads_up[half][rows] = grad_upper
            bias_sums_ref[half : half + 1] += jnp.sum(grad_upper.astype(jnp.float32), axis=0, keepdims=True)
        grad_hidden = mm(gu_a[rows], up_w[0], NT) + mm(gu_b[rows], up_w[1], NT)
        scaled = grad_hidden * gain
        wide = grad.astype(jnp.float32)
        grad_middle = wide + inverse * (scaled - mean(scaled) - normed * mean(scaled * normed))
        gm_ref[rows] = grad_middle
        branch = grad_middle.astype(jnp.bfloat16)
        low, high = branch[:, :HALF], branch[:, HALF:]
        branches = jnp.where(core == 0, low, high), jnp.where(core == 0, high, low)
        gb_a[rows], gb_b[rows] = branches
        for go_ref, heads in ((go_a, slice(0, HALF)), (go_b, slice(HALF, D))):
            total = mm(branches[0], wo_a[heads], NT) + mm(branches[1], wo_b[heads], NT)
            go_ref[rows] = total.astype(jnp.bfloat16)
        for n, value in enumerate([branch.astype(jnp.float32), grad_hidden * normed, grad_hidden, wide]):
            sums_ref[n : n + 1] += jnp.sum(value, axis=0, keepdims=True)
        return carry

    lax.fori_loop(0, x_ref.shape[0] // MLP_ROWS, tile, 0)


def mlp(x, landing, grad, wos, ups, downs, vecs, biases):
    rows = x.shape[0]
    vmem, hbm = pl.BlockSpec(memory_space=pltpu.VMEM), pl.BlockSpec(memory_space=pl.ANY)
    low = lambda width: jax.ShapeDtypeStruct((rows, width), jnp.bfloat16)
    wide = lambda *shape: jax.ShapeDtypeStruct(shape, jnp.float32)
    return pl.pallas_call(
        mlp_kernel,
        out_shape=[low(HALF), low(HALF), low(D)] + [low(FFH)] * 4 + [low(D), low(HALF), low(HALF), wide(rows, D), low(HALF), low(HALF), wide(8, D), wide(8, FFH)],
        in_specs=[vmem] * 5 + [hbm] * 4 + [vmem] * 2,
        out_specs=[vmem] * 15,
        scratch_shapes=[
            pltpu.VMEM((2, D, FFH), jnp.bfloat16),
            pltpu.VMEM((2, FFH, D), jnp.bfloat16),
            pltpu.VMEM((2, MLP_ROWS, FFH), jnp.float32),
            pltpu.SemaphoreType.DMA((4,)),
        ],
        compiler_params=pltpu.CompilerParams(vmem_limit_bytes=62 * 1024 * 1024),
        cost_estimate=pl.CostEstimate(flops=0, bytes_accessed=130 * 10**6, transcendentals=0),
        name="mlp",
    )(x, landing, grad, *wos, *ups, *downs, vecs, biases)


def topo_local(tokens, counts, qkv_weight, out_weight, up_weight, down_weight, vectors, cotangent):
    device = lax.axis_index("dev")
    core, chip = device % 2, device // 2
    batches = tokens.shape[0]
    share = vectors.shape[0]
    own_rows = batches * SHARD

    qkv36 = qkv_weight.reshape(ROWS // 2, 3 * D)
    out36 = out_weight.reshape(ROWS // 2, D)
    sides = [
        jnp.concatenate(
            [out36[:, s * HALF :][:, :HALF]] + [qkv36[:, s * HALF + j * D :][:, :HALF] for j in range(3)],
            axis=1,
        )
        for s in range(2)
    ]
    up36 = up_weight.reshape(ROWS // 2, CHIPS, UNIT)
    up_low = up36[:, :, :UNIT_HALF].reshape(ROWS // 2, FFH)
    up_high = jnp.pad(up36[:, :, UNIT_HALF:], ((0, 0), (0, 0), (0, 2 * UNIT_HALF - UNIT))).reshape(
        ROWS // 2, FFH
    )
    spill = UNIT_HALF * D - down_weight.shape[0]
    borrowed = lax.ppermute(
        down_weight[:spill], "dev", [(i + 1, i) for i in range(0, 2 * CHIPS, 2)]
    )
    down_unit = by_core(
        core,
        jnp.concatenate([down_weight, borrowed]),
        jnp.concatenate([down_weight[spill:], jnp.zeros((2 * spill,), jnp.bfloat16)]),
    ).reshape(UNIT_HALF, D)
    first_unit = chip_unit(
        core,
        jnp.concatenate([sides[0], up_low], axis=1),
        jnp.concatenate([sides[1], up_high], axis=1),
    )
    shares = jnp.pad(vectors, (0, 512 - share)).reshape(1, 512)
    shares = joined(core, shares, swap(shares), 0).reshape(1, 1024)
    extra = jnp.pad(shares, ((0, 7), (0, 4 * HALF - 1024)))
    query, keys, values, hidden_one, attended, log_sums, landing, full, full_other, up_mine, up_theirs, down_mine, down_theirs = forward(
        counts, jnp.concatenate([first_unit[:, : 4 * HALF], extra], axis=0), first_unit[:, 4 * HALF :], down_unit, tokens, 1
    )
    unpad = lambda units, first, end: units[:, :ROWS, first:end].reshape(D, end - first)
    out_mine, out_theirs, qkv_w = unpad(full, 0, HALF), unpad(full_other, 0, HALF), unpad(full, HALF, 4 * HALF)
    packed = full[:, ROWS, :1024].reshape(2 * CHIPS, 512)[:, :share].reshape(-1).astype(jnp.float32)
    pieces = [packed[segment * D : (segment + 1) * D] for segment in range(8)]
    bias_units = packed[8 * D : 8 * D + FF].reshape(CHIPS, UNIT)
    bias_low = bias_units[:, :UNIT_HALF].reshape(-1)
    bias_high = jnp.pad(bias_units[:, UNIT_HALF:], ((0, 0), (0, 2 * UNIT_HALF - UNIT))).reshape(-1)
    up_bias_mine = by_core(core, bias_low, bias_high)
    up_bias_theirs = by_core(core, bias_high, bias_low)
    def dot_tn(left, right):
        return lax.dot_general(left, right, (((0,), (0,)), ((), ())), preferred_element_type=jnp.float32)

    inputs = tokens.reshape(own_rows, D).astype(jnp.float32)
    grad_output = cotangent.reshape(own_rows, D)
    eight = lambda rows: jnp.pad(jnp.stack(rows), ((0, 8 - len(rows)), (0, 0)))
    (
        att_low, att_high, result, active_mine, active_theirs, grad_upper_mine, grad_upper_theirs,
        hidden_two, branch_mine, branch_theirs, grad_middle, heads_low, heads_high, vec_sums, bias_sums,
    ) = mlp(
        tokens.reshape(own_rows, D), landing, grad_output, (out_mine, out_theirs), (up_mine, up_theirs), (down_mine, down_theirs),
        eight([pieces[4], pieces[5], pieces[6], pieces[7]]), eight([up_bias_mine, up_bias_theirs]),
    )

    pair = lambda mine, theirs: jnp.concatenate([mine, swap(theirs)], axis=0)
    grad_down = dot_tn(pair(active_mine, active_theirs), pair(grad_output, grad_output)).astype(jnp.bfloat16)
    grad_up = dot_tn(pair(hidden_two, hidden_two), pair(grad_upper_mine, grad_upper_theirs)).astype(jnp.bfloat16)
    branch_pair = pair(branch_mine, branch_theirs)
    grad_out = jnp.concatenate([dot_tn(pair(att, att), branch_pair) for att in (att_low, att_high)], axis=0).astype(jnp.bfloat16)
    grad_query, grad_keys, grad_values, landing, down_total, up_total, out_total, qkv_total = backward(
        counts, query, keys, values, hidden_one, qkv_w, attended, log_sums,
        heads_low.reshape(batches, SHARD, HALF), heads_high.reshape(batches, SHARD, HALF),
        grad_down.reshape(CHIPS, UNIT_HALF, D), grad_up.reshape(CHIPS, ROWS, FFH), grad_out.reshape(CHIPS, ROWS, HALF), 4,
    )
    flat = lambda block: block.reshape(batches * SPAN, -1)
    grad_query, grad_keys, grad_values = flat(grad_query), flat(grad_keys), flat(grad_values)
    attention_total = jnp.concatenate([qkv_total, out_total], axis=1)
    later = later_image(device)[None]
    grad_hidden_one = jnp.where(later, landing[1], landing[0]).astype(jnp.float32).reshape(own_rows, D)
    normed_one, inverse_one = layer_stats(inputs)
    grad_input = grad_middle + layer_back(grad_hidden_one, normed_one, inverse_one, pieces[0])

    sums = lambda values: jnp.sum(values.astype(jnp.float32), axis=0)
    at_heads = lambda vector: lax.dynamic_update_slice_in_dim(
        jnp.zeros((D,), jnp.float32), vector, core * HALF, 0
    )
    bias_mine, bias_theirs = bias_sums[0], bias_sums[1]
    bias_low = by_core(core, bias_mine, bias_theirs).reshape(CHIPS, UNIT_HALF)
    bias_high = by_core(core, bias_theirs, bias_mine).reshape(CHIPS, UNIT_HALF)
    grad_up_bias = jnp.concatenate([bias_low, bias_high[:, : UNIT - UNIT_HALF]], axis=1).reshape(-1)
    vector_grad = jnp.concatenate(
        [
            sums(grad_hidden_one * normed_one),
            sums(grad_hidden_one),
            at_heads(sums(grad_query)),
            at_heads(sums(grad_values)),
            *(vec_sums[n] for n in range(4)),
            grad_up_bias,
            jnp.zeros((32 * share - 8 * D - FF,), jnp.float32),
        ]
    )
    vector_grad = scatter_vector(vector_grad, share, 2)

    half_rows = ROWS // 2

    def whole_rows(total):
        kept = by_core(core, total[:half_rows], total[half_rows:])
        theirs = swap(by_core(core, total[half_rows:], total[:half_rows]))
        return by_core(core, kept, theirs), by_core(core, theirs, kept)

    low, high = whole_rows(attention_total)
    columns = [
        jnp.concatenate([low[:, j * HALF : (j + 1) * HALF], high[:, j * HALF : (j + 1) * HALF]], axis=1)
        for j in range(4)
    ]
    qkv_grad = jnp.concatenate(columns[:3], axis=1).reshape(-1)
    out_grad = columns[3].reshape(-1)
    low, high = whole_rows(up_total)
    up_grad = jnp.concatenate(
        [
            low.reshape(half_rows, CHIPS, UNIT_HALF),
            high.reshape(half_rows, CHIPS, UNIT_HALF)[:, :, : UNIT - UNIT_HALF],
        ],
        axis=2,
    ).reshape(-1)
    down_flat = down_total.reshape(-1)
    returned = lax.ppermute(
        down_flat[down_flat.shape[0] - spill :], "dev", [(i, i + 1) for i in range(0, 2 * CHIPS, 2)]
    )
    down_grad = by_core(
        core,
        down_flat[: down_weight.shape[0]],
        jnp.concatenate([returned, down_flat[: down_weight.shape[0] - spill]]),
    )
    return (
        result.reshape(tokens.shape),
        grad_input.astype(jnp.bfloat16).reshape(tokens.shape),
        qkv_grad,
        out_grad,
        up_grad,
        down_grad,
        vector_grad,
    )


def solution(mesh):
    local = topo_local if mesh.shape["dev"] == 32 else generic_local
    return jax.shard_map(
        local,
        mesh=mesh,
        in_specs=(
            P(None, "dev", None),
            P(),
            P("dev"),
            P("dev"),
            P("dev"),
            P("dev"),
            P("dev"),
            P(None, "dev", None),
        ),
        out_specs=(
            P(None, "dev", None),
            P(None, "dev", None),
            P("dev"),
            P("dev"),
            P("dev"),
            P("dev"),
            P("dev"),
        ),
        check_vma=False,
    )
```

```python
from functools import partial

import jax
import jax.numpy as jnp
import numpy as np
from jax import lax
from jax.experimental import pallas as pl
from jax.experimental.pallas import tpu as pltpu
from jax.sharding import PartitionSpec as P

D = 1152
HEADS = 16
FF = 4304
IMG_LEN = 729


heads_per_block = 4
EPSILON = 1e-06
MASKED = -1e30


def passed_along(block, axis, distance):
    devices = range(lax.axis_size(axis))
    route = [(i - distance, i) for i in devices if i - distance in devices]
    return lax.ppermute(block, axis, route)


def layer_stats(values):
    centered = values - jnp.mean(values, axis=-1, keepdims=True)
    inverse = lax.rsqrt(jnp.mean(centered * centered, axis=-1, keepdims=True) + EPSILON)
    return (centered * inverse, inverse)


def layer_back(grad_output, normed, inverse, gain):
    scaled = grad_output * gain
    return inverse * (
        scaled
        - jnp.mean(scaled, axis=-1, keepdims=True)
        - normed * jnp.mean(scaled * normed, axis=-1, keepdims=True)
    )


def image_of(positions, image_count):
    return jnp.where(positions < image_count * IMG_LEN, positions // IMG_LEN, -positions - 1)


def reach_sizes(shard_rows):
    rim_rows = IMG_LEN - 1
    reach_count = (rim_rows + shard_rows - 1) // shard_rows
    return [
        min(shard_rows, rim_rows - (distance - 1) * shard_rows)
        for distance in range(1, reach_count + 1)
    ]


def widen(key_value, shard_rows):
    edge_sizes = reach_sizes(shard_rows)
    arrived = {}
    for distance, amount in enumerate(edge_sizes, start=1):
        for direction in (1, -1):
            sent_rows = key_value[shard_rows - amount :] if direction > 0 else key_value[:amount]
            arrived[distance, direction] = passed_along(sent_rows, "dev", direction * distance)
    before = [arrived[distance, 1] for distance in range(len(edge_sizes), 0, -1)]
    after = [arrived[distance, -1] for distance in range(1, len(edge_sizes) + 1)]
    return jnp.concatenate(before + [key_value] + after, axis=0)


def return_edges(grad_extended, shard_rows):
    edge_sizes = reach_sizes(shard_rows)
    rim_rows = IMG_LEN - 1
    combined = grad_extended[rim_rows : rim_rows + shard_rows]
    for distance, amount in enumerate(edge_sizes, start=1):
        for direction in (1, -1):
            if direction > 0:
                begin_row = rim_rows - sum(edge_sizes[:distance])
            else:
                begin_row = rim_rows + shard_rows + sum(edge_sizes[: distance - 1])
            arrived = passed_along(
                grad_extended[begin_row : begin_row + amount].astype(jnp.bfloat16),
                "dev",
                -direction * distance,
            ).astype(jnp.float32)
            if direction > 0:
                combined = combined.at[shard_rows - amount :].add(arrived)
            else:
                combined = combined.at[:amount].add(arrived)
    return combined


def key_window(device_index, shard_rows, image_count):
    span_rows = ((shard_rows + IMG_LEN - 2) // IMG_LEN + 1) * IMG_LEN
    shard_start = device_index * shard_rows
    window_start = shard_start // IMG_LEN * IMG_LEN
    offset_rows = window_start - shard_start + IMG_LEN - 1
    query_images = image_of(shard_start + jnp.arange(shard_rows, dtype=jnp.int32), image_count)
    key_images = image_of(window_start + jnp.arange(span_rows, dtype=jnp.int32), image_count)
    return (span_rows, offset_rows, query_images[:, None] == key_images[None, :])


def head_slices(query, window_kv, block_index):
    head_dim = D // HEADS
    block_width = heads_per_block * head_dim
    first_column = block_index * block_width
    query_block = query[:, first_column : first_column + block_width].reshape(
        query.shape[0], heads_per_block, head_dim
    )
    key_block = window_kv[:, first_column : first_column + block_width].reshape(
        window_kv.shape[0], heads_per_block, head_dim
    )
    value_block = window_kv[:, D + first_column : D + first_column + block_width].reshape(
        window_kv.shape[0], heads_per_block, head_dim
    )
    return (query_block, key_block, value_block, first_column, block_width)


def attend(query, window_kv, visible):
    score_scale = (D // HEADS) ** (-0.5)
    outputs, log_sums = ([], [])
    for block_index in range(HEADS // heads_per_block):
        query_block, key_block, value_block, first_column, block_width = head_slices(
            query, window_kv, block_index
        )
        raw_scores = jnp.einsum(
            "qhd,khd->hqk", query_block, key_block, preferred_element_type=jnp.float32
        )
        scores = jnp.where(visible[None], raw_scores * score_scale, MASKED)
        largest = jnp.max(scores, axis=-1, keepdims=True)
        exponent = jnp.exp(scores - largest)
        row_totals = jnp.sum(exponent, axis=-1, keepdims=True)
        probabilities = (exponent / row_totals).astype(jnp.bfloat16)
        log_sums.append(largest + jnp.log(row_totals))
        attended = jnp.einsum(
            "hqk,khd->qhd", probabilities, value_block, preferred_element_type=jnp.float32
        )
        outputs.append(attended.reshape(query.shape[0], block_width))
    return (jnp.concatenate(outputs, axis=1), log_sums)


def attend_back(query, window_kv, visible, log_sums, grad_attended):
    score_scale = (D // HEADS) ** (-0.5)
    grad_queries, grad_keys, grad_values = ([], [], [])
    for block_index in range(HEADS // heads_per_block):
        query_block, key_block, value_block, first_column, block_width = head_slices(
            query, window_kv, block_index
        )
        grad_block = grad_attended[:, first_column : first_column + block_width].reshape(
            query.shape[0], heads_per_block, block_width // heads_per_block
        )
        raw_scores = jnp.einsum(
            "qhd,khd->hqk", query_block, key_block, preferred_element_type=jnp.float32
        )
        scores = jnp.where(visible[None], raw_scores * score_scale, MASKED)
        probabilities = jnp.exp(scores - log_sums[block_index])
        grad_values.append(
            jnp.einsum(
                "hqk,qhd->khd",
                probabilities.astype(jnp.bfloat16),
                grad_block,
                preferred_element_type=jnp.float32,
            ).reshape(window_kv.shape[0], block_width)
        )
        grad_probs = jnp.einsum(
            "qhd,khd->hqk", grad_block, value_block, preferred_element_type=jnp.float32
        )
        inner = jnp.sum(probabilities * grad_probs, axis=-1, keepdims=True)
        grad_raw = (probabilities * (grad_probs - inner) * score_scale).astype(jnp.bfloat16)
        grad_queries.append(
            jnp.einsum(
                "hqk,khd->qhd", grad_raw, key_block, preferred_element_type=jnp.float32
            ).reshape(query.shape[0], block_width)
        )
        grad_keys.append(
            jnp.einsum(
                "hqk,qhd->khd", grad_raw, query_block, preferred_element_type=jnp.float32
            ).reshape(window_kv.shape[0], block_width)
        )
    return (jnp.concatenate(grad_queries, axis=1), jnp.concatenate(grad_keys + grad_values, axis=1))


def unpack(gathered):
    qkv_flat, out_flat, up_flat, down_flat, packed = gathered
    packed = packed.astype(jnp.float32)
    pieces = [packed[segment * D : (segment + 1) * D] for segment in range(8)]
    up_bias = packed[8 * D : 8 * D + FF]
    return (
        qkv_flat.reshape(D, 3 * D),
        out_flat.reshape(D, D),
        up_flat.reshape(D, FF),
        down_flat.reshape(FF, D),
        pieces,
        up_bias,
    )


def forward_batch(tokens_batch, image_count, weights, device_index):
    qkv_w, out_w, up_w, down_w, pieces, up_bias = weights
    shard_rows = tokens_batch.shape[0]
    rim_rows = IMG_LEN - 1
    inputs = tokens_batch.astype(jnp.float32)
    normed_one, inverse_one = layer_stats(inputs)
    hidden_one = (normed_one * pieces[0] + pieces[1]).astype(jnp.bfloat16)
    projected = jnp.dot(hidden_one, qkv_w, preferred_element_type=jnp.float32)
    query = (projected[:, :D] + pieces[2]).astype(jnp.bfloat16)
    key_value = jnp.concatenate(
        [projected[:, D : 2 * D], projected[:, 2 * D :] + pieces[3]], axis=1
    ).astype(jnp.bfloat16)
    extended = widen(key_value, shard_rows)
    span_rows, offset_rows, visible = key_window(device_index, shard_rows, image_count)
    padded = jnp.pad(extended, ((0, rim_rows + span_rows - extended.shape[0]), (0, 0)))
    window_kv = lax.dynamic_slice_in_dim(padded, offset_rows, span_rows, 0)
    attended, log_sums = attend(query, window_kv, visible)
    attended_low = attended.astype(jnp.bfloat16)
    middle = inputs + (jnp.dot(attended_low, out_w, preferred_element_type=jnp.float32) + pieces[4])
    normed_two, inverse_two = layer_stats(middle)
    hidden_two = (normed_two * pieces[5] + pieces[6]).astype(jnp.bfloat16)
    upper = jnp.dot(hidden_two, up_w, preferred_element_type=jnp.float32) + up_bias
    active = jax.nn.gelu(upper, approximate=True).astype(jnp.bfloat16)
    output = middle + (jnp.dot(active, down_w, preferred_element_type=jnp.float32) + pieces[7])
    saved = (
        normed_one,
        inverse_one,
        hidden_one,
        query,
        window_kv,
        offset_rows,
        visible,
        log_sums,
        attended_low,
        normed_two,
        inverse_two,
        hidden_two,
        upper,
        active,
    )
    return (output.astype(jnp.bfloat16), saved)


def backward_batch(grad_output, saved, weights, vector_length):
    qkv_w, out_w, up_w, down_w, pieces, up_bias = weights
    (
        normed_one,
        inverse_one,
        hidden_one,
        query,
        window_kv,
        offset_rows,
        visible,
        log_sums,
        attended_low,
        normed_two,
        inverse_two,
        hidden_two,
        upper,
        active,
    ) = saved
    shard_rows = query.shape[0]
    span_rows = window_kv.shape[0]
    rim_rows = IMG_LEN - 1
    grad_wide = grad_output.astype(jnp.float32)
    grad_down = jnp.einsum("tf,td->fd", active, grad_output, preferred_element_type=jnp.float32)
    grad_down_bias = jnp.sum(grad_wide, axis=0)
    grad_active = jnp.einsum("td,fd->tf", grad_output, down_w, preferred_element_type=jnp.float32)
    gelu_back = jax.vjp(partial(jax.nn.gelu, approximate=True), upper)[1]
    grad_upper = gelu_back(grad_active)[0].astype(jnp.bfloat16)
    grad_up = jnp.einsum("td,tf->df", hidden_two, grad_upper, preferred_element_type=jnp.float32)
    grad_up_bias = jnp.sum(grad_upper.astype(jnp.float32), axis=0)
    grad_hidden_two = jnp.einsum("tf,df->td", grad_upper, up_w, preferred_element_type=jnp.float32)
    grad_gain_two = jnp.sum(grad_hidden_two * normed_two, axis=0)
    grad_bias_two = jnp.sum(grad_hidden_two, axis=0)
    grad_middle = grad_wide + layer_back(grad_hidden_two, normed_two, inverse_two, pieces[5])
    grad_branch = grad_middle.astype(jnp.bfloat16)
    grad_out = jnp.einsum(
        "td,te->de", attended_low, grad_branch, preferred_element_type=jnp.float32
    )
    grad_out_bias = jnp.sum(grad_branch.astype(jnp.float32), axis=0)
    grad_attended = jnp.einsum(
        "te,de->td", grad_branch, out_w, preferred_element_type=jnp.float32
    ).astype(jnp.bfloat16)
    grad_query, grad_window = attend_back(query, window_kv, visible, log_sums, grad_attended)
    grad_padded = lax.dynamic_update_slice_in_dim(
        jnp.zeros((rim_rows + span_rows, 2 * D), jnp.float32), grad_window, offset_rows, 0
    )
    grad_kv = return_edges(grad_padded[: shard_rows + 2 * rim_rows], shard_rows)
    grad_query_low = grad_query.astype(jnp.bfloat16)
    grad_kv_low = grad_kv.astype(jnp.bfloat16)
    grad_projected = jnp.concatenate([grad_query_low, grad_kv_low], axis=1)
    grad_qkv = jnp.einsum(
        "td,te->de", hidden_one, grad_projected, preferred_element_type=jnp.float32
    )
    grad_query_bias = jnp.sum(grad_query_low.astype(jnp.float32), axis=0)
    grad_value_bias = jnp.sum(grad_kv_low[:, D:].astype(jnp.float32), axis=0)
    grad_hidden_one = jnp.einsum(
        "te,de->td", grad_projected, qkv_w, preferred_element_type=jnp.float32
    )
    grad_gain_one = jnp.sum(grad_hidden_one * normed_one, axis=0)
    grad_bias_one = jnp.sum(grad_hidden_one, axis=0)
    grad_input = grad_middle + layer_back(grad_hidden_one, normed_one, inverse_one, pieces[0])
    vector_grad = jnp.concatenate(
        [
            grad_gain_one,
            grad_bias_one,
            grad_query_bias,
            grad_value_bias,
            grad_out_bias,
            grad_gain_two,
            grad_bias_two,
            grad_down_bias,
            grad_up_bias,
            jnp.zeros((vector_length - 8 * D - FF,), jnp.float32),
        ]
    )
    flat_grads = (
        grad_qkv.reshape(-1),
        grad_out.reshape(-1),
        grad_up.reshape(-1),
        grad_down.reshape(-1),
        vector_grad,
    )
    return (grad_input.astype(jnp.bfloat16), flat_grads)


def generic_local(tokens, counts, qkv_weight, out_weight, up_weight, down_weight, vectors, cotangent):
    device_index = lax.axis_index("dev")
    vector_length = vectors.shape[0] * lax.axis_size("dev")
    gathered = (
        lax.all_gather(qkv_weight, "dev", axis=0, tiled=True),
        lax.all_gather(out_weight, "dev", axis=0, tiled=True),
        lax.all_gather(up_weight, "dev", axis=0, tiled=True),
        lax.all_gather(down_weight, "dev", axis=0, tiled=True),
        lax.all_gather(vectors, "dev", axis=0, tiled=True),
    )
    weights = unpack(gathered)
    results, kept_state = ([], [])
    for batch_index in range(tokens.shape[0]):
        output, saved = forward_batch(
            tokens[batch_index], counts[batch_index], weights, device_index
        )
        results.append(output)
        kept_state.append(saved)
    weights = unpack(
        (
            lax.all_gather(qkv_weight, "dev", axis=0, tiled=True),
            lax.all_gather(out_weight, "dev", axis=0, tiled=True),
            lax.all_gather(up_weight, "dev", axis=0, tiled=True),
            lax.all_gather(down_weight, "dev", axis=0, tiled=True),
            lax.all_gather(vectors, "dev", axis=0, tiled=True),
        )
    )
    grad_inputs = []
    totals = None
    for batch_index in range(tokens.shape[0]):
        grad_input, flat_grads = backward_batch(
            cotangent[batch_index], kept_state[batch_index], weights, vector_length
        )
        grad_inputs.append(grad_input)
        totals = (
            flat_grads
            if totals is None
            else tuple((earlier + current for earlier, current in zip(totals, flat_grads)))
        )
    totals = lax.psum_scatter(totals, "dev", scatter_dimension=0, tiled=True)
    return (
        jnp.stack(results),
        jnp.stack(grad_inputs),
        totals[0],
        totals[1],
        totals[2],
        totals[3],
        totals[4],
    )


CHIPS = 16
HEAD = D // HEADS
HALF = D // 2
CORE_HEADS = HEADS // 2
ROWS = D // CHIPS
UNIT = FF // CHIPS
UNIT_HALF = 136
FFH = CHIPS * UNIT_HALF
SHARD = 256
CHIP_ROWS = 2 * SHARD
TILE = 128
CHUNK = 16
SPAN = 768
SPAN_CHUNKS = SPAN // CHUNK
SHARD_CHUNKS = SHARD // CHUNK
SPAN_DEVICES = 4
TOKENS = 2 * CHIPS * SHARD
SCALE = HEAD**-0.5


def route(target):
    return [(i, target(i)) for i in range(2 * CHIPS)]


def swap(block):
    return lax.ppermute(block, "dev", route(lambda i: i ^ 1))


def by_core(core, first, second):
    return jnp.where(core == 0, first, second)


def joined(core, mine, theirs, axis):
    return by_core(
        core,
        jnp.concatenate([mine, theirs], axis=axis),
        jnp.concatenate([theirs, mine], axis=axis),
    )


def head_lanes(head):
    first = head * HEAD
    low = first // 128 * 128
    high = min((first + HEAD + 127) // 128 * 128, HALF)
    return low, high, first - low


def head_mask(head):
    low, high, skip = head_lanes(head)
    lanes = lax.broadcasted_iota(jnp.int32, (1, high - low), 1)
    return (lanes >= skip) & (lanes < skip + HEAD)


NT = (((1,), (1,)), ((), ()))
NN = (((1,), (0,)), ((), ()))
TN = (((0,), (0,)), ((), ()))


def mm(left, right, dims):
    return lax.dot_general(left, right, dims, preferred_element_type=jnp.float32)


def image_of_chip(chip):
    image = (CHIP_ROWS * chip + IMG_LEN // 2) // IMG_LEN
    has = owner_of_image(image) == chip
    first = image * IMG_LEN // CHUNK
    last = jnp.minimum((image * IMG_LEN + IMG_LEN - 1) // CHUNK, TOKENS // CHUNK - 1)
    return image, has, first, jnp.where(has, last - first + 1, 0)


def owner_of_image(image):
    return jnp.minimum((image * IMG_LEN + IMG_LEN // 2) // CHIP_ROWS, CHIPS - 1)


def in_image(image, has, first, rows, axis):
    shape = (rows, 1) if axis == 0 else (1, rows)
    at = first * CHUNK + lax.broadcasted_iota(jnp.int32, shape, axis)
    there = (at >= image * IMG_LEN) & (at < jnp.minimum((image + 1) * IMG_LEN, TOKENS))
    return there & has


def diagonal_tile(tile):
    row = tile * TILE + lax.broadcasted_iota(jnp.int32, (TILE, SPAN), 0)
    return row == lax.broadcasted_iota(jnp.int32, (TILE, SPAN), 1)


def attend_tile(image, has, first, batch, tile, live, q_ref, k_ref, v_ref, att_ref, lse_ref, acc):
    rows = pl.ds(pl.multiple_of(tile * TILE, TILE), TILE)
    visible = in_image(image, has, first, SPAN, 1) & (live | diagonal_tile(tile))
    stats = jnp.zeros((TILE, 128), jnp.float32)
    lane = lax.broadcasted_iota(jnp.int32, (TILE, 128), 1)
    acc[...] = jnp.zeros_like(acc)
    for head in range(CORE_HEADS):
        low, high, _ = head_lanes(head)
        mask = head_mask(head)
        query = jnp.where(mask, q_ref[batch, rows, low:high], 0)
        scores = jnp.where(visible, mm(query, k_ref[batch, :, low:high], NT) * SCALE, MASKED)
        largest = jnp.max(scores, axis=1, keepdims=True)
        exponent = jnp.exp(scores - largest)
        total = jnp.sum(exponent, axis=1, keepdims=True)
        probs = (exponent * (1.0 / total)).astype(jnp.bfloat16)
        part = mm(probs, v_ref[batch, :, low:high], NN)
        acc[:, low:high] += jnp.where(mask, part, 0.0)
        stats = jnp.where(lane == head, largest + jnp.log(total), stats)
    lse_ref[batch, rows] = stats
    att_ref[batch, rows] = acc[...].astype(jnp.bfloat16)


class Scatter:
    def __init__(self, place, grad_ref, total_ref, split, scratch):
        self.core, self.x, self.y, self.z = place
        self.grad_ref, self.total_ref, self.split = grad_ref, total_ref, split
        (self.half_x, self.half_y, self.whole_x, self.whole_y, self.from_z) = scratch[:5]
        (self.half_out, self.half_in, self.pair_out, self.pair_in, self.z_out, self.z_in) = scratch[5:]

    @staticmethod
    def scratch(shape, split):
        rows, columns = shape[1:]
        dma = pltpu.SemaphoreType.DMA
        block = lambda count, width: pltpu.VMEM((count, rows, width), jnp.bfloat16)
        return (
            [block(4, split), block(4, columns - split)]
            + [block(4, columns), block(4, columns), block(3, columns)]
            + [dma((2, 4)), dma((2, 4)), dma((2, 4)), dma((2, 4)), dma((3,)), dma((3,))]
        )

    COUNT = 11

    def unit(self, at_x, at_y, turn):
        at_z = (self.z + 1 + turn) % 4
        return self.grad_ref.at[(at_z * 2 + at_y) * 2 + at_x]

    def remote(self, source, target_ref, send_sem, recv_sem, device):
        return pltpu.make_async_remote_copy(
            src_ref=source,
            dst_ref=target_ref,
            send_sem=send_sem,
            recv_sem=recv_sem,
            device_id=device,
            device_id_type=MESH_ID,
        )

    def half(self, turn, axis):
        diagonal = self.unit(1 - self.x, 1 - self.y, turn)
        columns = self.grad_ref.shape[2]
        source = diagonal.at[:, pl.ds(0, self.split) if axis == 0 else pl.ds(self.split, columns - self.split)]
        device = (peer(1 - self.x, self.y, self.z, self.core), peer(self.x, 1 - self.y, self.z, self.core))[axis]
        target = (self.half_x, self.half_y)[axis].at[turn]
        return self.remote(source, target, self.half_out.at[axis, turn], self.half_in.at[axis, turn], device)

    def whole(self, turn, axis):
        device = (peer(1 - self.x, self.y, self.z, self.core), peer(self.x, 1 - self.y, self.z, self.core))[axis]
        source = (self.unit(1 - self.x, self.y, turn), self.unit(self.x, 1 - self.y, turn))[axis]
        target = (self.whole_x, self.whole_y)[axis]
        return self.remote(
            source, target.at[turn], self.pair_out.at[axis, turn], self.pair_in.at[axis, turn], device
        )

    def along(self, turn):
        device = peer(self.x, self.y, (self.z + 1 + turn) % 4, self.core)
        return self.remote(self.unit(self.x, self.y, turn), self.from_z.at[turn], self.z_out.at[turn], self.z_in.at[turn], device)

    def begin(self, turn):
        self.half(turn, 0).start()
        self.half(turn, 1).start()

    def pair(self, turn):
        split = self.split
        wide = lambda value: value.astype(jnp.float32)
        self.half(turn, 0).wait_recv()
        grad = self.unit(self.x, 1 - self.y, turn)
        grad[:, :split] = (wide(grad[:, :split]) + wide(self.half_x[turn])).astype(jnp.bfloat16)
        self.whole(turn, 1).start()
        self.half(turn, 1).wait_recv()
        grad = self.unit(1 - self.x, self.y, turn)
        grad[:, split:] = (wide(grad[:, split:]) + wide(self.half_y[turn])).astype(jnp.bfloat16)
        self.whole(turn, 0).start()

    def join(self, turn):
        wide = lambda value: value.astype(jnp.float32)
        self.whole(turn, 0).wait_recv()
        self.whole(turn, 1).wait_recv()
        own = self.unit(self.x, self.y, turn)
        total = wide(own[...]) + (wide(self.whole_x[turn]) + wide(self.whole_y[turn]))

        @pl.when(turn < 3)
        def _():
            own[...] = total.astype(jnp.bfloat16)
            self.along(turn).start()

        @pl.when(turn == 3)
        def _():
            self.total_ref[...] = total

    def total(self, turn):
        self.along(turn).wait_recv()
        self.total_ref[...] += self.from_z[turn].astype(jnp.float32)

    def finish(self):
        def pairs(turn, carry):
            for axis in range(2):
                self.half(turn, axis).wait_send()
                self.whole(turn, axis).wait_send()
            return carry

        def lines(turn, carry):
            self.along(turn).wait_send()
            return carry

        lax.fori_loop(0, 4, pairs, 0)
        lax.fori_loop(0, 3, lines, 0)


def each_turn(action, count=4):
    def body(turn, carry):
        action(turn)
        return carry

    lax.fori_loop(0, count, body, 0)


def attend_back_tile(
    image, has, first, batch, tile, live,
    q_ref, k_ref, v_ref, g_ref, stt_ref, dq_acc, dk_acc, dv_acc,
):
    rows = pl.ds(pl.multiple_of(tile * TILE, TILE), TILE)
    queries_there = in_image(image, has, first, SPAN, 1)
    at = first * CHUNK + tile * TILE + lax.broadcasted_iota(jnp.int32, (TILE, 1), 0)
    keys_there = (at >= image * IMG_LEN) & (at < jnp.minimum((image + 1) * IMG_LEN, TOKENS)) & has
    visible = queries_there & keys_there & (live | diagonal_tile(tile))
    dk_acc[...] = jnp.zeros_like(dk_acc)
    dv_acc[...] = jnp.zeros_like(dv_acc)

    @pl.when(tile == 0)
    def _():
        dq_acc[...] = jnp.zeros_like(dq_acc)

    for head in range(CORE_HEADS):
        low, high, _ = head_lanes(head)
        mask = head_mask(head)
        keys = jnp.where(mask, k_ref[batch, rows, low:high], 0)
        values = jnp.where(mask, v_ref[batch, rows, low:high], 0)
        queries = q_ref[batch, :, low:high]
        grads = g_ref[batch, :, low:high]
        lse = stt_ref[batch, head : head + 1]
        delta = stt_ref[batch, CORE_HEADS + head : CORE_HEADS + head + 1]
        probs = jnp.where(visible, jnp.exp(mm(keys, queries, NT) * SCALE - lse), 0.0)
        dv_acc[:, low:high] += jnp.where(mask, mm(probs.astype(jnp.bfloat16), grads, NN), 0.0)
        grad_probs = mm(values, grads, NT)
        grad_raw = (probs * (grad_probs - delta) * SCALE).astype(jnp.bfloat16)
        dk_acc[:, low:high] += jnp.where(mask, mm(grad_raw, queries, NN), 0.0)
        dq_acc[:, low:high] += mm(grad_raw, keys, TN)
    k_ref[batch, rows] = dk_acc[...].astype(jnp.bfloat16)
    v_ref[batch, rows] = dv_acc[...].astype(jnp.bfloat16)

    @pl.when(tile == SPAN // TILE - 1)
    def _():
        q_ref[batch] = dq_acc[:, :HALF].astype(jnp.bfloat16)


BACK_SPLITS = (640, 1152, 256, 896)


class Rows:
    def __init__(self, place):
        core, x, y, z = place
        self.core = core
        self.chip = (z * 2 + y) * 2 + x
        self.device = self.chip * 2 + core
        self.image, self.has, self.first, self.count = image_of_chip(self.chip)
        start = self.device * SHARD
        images = [start // IMG_LEN, (start + SHARD - 1) // IMG_LEN]
        self.parts = []
        for part, image in enumerate(images):
            low = jnp.maximum(image * IMG_LEN - start, 0) // CHUNK
            high = jnp.minimum((image + 1) * IMG_LEN - 1 - start, SHARD - 1) // CHUNK + 1
            if part == 1:
                high = jnp.where(images[1] == images[0], low, high)
            self.parts.append((owner_of_image(image), image * IMG_LEN // CHUNK, low, high))

    def peers(self):
        holders = [
            ((self.first // SHARD_CHUNKS + n,), self.holds(n)) for n in range(SPAN_DEVICES)
        ]
        images = [
            ((owner * 2 + side,), jnp.logical_and(high > low, owner * 2 + side != self.device))
            for owner, _, low, high in self.parts
            for side in range(2)
        ]
        return holders + images

    def holds(self, n):
        device = self.first // SHARD_CHUNKS + n
        last = (self.first + self.count - 1) // SHARD_CHUNKS
        there = jnp.logical_and(self.count > 0, device <= last)
        return jnp.logical_and(there, device != self.device)

    @staticmethod
    def scratch():
        dma = pltpu.SemaphoreType.DMA
        return [dma((2, 2, SHARD_CHUNKS)), dma((SPAN_CHUNKS,))]

    def span_rows(self, ref, chunk):
        return ref.at[:, pl.ds(pl.multiple_of(chunk * CHUNK, CHUNK), CHUNK)]

    def chunk_rows(self, ref, chunk):
        return ref.at[pl.ds(pl.multiple_of(chunk * CHUNK, CHUNK), CHUNK)]

    def each_own(self, action):
        for part, (owner, first, low, high) in enumerate(self.parts):
            for side in range(2):
                def body(chunk, carry):
                    action(part, side, chunk, owner * 2 + side, self.device * SHARD_CHUNKS + chunk - first)
                    return carry

                lax.fori_loop(low, high, body, 0)

    def each_span(self, action):
        def body(chunk, carry):
            at = self.first + chunk
            device = at // SHARD_CHUNKS
            part = jnp.where(device * SHARD // IMG_LEN == self.image, 0, 1)
            action(chunk, device, at % SHARD_CHUNKS, part)
            return carry

        lax.fori_loop(0, self.count, body, 0)

    def elsewhere(self, device, action, here):
        @pl.when(device != self.device)
        def _():
            action()

        if here is not None:
            @pl.when(device == self.device)
            def _():
                here()

    def to_images(self, sources, span_ref, sems):
        token_sems, span_sems = sems

        def start(part, side, chunk, device, at):
            source, target = self.span_rows(sources[side], chunk), self.span_rows(span_ref, at)
            copy = remote(source, target, token_sems.at[part, side, chunk], span_sems.at[at], (device,))
            self.elsewhere(device, copy.start, pltpu.make_async_copy(source, target, span_sems.at[at]).start)

        self.each_own(start)

    def images_arrived(self, sources, span_ref, sems):
        token_sems, span_sems = sems

        def wait(chunk, device, at, part):
            block = self.span_rows(span_ref, chunk)
            span_sem = span_sems.at[chunk]
            copy = remote(block, block, token_sems.at[0, 0, 0], span_sem, (device,))
            local = pltpu.make_async_copy(self.span_rows(sources[0], at), block, span_sem)
            self.elsewhere(device, copy.wait_recv, local.wait)

        def sent(part, side, chunk, device, at):
            source = self.span_rows(sources[side], chunk)
            copy = remote(source, source, token_sems.at[part, side, chunk], span_sems.at[0], (device,))
            self.elsewhere(device, copy.wait_send, None)

        self.each_span(wait)
        self.each_own(sent)

    def to_both(self, own_ref, span_ref, sems):
        token_sems, span_sems, _, _ = sems

        def start(part, side, chunk, device, at):
            source, target = self.span_rows(own_ref, chunk), self.span_rows(span_ref, at)
            copy = remote(source, target, token_sems.at[part, 0, chunk], span_sems.at[at], (device,))

            def here():
                target[...] = source[...]

            @pl.when(side == self.core)
            def _():
                self.elsewhere(device, copy.start, here)

        self.each_own(start)

    def trade(self, span_ref, chunk, sems):
        block = self.span_rows(span_ref, chunk)
        return remote(block, block, sems[2].at[chunk], sems[3].at[chunk], (self.chip * 2 + 1 - self.core,))

    def relay(self, span_ref, sems):
        token_sems, span_sems, _, _ = sems

        def pass_on(chunk, device, at, part):
            block = self.span_rows(span_ref, chunk)
            copy = remote(block, block, token_sems.at[0, 0, 0], span_sems.at[chunk], (device,))

            @pl.when(device % 2 == self.core)
            def _():
                self.elsewhere(device, copy.wait_recv, None)
                self.trade(span_ref, chunk, sems).start()

        self.each_span(pass_on)

    def both_arrived(self, own_ref, span_ref, sems):
        token_sems, span_sems, _, _ = sems

        def traded(chunk, device, at, part):
            @pl.when(device % 2 == self.core)
            def _():
                self.trade(span_ref, chunk, sems).wait_send()

            @pl.when(device % 2 != self.core)
            def _():
                self.trade(span_ref, chunk, sems).wait_recv()

        def sent(part, side, chunk, device, at):
            source = self.span_rows(own_ref, chunk)
            copy = remote(source, source, token_sems.at[part, 0, chunk], span_sems.at[0], (device,))

            @pl.when(side == self.core)
            def _():
                self.elsewhere(device, copy.wait_send, None)

        self.each_span(traded)
        self.each_own(sent)

    def batch_to_tokens(self, span_ref, landing, sems):
        token_sems, span_sems = sems

        def start(chunk, device, at, part):
            source, target = self.chunk_rows(span_ref, chunk), self.chunk_rows(landing.at[part, self.core], at)
            token_sem = token_sems.at[part, self.core, at]
            copy = remote(source, target, span_sems.at[chunk], token_sem, (device,))
            self.elsewhere(device, copy.start, pltpu.make_async_copy(source, target, token_sem).start)

        self.each_span(start)

    def batches_arrived(self, span_ref, landing, sems):
        token_sems, span_sems = sems

        def wait(part, side, chunk, device, at):
            source, target = self.chunk_rows(span_ref, at), self.chunk_rows(landing.at[part, side], chunk)
            token_sem = token_sems.at[part, side, chunk]
            copy = remote(target, target, span_sems.at[0], token_sem, (device,))
            self.elsewhere(device, copy.wait_recv, pltpu.make_async_copy(source, target, token_sem).wait)

        def sent(chunk, device, at, part):
            block = self.chunk_rows(span_ref, chunk)
            copy = remote(block, block, span_sems.at[chunk], token_sems.at[0, 0, 0], (device,))
            self.elsewhere(device, copy.wait_send, None)

        self.each_own(wait)
        self.each_span(sent)

    def to_tokens(self, span_ref, landing, sems):
        token_sems, span_sems = sems

        def start(chunk, device, at, part):
            source = self.span_rows(span_ref, chunk)
            target = self.span_rows(landing.at[part, self.core], at)
            copy = remote(source, target, span_sems.at[chunk], token_sems.at[part, self.core, at], (device,))

            def here():
                target[...] = source[...]

            self.elsewhere(device, copy.start, here)

        self.each_span(start)

    def tokens_arrived(self, span_ref, landing, sems):
        token_sems, span_sems = sems

        def wait(part, side, chunk, device, at):
            block = self.span_rows(landing.at[part, side], chunk)
            copy = remote(block, block, span_sems.at[0], token_sems.at[part, side, chunk], (device,))
            self.elsewhere(device, copy.wait_recv, None)

        def sent(chunk, device, at, part):
            block = self.span_rows(span_ref, chunk)
            copy = remote(block, block, span_sems.at[chunk], token_sems.at[0, 0, 0], (device,))
            self.elsewhere(device, copy.wait_send, None)

        self.each_own(wait)
        self.each_span(sent)


def backward_kernel(
    counts, q_in, k_in, v_in, hidden_in, weight_in, att_ref, lse_ref, low_ref, high_ref, down_in, *rest
):
    pairs_in, rest = rest[:8], rest[8:]
    sums_ref, landing, down_total, up_total, out_total, qkv_total = rest[:6]
    (
        arrived, down_ref, up_ref, out_ref, qkv_ref, dq_acc, dk_acc, dv_acc, span, stt_ref,
        load_sems, token_sems, span_sems, back_token_sems, back_span_sems, swap_out, swap_in,
    ) = rest[6:23]
    scratch = rest[23:]
    place = position_of()
    rows = Rows(place)
    batches = span.shape[0]

    def loading(pairs):
        loads = [pltpu.make_async_copy(a, b, load_sems.at[n]) for n, (a, b) in enumerate(pairs)]
        for load in loads:
            load.start()
        return loads

    first_load = loading([(down_in, down_ref)])
    greet(pair_peers(*place) + line_peers(*place) + [(partner_of(*place), True)] + rows.peers())
    sems, sources = (token_sems, span_sems), (low_ref, high_ref)
    rows.to_images(sources, span, sems)
    count = Scatter.COUNT
    down, up, out, qkv = [
        Scatter(place, grad, total, split, scratch[n * count : (n + 1) * count])
        for n, (grad, total, split) in enumerate(
            zip((down_ref, up_ref, out_ref, qkv_ref), (down_total, up_total, out_total, qkv_total), BACK_SPLITS)
        )
    ]
    first_load[0].wait()
    each_turn(down.begin)

    def loop(action, first, last):
        def body(turn, carry):
            action(turn)
            return carry

        lax.fori_loop(first, last, body, 0)

    def rows_grad(left, right, grad_ref, blocks):
        for half in range(2):
            units = slice(half * CHIPS // 2, (half + 1) * CHIPS // 2)
            for first, end in blocks:
                width = end - first
                dq_acc[:HALF, :width] = mm(left[half * HALF : (half + 1) * HALF], right[:, first:end], NN)
                grad_ref[units, :, first:end] = dq_acc[:HALF, :width].reshape(CHIPS // 2, ROWS, width).astype(jnp.bfloat16)

    def weight_grads(left, turned, wide, narrow):
        own = pl.ds(0, SHARD * batches), pl.ds(SHARD * batches, SHARD * batches)
        h2, h2_swap, gu, gu_swap, att, att_swap, gb, gb_swap = pairs_in
        loads = loading(
            [(h2, left.at[own[0]]), (h2_swap, left.at[own[1]]), (gu, wide.at[own[0]]), (gu_swap, wide.at[own[1]])]
            + [(gb, narrow.at[own[0]]), (gb_swap, narrow.at[own[1]])]
        )
        for load in loads:
            load.wait()
        turned[...] = left[...].T
        loads = loading([(att, left.at[own[0]]), (att_swap, left.at[own[1]])])
        rows_grad(turned, wide, up_ref, [(0, 640), (640, 1280), (1280, 1920), (1920, FFH)])
        loop(down.pair, 0, 4)
        each_turn(up.begin)
        for load in loads:
            load.wait()
        turned[...] = left[...].T
        rows_grad(turned, narrow, out_ref, [(0, HALF)])

    tokens = 2 * SHARD * batches
    pl.run_scoped(
        weight_grads,
        pltpu.VMEM((tokens, D), jnp.bfloat16),
        pltpu.VMEM((D, tokens), jnp.bfloat16),
        pltpu.VMEM((tokens, FFH), jnp.bfloat16),
        pltpu.VMEM((tokens, HALF), jnp.bfloat16),
    )

    def attention(q_ref, k_ref, v_ref, hidden, weight):
        loads = loading([(q_in, q_ref), (k_in, k_ref), (v_in, v_ref), (hidden_in, hidden), (weight_in, weight)])
        each_turn(out.begin)
        rows.images_arrived(sources, span, sems)

        def prepare(batch, carry):
            there = in_image(rows.image, rows.has, rows.first, SPAN, 0)
            grads = jnp.where(there, span[batch], 0)
            span[batch] = grads
            lane = lax.broadcasted_iota(jnp.int32, (SPAN, 128), 1)
            stats = jnp.where(lane < CORE_HEADS, lse_ref[batch], 0.0)
            for head in range(CORE_HEADS):
                low, high, _ = head_lanes(head)
                product = grads[:, low:high].astype(jnp.float32) * att_ref[batch, :, low:high].astype(jnp.float32)
                total = jnp.sum(jnp.where(head_mask(head), product, 0.0), axis=1, keepdims=True)
                stats = jnp.where(lane == CORE_HEADS + head, total, stats)
            stt_ref[batch] = stats.T[: 2 * CORE_HEADS]
            return carry

        lax.fori_loop(0, batches, prepare, 0)
        for load in loads:
            load.wait()
        tiles = SPAN // TILE
        work = {
            1: [(down.join, 0, 1)],
            3: [(down.join, 1, 2), (up.pair, 0, 1)],
            5: [(down.join, 2, 3), (up.pair, 1, 2)],
            7: [(down.join, 3, 4), (up.pair, 2, 3)],
            9: [(up.pair, 3, 4)],
            11: [(out.pair, 0, 4), (up.join, 0, 1)],
        }

        def attend(index, carry):
            batch, tile = index // tiles, index % tiles
            attend_back_tile(
                rows.image, rows.has, rows.first, batch, tile, rows.image < counts[batch],
                q_ref, k_ref, v_ref, span, stt_ref, dq_acc, dk_acc, dv_acc,
            )
            for at, actions in work.items():
                @pl.when(index == at)
                def _():
                    for action, first, last in actions:
                        loop(action, first, last)
            return carry

        lax.fori_loop(0, batches * tiles, attend, 0)
        columns = lambda ref: sum(jnp.sum(ref[b].astype(jnp.float32), axis=0, keepdims=True) for b in range(batches))
        sums_ref[0:1] = columns(q_ref)
        sums_ref[1:2] = columns(v_ref)

        def weight_grad(first, end, grads):
            for half in range(2):
                units = slice(half * CHIPS // 2, (half + 1) * CHIPS // 2)
                for batch in range(batches):
                    part = mm(hidden[batch, :, half * HALF : (half + 1) * HALF], grads(batch), TN)
                    if batch == 0:
                        dq_acc[:HALF, : end - first] = part
                    else:
                        dq_acc[:HALF, : end - first] += part
                total = dq_acc[:HALF, : end - first].reshape(CHIPS // 2, ROWS, end - first)
                qkv_ref[units, :, first:end] = total.astype(jnp.bfloat16)

        weight_grad(0, 640, lambda batch: jnp.concatenate([q_ref[batch], k_ref[batch, :, :64]], axis=1))
        weight_grad(640, D, lambda batch: k_ref[batch, :, 64:])
        weight_grad(D, 3 * HALF, lambda batch: v_ref[batch])
        each_turn(qkv.begin)

        def token_grad(batch, others):
            def block(index, carry):
                here = pl.ds(pl.multiple_of(index * TILE, TILE), TILE)
                grads = jnp.concatenate([ref[batch, here] for ref in (q_ref, k_ref, v_ref)], axis=1)
                total = mm(grads, weight[...], NT)
                if others is not None:
                    total = total + others[here].astype(jnp.float32)
                hidden[batch, here] = total.astype(jnp.bfloat16)
                return carry

            lax.fori_loop(0, SPAN // TILE, block, 0)

        core = place[0]
        token_grad(1 - core, None)
        trade = remote(hidden.at[1 - core], arrived, swap_out, swap_in, partner_of(*place))
        trade.start()
        loop(up.join, 1, 2)
        trade.wait_recv()
        token_grad(core, arrived)
        back_sems = (back_token_sems, back_span_sems)
        rows.batch_to_tokens(hidden.at[core], landing, back_sems)
        loop(up.join, 2, 4)
        each_turn(qkv.pair)
        each_turn(out.join)
        each_turn(down.total, 3)
        each_turn(qkv.join)
        each_turn(up.total, 3)
        each_turn(out.total, 3)
        each_turn(qkv.total, 3)
        trade.wait_send()
        rows.batches_arrived(hidden.at[core], landing, back_sems)

    held = lambda *shape: pltpu.VMEM(shape, jnp.bfloat16)
    pl.run_scoped(
        attention, *[held(batches, SPAN, HALF)] * 3, held(batches, SPAN, D), held(D, 3 * HALF)
    )
    for scatter in (down, up, out, qkv):
        scatter.finish()


def backward(counts, query, keys, values, hidden, weight, attended, lse, low, high, down, pairs, collective_id):
    batches = query.shape[0]
    vmem, hbm = pl.BlockSpec(memory_space=pltpu.VMEM), pl.BlockSpec(memory_space=pl.ANY)
    shapes = [down.shape, (CHIPS, ROWS, FFH), (CHIPS, ROWS, HALF), (CHIPS, ROWS, 3 * HALF)]
    held = lambda *shape: pltpu.VMEM(shape, jnp.bfloat16)
    dma = pltpu.SemaphoreType.DMA
    return pl.pallas_call(
        backward_kernel,
        out_shape=[jax.ShapeDtypeStruct((2, HALF), jnp.float32)]
        + [jax.ShapeDtypeStruct((2, batches, SHARD, D), jnp.bfloat16)]
        + [jax.ShapeDtypeStruct(shape[1:], jnp.float32) for shape in shapes],
        in_specs=[pl.BlockSpec(memory_space=pltpu.SMEM)] + [hbm] * 5 + [vmem] * 2 + [hbm] * (3 + len(pairs)),
        out_specs=[vmem, hbm] + [vmem] * 4,
        scratch_shapes=[held(SPAN, D)]
        + [held(*shape) for shape in shapes]
        + [
            pltpu.VMEM((SPAN, HALF + 64), jnp.float32),
            pltpu.VMEM((TILE, HALF), jnp.float32),
            pltpu.VMEM((TILE, HALF), jnp.float32),
            held(batches, SPAN, HALF),
            pltpu.VMEM((batches, 2 * CORE_HEADS, SPAN), jnp.float32),
            dma((8,)),
        ]
        + Rows.scratch() * 2
        + [dma] * 2
        + sum([Scatter.scratch(shape, split) for shape, split in zip(shapes, BACK_SPLITS)], []),
        compiler_params=pltpu.CompilerParams(
            collective_id=collective_id, has_side_effects=True, vmem_limit_bytes=60 * 1024 * 1024
        ),
        cost_estimate=pl.CostEstimate(flops=0, bytes_accessed=500 * 10**6, transcendentals=0),
        name="backward",
    )(counts, query, keys, values, hidden, weight, attended, lse, low, high, down, *pairs)


def chip_unit(core, low, high):
    theirs = swap(by_core(core, high, low))
    return joined(core, by_core(core, low, high), theirs, 0)


def peer(x, y, z, core):
    return (((z * 2 + y) * 2 + x) * 2 + core,)


MESH_ID = pl.DeviceIdType.MESH


def position_of():
    device = lax.axis_index("dev")
    return device % 2, device // 2 % 2, device // 4 % 2, device // 8


def greet(targets):
    barrier = pltpu.get_barrier_semaphore()
    count = 0
    for target, there in targets:
        if there is True:
            pl.semaphore_signal(barrier, inc=1, device_id=target, device_id_type=MESH_ID)
            count = count + 1
        else:
            @pl.when(there)
            def _():
                pl.semaphore_signal(barrier, inc=1, device_id=target, device_id_type=MESH_ID)
            count = count + there.astype(jnp.int32)
    pl.semaphore_wait(barrier, count)


def pair_peers(core, x, y, z):
    return [(peer(1 - x, y, z, core), True), (peer(x, 1 - y, z, core), True)]


def next_peers(core, x, y, z):
    return [(peer(x, y, z - 1, core), z > 0), (peer(x, y, z + 1, core), z < 3)]


def line_peers(core, x, y, z):
    return [(peer(x, y, (z + step) % 4, core), True) for step in (1, 2, 3)]


def partner_of(core, x, y, z):
    return peer(x, y, z, 1 - core)


class Gather:
    def __init__(self, place, unit_ref, full_ref, other_ref, split, sems):
        self.core, self.x, self.y, self.z = place
        self.unit_ref, self.full_ref, self.other_ref, self.split = unit_ref, full_ref, other_ref, split
        (
            self.z_out,
            self.z_in,
            self.pair_out,
            self.pair_in,
            self.half_out,
            self.half_in,
            self.chain_out,
            self.chain_in,
            self.own_sem,
        ) = sems[:9]
        if other_ref is not None:
            self.swap_out, self.swap_in = sems[9:]
        self.sides = ((-1, self.z > 0), (1, self.z < 3))
        self.x_peer = peer(1 - self.x, self.y, self.z, self.core)
        self.y_peer = peer(self.x, 1 - self.y, self.z, self.core)

    @staticmethod
    def scratch(partner):
        dma = pltpu.SemaphoreType.DMA
        shapes = [(2, 4), (4,), (2, 4), (2, 4), (2, 4), (2, 4), (2, 4), (4,)]
        return [dma(shape) for shape in shapes] + [dma] + ([dma((CHIPS,))] * 2 if partner else [])

    def unit_index(self, at_x, at_y, at_z):
        return (at_z * 2 + at_y) * 2 + at_x

    def slot(self, at_x, at_y, at_z):
        return self.full_ref.at[self.unit_index(at_x, at_y, at_z)]

    def column(self, turn, at_z):
        at_x, at_y = [(self.x, self.y), (self.x, 1 - self.y), (1 - self.x, self.y), (1 - self.x, 1 - self.y)][turn]
        return self.slot(at_x, at_y, at_z)

    def copy(self, block, send_sem, recv_sem, target, source=None):
        return pltpu.make_async_remote_copy(
            src_ref=block if source is None else source,
            dst_ref=block,
            send_sem=send_sem,
            recv_sem=recv_sem,
            device_id=target,
            device_id_type=MESH_ID,
        )

    def along(self, at_z, side, source=None):
        index = 0 if side < 0 else 1
        target = peer(self.x, self.y, self.z + side, self.core)
        return self.copy(self.column(0, at_z), self.z_out.at[index, at_z], self.z_in.at[at_z], target, source)

    def chain(self, at_z, side):
        index = 0 if side < 0 else 1
        target = peer(self.x, self.y, self.z + side, self.core)
        return self.copy(self.column(3, at_z), self.chain_out.at[index, at_z], self.chain_in.at[at_z], target)

    def whole(self, at_z, axis, source=None):
        target = (self.x_peer, self.y_peer)[axis]
        return self.copy(self.column(0, at_z), self.pair_out.at[axis, at_z], self.pair_in.at[axis, at_z], target, source)

    def part(self, block, axis):
        width = self.full_ref.shape[2]
        return block.at[:, pl.ds(0, self.split) if axis == 0 else pl.ds(self.split, width - self.split)]

    def half(self, at_z, axis):
        block = self.part(self.column(1 + axis, at_z), axis)
        target = (self.x_peer, self.y_peer)[axis]
        return self.copy(block, self.half_out.at[axis, at_z], self.half_in.at[axis, at_z], target)

    def half_arrival(self, at_z, axis):
        block = self.part(self.column(3, at_z), axis)
        return self.copy(block, self.half_out.at[axis, at_z], self.half_in.at[axis, at_z], self.x_peer)

    def by_halves(self, at_z):
        near = jnp.logical_and(jnp.abs(at_z - self.z) == 1, jnp.logical_or(at_z == 1, at_z == 2))
        return jnp.logical_or(at_z == self.z, near)

    def trade(self, turn, at_z, source=None):
        at_x, at_y = [(self.x, self.y), (self.x, 1 - self.y), (1 - self.x, self.y), (1 - self.x, 1 - self.y)][turn]
        index = self.unit_index(at_x, at_y, at_z)
        block = self.full_ref.at[index] if source is None else source
        width = self.other_ref.shape[2]
        if width < self.full_ref.shape[2]:
            block = block.at[:, pl.ds(0, width)]
        return pltpu.make_async_remote_copy(
            src_ref=block,
            dst_ref=self.other_ref.at[index],
            send_sem=self.swap_out.at[index],
            recv_sem=self.swap_in.at[index],
            device_id=peer(self.x, self.y, self.z, 1 - self.core),
            device_id_type=MESH_ID,
        )

    def share(self, turn, at_z, source=None):
        if self.other_ref is not None:
            self.trade(turn, at_z, source).start()

    def each(self, distance, action):
        if distance == 0:
            action(self.z, 0)
            return
        for side in (-1, 1):
            at_z = self.z + side * distance
            @pl.when(jnp.logical_and(at_z >= 0, at_z <= 3))
            def _():
                action(at_z, side)

    def onwards(self, side, action):
        for to, there in self.sides:
            if side == 0 or to == -side:
                @pl.when(there)
                def _():
                    action(to)

    def arrive(self, at_z, side):
        source = None
        if side == 0:
            source = self.unit_ref
            pltpu.make_async_copy(self.unit_ref, self.column(0, at_z), self.own_sem).start()
        else:
            self.along(at_z, side).wait_recv()
        self.onwards(side, lambda to: self.along(at_z, to, source).start())
        self.whole(at_z, 0, source).start()
        self.whole(at_z, 1, source).start()
        self.share(0, at_z, source)

    def cross(self, at_z, side):
        for axis in (1, 0):
            arrived = self.column(2 - axis, at_z)
            self.copy(arrived, self.pair_out.at[axis, at_z], self.pair_in.at[axis, at_z], self.x_peer).wait_recv()
            @pl.when(self.by_halves(at_z))
            def _():
                self.half(at_z, 1 - axis).start()
            self.share(2 - axis, at_z)

    def far_chain(self, at_z, side):
        return jnp.logical_or(at_z == 0, at_z == 3) if side == 0 else True

    def diagonal(self, at_z, side):
        halves = self.by_halves(at_z)
        @pl.when(halves)
        def _():
            self.half_arrival(at_z, 0).wait_recv()
            self.half_arrival(at_z, 1).wait_recv()
        if side != 0:
            @pl.when(jnp.logical_not(halves))
            def _():
                self.chain(at_z, side).wait_recv()
        @pl.when(self.far_chain(at_z, side))
        def _():
            self.onwards(side, lambda to: self.chain(at_z, to).start())
        self.share(3, at_z)

    def steps(self):
        order = [
            (0, self.arrive),
            (1, self.arrive),
            (0, self.cross),
            (2, self.arrive),
            (0, self.diagonal),
            (1, self.cross),
            (3, self.arrive),
            (1, self.diagonal),
            (2, self.cross),
            (2, self.diagonal),
            (3, self.cross),
            (3, self.diagonal),
        ]
        return [partial(self.each, distance, action) for distance, action in order]

    def settle(self, at_z, side):
        self.onwards(side, lambda to: self.along(at_z, to).wait_send())
        @pl.when(self.far_chain(at_z, side))
        def _():
            self.onwards(side, lambda to: self.chain(at_z, to).wait_send())
        for axis in range(2):
            self.whole(at_z, axis).wait_send()
            @pl.when(self.by_halves(at_z))
            def _():
                self.half(at_z, axis).wait_send()

    def own_ready(self):
        pltpu.make_async_copy(self.unit_ref, self.column(0, self.z), self.own_sem).wait()

    def finish(self):
        for distance in range(4):
            self.each(distance, self.settle)
        if self.other_ref is not None:
            def traded(at_z, carry):
                for turn in range(4):
                    self.trade(turn, at_z).wait()
                return carry

            lax.fori_loop(0, 4, traded, 0)


def remote(source, target, send_sem, recv_sem, device):
    return pltpu.make_async_remote_copy(
        src_ref=source,
        dst_ref=target,
        send_sem=send_sem,
        recv_sem=recv_sem,
        device_id=device,
        device_id_type=MESH_ID,
    )


PADDED = 80
WIDE = CHIPS * PADDED
SHARE = 423


def vector_part(full_ref, start, length, width):
    lane = lax.broadcasted_iota(jnp.int32, (1, width), 1)
    total = jnp.zeros((1, width), jnp.float32)
    for device in range(start // SHARE, (start + length - 1) // SHARE + 1):
        base = 512 * (device % 2)
        tile = full_ref[device // 2, PADDED - 16 :, base : base + 512].astype(jnp.float32)
        row = tile[ROWS - PADDED + 16 : ROWS - PADDED + 17]
        if width > 512:
            row = jnp.concatenate([row, jnp.zeros((1, width - 512), jnp.float32)], axis=1)
        shift = device * SHARE - start
        row = pltpu.roll(row, shift % width, 1) if shift % width else row
        first, last = max(shift, 0), min(shift + SHARE, length)
        total = total + jnp.where((lane >= first) & (lane < last), row, 0.0)
    return total


LAG = 5
ROWS_AT = (0, 2, 6)
PROJECT_STEPS = ((0, 0, 7, 8), (1, 1, 2, 3), (2, 0, 8, 9), (3, 1, 3, 4), (4, 0, 9, 10), (5, 1, 4, 5))
ATTEND_STEPS = ((2, 0, 10, 11), (4, 1, 5, 6), (6, 0, 11, 12), (8, 1, 6, 7), (10, 1, 7, 8))
LAST_STEPS = ((1, 8, 12),)


def forward_kernel(
    splits, counts, unit, up_unit, down_unit, tokens_ref, pad_ref,
    q_out, k_out, v_out, hidden_out, att_out, lse_out, full_out, landing, up_ref, up_other, down_ref, down_other,
    q_ref, k_ref, v_ref, hidden_ref, att_ref, lse_ref, full_ref, store_sems, span, padded, acc, token_sems, span_sems, trade_out, trade_in, back_token_sems, back_span_sems, *sems
):
    place = position_of()
    rows = Rows(place)
    greet(pair_peers(*place) + next_peers(*place) + [(partner_of(*place), True)] + rows.peers())
    plain, more = len(Gather.scratch(False)), len(Gather.scratch(True))
    first = Gather(place, unit, full_ref, None, splits[0], sems[:plain])
    second = Gather(place, up_unit, up_ref, up_other, splits[1], sems[plain : plain + more])
    third = Gather(place, down_unit, down_ref, down_other, splits[2], sems[plain + more :])
    held = (q_ref, k_ref, v_ref, hidden_ref, att_ref, lse_ref, full_ref)
    outs = (q_out, k_out, v_out, hidden_out, att_out, lse_out, full_out)
    stores = [pltpu.make_async_copy(a, b, store_sems.at[n]) for n, (a, b) in enumerate(zip(held, outs))]
    one, two, three = first.steps(), second.steps(), third.steps()
    row_sems = (token_sems, span_sems, trade_out, trade_in)

    def run(steps, start, stop):
        for step in steps[start:stop]:
            step()

    row_steps = {
        ROWS_AT[0]: partial(rows.to_both, tokens_ref, span, row_sems),
        ROWS_AT[1]: partial(rows.relay, span, row_sems),
        ROWS_AT[2]: partial(rows.both_arrived, tokens_ref, span, row_sems),
    }
    for turn in range(len(one)):
        for lag, steps in enumerate((one, two, three)):
            if turn >= lag * LAG:
                run(steps, turn - lag * LAG, turn - lag * LAG + 1)
        if turn in row_steps:
            row_steps[turn]()
    first.own_ready()
    stores[6].start()
    batches = tokens_ref.shape[0]
    gain, bias = vector_part(full_ref, 0, D, WIDE)[:, :D], vector_part(full_ref, D, D, WIDE)[:, :D]
    core = place[0]
    half = lambda start: jnp.where(
        core == 0, vector_part(full_ref, start, HALF, 1024), vector_part(full_ref, start + HALF, HALF, 1024)
    )[:, :HALF]
    query_bias, value_bias = half(2 * D), half(3 * D)
    block = 256

    def between(table, index):
        for at, steps, start, stop in table:
            @pl.when(index == at)
            def _():
                run((two, three)[steps], start, stop)

    def project(index, carry):
        batch, at = index // (SPAN // block), index % (SPAN // block)
        here = pl.ds(pl.multiple_of(at * block, block), block)
        token = rows.first * CHUNK + at * block + lax.broadcasted_iota(jnp.int32, (block, 1), 0)
        there = (token >= rows.image * IMG_LEN) & (token < jnp.minimum((rows.image + 1) * IMG_LEN, TOKENS)) & rows.has
        value = jnp.where(there, span[batch, here], 0).astype(jnp.float32)
        centered = value - jnp.mean(value, axis=1, keepdims=True)
        inverse = lax.rsqrt(jnp.mean(centered * centered, axis=1, keepdims=True) + EPSILON)
        hidden = (centered * inverse * gain + bias).astype(jnp.bfloat16)
        hidden_ref[batch, here] = hidden
        padded[...] = mm(hidden, pad_ref[...], NN).astype(jnp.bfloat16)
        wide = mm(padded[...], full_ref[:, :, :D].reshape(WIDE, D), NN)
        q_ref[batch, here] = (wide[:, :HALF] + query_bias).astype(jnp.bfloat16)
        k_ref[batch, here] = wide[:, HALF:].astype(jnp.bfloat16)
        wide = mm(padded[...], full_ref[:, :, D:].reshape(WIDE, HALF), NN)
        v_ref[batch, here] = (wide + value_bias).astype(jnp.bfloat16)
        between(PROJECT_STEPS, index)
        return carry

    lax.fori_loop(0, batches * (SPAN // block), project, 0)
    for store in stores[:4]:
        store.start()
    tiles = SPAN // TILE

    def attend(index, carry):
        batch, tile = index // tiles, index % tiles
        attend_tile(
            rows.image, rows.has, rows.first, batch, tile, rows.image < counts[batch],
            q_ref, k_ref, v_ref, att_ref, lse_ref, acc,
        )
        between(ATTEND_STEPS, index)
        return carry

    lax.fori_loop(0, batches * tiles, attend, 0)
    for store in stores[4:6]:
        store.start()
    back_sems = (back_token_sems, back_span_sems)
    rows.to_tokens(att_ref, landing, back_sems)
    for steps, start, stop in LAST_STEPS:
        run((two, three)[steps], start, stop)
    rows.tokens_arrived(att_ref, landing, back_sems)
    second.own_ready()
    third.own_ready()
    for store in stores:
        store.wait()
    for gather in (first, second, third):
        gather.finish()


def forward(counts, unit, up_unit, down_unit, tokens, collective_id):
    batches = tokens.shape[0]
    full = lambda unit: jax.ShapeDtypeStruct((CHIPS,) + unit.shape, unit.dtype)
    low = lambda *shape: jax.ShapeDtypeStruct(shape, jnp.bfloat16)
    vmem, hbm = pl.BlockSpec(memory_space=pltpu.VMEM), pl.BlockSpec(memory_space=pl.ANY)
    dma = pltpu.SemaphoreType.DMA
    feature, lane = np.arange(D)[:, None], np.arange(WIDE)[None]
    pad = jnp.asarray(feature // ROWS * PADDED + feature % ROWS == lane, jnp.bfloat16)
    spans = [(batches, SPAN, HALF)] * 3 + [(batches, SPAN, D), (batches, SPAN, HALF)]
    outs = pl.pallas_call(
        partial(forward_kernel, (896, 1408, 640)),
        out_shape=[low(*shape) for shape in spans]
        + [
            jax.ShapeDtypeStruct((batches, SPAN, 128), jnp.float32),
            full(unit),
            low(2, 2, batches, SHARD, HALF),
            full(up_unit),
            full(up_unit),
            full(down_unit),
            full(down_unit),
        ],
        in_specs=[pl.BlockSpec(memory_space=pltpu.SMEM)] + [vmem] * 5,
        out_specs=[hbm] * 7 + [vmem] + [hbm] * 4,
        scratch_shapes=[pltpu.VMEM(shape, jnp.bfloat16) for shape in spans]
        + [
            pltpu.VMEM((batches, SPAN, 128), jnp.float32),
            pltpu.VMEM((CHIPS,) + unit.shape, unit.dtype),
            dma((7,)),
            pltpu.VMEM((batches, SPAN, D), jnp.bfloat16),
            pltpu.VMEM((256, WIDE), jnp.bfloat16),
            pltpu.VMEM((TILE, HALF), jnp.float32),
        ]
        + Rows.scratch()
        + [dma((SPAN_CHUNKS,)), dma((SPAN_CHUNKS,))]
        + Rows.scratch()
        + Gather.scratch(False)
        + Gather.scratch(True) * 2,
        compiler_params=pltpu.CompilerParams(
            collective_id=collective_id, has_side_effects=True, vmem_limit_bytes=60 * 1024 * 1024
        ),
        cost_estimate=pl.CostEstimate(flops=0, bytes_accessed=500 * 10**6, transcendentals=0),
        name="forward",
    )(counts, unit, up_unit, down_unit, tokens, pad)
    return list(outs[:8]) + [w.reshape(-1, w.shape[2]) for w in outs[8:]]


def vector_kernel(sent_ref, total_ref, arrived, send_sems, recv_sems):
    device = lax.axis_index("dev")
    devices = 2 * CHIPS
    mesh_id = pl.DeviceIdType.MESH
    barrier = pltpu.get_barrier_semaphore()

    def greet(step, carry):
        pl.semaphore_signal(
            barrier, inc=1, device_id=(lax.rem(device + step, devices),), device_id_type=mesh_id
        )
        return carry

    lax.fori_loop(1, devices, greet, 0)
    pl.semaphore_wait(barrier, devices - 1)

    def copy(step):
        target = lax.rem(device + step, devices)
        return pltpu.make_async_remote_copy(
            src_ref=sent_ref.at[target],
            dst_ref=arrived.at[step],
            send_sem=send_sems.at[step],
            recv_sem=recv_sems.at[step],
            device_id=(target,),
            device_id_type=mesh_id,
        )

    def start(step, carry):
        copy(step).start()
        return carry

    lax.fori_loop(1, devices, start, 0)

    def add(step, total):
        copy(step).wait()
        return total + arrived[step]

    total_ref[...] = lax.fori_loop(1, devices, add, sent_ref[device])


def scatter_vector(vector, share, collective_id):
    rows = jnp.pad(vector.reshape(2 * CHIPS, share), ((0, 0), (0, 1024 - share)))
    dma = pltpu.SemaphoreType.DMA
    total = pl.pallas_call(
        vector_kernel,
        out_shape=jax.ShapeDtypeStruct((8, 128), jnp.float32),
        in_specs=[pl.BlockSpec(memory_space=pltpu.VMEM)],
        out_specs=pl.BlockSpec(memory_space=pltpu.VMEM),
        scratch_shapes=[
            pltpu.VMEM((2 * CHIPS, 8, 128), jnp.float32),
            dma((2 * CHIPS,)),
            dma((2 * CHIPS,)),
        ],
        compiler_params=pltpu.CompilerParams(collective_id=collective_id, has_side_effects=True),
        cost_estimate=pl.CostEstimate(flops=0, bytes_accessed=20 * 10**6, transcendentals=0),
        name="scatter_vector",
    )(rows.reshape(2 * CHIPS, 8, 128))
    return total.reshape(-1)[:share]


def later_image(device):
    start = device * SHARD
    at = start + lax.broadcasted_iota(jnp.int32, (SHARD, 1), 0)
    return at >= (start // IMG_LEN + 1) * IMG_LEN


MLP_ROWS = SHARD
GELU_A, GELU_B = 0.7978845608028654, 0.044715


def mlp_kernel(
    x_ref, landing, g_ref, up_a, up_b, down_a, down_b, vec_ref, bias_ref,
    att_ref, result_ref, act_a, act_b, gu_a, gu_b, h2_ref, gb_a, gb_b, gm_ref, go_a, go_b, sums_ref, bias_sums_ref,
    wo_a, wo_b, up_w, down_w, slope, sems,
):
    loads = [
        pltpu.make_async_copy(source, target, sems.at[n])
        for n, (source, target) in enumerate(
            [
                (up_a.at[:, pl.ds(0, FFH)], up_w.at[0]),
                (up_b.at[:, pl.ds(0, FFH)], up_w.at[1]),
                (down_a, down_w.at[0]),
                (down_b, down_w.at[1]),
                (up_a.at[:, pl.ds(FFH, HALF)], wo_a),
                (up_b.at[:, pl.ds(FFH, HALF)], wo_b),
            ]
        )
    ]
    for load in loads[4:] + loads[:4]:
        load.start()
    sums_ref[...] = jnp.zeros_like(sums_ref)
    bias_sums_ref[...] = jnp.zeros_like(bias_sums_ref)
    acts, grads_up = (act_a, act_b), (gu_a, gu_b)
    device = lax.axis_index("dev")
    core = device % 2
    later = later_image(device)
    mean = lambda value: jnp.mean(value, axis=1, keepdims=True)

    def tile(index, carry):
        rows = pl.ds(pl.multiple_of(index * MLP_ROWS, MLP_ROWS), MLP_ROWS)

        def ready(load):
            @pl.when(index == 0)
            def _():
                load.wait()

        ready(loads[4])
        ready(loads[5])
        atts = [jnp.where(later, landing[1, side, index], landing[0, side, index]) for side in range(2)]
        att_ref[rows] = jnp.concatenate(atts, axis=1)
        sides = [mm(atts[0], wo[:HALF], NN) + mm(atts[1], wo[HALF:], NN) for wo in (wo_a, wo_b)]
        branch = jnp.where(core == 0, jnp.concatenate(sides, axis=1), jnp.concatenate(sides[::-1], axis=1))
        middle = x_ref[rows].astype(jnp.float32) + (branch + vec_ref[0:1])
        centered = middle - mean(middle)
        inverse = lax.rsqrt(mean(centered * centered) + EPSILON)
        normed = centered * inverse
        gain = vec_ref[1:2]
        hidden = (normed * gain + vec_ref[2:3]).astype(jnp.bfloat16)
        h2_ref[rows] = hidden
        for half in range(2):
            ready(loads[half])
            upper = mm(hidden, up_w[half], NN) + bias_ref[half : half + 1]
            square = upper * upper
            tanh = jnp.tanh(GELU_A * (upper + GELU_B * (square * upper)))
            acts[half][rows] = (0.5 * upper * (1.0 + tanh)).astype(jnp.bfloat16)
            slope[half] = 0.5 * (1.0 + tanh) + (0.5 * GELU_A) * upper * (1.0 - tanh * tanh) * (
                1.0 + (3.0 * GELU_B) * square
            )
        for half in range(2):
            ready(loads[2 + half])
        lower = mm(act_a[rows], down_w[0], NN) + mm(act_b[rows], down_w[1], NN)
        result_ref[rows] = (middle + (lower + vec_ref[3:4])).astype(jnp.bfloat16)
        grad = g_ref[rows]
        for half in range(2):
            grad_upper = (mm(grad, down_w[half], NT) * slope[half]).astype(jnp.bfloat16)
            grads_up[half][rows] = grad_upper
            bias_sums_ref[half : half + 1] += jnp.sum(grad_upper.astype(jnp.float32), axis=0, keepdims=True)
        grad_hidden = mm(gu_a[rows], up_w[0], NT) + mm(gu_b[rows], up_w[1], NT)
        scaled = grad_hidden * gain
        wide = grad.astype(jnp.float32)
        grad_middle = wide + inverse * (scaled - mean(scaled) - normed * mean(scaled * normed))
        gm_ref[rows] = grad_middle
        branch = grad_middle.astype(jnp.bfloat16)
        low, high = branch[:, :HALF], branch[:, HALF:]
        branches = jnp.where(core == 0, low, high), jnp.where(core == 0, high, low)
        gb_a[rows], gb_b[rows] = branches
        for go_ref, heads in ((go_a, slice(0, HALF)), (go_b, slice(HALF, D))):
            total = mm(branches[0], wo_a[heads], NT) + mm(branches[1], wo_b[heads], NT)
            go_ref[rows] = total.astype(jnp.bfloat16)
        for n, value in enumerate([branch.astype(jnp.float32), grad_hidden * normed, grad_hidden, wide]):
            sums_ref[n : n + 1] += jnp.sum(value, axis=0, keepdims=True)
        return carry

    lax.fori_loop(0, x_ref.shape[0] // MLP_ROWS, tile, 0)


def mlp(x, landing, grad, ups, downs, vecs, biases):
    rows = x.shape[0]
    vmem, hbm = pl.BlockSpec(memory_space=pltpu.VMEM), pl.BlockSpec(memory_space=pl.ANY)
    low = lambda width: jax.ShapeDtypeStruct((rows, width), jnp.bfloat16)
    wide = lambda *shape: jax.ShapeDtypeStruct(shape, jnp.float32)
    return pl.pallas_call(
        mlp_kernel,
        out_shape=[low(D), low(D)] + [low(FFH)] * 4 + [low(D), low(HALF), low(HALF), wide(rows, D), low(HALF), low(HALF), wide(8, D), wide(8, FFH)],
        in_specs=[vmem] * 3 + [hbm] * 4 + [vmem] * 2,
        out_specs=[vmem] * 14,
        scratch_shapes=[
            pltpu.VMEM((D, HALF), jnp.bfloat16),
            pltpu.VMEM((D, HALF), jnp.bfloat16),
            pltpu.VMEM((2, D, FFH), jnp.bfloat16),
            pltpu.VMEM((2, FFH, D), jnp.bfloat16),
            pltpu.VMEM((2, MLP_ROWS, FFH), jnp.float32),
            pltpu.SemaphoreType.DMA((6,)),
        ],
        compiler_params=pltpu.CompilerParams(vmem_limit_bytes=62 * 1024 * 1024),
        cost_estimate=pl.CostEstimate(flops=0, bytes_accessed=130 * 10**6, transcendentals=0),
        name="mlp",
    )(x, landing, grad, *ups, *downs, vecs, biases)


def topo_local(tokens, counts, qkv_weight, out_weight, up_weight, down_weight, vectors, cotangent):
    device = lax.axis_index("dev")
    core, chip = device % 2, device // 2
    batches = tokens.shape[0]
    share = vectors.shape[0]
    own_rows = batches * SHARD

    qkv36 = qkv_weight.reshape(ROWS // 2, 3 * D)
    out36 = out_weight.reshape(ROWS // 2, D)
    side_qkv = [
        jnp.concatenate([qkv36[:, s * HALF + j * D :][:, :HALF] for j in range(3)], axis=1) for s in range(2)
    ]
    side_out = [out36[:, s * HALF :][:, :HALF] for s in range(2)]
    up36 = up_weight.reshape(ROWS // 2, CHIPS, UNIT)
    up_low = up36[:, :, :UNIT_HALF].reshape(ROWS // 2, FFH)
    up_high = jnp.pad(up36[:, :, UNIT_HALF:], ((0, 0), (0, 0), (0, 2 * UNIT_HALF - UNIT))).reshape(
        ROWS // 2, FFH
    )
    spill = UNIT_HALF * D - down_weight.shape[0]
    borrowed = lax.ppermute(
        down_weight[:spill], "dev", [(i + 1, i) for i in range(0, 2 * CHIPS, 2)]
    )
    down_unit = by_core(
        core,
        jnp.concatenate([down_weight, borrowed]),
        jnp.concatenate([down_weight[spill:], jnp.zeros((2 * spill,), jnp.bfloat16)]),
    ).reshape(UNIT_HALF, D)
    first_unit = chip_unit(
        core,
        jnp.concatenate([side_qkv[0], side_out[0], up_low], axis=1),
        jnp.concatenate([side_qkv[1], side_out[1], up_high], axis=1),
    )
    shares = jnp.pad(vectors, (0, 512 - share)).reshape(1, 512)
    shares = joined(core, shares, swap(shares), 0).reshape(1, 1024)
    extra = jnp.pad(shares, ((0, 7), (0, 3 * HALF - 1024)))
    up_unit = jnp.concatenate([first_unit[:, 4 * HALF :], first_unit[:, 3 * HALF : 4 * HALF]], axis=1)
    (
        query, keys, values, hidden_one, attended, log_sums, full, landing, up_mine, up_theirs, down_mine, down_theirs
    ) = forward(counts, jnp.concatenate([first_unit[:, : 3 * HALF], extra], axis=0), up_unit, down_unit, tokens, 1)
    qkv_w = full[:, :ROWS].reshape(D, 3 * HALF)
    packed = full[:, ROWS, :1024].reshape(2 * CHIPS, 512)[:, :share].reshape(-1).astype(jnp.float32)
    pieces = [packed[segment * D : (segment + 1) * D] for segment in range(8)]
    bias_units = packed[8 * D : 8 * D + FF].reshape(CHIPS, UNIT)
    bias_low = bias_units[:, :UNIT_HALF].reshape(-1)
    bias_high = jnp.pad(bias_units[:, UNIT_HALF:], ((0, 0), (0, 2 * UNIT_HALF - UNIT))).reshape(-1)
    up_bias_mine = by_core(core, bias_low, bias_high)
    up_bias_theirs = by_core(core, bias_high, bias_low)
    def dot_tn(left, right):
        return lax.dot_general(left, right, (((0,), (0,)), ((), ())), preferred_element_type=jnp.float32)

    inputs = tokens.reshape(own_rows, D).astype(jnp.float32)
    grad_output = cotangent.reshape(own_rows, D)
    eight = lambda rows: jnp.pad(jnp.stack(rows), ((0, 8 - len(rows)), (0, 0)))
    (
        att_own, result, active_mine, active_theirs, grad_upper_mine, grad_upper_theirs,
        hidden_two, branch_mine, branch_theirs, grad_middle, heads_low, heads_high, vec_sums, bias_sums,
    ) = mlp(
        tokens.reshape(own_rows, D), landing, grad_output, (up_mine, up_theirs), (down_mine, down_theirs),
        eight([pieces[4], pieces[5], pieces[6], pieces[7]]), eight([up_bias_mine, up_bias_theirs]),
    )

    pair = lambda mine, theirs: jnp.concatenate([mine, swap(theirs)], axis=0)
    grad_down = dot_tn(pair(active_mine, active_theirs), pair(grad_output, grad_output)).astype(jnp.bfloat16)
    both = lambda mine, theirs: [mine, swap(theirs)]
    pairs = (
        both(hidden_two, hidden_two) + both(grad_upper_mine, grad_upper_theirs) + both(att_own, att_own)
        + both(branch_mine, branch_theirs)
    )
    head_sums, landing, down_total, up_total, out_total, qkv_total = backward(
        counts, query, keys, values, hidden_one, qkv_w, attended, log_sums,
        heads_low.reshape(batches, SHARD, HALF), heads_high.reshape(batches, SHARD, HALF),
        grad_down.reshape(CHIPS, UNIT_HALF, D), pairs, 4,
    )
    attention_total = jnp.concatenate([qkv_total, out_total], axis=1)
    later = later_image(device)[None]
    grad_hidden_one = jnp.where(later, landing[1], landing[0]).astype(jnp.float32).reshape(own_rows, D)
    normed_one, inverse_one = layer_stats(inputs)
    grad_input = grad_middle + layer_back(grad_hidden_one, normed_one, inverse_one, pieces[0])

    sums = lambda values: jnp.sum(values.astype(jnp.float32), axis=0)
    at_heads = lambda vector: lax.dynamic_update_slice_in_dim(
        jnp.zeros((D,), jnp.float32), vector, core * HALF, 0
    )
    bias_mine, bias_theirs = bias_sums[0], bias_sums[1]
    bias_low = by_core(core, bias_mine, bias_theirs).reshape(CHIPS, UNIT_HALF)
    bias_high = by_core(core, bias_theirs, bias_mine).reshape(CHIPS, UNIT_HALF)
    grad_up_bias = jnp.concatenate([bias_low, bias_high[:, : UNIT - UNIT_HALF]], axis=1).reshape(-1)
    vector_grad = jnp.concatenate(
        [
            sums(grad_hidden_one * normed_one),
            sums(grad_hidden_one),
            at_heads(head_sums[0]),
            at_heads(head_sums[1]),
            *(vec_sums[n] for n in range(4)),
            grad_up_bias,
            jnp.zeros((32 * share - 8 * D - FF,), jnp.float32),
        ]
    )
    vector_grad = scatter_vector(vector_grad, share, 2)

    half_rows = ROWS // 2

    def whole_rows(total):
        kept = by_core(core, total[:half_rows], total[half_rows:])
        theirs = swap(by_core(core, total[half_rows:], total[:half_rows]))
        return by_core(core, kept, theirs), by_core(core, theirs, kept)

    low, high = whole_rows(attention_total)
    columns = [
        jnp.concatenate([low[:, j * HALF : (j + 1) * HALF], high[:, j * HALF : (j + 1) * HALF]], axis=1)
        for j in range(4)
    ]
    qkv_grad = jnp.concatenate(columns[:3], axis=1).reshape(-1)
    out_grad = columns[3].reshape(-1)
    low, high = whole_rows(up_total)
    up_grad = jnp.concatenate(
        [
            low.reshape(half_rows, CHIPS, UNIT_HALF),
            high.reshape(half_rows, CHIPS, UNIT_HALF)[:, :, : UNIT - UNIT_HALF],
        ],
        axis=2,
    ).reshape(-1)
    down_flat = down_total.reshape(-1)
    returned = lax.ppermute(
        down_flat[down_flat.shape[0] - spill :], "dev", [(i, i + 1) for i in range(0, 2 * CHIPS, 2)]
    )
    down_grad = by_core(
        core,
        down_flat[: down_weight.shape[0]],
        jnp.concatenate([returned, down_flat[: down_weight.shape[0] - spill]]),
    )
    return (
        result.reshape(tokens.shape),
        grad_input.astype(jnp.bfloat16).reshape(tokens.shape),
        qkv_grad,
        out_grad,
        up_grad,
        down_grad,
        vector_grad,
    )


def solution(mesh):
    local = topo_local if mesh.shape["dev"] == 32 else generic_local
    return jax.shard_map(
        local,
        mesh=mesh,
        in_specs=(
            P(None, "dev", None),
            P(),
            P("dev"),
            P("dev"),
            P("dev"),
            P("dev"),
            P("dev"),
            P(None, "dev", None),
        ),
        out_specs=(
            P(None, "dev", None),
            P(None, "dev", None),
            P("dev"),
            P("dev"),
            P("dev"),
            P("dev"),
            P("dev"),
        ),
        check_vma=False,
    )
```

```python
from functools import partial

import jax
import jax.numpy as jnp
import numpy as np
from jax import lax
from jax.experimental import pallas as pl
from jax.experimental.pallas import tpu as pltpu
from jax.sharding import PartitionSpec as P

D = 1152
HEADS = 16
FF = 4304
IMG_LEN = 729


heads_per_block = 4
EPSILON = 1e-06
MASKED = -1e30


def passed_along(block, axis, distance):
    devices = range(lax.axis_size(axis))
    route = [(i - distance, i) for i in devices if i - distance in devices]
    return lax.ppermute(block, axis, route)


def layer_stats(values):
    centered = values - jnp.mean(values, axis=-1, keepdims=True)
    inverse = lax.rsqrt(jnp.mean(centered * centered, axis=-1, keepdims=True) + EPSILON)
    return (centered * inverse, inverse)


def layer_back(grad_output, normed, inverse, gain):
    scaled = grad_output * gain
    return inverse * (
        scaled
        - jnp.mean(scaled, axis=-1, keepdims=True)
        - normed * jnp.mean(scaled * normed, axis=-1, keepdims=True)
    )


def image_of(positions, image_count):
    return jnp.where(positions < image_count * IMG_LEN, positions // IMG_LEN, -positions - 1)


def reach_sizes(shard_rows):
    rim_rows = IMG_LEN - 1
    reach_count = (rim_rows + shard_rows - 1) // shard_rows
    return [
        min(shard_rows, rim_rows - (distance - 1) * shard_rows)
        for distance in range(1, reach_count + 1)
    ]


def widen(key_value, shard_rows):
    edge_sizes = reach_sizes(shard_rows)
    arrived = {}
    for distance, amount in enumerate(edge_sizes, start=1):
        for direction in (1, -1):
            sent_rows = key_value[shard_rows - amount :] if direction > 0 else key_value[:amount]
            arrived[distance, direction] = passed_along(sent_rows, "dev", direction * distance)
    before = [arrived[distance, 1] for distance in range(len(edge_sizes), 0, -1)]
    after = [arrived[distance, -1] for distance in range(1, len(edge_sizes) + 1)]
    return jnp.concatenate(before + [key_value] + after, axis=0)


def return_edges(grad_extended, shard_rows):
    edge_sizes = reach_sizes(shard_rows)
    rim_rows = IMG_LEN - 1
    combined = grad_extended[rim_rows : rim_rows + shard_rows]
    for distance, amount in enumerate(edge_sizes, start=1):
        for direction in (1, -1):
            if direction > 0:
                begin_row = rim_rows - sum(edge_sizes[:distance])
            else:
                begin_row = rim_rows + shard_rows + sum(edge_sizes[: distance - 1])
            arrived = passed_along(
                grad_extended[begin_row : begin_row + amount].astype(jnp.bfloat16),
                "dev",
                -direction * distance,
            ).astype(jnp.float32)
            if direction > 0:
                combined = combined.at[shard_rows - amount :].add(arrived)
            else:
                combined = combined.at[:amount].add(arrived)
    return combined


def key_window(device_index, shard_rows, image_count):
    span_rows = ((shard_rows + IMG_LEN - 2) // IMG_LEN + 1) * IMG_LEN
    shard_start = device_index * shard_rows
    window_start = shard_start // IMG_LEN * IMG_LEN
    offset_rows = window_start - shard_start + IMG_LEN - 1
    query_images = image_of(shard_start + jnp.arange(shard_rows, dtype=jnp.int32), image_count)
    key_images = image_of(window_start + jnp.arange(span_rows, dtype=jnp.int32), image_count)
    return (span_rows, offset_rows, query_images[:, None] == key_images[None, :])


def head_slices(query, window_kv, block_index):
    head_dim = D // HEADS
    block_width = heads_per_block * head_dim
    first_column = block_index * block_width
    query_block = query[:, first_column : first_column + block_width].reshape(
        query.shape[0], heads_per_block, head_dim
    )
    key_block = window_kv[:, first_column : first_column + block_width].reshape(
        window_kv.shape[0], heads_per_block, head_dim
    )
    value_block = window_kv[:, D + first_column : D + first_column + block_width].reshape(
        window_kv.shape[0], heads_per_block, head_dim
    )
    return (query_block, key_block, value_block, first_column, block_width)


def attend(query, window_kv, visible):
    score_scale = (D // HEADS) ** (-0.5)
    outputs, log_sums = ([], [])
    for block_index in range(HEADS // heads_per_block):
        query_block, key_block, value_block, first_column, block_width = head_slices(
            query, window_kv, block_index
        )
        raw_scores = jnp.einsum(
            "qhd,khd->hqk", query_block, key_block, preferred_element_type=jnp.float32
        )
        scores = jnp.where(visible[None], raw_scores * score_scale, MASKED)
        largest = jnp.max(scores, axis=-1, keepdims=True)
        exponent = jnp.exp(scores - largest)
        row_totals = jnp.sum(exponent, axis=-1, keepdims=True)
        probabilities = (exponent / row_totals).astype(jnp.bfloat16)
        log_sums.append(largest + jnp.log(row_totals))
        attended = jnp.einsum(
            "hqk,khd->qhd", probabilities, value_block, preferred_element_type=jnp.float32
        )
        outputs.append(attended.reshape(query.shape[0], block_width))
    return (jnp.concatenate(outputs, axis=1), log_sums)


def attend_back(query, window_kv, visible, log_sums, grad_attended):
    score_scale = (D // HEADS) ** (-0.5)
    grad_queries, grad_keys, grad_values = ([], [], [])
    for block_index in range(HEADS // heads_per_block):
        query_block, key_block, value_block, first_column, block_width = head_slices(
            query, window_kv, block_index
        )
        grad_block = grad_attended[:, first_column : first_column + block_width].reshape(
            query.shape[0], heads_per_block, block_width // heads_per_block
        )
        raw_scores = jnp.einsum(
            "qhd,khd->hqk", query_block, key_block, preferred_element_type=jnp.float32
        )
        scores = jnp.where(visible[None], raw_scores * score_scale, MASKED)
        probabilities = jnp.exp(scores - log_sums[block_index])
        grad_values.append(
            jnp.einsum(
                "hqk,qhd->khd",
                probabilities.astype(jnp.bfloat16),
                grad_block,
                preferred_element_type=jnp.float32,
            ).reshape(window_kv.shape[0], block_width)
        )
        grad_probs = jnp.einsum(
            "qhd,khd->hqk", grad_block, value_block, preferred_element_type=jnp.float32
        )
        inner = jnp.sum(probabilities * grad_probs, axis=-1, keepdims=True)
        grad_raw = (probabilities * (grad_probs - inner) * score_scale).astype(jnp.bfloat16)
        grad_queries.append(
            jnp.einsum(
                "hqk,khd->qhd", grad_raw, key_block, preferred_element_type=jnp.float32
            ).reshape(query.shape[0], block_width)
        )
        grad_keys.append(
            jnp.einsum(
                "hqk,qhd->khd", grad_raw, query_block, preferred_element_type=jnp.float32
            ).reshape(window_kv.shape[0], block_width)
        )
    return (jnp.concatenate(grad_queries, axis=1), jnp.concatenate(grad_keys + grad_values, axis=1))


def unpack(gathered):
    qkv_flat, out_flat, up_flat, down_flat, packed = gathered
    packed = packed.astype(jnp.float32)
    pieces = [packed[segment * D : (segment + 1) * D] for segment in range(8)]
    up_bias = packed[8 * D : 8 * D + FF]
    return (
        qkv_flat.reshape(D, 3 * D),
        out_flat.reshape(D, D),
        up_flat.reshape(D, FF),
        down_flat.reshape(FF, D),
        pieces,
        up_bias,
    )


def forward_batch(tokens_batch, image_count, weights, device_index):
    qkv_w, out_w, up_w, down_w, pieces, up_bias = weights
    shard_rows = tokens_batch.shape[0]
    rim_rows = IMG_LEN - 1
    inputs = tokens_batch.astype(jnp.float32)
    normed_one, inverse_one = layer_stats(inputs)
    hidden_one = (normed_one * pieces[0] + pieces[1]).astype(jnp.bfloat16)
    projected = jnp.dot(hidden_one, qkv_w, preferred_element_type=jnp.float32)
    query = (projected[:, :D] + pieces[2]).astype(jnp.bfloat16)
    key_value = jnp.concatenate(
        [projected[:, D : 2 * D], projected[:, 2 * D :] + pieces[3]], axis=1
    ).astype(jnp.bfloat16)
    extended = widen(key_value, shard_rows)
    span_rows, offset_rows, visible = key_window(device_index, shard_rows, image_count)
    padded = jnp.pad(extended, ((0, rim_rows + span_rows - extended.shape[0]), (0, 0)))
    window_kv = lax.dynamic_slice_in_dim(padded, offset_rows, span_rows, 0)
    attended, log_sums = attend(query, window_kv, visible)
    attended_low = attended.astype(jnp.bfloat16)
    middle = inputs + (jnp.dot(attended_low, out_w, preferred_element_type=jnp.float32) + pieces[4])
    normed_two, inverse_two = layer_stats(middle)
    hidden_two = (normed_two * pieces[5] + pieces[6]).astype(jnp.bfloat16)
    upper = jnp.dot(hidden_two, up_w, preferred_element_type=jnp.float32) + up_bias
    active = jax.nn.gelu(upper, approximate=True).astype(jnp.bfloat16)
    output = middle + (jnp.dot(active, down_w, preferred_element_type=jnp.float32) + pieces[7])
    saved = (
        normed_one,
        inverse_one,
        hidden_one,
        query,
        window_kv,
        offset_rows,
        visible,
        log_sums,
        attended_low,
        normed_two,
        inverse_two,
        hidden_two,
        upper,
        active,
    )
    return (output.astype(jnp.bfloat16), saved)


def backward_batch(grad_output, saved, weights, vector_length):
    qkv_w, out_w, up_w, down_w, pieces, up_bias = weights
    (
        normed_one,
        inverse_one,
        hidden_one,
        query,
        window_kv,
        offset_rows,
        visible,
        log_sums,
        attended_low,
        normed_two,
        inverse_two,
        hidden_two,
        upper,
        active,
    ) = saved
    shard_rows = query.shape[0]
    span_rows = window_kv.shape[0]
    rim_rows = IMG_LEN - 1
    grad_wide = grad_output.astype(jnp.float32)
    grad_down = jnp.einsum("tf,td->fd", active, grad_output, preferred_element_type=jnp.float32)
    grad_down_bias = jnp.sum(grad_wide, axis=0)
    grad_active = jnp.einsum("td,fd->tf", grad_output, down_w, preferred_element_type=jnp.float32)
    gelu_back = jax.vjp(partial(jax.nn.gelu, approximate=True), upper)[1]
    grad_upper = gelu_back(grad_active)[0].astype(jnp.bfloat16)
    grad_up = jnp.einsum("td,tf->df", hidden_two, grad_upper, preferred_element_type=jnp.float32)
    grad_up_bias = jnp.sum(grad_upper.astype(jnp.float32), axis=0)
    grad_hidden_two = jnp.einsum("tf,df->td", grad_upper, up_w, preferred_element_type=jnp.float32)
    grad_gain_two = jnp.sum(grad_hidden_two * normed_two, axis=0)
    grad_bias_two = jnp.sum(grad_hidden_two, axis=0)
    grad_middle = grad_wide + layer_back(grad_hidden_two, normed_two, inverse_two, pieces[5])
    grad_branch = grad_middle.astype(jnp.bfloat16)
    grad_out = jnp.einsum(
        "td,te->de", attended_low, grad_branch, preferred_element_type=jnp.float32
    )
    grad_out_bias = jnp.sum(grad_branch.astype(jnp.float32), axis=0)
    grad_attended = jnp.einsum(
        "te,de->td", grad_branch, out_w, preferred_element_type=jnp.float32
    ).astype(jnp.bfloat16)
    grad_query, grad_window = attend_back(query, window_kv, visible, log_sums, grad_attended)
    grad_padded = lax.dynamic_update_slice_in_dim(
        jnp.zeros((rim_rows + span_rows, 2 * D), jnp.float32), grad_window, offset_rows, 0
    )
    grad_kv = return_edges(grad_padded[: shard_rows + 2 * rim_rows], shard_rows)
    grad_query_low = grad_query.astype(jnp.bfloat16)
    grad_kv_low = grad_kv.astype(jnp.bfloat16)
    grad_projected = jnp.concatenate([grad_query_low, grad_kv_low], axis=1)
    grad_qkv = jnp.einsum(
        "td,te->de", hidden_one, grad_projected, preferred_element_type=jnp.float32
    )
    grad_query_bias = jnp.sum(grad_query_low.astype(jnp.float32), axis=0)
    grad_value_bias = jnp.sum(grad_kv_low[:, D:].astype(jnp.float32), axis=0)
    grad_hidden_one = jnp.einsum(
        "te,de->td", grad_projected, qkv_w, preferred_element_type=jnp.float32
    )
    grad_gain_one = jnp.sum(grad_hidden_one * normed_one, axis=0)
    grad_bias_one = jnp.sum(grad_hidden_one, axis=0)
    grad_input = grad_middle + layer_back(grad_hidden_one, normed_one, inverse_one, pieces[0])
    vector_grad = jnp.concatenate(
        [
            grad_gain_one,
            grad_bias_one,
            grad_query_bias,
            grad_value_bias,
            grad_out_bias,
            grad_gain_two,
            grad_bias_two,
            grad_down_bias,
            grad_up_bias,
            jnp.zeros((vector_length - 8 * D - FF,), jnp.float32),
        ]
    )
    flat_grads = (
        grad_qkv.reshape(-1),
        grad_out.reshape(-1),
        grad_up.reshape(-1),
        grad_down.reshape(-1),
        vector_grad,
    )
    return (grad_input.astype(jnp.bfloat16), flat_grads)


def generic_local(tokens, counts, qkv_weight, out_weight, up_weight, down_weight, vectors, cotangent):
    device_index = lax.axis_index("dev")
    vector_length = vectors.shape[0] * lax.axis_size("dev")
    gathered = (
        lax.all_gather(qkv_weight, "dev", axis=0, tiled=True),
        lax.all_gather(out_weight, "dev", axis=0, tiled=True),
        lax.all_gather(up_weight, "dev", axis=0, tiled=True),
        lax.all_gather(down_weight, "dev", axis=0, tiled=True),
        lax.all_gather(vectors, "dev", axis=0, tiled=True),
    )
    weights = unpack(gathered)
    results, kept_state = ([], [])
    for batch_index in range(tokens.shape[0]):
        output, saved = forward_batch(
            tokens[batch_index], counts[batch_index], weights, device_index
        )
        results.append(output)
        kept_state.append(saved)
    weights = unpack(
        (
            lax.all_gather(qkv_weight, "dev", axis=0, tiled=True),
            lax.all_gather(out_weight, "dev", axis=0, tiled=True),
            lax.all_gather(up_weight, "dev", axis=0, tiled=True),
            lax.all_gather(down_weight, "dev", axis=0, tiled=True),
            lax.all_gather(vectors, "dev", axis=0, tiled=True),
        )
    )
    grad_inputs = []
    totals = None
    for batch_index in range(tokens.shape[0]):
        grad_input, flat_grads = backward_batch(
            cotangent[batch_index], kept_state[batch_index], weights, vector_length
        )
        grad_inputs.append(grad_input)
        totals = (
            flat_grads
            if totals is None
            else tuple((earlier + current for earlier, current in zip(totals, flat_grads)))
        )
    totals = lax.psum_scatter(totals, "dev", scatter_dimension=0, tiled=True)
    return (
        jnp.stack(results),
        jnp.stack(grad_inputs),
        totals[0],
        totals[1],
        totals[2],
        totals[3],
        totals[4],
    )


CHIPS = 16
HEAD = D // HEADS
HALF = D // 2
CORE_HEADS = HEADS // 2
ROWS = D // CHIPS
UNIT = FF // CHIPS
UNIT_HALF = 136
FFH = CHIPS * UNIT_HALF
SHARD = 256
CHIP_ROWS = 2 * SHARD
TILE = 128
CHUNK = 16
SPAN = 768
SPAN_CHUNKS = SPAN // CHUNK
SHARD_CHUNKS = SHARD // CHUNK
SPAN_DEVICES = 4
TOKENS = 2 * CHIPS * SHARD
SCALE = HEAD**-0.5


def route(target):
    return [(i, target(i)) for i in range(2 * CHIPS)]


def swap(block):
    return lax.ppermute(block, "dev", route(lambda i: i ^ 1))


def by_core(core, first, second):
    return jnp.where(core == 0, first, second)


def joined(core, mine, theirs, axis):
    return by_core(
        core,
        jnp.concatenate([mine, theirs], axis=axis),
        jnp.concatenate([theirs, mine], axis=axis),
    )


def head_lanes(head):
    first = head * HEAD
    low = first // 128 * 128
    high = min((first + HEAD + 127) // 128 * 128, HALF)
    return low, high, first - low


def head_mask(head):
    low, high, skip = head_lanes(head)
    lanes = lax.broadcasted_iota(jnp.int32, (1, high - low), 1)
    return (lanes >= skip) & (lanes < skip + HEAD)


NT = (((1,), (1,)), ((), ()))
NN = (((1,), (0,)), ((), ()))
TN = (((0,), (0,)), ((), ()))


def mm(left, right, dims):
    return lax.dot_general(left, right, dims, preferred_element_type=jnp.float32)


def image_of_chip(chip):
    image = (CHIP_ROWS * chip + IMG_LEN // 2) // IMG_LEN
    has = owner_of_image(image) == chip
    first = image * IMG_LEN // CHUNK
    last = jnp.minimum((image * IMG_LEN + IMG_LEN - 1) // CHUNK, TOKENS // CHUNK - 1)
    return image, has, first, jnp.where(has, last - first + 1, 0)


def owner_of_image(image):
    return jnp.minimum((image * IMG_LEN + IMG_LEN // 2) // CHIP_ROWS, CHIPS - 1)


def in_image(image, has, first, rows, axis):
    shape = (rows, 1) if axis == 0 else (1, rows)
    at = first * CHUNK + lax.broadcasted_iota(jnp.int32, shape, axis)
    there = (at >= image * IMG_LEN) & (at < jnp.minimum((image + 1) * IMG_LEN, TOKENS))
    return there & has


def diagonal_tile(tile):
    row = tile * TILE + lax.broadcasted_iota(jnp.int32, (TILE, SPAN), 0)
    return row == lax.broadcasted_iota(jnp.int32, (TILE, SPAN), 1)


def attend_tile(image, has, first, batch, tile, live, q_ref, k_ref, v_ref, att_ref, lse_ref, acc):
    rows = pl.ds(pl.multiple_of(tile * TILE, TILE), TILE)
    visible = in_image(image, has, first, SPAN, 1) & (live | diagonal_tile(tile))
    stats = jnp.zeros((TILE, 128), jnp.float32)
    lane = lax.broadcasted_iota(jnp.int32, (TILE, 128), 1)
    acc[...] = jnp.zeros_like(acc)
    for head in range(CORE_HEADS):
        low, high, _ = head_lanes(head)
        mask = head_mask(head)
        query = jnp.where(mask, q_ref[batch, rows, low:high], 0)
        scores = jnp.where(visible, mm(query, k_ref[batch, :, low:high], NT) * SCALE, MASKED)
        largest = jnp.max(scores, axis=1, keepdims=True)
        exponent = jnp.exp(scores - largest)
        total = jnp.sum(exponent, axis=1, keepdims=True)
        probs = (exponent * (1.0 / total)).astype(jnp.bfloat16)
        part = mm(probs, v_ref[batch, :, low:high], NN)
        acc[:, low:high] += jnp.where(mask, part, 0.0)
        stats = jnp.where(lane == head, largest + jnp.log(total), stats)
    lse_ref[batch, rows] = stats
    att_ref[batch, rows] = acc[...].astype(jnp.bfloat16)


class Scatter:
    def __init__(self, place, grad_ref, total_ref, split, scratch):
        self.core, self.x, self.y, self.z = place
        self.grad_ref, self.total_ref, self.split = grad_ref, total_ref, split
        (self.half_x, self.half_y, self.whole_x, self.whole_y, self.from_z) = scratch[:5]
        (self.half_out, self.half_in, self.pair_out, self.pair_in, self.z_out, self.z_in) = scratch[5:]

    @staticmethod
    def scratch(shape, split):
        rows, columns = shape[1:]
        dma = pltpu.SemaphoreType.DMA
        block = lambda count, width: pltpu.VMEM((count, rows, width), jnp.bfloat16)
        return (
            [block(4, split), block(4, columns - split)]
            + [block(4, columns), block(4, columns), block(3, columns)]
            + [dma((2, 4)), dma((2, 4)), dma((2, 4)), dma((2, 4)), dma((3,)), dma((3,))]
        )

    COUNT = 11

    def unit(self, at_x, at_y, turn):
        at_z = (self.z + 1 + turn) % 4
        return self.grad_ref.at[(at_z * 2 + at_y) * 2 + at_x]

    def remote(self, source, target_ref, send_sem, recv_sem, device):
        return pltpu.make_async_remote_copy(
            src_ref=source,
            dst_ref=target_ref,
            send_sem=send_sem,
            recv_sem=recv_sem,
            device_id=device,
            device_id_type=MESH_ID,
        )

    def half(self, turn, axis):
        diagonal = self.unit(1 - self.x, 1 - self.y, turn)
        columns = self.grad_ref.shape[2]
        source = diagonal.at[:, pl.ds(0, self.split) if axis == 0 else pl.ds(self.split, columns - self.split)]
        device = (peer(1 - self.x, self.y, self.z, self.core), peer(self.x, 1 - self.y, self.z, self.core))[axis]
        target = (self.half_x, self.half_y)[axis].at[turn]
        return self.remote(source, target, self.half_out.at[axis, turn], self.half_in.at[axis, turn], device)

    def whole(self, turn, axis):
        device = (peer(1 - self.x, self.y, self.z, self.core), peer(self.x, 1 - self.y, self.z, self.core))[axis]
        source = (self.unit(1 - self.x, self.y, turn), self.unit(self.x, 1 - self.y, turn))[axis]
        target = (self.whole_x, self.whole_y)[axis]
        return self.remote(
            source, target.at[turn], self.pair_out.at[axis, turn], self.pair_in.at[axis, turn], device
        )

    def along(self, turn):
        device = peer(self.x, self.y, (self.z + 1 + turn) % 4, self.core)
        return self.remote(self.unit(self.x, self.y, turn), self.from_z.at[turn], self.z_out.at[turn], self.z_in.at[turn], device)

    def begin(self, turn):
        self.half(turn, 0).start()
        self.half(turn, 1).start()

    def pair(self, turn):
        split = self.split
        wide = lambda value: value.astype(jnp.float32)
        self.half(turn, 0).wait_recv()
        grad = self.unit(self.x, 1 - self.y, turn)
        grad[:, :split] = (wide(grad[:, :split]) + wide(self.half_x[turn])).astype(jnp.bfloat16)
        self.whole(turn, 1).start()
        self.half(turn, 1).wait_recv()
        grad = self.unit(1 - self.x, self.y, turn)
        grad[:, split:] = (wide(grad[:, split:]) + wide(self.half_y[turn])).astype(jnp.bfloat16)
        self.whole(turn, 0).start()

    def join(self, turn):
        wide = lambda value: value.astype(jnp.float32)
        self.whole(turn, 0).wait_recv()
        self.whole(turn, 1).wait_recv()
        own = self.unit(self.x, self.y, turn)
        total = wide(own[...]) + (wide(self.whole_x[turn]) + wide(self.whole_y[turn]))

        @pl.when(turn < 3)
        def _():
            own[...] = total.astype(jnp.bfloat16)
            self.along(turn).start()

        @pl.when(turn == 3)
        def _():
            self.total_ref[...] = total

    def total(self, turn):
        self.along(turn).wait_recv()
        self.total_ref[...] += self.from_z[turn].astype(jnp.float32)

    def finish(self):
        def pairs(turn, carry):
            for axis in range(2):
                self.half(turn, axis).wait_send()
                self.whole(turn, axis).wait_send()
            return carry

        def lines(turn, carry):
            self.along(turn).wait_send()
            return carry

        lax.fori_loop(0, 4, pairs, 0)
        lax.fori_loop(0, 3, lines, 0)


def each_turn(action, count=4):
    def body(turn, carry):
        action(turn)
        return carry

    lax.fori_loop(0, count, body, 0)


def attend_back_tile(
    image, has, first, batch, tile, live,
    q_ref, k_ref, v_ref, g_ref, stt_ref, dq_acc, dk_acc, dv_acc,
):
    rows = pl.ds(pl.multiple_of(tile * TILE, TILE), TILE)
    queries_there = in_image(image, has, first, SPAN, 1)
    at = first * CHUNK + tile * TILE + lax.broadcasted_iota(jnp.int32, (TILE, 1), 0)
    keys_there = (at >= image * IMG_LEN) & (at < jnp.minimum((image + 1) * IMG_LEN, TOKENS)) & has
    visible = queries_there & keys_there & (live | diagonal_tile(tile))
    dk_acc[...] = jnp.zeros_like(dk_acc)
    dv_acc[...] = jnp.zeros_like(dv_acc)

    @pl.when(tile == 0)
    def _():
        dq_acc[...] = jnp.zeros_like(dq_acc)

    for head in range(CORE_HEADS):
        low, high, _ = head_lanes(head)
        mask = head_mask(head)
        keys = jnp.where(mask, k_ref[batch, rows, low:high], 0)
        values = jnp.where(mask, v_ref[batch, rows, low:high], 0)
        queries = q_ref[batch, :, low:high]
        grads = g_ref[batch, :, low:high]
        lse = stt_ref[batch, head : head + 1]
        delta = stt_ref[batch, CORE_HEADS + head : CORE_HEADS + head + 1]
        probs = jnp.where(visible, jnp.exp(mm(keys, queries, NT) * SCALE - lse), 0.0)
        dv_acc[:, low:high] += jnp.where(mask, mm(probs.astype(jnp.bfloat16), grads, NN), 0.0)
        grad_probs = mm(values, grads, NT)
        grad_raw = (probs * (grad_probs - delta) * SCALE).astype(jnp.bfloat16)
        dk_acc[:, low:high] += jnp.where(mask, mm(grad_raw, queries, NN), 0.0)
        dq_acc[:, low:high] += mm(grad_raw, keys, TN)
    k_ref[batch, rows] = dk_acc[...].astype(jnp.bfloat16)
    v_ref[batch, rows] = dv_acc[...].astype(jnp.bfloat16)

    @pl.when(tile == SPAN // TILE - 1)
    def _():
        q_ref[batch] = dq_acc[:, :HALF].astype(jnp.bfloat16)


BACK_SPLITS = (640, 1152, 256, 896)


class Rows:
    def __init__(self, place):
        core, x, y, z = place
        self.core = core
        self.chip = (z * 2 + y) * 2 + x
        self.device = self.chip * 2 + core
        self.image, self.has, self.first, self.count = image_of_chip(self.chip)
        start = self.device * SHARD
        images = [start // IMG_LEN, (start + SHARD - 1) // IMG_LEN]
        self.parts = []
        for part, image in enumerate(images):
            low = jnp.maximum(image * IMG_LEN - start, 0) // CHUNK
            high = jnp.minimum((image + 1) * IMG_LEN - 1 - start, SHARD - 1) // CHUNK + 1
            if part == 1:
                high = jnp.where(images[1] == images[0], low, high)
            self.parts.append((owner_of_image(image), image * IMG_LEN // CHUNK, low, high))

    def peers(self):
        holders = [
            ((self.first // SHARD_CHUNKS + n,), self.holds(n)) for n in range(SPAN_DEVICES)
        ]
        images = [
            ((owner * 2 + side,), jnp.logical_and(high > low, owner * 2 + side != self.device))
            for owner, _, low, high in self.parts
            for side in range(2)
        ]
        return holders + images

    def holds(self, n):
        device = self.first // SHARD_CHUNKS + n
        last = (self.first + self.count - 1) // SHARD_CHUNKS
        there = jnp.logical_and(self.count > 0, device <= last)
        return jnp.logical_and(there, device != self.device)

    @staticmethod
    def scratch():
        dma = pltpu.SemaphoreType.DMA
        return [dma((2, 2, SHARD_CHUNKS)), dma((SPAN_CHUNKS,))]

    def span_rows(self, ref, chunk):
        return ref.at[:, pl.ds(pl.multiple_of(chunk * CHUNK, CHUNK), CHUNK)]

    def chunk_rows(self, ref, chunk):
        return ref.at[pl.ds(pl.multiple_of(chunk * CHUNK, CHUNK), CHUNK)]

    def each_own(self, action):
        for part, (owner, first, low, high) in enumerate(self.parts):
            for side in range(2):
                def body(chunk, carry):
                    action(part, side, chunk, owner * 2 + side, self.device * SHARD_CHUNKS + chunk - first)
                    return carry

                lax.fori_loop(low, high, body, 0)

    def each_span(self, action):
        def body(chunk, carry):
            at = self.first + chunk
            device = at // SHARD_CHUNKS
            part = jnp.where(device * SHARD // IMG_LEN == self.image, 0, 1)
            action(chunk, device, at % SHARD_CHUNKS, part)
            return carry

        lax.fori_loop(0, self.count, body, 0)

    def elsewhere(self, device, action, here):
        @pl.when(device != self.device)
        def _():
            action()

        if here is not None:
            @pl.when(device == self.device)
            def _():
                here()

    def to_images(self, sources, span_ref, sems):
        token_sems, span_sems = sems

        def start(part, side, chunk, device, at):
            source, target = self.span_rows(sources[side], chunk), self.span_rows(span_ref, at)
            copy = remote(source, target, token_sems.at[part, side, chunk], span_sems.at[at], (device,))
            self.elsewhere(device, copy.start, pltpu.make_async_copy(source, target, span_sems.at[at]).start)

        self.each_own(start)

    def images_arrived(self, sources, span_ref, sems):
        token_sems, span_sems = sems

        def wait(chunk, device, at, part):
            block = self.span_rows(span_ref, chunk)
            span_sem = span_sems.at[chunk]
            copy = remote(block, block, token_sems.at[0, 0, 0], span_sem, (device,))
            local = pltpu.make_async_copy(self.span_rows(sources[0], at), block, span_sem)
            self.elsewhere(device, copy.wait_recv, local.wait)

        def sent(part, side, chunk, device, at):
            source = self.span_rows(sources[side], chunk)
            copy = remote(source, source, token_sems.at[part, side, chunk], span_sems.at[0], (device,))
            self.elsewhere(device, copy.wait_send, None)

        self.each_span(wait)
        self.each_own(sent)

    def to_both(self, own_ref, span_ref, sems):
        token_sems, span_sems, _, _ = sems

        def start(part, side, chunk, device, at):
            source, target = self.span_rows(own_ref, chunk), self.span_rows(span_ref, at)
            copy = remote(source, target, token_sems.at[part, 0, chunk], span_sems.at[at], (device,))

            def here():
                target[...] = source[...]

            @pl.when(side == self.core)
            def _():
                self.elsewhere(device, copy.start, here)

        self.each_own(start)

    def trade(self, span_ref, chunk, sems):
        block = self.span_rows(span_ref, chunk)
        return remote(block, block, sems[2].at[chunk], sems[3].at[chunk], (self.chip * 2 + 1 - self.core,))

    def relay(self, span_ref, sems):
        token_sems, span_sems, _, _ = sems

        def pass_on(chunk, device, at, part):
            block = self.span_rows(span_ref, chunk)
            copy = remote(block, block, token_sems.at[0, 0, 0], span_sems.at[chunk], (device,))

            @pl.when(device % 2 == self.core)
            def _():
                self.elsewhere(device, copy.wait_recv, None)
                self.trade(span_ref, chunk, sems).start()

        self.each_span(pass_on)

    def both_arrived(self, own_ref, span_ref, sems):
        token_sems, span_sems, _, _ = sems

        def traded(chunk, device, at, part):
            @pl.when(device % 2 == self.core)
            def _():
                self.trade(span_ref, chunk, sems).wait_send()

            @pl.when(device % 2 != self.core)
            def _():
                self.trade(span_ref, chunk, sems).wait_recv()

        def sent(part, side, chunk, device, at):
            source = self.span_rows(own_ref, chunk)
            copy = remote(source, source, token_sems.at[part, 0, chunk], span_sems.at[0], (device,))

            @pl.when(side == self.core)
            def _():
                self.elsewhere(device, copy.wait_send, None)

        self.each_span(traded)
        self.each_own(sent)

    def batch_to_tokens(self, span_ref, landing, sems):
        token_sems, span_sems = sems

        def start(chunk, device, at, part):
            source, target = self.chunk_rows(span_ref, chunk), self.chunk_rows(landing.at[part, self.core], at)
            token_sem = token_sems.at[part, self.core, at]
            copy = remote(source, target, span_sems.at[chunk], token_sem, (device,))
            self.elsewhere(device, copy.start, pltpu.make_async_copy(source, target, token_sem).start)

        self.each_span(start)

    def batches_arrived(self, span_ref, landing, sems):
        token_sems, span_sems = sems

        def wait(part, side, chunk, device, at):
            source, target = self.chunk_rows(span_ref, at), self.chunk_rows(landing.at[part, side], chunk)
            token_sem = token_sems.at[part, side, chunk]
            copy = remote(target, target, span_sems.at[0], token_sem, (device,))
            self.elsewhere(device, copy.wait_recv, pltpu.make_async_copy(source, target, token_sem).wait)

        def sent(chunk, device, at, part):
            block = self.chunk_rows(span_ref, chunk)
            copy = remote(block, block, span_sems.at[chunk], token_sems.at[0, 0, 0], (device,))
            self.elsewhere(device, copy.wait_send, None)

        self.each_own(wait)
        self.each_span(sent)

    def to_tokens(self, span_ref, landing, sems):
        token_sems, span_sems = sems

        def start(chunk, device, at, part):
            source = self.span_rows(span_ref, chunk)
            target = self.span_rows(landing.at[part, self.core], at)
            copy = remote(source, target, span_sems.at[chunk], token_sems.at[part, self.core, at], (device,))

            def here():
                target[...] = source[...]

            self.elsewhere(device, copy.start, here)

        self.each_span(start)

    def tokens_arrived(self, span_ref, landing, sems):
        token_sems, span_sems = sems

        def wait(part, side, chunk, device, at):
            block = self.span_rows(landing.at[part, side], chunk)
            copy = remote(block, block, span_sems.at[0], token_sems.at[part, side, chunk], (device,))
            self.elsewhere(device, copy.wait_recv, None)

        def sent(chunk, device, at, part):
            block = self.span_rows(span_ref, chunk)
            copy = remote(block, block, span_sems.at[chunk], token_sems.at[0, 0, 0], (device,))
            self.elsewhere(device, copy.wait_send, None)

        self.each_own(wait)
        self.each_span(sent)


def backward_kernel(
    counts, q_in, k_in, v_in, hidden_in, weight_in, att_ref, lse_ref, low_ref, high_ref, down_in, *rest
):
    pairs_in, rest = rest[:8], rest[8:]
    sums_ref, landing, down_total, up_total, out_total, qkv_total = rest[:6]
    (
        arrived, down_ref, up_ref, out_ref, qkv_ref, dq_acc, dk_acc, dv_acc, span, stt_ref,
        load_sems, token_sems, span_sems, back_token_sems, back_span_sems, swap_out, swap_in,
    ) = rest[6:23]
    scratch = rest[23:]
    place = position_of()
    rows = Rows(place)
    batches = span.shape[0]

    def loading(pairs):
        loads = [pltpu.make_async_copy(a, b, load_sems.at[n]) for n, (a, b) in enumerate(pairs)]
        for load in loads:
            load.start()
        return loads

    first_load = loading([(down_in, down_ref)])
    greet(pair_peers(*place) + line_peers(*place) + [(partner_of(*place), True)] + rows.peers())
    sems, sources = (token_sems, span_sems), (low_ref, high_ref)
    rows.to_images(sources, span, sems)
    count = Scatter.COUNT
    down, up, out, qkv = [
        Scatter(place, grad, total, split, scratch[n * count : (n + 1) * count])
        for n, (grad, total, split) in enumerate(
            zip((down_ref, up_ref, out_ref, qkv_ref), (down_total, up_total, out_total, qkv_total), BACK_SPLITS)
        )
    ]
    first_load[0].wait()
    each_turn(down.begin)

    def loop(action, first, last):
        def body(turn, carry):
            action(turn)
            return carry

        lax.fori_loop(first, last, body, 0)

    def rows_grad(left, right, grad_ref, blocks):
        for half in range(2):
            units = slice(half * CHIPS // 2, (half + 1) * CHIPS // 2)
            for first, end in blocks:
                width = end - first
                dq_acc[:HALF, :width] = mm(left[half * HALF : (half + 1) * HALF], right[:, first:end], NN)
                grad_ref[units, :, first:end] = dq_acc[:HALF, :width].reshape(CHIPS // 2, ROWS, width).astype(jnp.bfloat16)

    def weight_grads(left, turned, wide, narrow):
        own = pl.ds(0, SHARD * batches), pl.ds(SHARD * batches, SHARD * batches)
        h2, h2_swap, gu, gu_swap, att, att_swap, gb, gb_swap = pairs_in
        loads = loading(
            [(h2, left.at[own[0]]), (h2_swap, left.at[own[1]]), (gu, wide.at[own[0]]), (gu_swap, wide.at[own[1]])]
            + [(gb, narrow.at[own[0]]), (gb_swap, narrow.at[own[1]])]
        )
        for load in loads:
            load.wait()
        turned[...] = left[...].T
        loads = loading([(att, left.at[own[0]]), (att_swap, left.at[own[1]])])
        rows_grad(turned, wide, up_ref, [(0, 640), (640, 1280), (1280, 1920), (1920, FFH)])
        loop(down.pair, 0, 4)
        each_turn(up.begin)
        for load in loads:
            load.wait()
        turned[...] = left[...].T
        rows_grad(turned, narrow, out_ref, [(0, HALF)])

    tokens = 2 * SHARD * batches
    pl.run_scoped(
        weight_grads,
        pltpu.VMEM((tokens, D), jnp.bfloat16),
        pltpu.VMEM((D, tokens), jnp.bfloat16),
        pltpu.VMEM((tokens, FFH), jnp.bfloat16),
        pltpu.VMEM((tokens, HALF), jnp.bfloat16),
    )

    def attention(q_ref, k_ref, v_ref, hidden, weight):
        loads = loading([(q_in, q_ref), (k_in, k_ref), (v_in, v_ref), (hidden_in, hidden), (weight_in, weight)])
        each_turn(out.begin)
        rows.images_arrived(sources, span, sems)

        def prepare(batch, carry):
            there = in_image(rows.image, rows.has, rows.first, SPAN, 0)
            grads = jnp.where(there, span[batch], 0)
            span[batch] = grads
            lane = lax.broadcasted_iota(jnp.int32, (SPAN, 128), 1)
            stats = jnp.where(lane < CORE_HEADS, lse_ref[batch], 0.0)
            for head in range(CORE_HEADS):
                low, high, _ = head_lanes(head)
                product = grads[:, low:high].astype(jnp.float32) * att_ref[batch, :, low:high].astype(jnp.float32)
                total = jnp.sum(jnp.where(head_mask(head), product, 0.0), axis=1, keepdims=True)
                stats = jnp.where(lane == CORE_HEADS + head, total, stats)
            stt_ref[batch] = stats.T[: 2 * CORE_HEADS]
            return carry

        lax.fori_loop(0, batches, prepare, 0)
        for load in loads:
            load.wait()
        tiles = SPAN // TILE
        work = {
            1: [(down.join, 0, 1)],
            3: [(down.join, 1, 2), (up.pair, 0, 1)],
            5: [(down.join, 2, 3), (up.pair, 1, 2)],
            7: [(down.join, 3, 4), (up.pair, 2, 3)],
            9: [(up.pair, 3, 4)],
            11: [(out.pair, 0, 4), (up.join, 0, 1)],
        }

        def attend(index, carry):
            batch, tile = index // tiles, index % tiles
            attend_back_tile(
                rows.image, rows.has, rows.first, batch, tile, rows.image < counts[batch],
                q_ref, k_ref, v_ref, span, stt_ref, dq_acc, dk_acc, dv_acc,
            )
            for at, actions in work.items():
                @pl.when(index == at)
                def _():
                    for action, first, last in actions:
                        loop(action, first, last)
            return carry

        lax.fori_loop(0, batches * tiles, attend, 0)
        columns = lambda ref: sum(jnp.sum(ref[b].astype(jnp.float32), axis=0, keepdims=True) for b in range(batches))
        sums_ref[0:1] = columns(q_ref)
        sums_ref[1:2] = columns(v_ref)

        def weight_grad(first, end, grads):
            for half in range(2):
                units = slice(half * CHIPS // 2, (half + 1) * CHIPS // 2)
                for batch in range(batches):
                    part = mm(hidden[batch, :, half * HALF : (half + 1) * HALF], grads(batch), TN)
                    if batch == 0:
                        dq_acc[:HALF, : end - first] = part
                    else:
                        dq_acc[:HALF, : end - first] += part
                total = dq_acc[:HALF, : end - first].reshape(CHIPS // 2, ROWS, end - first)
                qkv_ref[units, :, first:end] = total.astype(jnp.bfloat16)

        weight_grad(0, 640, lambda batch: jnp.concatenate([q_ref[batch], k_ref[batch, :, :64]], axis=1))
        weight_grad(640, D, lambda batch: k_ref[batch, :, 64:])
        weight_grad(D, 3 * HALF, lambda batch: v_ref[batch])
        each_turn(qkv.begin)

        def token_grad(batch, others):
            def block(index, carry):
                here = pl.ds(pl.multiple_of(index * TILE, TILE), TILE)
                grads = jnp.concatenate([ref[batch, here] for ref in (q_ref, k_ref, v_ref)], axis=1)
                total = mm(grads, weight[...], NT)
                if others is not None:
                    total = total + others[here].astype(jnp.float32)
                hidden[batch, here] = total.astype(jnp.bfloat16)
                return carry

            lax.fori_loop(0, SPAN // TILE, block, 0)

        core = place[0]
        token_grad(1 - core, None)
        trade = remote(hidden.at[1 - core], arrived, swap_out, swap_in, partner_of(*place))
        trade.start()
        loop(up.join, 1, 2)
        trade.wait_recv()
        token_grad(core, arrived)
        back_sems = (back_token_sems, back_span_sems)
        rows.batch_to_tokens(hidden.at[core], landing, back_sems)
        loop(up.join, 2, 4)
        each_turn(qkv.pair)
        each_turn(out.join)
        each_turn(down.total, 3)
        each_turn(qkv.join)
        each_turn(up.total, 3)
        each_turn(out.total, 3)
        each_turn(qkv.total, 3)
        trade.wait_send()
        rows.batches_arrived(hidden.at[core], landing, back_sems)

    held = lambda *shape: pltpu.VMEM(shape, jnp.bfloat16)
    pl.run_scoped(
        attention, *[held(batches, SPAN, HALF)] * 3, held(batches, SPAN, D), held(D, 3 * HALF)
    )
    for scatter in (down, up, out, qkv):
        scatter.finish()


def backward(counts, query, keys, values, hidden, weight, attended, lse, low, high, down, pairs, collective_id):
    batches = query.shape[0]
    vmem, hbm = pl.BlockSpec(memory_space=pltpu.VMEM), pl.BlockSpec(memory_space=pl.ANY)
    shapes = [down.shape, (CHIPS, ROWS, FFH), (CHIPS, ROWS, HALF), (CHIPS, ROWS, 3 * HALF)]
    held = lambda *shape: pltpu.VMEM(shape, jnp.bfloat16)
    dma = pltpu.SemaphoreType.DMA
    return pl.pallas_call(
        backward_kernel,
        out_shape=[jax.ShapeDtypeStruct((2, HALF), jnp.float32)]
        + [jax.ShapeDtypeStruct((2, batches, SHARD, D), jnp.bfloat16)]
        + [jax.ShapeDtypeStruct(shape[1:], jnp.float32) for shape in shapes],
        in_specs=[pl.BlockSpec(memory_space=pltpu.SMEM)] + [hbm] * 5 + [vmem] * 2 + [hbm] * (3 + len(pairs)),
        out_specs=[vmem, hbm] + [vmem] * 4,
        scratch_shapes=[held(SPAN, D)]
        + [held(*shape) for shape in shapes]
        + [
            pltpu.VMEM((SPAN, HALF + 64), jnp.float32),
            pltpu.VMEM((TILE, HALF), jnp.float32),
            pltpu.VMEM((TILE, HALF), jnp.float32),
            held(batches, SPAN, HALF),
            pltpu.VMEM((batches, 2 * CORE_HEADS, SPAN), jnp.float32),
            dma((8,)),
        ]
        + Rows.scratch() * 2
        + [dma] * 2
        + sum([Scatter.scratch(shape, split) for shape, split in zip(shapes, BACK_SPLITS)], []),
        compiler_params=pltpu.CompilerParams(
            collective_id=collective_id, has_side_effects=True, vmem_limit_bytes=60 * 1024 * 1024
        ),
        cost_estimate=pl.CostEstimate(flops=0, bytes_accessed=500 * 10**6, transcendentals=0),
        name="backward",
    )(counts, query, keys, values, hidden, weight, attended, lse, low, high, down, *pairs)


def chip_unit(core, low, high):
    theirs = swap(by_core(core, high, low))
    return joined(core, by_core(core, low, high), theirs, 0)


def peer(x, y, z, core):
    return (((z * 2 + y) * 2 + x) * 2 + core,)


MESH_ID = pl.DeviceIdType.MESH


def position_of():
    device = lax.axis_index("dev")
    return device % 2, device // 2 % 2, device // 4 % 2, device // 8


def greet(targets):
    barrier = pltpu.get_barrier_semaphore()
    count = 0
    for target, there in targets:
        if there is True:
            pl.semaphore_signal(barrier, inc=1, device_id=target, device_id_type=MESH_ID)
            count = count + 1
        else:
            @pl.when(there)
            def _():
                pl.semaphore_signal(barrier, inc=1, device_id=target, device_id_type=MESH_ID)
            count = count + there.astype(jnp.int32)
    pl.semaphore_wait(barrier, count)


def pair_peers(core, x, y, z):
    return [(peer(1 - x, y, z, core), True), (peer(x, 1 - y, z, core), True)]


def next_peers(core, x, y, z):
    return [(peer(x, y, z - 1, core), z > 0), (peer(x, y, z + 1, core), z < 3)]


def line_peers(core, x, y, z):
    return [(peer(x, y, (z + step) % 4, core), True) for step in (1, 2, 3)]


def partner_of(core, x, y, z):
    return peer(x, y, z, 1 - core)


class Gather:
    def __init__(self, place, unit_ref, full_ref, other_ref, split, sems):
        self.core, self.x, self.y, self.z = place
        self.unit_ref, self.full_ref, self.other_ref, self.split = unit_ref, full_ref, other_ref, split
        (
            self.z_out,
            self.z_in,
            self.pair_out,
            self.pair_in,
            self.half_out,
            self.half_in,
            self.chain_out,
            self.chain_in,
            self.own_sem,
        ) = sems[:9]
        if other_ref is not None:
            self.swap_out, self.swap_in = sems[9:]
        self.sides = ((-1, self.z > 0), (1, self.z < 3))
        self.x_peer = peer(1 - self.x, self.y, self.z, self.core)
        self.y_peer = peer(self.x, 1 - self.y, self.z, self.core)

    @staticmethod
    def scratch(partner):
        dma = pltpu.SemaphoreType.DMA
        shapes = [(2, 4), (4,), (2, 4), (2, 4), (2, 4), (2, 4), (2, 4), (4,)]
        return [dma(shape) for shape in shapes] + [dma] + ([dma((CHIPS,))] * 2 if partner else [])

    def unit_index(self, at_x, at_y, at_z):
        return (at_z * 2 + at_y) * 2 + at_x

    def slot(self, at_x, at_y, at_z):
        return self.full_ref.at[self.unit_index(at_x, at_y, at_z)]

    def column(self, turn, at_z):
        at_x, at_y = [(self.x, self.y), (self.x, 1 - self.y), (1 - self.x, self.y), (1 - self.x, 1 - self.y)][turn]
        return self.slot(at_x, at_y, at_z)

    def copy(self, block, send_sem, recv_sem, target, source=None):
        return pltpu.make_async_remote_copy(
            src_ref=block if source is None else source,
            dst_ref=block,
            send_sem=send_sem,
            recv_sem=recv_sem,
            device_id=target,
            device_id_type=MESH_ID,
        )

    def along(self, at_z, side, source=None):
        index = 0 if side < 0 else 1
        target = peer(self.x, self.y, self.z + side, self.core)
        return self.copy(self.column(0, at_z), self.z_out.at[index, at_z], self.z_in.at[at_z], target, source)

    def chain(self, at_z, side):
        index = 0 if side < 0 else 1
        target = peer(self.x, self.y, self.z + side, self.core)
        return self.copy(self.column(3, at_z), self.chain_out.at[index, at_z], self.chain_in.at[at_z], target)

    def whole(self, at_z, axis, source=None):
        target = (self.x_peer, self.y_peer)[axis]
        return self.copy(self.column(0, at_z), self.pair_out.at[axis, at_z], self.pair_in.at[axis, at_z], target, source)

    def part(self, block, axis):
        width = self.full_ref.shape[2]
        return block.at[:, pl.ds(0, self.split) if axis == 0 else pl.ds(self.split, width - self.split)]

    def half(self, at_z, axis):
        block = self.part(self.column(1 + axis, at_z), axis)
        target = (self.x_peer, self.y_peer)[axis]
        return self.copy(block, self.half_out.at[axis, at_z], self.half_in.at[axis, at_z], target)

    def half_arrival(self, at_z, axis):
        block = self.part(self.column(3, at_z), axis)
        return self.copy(block, self.half_out.at[axis, at_z], self.half_in.at[axis, at_z], self.x_peer)

    def by_halves(self, at_z):
        near = jnp.logical_and(jnp.abs(at_z - self.z) == 1, jnp.logical_or(at_z == 1, at_z == 2))
        return jnp.logical_or(at_z == self.z, near)

    def trade(self, turn, at_z, source=None):
        at_x, at_y = [(self.x, self.y), (self.x, 1 - self.y), (1 - self.x, self.y), (1 - self.x, 1 - self.y)][turn]
        index = self.unit_index(at_x, at_y, at_z)
        block = self.full_ref.at[index] if source is None else source
        width = self.other_ref.shape[2]
        if width < self.full_ref.shape[2]:
            block = block.at[:, pl.ds(0, width)]
        return pltpu.make_async_remote_copy(
            src_ref=block,
            dst_ref=self.other_ref.at[index],
            send_sem=self.swap_out.at[index],
            recv_sem=self.swap_in.at[index],
            device_id=peer(self.x, self.y, self.z, 1 - self.core),
            device_id_type=MESH_ID,
        )

    def share(self, turn, at_z, source=None):
        if self.other_ref is not None:
            self.trade(turn, at_z, source).start()

    def each(self, distance, action):
        if distance == 0:
            action(self.z, 0)
            return
        for side in (-1, 1):
            at_z = self.z + side * distance
            @pl.when(jnp.logical_and(at_z >= 0, at_z <= 3))
            def _():
                action(at_z, side)

    def onwards(self, side, action):
        for to, there in self.sides:
            if side == 0 or to == -side:
                @pl.when(there)
                def _():
                    action(to)

    def arrive(self, at_z, side):
        source = None
        if side == 0:
            source = self.unit_ref
            pltpu.make_async_copy(self.unit_ref, self.column(0, at_z), self.own_sem).start()
        else:
            self.along(at_z, side).wait_recv()
        self.onwards(side, lambda to: self.along(at_z, to, source).start())
        self.whole(at_z, 0, source).start()
        self.whole(at_z, 1, source).start()
        self.share(0, at_z, source)

    def cross(self, at_z, side):
        for axis in (1, 0):
            arrived = self.column(2 - axis, at_z)
            self.copy(arrived, self.pair_out.at[axis, at_z], self.pair_in.at[axis, at_z], self.x_peer).wait_recv()
            @pl.when(self.by_halves(at_z))
            def _():
                self.half(at_z, 1 - axis).start()
            self.share(2 - axis, at_z)

    def far_chain(self, at_z, side):
        return jnp.logical_or(at_z == 0, at_z == 3) if side == 0 else True

    def diagonal(self, at_z, side):
        halves = self.by_halves(at_z)
        @pl.when(halves)
        def _():
            self.half_arrival(at_z, 0).wait_recv()
            self.half_arrival(at_z, 1).wait_recv()
        if side != 0:
            @pl.when(jnp.logical_not(halves))
            def _():
                self.chain(at_z, side).wait_recv()
        @pl.when(self.far_chain(at_z, side))
        def _():
            self.onwards(side, lambda to: self.chain(at_z, to).start())
        self.share(3, at_z)

    def steps(self):
        order = [
            (0, self.arrive),
            (1, self.arrive),
            (0, self.cross),
            (2, self.arrive),
            (0, self.diagonal),
            (1, self.cross),
            (3, self.arrive),
            (1, self.diagonal),
            (2, self.cross),
            (2, self.diagonal),
            (3, self.cross),
            (3, self.diagonal),
        ]
        return [partial(self.each, distance, action) for distance, action in order]

    def settle(self, at_z, side):
        self.onwards(side, lambda to: self.along(at_z, to).wait_send())
        @pl.when(self.far_chain(at_z, side))
        def _():
            self.onwards(side, lambda to: self.chain(at_z, to).wait_send())
        for axis in range(2):
            self.whole(at_z, axis).wait_send()
            @pl.when(self.by_halves(at_z))
            def _():
                self.half(at_z, axis).wait_send()

    def own_ready(self):
        pltpu.make_async_copy(self.unit_ref, self.column(0, self.z), self.own_sem).wait()

    def finish(self):
        for distance in range(4):
            self.each(distance, self.settle)
        if self.other_ref is not None:
            def traded(at_z, carry):
                for turn in range(4):
                    self.trade(turn, at_z).wait()
                return carry

            lax.fori_loop(0, 4, traded, 0)


def remote(source, target, send_sem, recv_sem, device):
    return pltpu.make_async_remote_copy(
        src_ref=source,
        dst_ref=target,
        send_sem=send_sem,
        recv_sem=recv_sem,
        device_id=device,
        device_id_type=MESH_ID,
    )


PADDED = 80
WIDE = CHIPS * PADDED
SHARE = 423


def vector_part(full_ref, start, length, width):
    lane = lax.broadcasted_iota(jnp.int32, (1, width), 1)
    total = jnp.zeros((1, width), jnp.float32)
    for device in range(start // SHARE, (start + length - 1) // SHARE + 1):
        base = 512 * (device % 2)
        tile = full_ref[device // 2, PADDED - 16 :, base : base + 512].astype(jnp.float32)
        row = tile[ROWS - PADDED + 16 : ROWS - PADDED + 17]
        if width > 512:
            row = jnp.concatenate([row, jnp.zeros((1, width - 512), jnp.float32)], axis=1)
        shift = device * SHARE - start
        row = pltpu.roll(row, shift % width, 1) if shift % width else row
        first, last = max(shift, 0), min(shift + SHARE, length)
        total = total + jnp.where((lane >= first) & (lane < last), row, 0.0)
    return total


FIRST_STEPS = (
    (0, 0), (3, 0), (0, 1), (0, 2), (3, 1), (0, 3), (0, 4), (0, 5), (0, 6), (3, 2), (0, 7), (0, 8), (0, 9), (0, 10), (0, 11),
    (1, 0), (2, 0),
)
PROJECT_STEPS = ((0, 0, 1, 2), (1, 0, 2, 3), (2, 1, 1, 2), (3, 0, 3, 4), (4, 1, 2, 3), (5, 0, 4, 6))
ATTEND_STEPS = (
    (1, 1, 3, 4), (3, 0, 6, 7), (5, 1, 4, 5), (6, 0, 7, 8), (7, 1, 5, 6), (8, 0, 8, 9), (9, 1, 6, 7), (10, 0, 9, 10), (11, 1, 7, 8),
)
LAST_STEPS = ((0, 10, 12), (1, 8, 12))


def forward_kernel(
    splits, counts, unit, up_unit, down_unit, tokens_ref, pad_ref,
    q_out, k_out, v_out, hidden_out, att_out, lse_out, full_out, landing, up_ref, up_other, down_ref, down_other,
    q_ref, k_ref, v_ref, hidden_ref, att_ref, lse_ref, full_ref, store_sems, span, padded, acc, token_sems, span_sems, trade_out, trade_in, back_token_sems, back_span_sems, *sems
):
    place = position_of()
    rows = Rows(place)
    greet(pair_peers(*place) + next_peers(*place) + [(partner_of(*place), True)] + rows.peers())
    plain, more = len(Gather.scratch(False)), len(Gather.scratch(True))
    first = Gather(place, unit, full_ref, None, splits[0], sems[:plain])
    second = Gather(place, up_unit, up_ref, up_other, splits[1], sems[plain : plain + more])
    third = Gather(place, down_unit, down_ref, down_other, splits[2], sems[plain + more :])
    held = (q_ref, k_ref, v_ref, hidden_ref, att_ref, lse_ref, full_ref)
    outs = (q_out, k_out, v_out, hidden_out, att_out, lse_out, full_out)
    stores = [pltpu.make_async_copy(a, b, store_sems.at[n]) for n, (a, b) in enumerate(zip(held, outs))]
    one, two, three = first.steps(), second.steps(), third.steps()
    row_sems = (token_sems, span_sems, trade_out, trade_in)

    def run(steps, start, stop):
        for step in steps[start:stop]:
            step()

    row_steps = (
        partial(rows.to_both, tokens_ref, span, row_sems),
        partial(rows.relay, span, row_sems),
        partial(rows.both_arrived, tokens_ref, span, row_sems),
    )

    def start(table):
        for which, step in table:
            if which == 3:
                row_steps[step]()
            else:
                run((one, two, three)[which], step, step + 1)

    start(FIRST_STEPS)
    first.own_ready()
    stores[6].start()
    batches = tokens_ref.shape[0]
    gain, bias = vector_part(full_ref, 0, D, WIDE)[:, :D], vector_part(full_ref, D, D, WIDE)[:, :D]
    core = place[0]
    half = lambda start: jnp.where(
        core == 0, vector_part(full_ref, start, HALF, 1024), vector_part(full_ref, start + HALF, HALF, 1024)
    )[:, :HALF]
    query_bias, value_bias = half(2 * D), half(3 * D)
    block = 256

    def between(table, index):
        for at, steps, begin, stop in table:
            @pl.when(index == at)
            def _():
                run((two, three)[steps], begin, stop)

    def project(index, carry):
        batch, at = index // (SPAN // block), index % (SPAN // block)
        here = pl.ds(pl.multiple_of(at * block, block), block)
        token = rows.first * CHUNK + at * block + lax.broadcasted_iota(jnp.int32, (block, 1), 0)
        there = (token >= rows.image * IMG_LEN) & (token < jnp.minimum((rows.image + 1) * IMG_LEN, TOKENS)) & rows.has
        value = jnp.where(there, span[batch, here], 0).astype(jnp.float32)
        centered = value - jnp.mean(value, axis=1, keepdims=True)
        inverse = lax.rsqrt(jnp.mean(centered * centered, axis=1, keepdims=True) + EPSILON)
        hidden = (centered * inverse * gain + bias).astype(jnp.bfloat16)
        hidden_ref[batch, here] = hidden
        padded[...] = mm(hidden, pad_ref[...], NN).astype(jnp.bfloat16)
        wide = mm(padded[...], full_ref[:, :, :D].reshape(WIDE, D), NN)
        q_ref[batch, here] = (wide[:, :HALF] + query_bias).astype(jnp.bfloat16)
        k_ref[batch, here] = wide[:, HALF:].astype(jnp.bfloat16)
        wide = mm(padded[...], full_ref[:, :, D:].reshape(WIDE, HALF), NN)
        v_ref[batch, here] = (wide + value_bias).astype(jnp.bfloat16)
        between(PROJECT_STEPS, index)
        return carry

    lax.fori_loop(0, batches * (SPAN // block), project, 0)
    for store in stores[:4]:
        store.start()
    tiles = SPAN // TILE

    def attend(index, carry):
        batch, tile = index // tiles, index % tiles
        attend_tile(
            rows.image, rows.has, rows.first, batch, tile, rows.image < counts[batch],
            q_ref, k_ref, v_ref, att_ref, lse_ref, acc,
        )
        between(ATTEND_STEPS, index)
        return carry

    lax.fori_loop(0, batches * tiles, attend, 0)
    for store in stores[4:6]:
        store.start()
    back_sems = (back_token_sems, back_span_sems)
    rows.to_tokens(att_ref, landing, back_sems)
    for steps, begin, stop in LAST_STEPS:
        run((two, three)[steps], begin, stop)
    rows.tokens_arrived(att_ref, landing, back_sems)
    second.own_ready()
    third.own_ready()
    for store in stores:
        store.wait()
    for gather in (first, second, third):
        gather.finish()


def forward(counts, unit, up_unit, down_unit, tokens, collective_id):
    batches = tokens.shape[0]
    full = lambda unit: jax.ShapeDtypeStruct((CHIPS,) + unit.shape, unit.dtype)
    low = lambda *shape: jax.ShapeDtypeStruct(shape, jnp.bfloat16)
    vmem, hbm = pl.BlockSpec(memory_space=pltpu.VMEM), pl.BlockSpec(memory_space=pl.ANY)
    dma = pltpu.SemaphoreType.DMA
    feature, lane = np.arange(D)[:, None], np.arange(WIDE)[None]
    pad = jnp.asarray(feature // ROWS * PADDED + feature % ROWS == lane, jnp.bfloat16)
    spans = [(batches, SPAN, HALF)] * 3 + [(batches, SPAN, D), (batches, SPAN, HALF)]
    outs = pl.pallas_call(
        partial(forward_kernel, (896, 1408, 640)),
        out_shape=[low(*shape) for shape in spans]
        + [
            jax.ShapeDtypeStruct((batches, SPAN, 128), jnp.float32),
            full(unit),
            low(2, 2, batches, SHARD, HALF),
            full(up_unit),
            full(up_unit),
            full(down_unit),
            full(down_unit),
        ],
        in_specs=[pl.BlockSpec(memory_space=pltpu.SMEM)] + [vmem] * 5,
        out_specs=[hbm] * 7 + [vmem] + [hbm] * 4,
        scratch_shapes=[pltpu.VMEM(shape, jnp.bfloat16) for shape in spans]
        + [
            pltpu.VMEM((batches, SPAN, 128), jnp.float32),
            pltpu.VMEM((CHIPS,) + unit.shape, unit.dtype),
            dma((7,)),
            pltpu.VMEM((batches, SPAN, D), jnp.bfloat16),
            pltpu.VMEM((256, WIDE), jnp.bfloat16),
            pltpu.VMEM((TILE, HALF), jnp.float32),
        ]
        + Rows.scratch()
        + [dma((SPAN_CHUNKS,)), dma((SPAN_CHUNKS,))]
        + Rows.scratch()
        + Gather.scratch(False)
        + Gather.scratch(True) * 2,
        compiler_params=pltpu.CompilerParams(
            collective_id=collective_id, has_side_effects=True, vmem_limit_bytes=60 * 1024 * 1024
        ),
        cost_estimate=pl.CostEstimate(flops=0, bytes_accessed=500 * 10**6, transcendentals=0),
        name="forward",
    )(counts, unit, up_unit, down_unit, tokens, pad)
    return list(outs[:8]) + [w.reshape(-1, w.shape[2]) for w in outs[8:]]


def vector_kernel(sent_ref, total_ref, arrived, send_sems, recv_sems):
    device = lax.axis_index("dev")
    devices = 2 * CHIPS
    mesh_id = pl.DeviceIdType.MESH
    barrier = pltpu.get_barrier_semaphore()

    def greet(step, carry):
        pl.semaphore_signal(
            barrier, inc=1, device_id=(lax.rem(device + step, devices),), device_id_type=mesh_id
        )
        return carry

    lax.fori_loop(1, devices, greet, 0)
    pl.semaphore_wait(barrier, devices - 1)

    def copy(step):
        target = lax.rem(device + step, devices)
        return pltpu.make_async_remote_copy(
            src_ref=sent_ref.at[target],
            dst_ref=arrived.at[step],
            send_sem=send_sems.at[step],
            recv_sem=recv_sems.at[step],
            device_id=(target,),
            device_id_type=mesh_id,
        )

    def start(step, carry):
        copy(step).start()
        return carry

    lax.fori_loop(1, devices, start, 0)

    def add(step, total):
        copy(step).wait()
        return total + arrived[step]

    total_ref[...] = lax.fori_loop(1, devices, add, sent_ref[device])


def scatter_vector(vector, share, collective_id):
    rows = jnp.pad(vector.reshape(2 * CHIPS, share), ((0, 0), (0, 1024 - share)))
    dma = pltpu.SemaphoreType.DMA
    total = pl.pallas_call(
        vector_kernel,
        out_shape=jax.ShapeDtypeStruct((8, 128), jnp.float32),
        in_specs=[pl.BlockSpec(memory_space=pltpu.VMEM)],
        out_specs=pl.BlockSpec(memory_space=pltpu.VMEM),
        scratch_shapes=[
            pltpu.VMEM((2 * CHIPS, 8, 128), jnp.float32),
            dma((2 * CHIPS,)),
            dma((2 * CHIPS,)),
        ],
        compiler_params=pltpu.CompilerParams(collective_id=collective_id, has_side_effects=True),
        cost_estimate=pl.CostEstimate(flops=0, bytes_accessed=20 * 10**6, transcendentals=0),
        name="scatter_vector",
    )(rows.reshape(2 * CHIPS, 8, 128))
    return total.reshape(-1)[:share]


def later_image(device):
    start = device * SHARD
    at = start + lax.broadcasted_iota(jnp.int32, (SHARD, 1), 0)
    return at >= (start // IMG_LEN + 1) * IMG_LEN


MLP_ROWS = SHARD
GELU_A, GELU_B = 0.7978845608028654, 0.044715


def mlp_kernel(
    x_ref, landing, g_ref, up_a, up_b, down_a, down_b, vec_ref, bias_ref,
    att_ref, result_ref, act_a, act_b, gu_a, gu_b, h2_ref, gb_a, gb_b, gm_ref, go_a, go_b, sums_ref, bias_sums_ref,
    wo_a, wo_b, up_w, down_w, slope, sems,
):
    loads = [
        pltpu.make_async_copy(source, target, sems.at[n])
        for n, (source, target) in enumerate(
            [
                (up_a.at[:, pl.ds(0, FFH)], up_w.at[0]),
                (up_b.at[:, pl.ds(0, FFH)], up_w.at[1]),
                (down_a, down_w.at[0]),
                (down_b, down_w.at[1]),
                (up_a.at[:, pl.ds(FFH, HALF)], wo_a),
                (up_b.at[:, pl.ds(FFH, HALF)], wo_b),
            ]
        )
    ]
    for load in loads[4:] + loads[:4]:
        load.start()
    sums_ref[...] = jnp.zeros_like(sums_ref)
    bias_sums_ref[...] = jnp.zeros_like(bias_sums_ref)
    acts, grads_up = (act_a, act_b), (gu_a, gu_b)
    device = lax.axis_index("dev")
    core = device % 2
    later = later_image(device)
    mean = lambda value: jnp.mean(value, axis=1, keepdims=True)

    def tile(index, carry):
        rows = pl.ds(pl.multiple_of(index * MLP_ROWS, MLP_ROWS), MLP_ROWS)

        def ready(load):
            @pl.when(index == 0)
            def _():
                load.wait()

        ready(loads[4])
        ready(loads[5])
        atts = [jnp.where(later, landing[1, side, index], landing[0, side, index]) for side in range(2)]
        att_ref[rows] = jnp.concatenate(atts, axis=1)
        sides = [mm(atts[0], wo[:HALF], NN) + mm(atts[1], wo[HALF:], NN) for wo in (wo_a, wo_b)]
        branch = jnp.where(core == 0, jnp.concatenate(sides, axis=1), jnp.concatenate(sides[::-1], axis=1))
        middle = x_ref[rows].astype(jnp.float32) + (branch + vec_ref[0:1])
        centered = middle - mean(middle)
        inverse = lax.rsqrt(mean(centered * centered) + EPSILON)
        normed = centered * inverse
        gain = vec_ref[1:2]
        hidden = (normed * gain + vec_ref[2:3]).astype(jnp.bfloat16)
        h2_ref[rows] = hidden
        for half in range(2):
            ready(loads[half])
            upper = mm(hidden, up_w[half], NN) + bias_ref[half : half + 1]
            square = upper * upper
            tanh = jnp.tanh(GELU_A * (upper + GELU_B * (square * upper)))
            acts[half][rows] = (0.5 * upper * (1.0 + tanh)).astype(jnp.bfloat16)
            slope[half] = 0.5 * (1.0 + tanh) + (0.5 * GELU_A) * upper * (1.0 - tanh * tanh) * (
                1.0 + (3.0 * GELU_B) * square
            )
        for half in range(2):
            ready(loads[2 + half])
        lower = mm(act_a[rows], down_w[0], NN) + mm(act_b[rows], down_w[1], NN)
        result_ref[rows] = (middle + (lower + vec_ref[3:4])).astype(jnp.bfloat16)
        grad = g_ref[rows]
        for half in range(2):
            grad_upper = (mm(grad, down_w[half], NT) * slope[half]).astype(jnp.bfloat16)
            grads_up[half][rows] = grad_upper
            bias_sums_ref[half : half + 1] += jnp.sum(grad_upper.astype(jnp.float32), axis=0, keepdims=True)
        grad_hidden = mm(gu_a[rows], up_w[0], NT) + mm(gu_b[rows], up_w[1], NT)
        scaled = grad_hidden * gain
        wide = grad.astype(jnp.float32)
        grad_middle = wide + inverse * (scaled - mean(scaled) - normed * mean(scaled * normed))
        gm_ref[rows] = grad_middle
        branch = grad_middle.astype(jnp.bfloat16)
        low, high = branch[:, :HALF], branch[:, HALF:]
        branches = jnp.where(core == 0, low, high), jnp.where(core == 0, high, low)
        gb_a[rows], gb_b[rows] = branches
        for go_ref, heads in ((go_a, slice(0, HALF)), (go_b, slice(HALF, D))):
            total = mm(branches[0], wo_a[heads], NT) + mm(branches[1], wo_b[heads], NT)
            go_ref[rows] = total.astype(jnp.bfloat16)
        for n, value in enumerate([branch.astype(jnp.float32), grad_hidden * normed, grad_hidden, wide]):
            sums_ref[n : n + 1] += jnp.sum(value, axis=0, keepdims=True)
        return carry

    lax.fori_loop(0, x_ref.shape[0] // MLP_ROWS, tile, 0)


def mlp(x, landing, grad, ups, downs, vecs, biases):
    rows = x.shape[0]
    vmem, hbm = pl.BlockSpec(memory_space=pltpu.VMEM), pl.BlockSpec(memory_space=pl.ANY)
    low = lambda width: jax.ShapeDtypeStruct((rows, width), jnp.bfloat16)
    wide = lambda *shape: jax.ShapeDtypeStruct(shape, jnp.float32)
    return pl.pallas_call(
        mlp_kernel,
        out_shape=[low(D), low(D)] + [low(FFH)] * 4 + [low(D), low(HALF), low(HALF), wide(rows, D), low(HALF), low(HALF), wide(8, D), wide(8, FFH)],
        in_specs=[vmem] * 3 + [hbm] * 4 + [vmem] * 2,
        out_specs=[vmem] * 14,
        scratch_shapes=[
            pltpu.VMEM((D, HALF), jnp.bfloat16),
            pltpu.VMEM((D, HALF), jnp.bfloat16),
            pltpu.VMEM((2, D, FFH), jnp.bfloat16),
            pltpu.VMEM((2, FFH, D), jnp.bfloat16),
            pltpu.VMEM((2, MLP_ROWS, FFH), jnp.float32),
            pltpu.SemaphoreType.DMA((6,)),
        ],
        compiler_params=pltpu.CompilerParams(vmem_limit_bytes=62 * 1024 * 1024),
        cost_estimate=pl.CostEstimate(flops=0, bytes_accessed=130 * 10**6, transcendentals=0),
        name="mlp",
    )(x, landing, grad, *ups, *downs, vecs, biases)


def topo_local(tokens, counts, qkv_weight, out_weight, up_weight, down_weight, vectors, cotangent):
    device = lax.axis_index("dev")
    core, chip = device % 2, device // 2
    batches = tokens.shape[0]
    share = vectors.shape[0]
    own_rows = batches * SHARD

    qkv36 = qkv_weight.reshape(ROWS // 2, 3 * D)
    out36 = out_weight.reshape(ROWS // 2, D)
    side_qkv = [
        jnp.concatenate([qkv36[:, s * HALF + j * D :][:, :HALF] for j in range(3)], axis=1) for s in range(2)
    ]
    side_out = [out36[:, s * HALF :][:, :HALF] for s in range(2)]
    up36 = up_weight.reshape(ROWS // 2, CHIPS, UNIT)
    up_low = up36[:, :, :UNIT_HALF].reshape(ROWS // 2, FFH)
    up_high = jnp.pad(up36[:, :, UNIT_HALF:], ((0, 0), (0, 0), (0, 2 * UNIT_HALF - UNIT))).reshape(
        ROWS // 2, FFH
    )
    spill = UNIT_HALF * D - down_weight.shape[0]
    borrowed = lax.ppermute(
        down_weight[:spill], "dev", [(i + 1, i) for i in range(0, 2 * CHIPS, 2)]
    )
    down_unit = by_core(
        core,
        jnp.concatenate([down_weight, borrowed]),
        jnp.concatenate([down_weight[spill:], jnp.zeros((2 * spill,), jnp.bfloat16)]),
    ).reshape(UNIT_HALF, D)
    first_unit = chip_unit(
        core,
        jnp.concatenate([side_qkv[0], side_out[0], up_low], axis=1),
        jnp.concatenate([side_qkv[1], side_out[1], up_high], axis=1),
    )
    shares = jnp.pad(vectors, (0, 512 - share)).reshape(1, 512)
    shares = joined(core, shares, swap(shares), 0).reshape(1, 1024)
    extra = jnp.pad(shares, ((0, 7), (0, 3 * HALF - 1024)))
    up_unit = jnp.concatenate([first_unit[:, 4 * HALF :], first_unit[:, 3 * HALF : 4 * HALF]], axis=1)
    (
        query, keys, values, hidden_one, attended, log_sums, full, landing, up_mine, up_theirs, down_mine, down_theirs
    ) = forward(counts, jnp.concatenate([first_unit[:, : 3 * HALF], extra], axis=0), up_unit, down_unit, tokens, 1)
    qkv_w = full[:, :ROWS].reshape(D, 3 * HALF)
    packed = full[:, ROWS, :1024].reshape(2 * CHIPS, 512)[:, :share].reshape(-1).astype(jnp.float32)
    pieces = [packed[segment * D : (segment + 1) * D] for segment in range(8)]
    bias_units = packed[8 * D : 8 * D + FF].reshape(CHIPS, UNIT)
    bias_low = bias_units[:, :UNIT_HALF].reshape(-1)
    bias_high = jnp.pad(bias_units[:, UNIT_HALF:], ((0, 0), (0, 2 * UNIT_HALF - UNIT))).reshape(-1)
    up_bias_mine = by_core(core, bias_low, bias_high)
    up_bias_theirs = by_core(core, bias_high, bias_low)
    def dot_tn(left, right):
        return lax.dot_general(left, right, (((0,), (0,)), ((), ())), preferred_element_type=jnp.float32)

    inputs = tokens.reshape(own_rows, D).astype(jnp.float32)
    grad_output = cotangent.reshape(own_rows, D)
    eight = lambda rows: jnp.pad(jnp.stack(rows), ((0, 8 - len(rows)), (0, 0)))
    (
        att_own, result, active_mine, active_theirs, grad_upper_mine, grad_upper_theirs,
        hidden_two, branch_mine, branch_theirs, grad_middle, heads_low, heads_high, vec_sums, bias_sums,
    ) = mlp(
        tokens.reshape(own_rows, D), landing, grad_output, (up_mine, up_theirs), (down_mine, down_theirs),
        eight([pieces[4], pieces[5], pieces[6], pieces[7]]), eight([up_bias_mine, up_bias_theirs]),
    )

    pair = lambda mine, theirs: jnp.concatenate([mine, swap(theirs)], axis=0)
    grad_down = dot_tn(pair(active_mine, active_theirs), pair(grad_output, grad_output)).astype(jnp.bfloat16)
    both = lambda mine, theirs: [mine, swap(theirs)]
    pairs = (
        both(hidden_two, hidden_two) + both(grad_upper_mine, grad_upper_theirs) + both(att_own, att_own)
        + both(branch_mine, branch_theirs)
    )
    head_sums, landing, down_total, up_total, out_total, qkv_total = backward(
        counts, query, keys, values, hidden_one, qkv_w, attended, log_sums,
        heads_low.reshape(batches, SHARD, HALF), heads_high.reshape(batches, SHARD, HALF),
        grad_down.reshape(CHIPS, UNIT_HALF, D), pairs, 4,
    )
    attention_total = jnp.concatenate([qkv_total, out_total], axis=1)
    later = later_image(device)[None]
    grad_hidden_one = jnp.where(later, landing[1], landing[0]).astype(jnp.float32).reshape(own_rows, D)
    normed_one, inverse_one = layer_stats(inputs)
    grad_input = grad_middle + layer_back(grad_hidden_one, normed_one, inverse_one, pieces[0])

    sums = lambda values: jnp.sum(values.astype(jnp.float32), axis=0)
    at_heads = lambda vector: lax.dynamic_update_slice_in_dim(
        jnp.zeros((D,), jnp.float32), vector, core * HALF, 0
    )
    bias_mine, bias_theirs = bias_sums[0], bias_sums[1]
    bias_low = by_core(core, bias_mine, bias_theirs).reshape(CHIPS, UNIT_HALF)
    bias_high = by_core(core, bias_theirs, bias_mine).reshape(CHIPS, UNIT_HALF)
    grad_up_bias = jnp.concatenate([bias_low, bias_high[:, : UNIT - UNIT_HALF]], axis=1).reshape(-1)
    vector_grad = jnp.concatenate(
        [
            sums(grad_hidden_one * normed_one),
            sums(grad_hidden_one),
            at_heads(head_sums[0]),
            at_heads(head_sums[1]),
            *(vec_sums[n] for n in range(4)),
            grad_up_bias,
            jnp.zeros((32 * share - 8 * D - FF,), jnp.float32),
        ]
    )
    vector_grad = scatter_vector(vector_grad, share, 2)

    half_rows = ROWS // 2

    def whole_rows(total):
        kept = by_core(core, total[:half_rows], total[half_rows:])
        theirs = swap(by_core(core, total[half_rows:], total[:half_rows]))
        return by_core(core, kept, theirs), by_core(core, theirs, kept)

    low, high = whole_rows(attention_total)
    columns = [
        jnp.concatenate([low[:, j * HALF : (j + 1) * HALF], high[:, j * HALF : (j + 1) * HALF]], axis=1)
        for j in range(4)
    ]
    qkv_grad = jnp.concatenate(columns[:3], axis=1).reshape(-1)
    out_grad = columns[3].reshape(-1)
    low, high = whole_rows(up_total)
    up_grad = jnp.concatenate(
        [
            low.reshape(half_rows, CHIPS, UNIT_HALF),
            high.reshape(half_rows, CHIPS, UNIT_HALF)[:, :, : UNIT - UNIT_HALF],
        ],
        axis=2,
    ).reshape(-1)
    down_flat = down_total.reshape(-1)
    returned = lax.ppermute(
        down_flat[down_flat.shape[0] - spill :], "dev", [(i, i + 1) for i in range(0, 2 * CHIPS, 2)]
    )
    down_grad = by_core(
        core,
        down_flat[: down_weight.shape[0]],
        jnp.concatenate([returned, down_flat[: down_weight.shape[0] - spill]]),
    )
    return (
        result.reshape(tokens.shape),
        grad_input.astype(jnp.bfloat16).reshape(tokens.shape),
        qkv_grad,
        out_grad,
        up_grad,
        down_grad,
        vector_grad,
    )


def solution(mesh):
    local = topo_local if mesh.shape["dev"] == 32 else generic_local
    return jax.shard_map(
        local,
        mesh=mesh,
        in_specs=(
            P(None, "dev", None),
            P(),
            P("dev"),
            P("dev"),
            P("dev"),
            P("dev"),
            P("dev"),
            P(None, "dev", None),
        ),
        out_specs=(
            P(None, "dev", None),
            P(None, "dev", None),
            P("dev"),
            P("dev"),
            P("dev"),
            P("dev"),
            P("dev"),
        ),
        check_vma=False,
    )
```

```python
from functools import partial

import jax
import jax.numpy as jnp
import numpy as np
from jax import lax
from jax.experimental import pallas as pl
from jax.experimental.pallas import tpu as pltpu
from jax.sharding import PartitionSpec as P

D = 1152
HEADS = 16
FF = 4304
IMG_LEN = 729


heads_per_block = 4
EPSILON = 1e-06
MASKED = -1e30


def passed_along(block, axis, distance):
    devices = range(lax.axis_size(axis))
    route = [(i - distance, i) for i in devices if i - distance in devices]
    return lax.ppermute(block, axis, route)


def layer_stats(values):
    centered = values - jnp.mean(values, axis=-1, keepdims=True)
    inverse = lax.rsqrt(jnp.mean(centered * centered, axis=-1, keepdims=True) + EPSILON)
    return (centered * inverse, inverse)


def layer_back(grad_output, normed, inverse, gain):
    scaled = grad_output * gain
    return inverse * (
        scaled
        - jnp.mean(scaled, axis=-1, keepdims=True)
        - normed * jnp.mean(scaled * normed, axis=-1, keepdims=True)
    )


def image_of(positions, image_count):
    return jnp.where(positions < image_count * IMG_LEN, positions // IMG_LEN, -positions - 1)


def reach_sizes(shard_rows):
    rim_rows = IMG_LEN - 1
    reach_count = (rim_rows + shard_rows - 1) // shard_rows
    return [
        min(shard_rows, rim_rows - (distance - 1) * shard_rows)
        for distance in range(1, reach_count + 1)
    ]


def widen(key_value, shard_rows):
    edge_sizes = reach_sizes(shard_rows)
    arrived = {}
    for distance, amount in enumerate(edge_sizes, start=1):
        for direction in (1, -1):
            sent_rows = key_value[shard_rows - amount :] if direction > 0 else key_value[:amount]
            arrived[distance, direction] = passed_along(sent_rows, "dev", direction * distance)
    before = [arrived[distance, 1] for distance in range(len(edge_sizes), 0, -1)]
    after = [arrived[distance, -1] for distance in range(1, len(edge_sizes) + 1)]
    return jnp.concatenate(before + [key_value] + after, axis=0)


def return_edges(grad_extended, shard_rows):
    edge_sizes = reach_sizes(shard_rows)
    rim_rows = IMG_LEN - 1
    combined = grad_extended[rim_rows : rim_rows + shard_rows]
    for distance, amount in enumerate(edge_sizes, start=1):
        for direction in (1, -1):
            if direction > 0:
                begin_row = rim_rows - sum(edge_sizes[:distance])
            else:
                begin_row = rim_rows + shard_rows + sum(edge_sizes[: distance - 1])
            arrived = passed_along(
                grad_extended[begin_row : begin_row + amount].astype(jnp.bfloat16),
                "dev",
                -direction * distance,
            ).astype(jnp.float32)
            if direction > 0:
                combined = combined.at[shard_rows - amount :].add(arrived)
            else:
                combined = combined.at[:amount].add(arrived)
    return combined


def key_window(device_index, shard_rows, image_count):
    span_rows = ((shard_rows + IMG_LEN - 2) // IMG_LEN + 1) * IMG_LEN
    shard_start = device_index * shard_rows
    window_start = shard_start // IMG_LEN * IMG_LEN
    offset_rows = window_start - shard_start + IMG_LEN - 1
    query_images = image_of(shard_start + jnp.arange(shard_rows, dtype=jnp.int32), image_count)
    key_images = image_of(window_start + jnp.arange(span_rows, dtype=jnp.int32), image_count)
    return (span_rows, offset_rows, query_images[:, None] == key_images[None, :])


def head_slices(query, window_kv, block_index):
    head_dim = D // HEADS
    block_width = heads_per_block * head_dim
    first_column = block_index * block_width
    query_block = query[:, first_column : first_column + block_width].reshape(
        query.shape[0], heads_per_block, head_dim
    )
    key_block = window_kv[:, first_column : first_column + block_width].reshape(
        window_kv.shape[0], heads_per_block, head_dim
    )
    value_block = window_kv[:, D + first_column : D + first_column + block_width].reshape(
        window_kv.shape[0], heads_per_block, head_dim
    )
    return (query_block, key_block, value_block, first_column, block_width)


def attend(query, window_kv, visible):
    score_scale = (D // HEADS) ** (-0.5)
    outputs, log_sums = ([], [])
    for block_index in range(HEADS // heads_per_block):
        query_block, key_block, value_block, first_column, block_width = head_slices(
            query, window_kv, block_index
        )
        raw_scores = jnp.einsum(
            "qhd,khd->hqk", query_block, key_block, preferred_element_type=jnp.float32
        )
        scores = jnp.where(visible[None], raw_scores * score_scale, MASKED)
        largest = jnp.max(scores, axis=-1, keepdims=True)
        exponent = jnp.exp(scores - largest)
        row_totals = jnp.sum(exponent, axis=-1, keepdims=True)
        probabilities = (exponent / row_totals).astype(jnp.bfloat16)
        log_sums.append(largest + jnp.log(row_totals))
        attended = jnp.einsum(
            "hqk,khd->qhd", probabilities, value_block, preferred_element_type=jnp.float32
        )
        outputs.append(attended.reshape(query.shape[0], block_width))
    return (jnp.concatenate(outputs, axis=1), log_sums)


def attend_back(query, window_kv, visible, log_sums, grad_attended):
    score_scale = (D // HEADS) ** (-0.5)
    grad_queries, grad_keys, grad_values = ([], [], [])
    for block_index in range(HEADS // heads_per_block):
        query_block, key_block, value_block, first_column, block_width = head_slices(
            query, window_kv, block_index
        )
        grad_block = grad_attended[:, first_column : first_column + block_width].reshape(
            query.shape[0], heads_per_block, block_width // heads_per_block
        )
        raw_scores = jnp.einsum(
            "qhd,khd->hqk", query_block, key_block, preferred_element_type=jnp.float32
        )
        scores = jnp.where(visible[None], raw_scores * score_scale, MASKED)
        probabilities = jnp.exp(scores - log_sums[block_index])
        grad_values.append(
            jnp.einsum(
                "hqk,qhd->khd",
                probabilities.astype(jnp.bfloat16),
                grad_block,
                preferred_element_type=jnp.float32,
            ).reshape(window_kv.shape[0], block_width)
        )
        grad_probs = jnp.einsum(
            "qhd,khd->hqk", grad_block, value_block, preferred_element_type=jnp.float32
        )
        inner = jnp.sum(probabilities * grad_probs, axis=-1, keepdims=True)
        grad_raw = (probabilities * (grad_probs - inner) * score_scale).astype(jnp.bfloat16)
        grad_queries.append(
            jnp.einsum(
                "hqk,khd->qhd", grad_raw, key_block, preferred_element_type=jnp.float32
            ).reshape(query.shape[0], block_width)
        )
        grad_keys.append(
            jnp.einsum(
                "hqk,qhd->khd", grad_raw, query_block, preferred_element_type=jnp.float32
            ).reshape(window_kv.shape[0], block_width)
        )
    return (jnp.concatenate(grad_queries, axis=1), jnp.concatenate(grad_keys + grad_values, axis=1))


def unpack(gathered):
    qkv_flat, out_flat, up_flat, down_flat, packed = gathered
    packed = packed.astype(jnp.float32)
    pieces = [packed[segment * D : (segment + 1) * D] for segment in range(8)]
    up_bias = packed[8 * D : 8 * D + FF]
    return (
        qkv_flat.reshape(D, 3 * D),
        out_flat.reshape(D, D),
        up_flat.reshape(D, FF),
        down_flat.reshape(FF, D),
        pieces,
        up_bias,
    )


def forward_batch(tokens_batch, image_count, weights, device_index):
    qkv_w, out_w, up_w, down_w, pieces, up_bias = weights
    shard_rows = tokens_batch.shape[0]
    rim_rows = IMG_LEN - 1
    inputs = tokens_batch.astype(jnp.float32)
    normed_one, inverse_one = layer_stats(inputs)
    hidden_one = (normed_one * pieces[0] + pieces[1]).astype(jnp.bfloat16)
    projected = jnp.dot(hidden_one, qkv_w, preferred_element_type=jnp.float32)
    query = (projected[:, :D] + pieces[2]).astype(jnp.bfloat16)
    key_value = jnp.concatenate(
        [projected[:, D : 2 * D], projected[:, 2 * D :] + pieces[3]], axis=1
    ).astype(jnp.bfloat16)
    extended = widen(key_value, shard_rows)
    span_rows, offset_rows, visible = key_window(device_index, shard_rows, image_count)
    padded = jnp.pad(extended, ((0, rim_rows + span_rows - extended.shape[0]), (0, 0)))
    window_kv = lax.dynamic_slice_in_dim(padded, offset_rows, span_rows, 0)
    attended, log_sums = attend(query, window_kv, visible)
    attended_low = attended.astype(jnp.bfloat16)
    middle = inputs + (jnp.dot(attended_low, out_w, preferred_element_type=jnp.float32) + pieces[4])
    normed_two, inverse_two = layer_stats(middle)
    hidden_two = (normed_two * pieces[5] + pieces[6]).astype(jnp.bfloat16)
    upper = jnp.dot(hidden_two, up_w, preferred_element_type=jnp.float32) + up_bias
    active = jax.nn.gelu(upper, approximate=True).astype(jnp.bfloat16)
    output = middle + (jnp.dot(active, down_w, preferred_element_type=jnp.float32) + pieces[7])
    saved = (
        normed_one,
        inverse_one,
        hidden_one,
        query,
        window_kv,
        offset_rows,
        visible,
        log_sums,
        attended_low,
        normed_two,
        inverse_two,
        hidden_two,
        upper,
        active,
    )
    return (output.astype(jnp.bfloat16), saved)


def backward_batch(grad_output, saved, weights, vector_length):
    qkv_w, out_w, up_w, down_w, pieces, up_bias = weights
    (
        normed_one,
        inverse_one,
        hidden_one,
        query,
        window_kv,
        offset_rows,
        visible,
        log_sums,
        attended_low,
        normed_two,
        inverse_two,
        hidden_two,
        upper,
        active,
    ) = saved
    shard_rows = query.shape[0]
    span_rows = window_kv.shape[0]
    rim_rows = IMG_LEN - 1
    grad_wide = grad_output.astype(jnp.float32)
    grad_down = jnp.einsum("tf,td->fd", active, grad_output, preferred_element_type=jnp.float32)
    grad_down_bias = jnp.sum(grad_wide, axis=0)
    grad_active = jnp.einsum("td,fd->tf", grad_output, down_w, preferred_element_type=jnp.float32)
    gelu_back = jax.vjp(partial(jax.nn.gelu, approximate=True), upper)[1]
    grad_upper = gelu_back(grad_active)[0].astype(jnp.bfloat16)
    grad_up = jnp.einsum("td,tf->df", hidden_two, grad_upper, preferred_element_type=jnp.float32)
    grad_up_bias = jnp.sum(grad_upper.astype(jnp.float32), axis=0)
    grad_hidden_two = jnp.einsum("tf,df->td", grad_upper, up_w, preferred_element_type=jnp.float32)
    grad_gain_two = jnp.sum(grad_hidden_two * normed_two, axis=0)
    grad_bias_two = jnp.sum(grad_hidden_two, axis=0)
    grad_middle = grad_wide + layer_back(grad_hidden_two, normed_two, inverse_two, pieces[5])
    grad_branch = grad_middle.astype(jnp.bfloat16)
    grad_out = jnp.einsum(
        "td,te->de", attended_low, grad_branch, preferred_element_type=jnp.float32
    )
    grad_out_bias = jnp.sum(grad_branch.astype(jnp.float32), axis=0)
    grad_attended = jnp.einsum(
        "te,de->td", grad_branch, out_w, preferred_element_type=jnp.float32
    ).astype(jnp.bfloat16)
    grad_query, grad_window = attend_back(query, window_kv, visible, log_sums, grad_attended)
    grad_padded = lax.dynamic_update_slice_in_dim(
        jnp.zeros((rim_rows + span_rows, 2 * D), jnp.float32), grad_window, offset_rows, 0
    )
    grad_kv = return_edges(grad_padded[: shard_rows + 2 * rim_rows], shard_rows)
    grad_query_low = grad_query.astype(jnp.bfloat16)
    grad_kv_low = grad_kv.astype(jnp.bfloat16)
    grad_projected = jnp.concatenate([grad_query_low, grad_kv_low], axis=1)
    grad_qkv = jnp.einsum(
        "td,te->de", hidden_one, grad_projected, preferred_element_type=jnp.float32
    )
    grad_query_bias = jnp.sum(grad_query_low.astype(jnp.float32), axis=0)
    grad_value_bias = jnp.sum(grad_kv_low[:, D:].astype(jnp.float32), axis=0)
    grad_hidden_one = jnp.einsum(
        "te,de->td", grad_projected, qkv_w, preferred_element_type=jnp.float32
    )
    grad_gain_one = jnp.sum(grad_hidden_one * normed_one, axis=0)
    grad_bias_one = jnp.sum(grad_hidden_one, axis=0)
    grad_input = grad_middle + layer_back(grad_hidden_one, normed_one, inverse_one, pieces[0])
    vector_grad = jnp.concatenate(
        [
            grad_gain_one,
            grad_bias_one,
            grad_query_bias,
            grad_value_bias,
            grad_out_bias,
            grad_gain_two,
            grad_bias_two,
            grad_down_bias,
            grad_up_bias,
            jnp.zeros((vector_length - 8 * D - FF,), jnp.float32),
        ]
    )
    flat_grads = (
        grad_qkv.reshape(-1),
        grad_out.reshape(-1),
        grad_up.reshape(-1),
        grad_down.reshape(-1),
        vector_grad,
    )
    return (grad_input.astype(jnp.bfloat16), flat_grads)


def generic_local(tokens, counts, qkv_weight, out_weight, up_weight, down_weight, vectors, cotangent):
    device_index = lax.axis_index("dev")
    vector_length = vectors.shape[0] * lax.axis_size("dev")
    gathered = (
        lax.all_gather(qkv_weight, "dev", axis=0, tiled=True),
        lax.all_gather(out_weight, "dev", axis=0, tiled=True),
        lax.all_gather(up_weight, "dev", axis=0, tiled=True),
        lax.all_gather(down_weight, "dev", axis=0, tiled=True),
        lax.all_gather(vectors, "dev", axis=0, tiled=True),
    )
    weights = unpack(gathered)
    results, kept_state = ([], [])
    for batch_index in range(tokens.shape[0]):
        output, saved = forward_batch(
            tokens[batch_index], counts[batch_index], weights, device_index
        )
        results.append(output)
        kept_state.append(saved)
    weights = unpack(
        (
            lax.all_gather(qkv_weight, "dev", axis=0, tiled=True),
            lax.all_gather(out_weight, "dev", axis=0, tiled=True),
            lax.all_gather(up_weight, "dev", axis=0, tiled=True),
            lax.all_gather(down_weight, "dev", axis=0, tiled=True),
            lax.all_gather(vectors, "dev", axis=0, tiled=True),
        )
    )
    grad_inputs = []
    totals = None
    for batch_index in range(tokens.shape[0]):
        grad_input, flat_grads = backward_batch(
            cotangent[batch_index], kept_state[batch_index], weights, vector_length
        )
        grad_inputs.append(grad_input)
        totals = (
            flat_grads
            if totals is None
            else tuple((earlier + current for earlier, current in zip(totals, flat_grads)))
        )
    totals = lax.psum_scatter(totals, "dev", scatter_dimension=0, tiled=True)
    return (
        jnp.stack(results),
        jnp.stack(grad_inputs),
        totals[0],
        totals[1],
        totals[2],
        totals[3],
        totals[4],
    )


CHIPS = 16
HEAD = D // HEADS
HALF = D // 2
CORE_HEADS = HEADS // 2
ROWS = D // CHIPS
UNIT = FF // CHIPS
UNIT_HALF = 136
FFH = CHIPS * UNIT_HALF
SHARD = 256
CHIP_ROWS = 2 * SHARD
TILE = 128
CHUNK = 16
SPAN = 768
SPAN_CHUNKS = SPAN // CHUNK
SHARD_CHUNKS = SHARD // CHUNK
SPAN_DEVICES = 4
TOKENS = 2 * CHIPS * SHARD
SCALE = HEAD**-0.5


def route(target):
    return [(i, target(i)) for i in range(2 * CHIPS)]


def swap(block):
    return lax.ppermute(block, "dev", route(lambda i: i ^ 1))


def by_core(core, first, second):
    return jnp.where(core == 0, first, second)


def joined(core, mine, theirs, axis):
    return by_core(
        core,
        jnp.concatenate([mine, theirs], axis=axis),
        jnp.concatenate([theirs, mine], axis=axis),
    )


def head_lanes(head):
    first = head * HEAD
    low = first // 128 * 128
    high = min((first + HEAD + 127) // 128 * 128, HALF)
    return low, high, first - low


def head_mask(head):
    low, high, skip = head_lanes(head)
    lanes = lax.broadcasted_iota(jnp.int32, (1, high - low), 1)
    return (lanes >= skip) & (lanes < skip + HEAD)


NT = (((1,), (1,)), ((), ()))
NN = (((1,), (0,)), ((), ()))
TN = (((0,), (0,)), ((), ()))


def mm(left, right, dims):
    return lax.dot_general(left, right, dims, preferred_element_type=jnp.float32)


def image_of_chip(chip):
    image = (CHIP_ROWS * chip + IMG_LEN // 2) // IMG_LEN
    has = owner_of_image(image) == chip
    first = image * IMG_LEN // CHUNK
    last = jnp.minimum((image * IMG_LEN + IMG_LEN - 1) // CHUNK, TOKENS // CHUNK - 1)
    return image, has, first, jnp.where(has, last - first + 1, 0)


def owner_of_image(image):
    return jnp.minimum((image * IMG_LEN + IMG_LEN // 2) // CHIP_ROWS, CHIPS - 1)


def in_image(image, has, first, rows, axis):
    shape = (rows, 1) if axis == 0 else (1, rows)
    at = first * CHUNK + lax.broadcasted_iota(jnp.int32, shape, axis)
    there = (at >= image * IMG_LEN) & (at < jnp.minimum((image + 1) * IMG_LEN, TOKENS))
    return there & has


def diagonal_tile(tile):
    row = tile * TILE + lax.broadcasted_iota(jnp.int32, (TILE, SPAN), 0)
    return row == lax.broadcasted_iota(jnp.int32, (TILE, SPAN), 1)


def attend_tile(image, has, first, batch, tile, live, q_ref, k_ref, v_ref, att_ref, lse_ref, acc):
    rows = pl.ds(pl.multiple_of(tile * TILE, TILE), TILE)
    visible = in_image(image, has, first, SPAN, 1) & (live | diagonal_tile(tile))
    stats = jnp.zeros((TILE, 128), jnp.float32)
    lane = lax.broadcasted_iota(jnp.int32, (TILE, 128), 1)
    acc[...] = jnp.zeros_like(acc)
    for head in range(CORE_HEADS):
        low, high, _ = head_lanes(head)
        mask = head_mask(head)
        query = jnp.where(mask, q_ref[batch, rows, low:high], 0)
        scores = jnp.where(visible, mm(query, k_ref[batch, :, low:high], NT) * SCALE, MASKED)
        largest = jnp.max(scores, axis=1, keepdims=True)
        exponent = jnp.exp(scores - largest)
        total = jnp.sum(exponent, axis=1, keepdims=True)
        probs = (exponent * (1.0 / total)).astype(jnp.bfloat16)
        part = mm(probs, v_ref[batch, :, low:high], NN)
        acc[:, low:high] += jnp.where(mask, part, 0.0)
        stats = jnp.where(lane == head, largest + jnp.log(total), stats)
    lse_ref[batch, rows] = stats
    att_ref[batch, rows] = acc[...].astype(jnp.bfloat16)


class Scatter:
    def __init__(self, place, grad_ref, total_ref, split, scratch):
        self.core, self.x, self.y, self.z = place
        self.grad_ref, self.total_ref, self.split = grad_ref, total_ref, split
        (self.half_x, self.half_y, self.whole_x, self.whole_y, self.from_z) = scratch[:5]
        (self.half_out, self.half_in, self.pair_out, self.pair_in, self.z_out, self.z_in) = scratch[5:]

    @staticmethod
    def scratch(shape, split):
        rows, columns = shape[1:]
        dma = pltpu.SemaphoreType.DMA
        block = lambda count, width: pltpu.VMEM((count, rows, width), jnp.bfloat16)
        return (
            [block(4, split), block(4, columns - split)]
            + [block(4, columns), block(4, columns), block(3, columns)]
            + [dma((2, 4)), dma((2, 4)), dma((2, 4)), dma((2, 4)), dma((3,)), dma((3,))]
        )

    COUNT = 11

    def unit(self, at_x, at_y, turn):
        at_z = (self.z + 1 + turn) % 4
        return self.grad_ref.at[(at_z * 2 + at_y) * 2 + at_x]

    def remote(self, source, target_ref, send_sem, recv_sem, device):
        return pltpu.make_async_remote_copy(
            src_ref=source,
            dst_ref=target_ref,
            send_sem=send_sem,
            recv_sem=recv_sem,
            device_id=device,
            device_id_type=MESH_ID,
        )

    def half(self, turn, axis):
        diagonal = self.unit(1 - self.x, 1 - self.y, turn)
        columns = self.grad_ref.shape[2]
        source = diagonal.at[:, pl.ds(0, self.split) if axis == 0 else pl.ds(self.split, columns - self.split)]
        device = (peer(1 - self.x, self.y, self.z, self.core), peer(self.x, 1 - self.y, self.z, self.core))[axis]
        target = (self.half_x, self.half_y)[axis].at[turn]
        return self.remote(source, target, self.half_out.at[axis, turn], self.half_in.at[axis, turn], device)

    def whole(self, turn, axis):
        device = (peer(1 - self.x, self.y, self.z, self.core), peer(self.x, 1 - self.y, self.z, self.core))[axis]
        source = (self.unit(1 - self.x, self.y, turn), self.unit(self.x, 1 - self.y, turn))[axis]
        target = (self.whole_x, self.whole_y)[axis]
        return self.remote(
            source, target.at[turn], self.pair_out.at[axis, turn], self.pair_in.at[axis, turn], device
        )

    def along(self, turn):
        device = peer(self.x, self.y, (self.z + 1 + turn) % 4, self.core)
        return self.remote(self.unit(self.x, self.y, turn), self.from_z.at[turn], self.z_out.at[turn], self.z_in.at[turn], device)

    def begin(self, turn):
        self.half(turn, 0).start()
        self.half(turn, 1).start()

    def pair(self, turn):
        split = self.split
        wide = lambda value: value.astype(jnp.float32)
        self.half(turn, 0).wait_recv()
        grad = self.unit(self.x, 1 - self.y, turn)
        grad[:, :split] = (wide(grad[:, :split]) + wide(self.half_x[turn])).astype(jnp.bfloat16)
        self.whole(turn, 1).start()
        self.half(turn, 1).wait_recv()
        grad = self.unit(1 - self.x, self.y, turn)
        grad[:, split:] = (wide(grad[:, split:]) + wide(self.half_y[turn])).astype(jnp.bfloat16)
        self.whole(turn, 0).start()

    def join(self, turn):
        wide = lambda value: value.astype(jnp.float32)
        self.whole(turn, 0).wait_recv()
        self.whole(turn, 1).wait_recv()
        own = self.unit(self.x, self.y, turn)
        total = wide(own[...]) + (wide(self.whole_x[turn]) + wide(self.whole_y[turn]))

        @pl.when(turn < 3)
        def _():
            own[...] = total.astype(jnp.bfloat16)
            self.along(turn).start()

        @pl.when(turn == 3)
        def _():
            self.total_ref[...] = total

    def total(self, turn):
        self.along(turn).wait_recv()
        self.total_ref[...] += self.from_z[turn].astype(jnp.float32)

    def finish(self):
        def pairs(turn, carry):
            for axis in range(2):
                self.half(turn, axis).wait_send()
                self.whole(turn, axis).wait_send()
            return carry

        def lines(turn, carry):
            self.along(turn).wait_send()
            return carry

        lax.fori_loop(0, 4, pairs, 0)
        lax.fori_loop(0, 3, lines, 0)


def each_turn(action, count=4):
    def body(turn, carry):
        action(turn)
        return carry

    lax.fori_loop(0, count, body, 0)


def attend_back_tile(
    image, has, first, batch, tile, live,
    q_ref, k_ref, v_ref, g_ref, stt_ref, dq_acc, dk_acc, dv_acc,
):
    rows = pl.ds(pl.multiple_of(tile * TILE, TILE), TILE)
    queries_there = in_image(image, has, first, SPAN, 1)
    at = first * CHUNK + tile * TILE + lax.broadcasted_iota(jnp.int32, (TILE, 1), 0)
    keys_there = (at >= image * IMG_LEN) & (at < jnp.minimum((image + 1) * IMG_LEN, TOKENS)) & has
    visible = queries_there & keys_there & (live | diagonal_tile(tile))
    dk_acc[...] = jnp.zeros_like(dk_acc)
    dv_acc[...] = jnp.zeros_like(dv_acc)

    @pl.when(tile == 0)
    def _():
        dq_acc[...] = jnp.zeros_like(dq_acc)

    for head in range(CORE_HEADS):
        low, high, _ = head_lanes(head)
        mask = head_mask(head)
        keys = jnp.where(mask, k_ref[batch, rows, low:high], 0)
        values = jnp.where(mask, v_ref[batch, rows, low:high], 0)
        queries = q_ref[batch, :, low:high]
        grads = g_ref[batch, :, low:high]
        lse = stt_ref[batch, head : head + 1]
        delta = stt_ref[batch, CORE_HEADS + head : CORE_HEADS + head + 1]
        probs = jnp.where(visible, jnp.exp(mm(keys, queries, NT) * SCALE - lse), 0.0)
        dv_acc[:, low:high] += jnp.where(mask, mm(probs.astype(jnp.bfloat16), grads, NN), 0.0)
        grad_probs = mm(values, grads, NT)
        grad_raw = (probs * (grad_probs - delta) * SCALE).astype(jnp.bfloat16)
        dk_acc[:, low:high] += jnp.where(mask, mm(grad_raw, queries, NN), 0.0)
        dq_acc[:, low:high] += mm(grad_raw, keys, TN)
    k_ref[batch, rows] = dk_acc[...].astype(jnp.bfloat16)
    v_ref[batch, rows] = dv_acc[...].astype(jnp.bfloat16)

    @pl.when(tile == SPAN // TILE - 1)
    def _():
        q_ref[batch] = dq_acc[:, :HALF].astype(jnp.bfloat16)


BACK_SPLITS = (384, 768, 128, 512)


class Rows:
    def __init__(self, place):
        core, x, y, z = place
        self.core = core
        self.chip = (z * 2 + y) * 2 + x
        self.device = self.chip * 2 + core
        self.image, self.has, self.first, self.count = image_of_chip(self.chip)
        start = self.device * SHARD
        images = [start // IMG_LEN, (start + SHARD - 1) // IMG_LEN]
        self.parts = []
        for part, image in enumerate(images):
            low = jnp.maximum(image * IMG_LEN - start, 0) // CHUNK
            high = jnp.minimum((image + 1) * IMG_LEN - 1 - start, SHARD - 1) // CHUNK + 1
            if part == 1:
                high = jnp.where(images[1] == images[0], low, high)
            self.parts.append((owner_of_image(image), image * IMG_LEN // CHUNK, low, high))

    def peers(self):
        holders = [
            ((self.first // SHARD_CHUNKS + n,), self.holds(n)) for n in range(SPAN_DEVICES)
        ]
        images = [
            ((owner * 2 + side,), jnp.logical_and(high > low, owner * 2 + side != self.device))
            for owner, _, low, high in self.parts
            for side in range(2)
        ]
        return holders + images

    def holds(self, n):
        device = self.first // SHARD_CHUNKS + n
        last = (self.first + self.count - 1) // SHARD_CHUNKS
        there = jnp.logical_and(self.count > 0, device <= last)
        return jnp.logical_and(there, device != self.device)

    @staticmethod
    def scratch():
        dma = pltpu.SemaphoreType.DMA
        return [dma((2, 2, SHARD_CHUNKS)), dma((SPAN_CHUNKS,))]

    def span_rows(self, ref, chunk):
        return ref.at[:, pl.ds(pl.multiple_of(chunk * CHUNK, CHUNK), CHUNK)]

    def chunk_rows(self, ref, chunk):
        return ref.at[pl.ds(pl.multiple_of(chunk * CHUNK, CHUNK), CHUNK)]

    def each_own(self, action):
        for part, (owner, first, low, high) in enumerate(self.parts):
            for side in range(2):
                def body(chunk, carry):
                    action(part, side, chunk, owner * 2 + side, self.device * SHARD_CHUNKS + chunk - first)
                    return carry

                lax.fori_loop(low, high, body, 0)

    def each_span(self, action):
        def body(chunk, carry):
            at = self.first + chunk
            device = at // SHARD_CHUNKS
            part = jnp.where(device * SHARD // IMG_LEN == self.image, 0, 1)
            action(chunk, device, at % SHARD_CHUNKS, part)
            return carry

        lax.fori_loop(0, self.count, body, 0)

    def elsewhere(self, device, action, here):
        @pl.when(device != self.device)
        def _():
            action()

        if here is not None:
            @pl.when(device == self.device)
            def _():
                here()

    def to_images(self, sources, span_ref, sems):
        token_sems, span_sems = sems

        def start(part, side, chunk, device, at):
            source, target = self.span_rows(sources[side], chunk), self.span_rows(span_ref, at)
            copy = remote(source, target, token_sems.at[part, side, chunk], span_sems.at[at], (device,))
            self.elsewhere(device, copy.start, pltpu.make_async_copy(source, target, span_sems.at[at]).start)

        self.each_own(start)

    def images_arrived(self, sources, span_ref, sems):
        token_sems, span_sems = sems

        def wait(chunk, device, at, part):
            block = self.span_rows(span_ref, chunk)
            span_sem = span_sems.at[chunk]
            copy = remote(block, block, token_sems.at[0, 0, 0], span_sem, (device,))
            local = pltpu.make_async_copy(self.span_rows(sources[0], at), block, span_sem)
            self.elsewhere(device, copy.wait_recv, local.wait)

        def sent(part, side, chunk, device, at):
            source = self.span_rows(sources[side], chunk)
            copy = remote(source, source, token_sems.at[part, side, chunk], span_sems.at[0], (device,))
            self.elsewhere(device, copy.wait_send, None)

        self.each_span(wait)
        self.each_own(sent)

    def to_both(self, own_ref, span_ref, sems):
        token_sems, span_sems, _, _ = sems

        def start(part, side, chunk, device, at):
            source, target = self.span_rows(own_ref, chunk), self.span_rows(span_ref, at)
            copy = remote(source, target, token_sems.at[part, 0, chunk], span_sems.at[at], (device,))

            def here():
                target[...] = source[...]

            @pl.when(side == self.core)
            def _():
                self.elsewhere(device, copy.start, here)

        self.each_own(start)

    def trade(self, span_ref, chunk, sems):
        block = self.span_rows(span_ref, chunk)
        return remote(block, block, sems[2].at[chunk], sems[3].at[chunk], (self.chip * 2 + 1 - self.core,))

    def relay(self, span_ref, sems):
        token_sems, span_sems, _, _ = sems

        def pass_on(chunk, device, at, part):
            block = self.span_rows(span_ref, chunk)
            copy = remote(block, block, token_sems.at[0, 0, 0], span_sems.at[chunk], (device,))

            @pl.when(device % 2 == self.core)
            def _():
                self.elsewhere(device, copy.wait_recv, None)
                self.trade(span_ref, chunk, sems).start()

        self.each_span(pass_on)

    def both_arrived(self, own_ref, span_ref, sems):
        token_sems, span_sems, _, _ = sems

        def traded(chunk, device, at, part):
            @pl.when(device % 2 == self.core)
            def _():
                self.trade(span_ref, chunk, sems).wait_send()

            @pl.when(device % 2 != self.core)
            def _():
                self.trade(span_ref, chunk, sems).wait_recv()

        def sent(part, side, chunk, device, at):
            source = self.span_rows(own_ref, chunk)
            copy = remote(source, source, token_sems.at[part, 0, chunk], span_sems.at[0], (device,))

            @pl.when(side == self.core)
            def _():
                self.elsewhere(device, copy.wait_send, None)

        self.each_span(traded)
        self.each_own(sent)

    def batch_to_tokens(self, span_ref, landing, sems):
        token_sems, span_sems = sems

        def start(chunk, device, at, part):
            source, target = self.chunk_rows(span_ref, chunk), self.chunk_rows(landing.at[part, self.core], at)
            token_sem = token_sems.at[part, self.core, at]
            copy = remote(source, target, span_sems.at[chunk], token_sem, (device,))
            self.elsewhere(device, copy.start, pltpu.make_async_copy(source, target, token_sem).start)

        self.each_span(start)

    def batches_arrived(self, span_ref, landing, sems):
        token_sems, span_sems = sems

        def wait(part, side, chunk, device, at):
            source, target = self.chunk_rows(span_ref, at), self.chunk_rows(landing.at[part, side], chunk)
            token_sem = token_sems.at[part, side, chunk]
            copy = remote(target, target, span_sems.at[0], token_sem, (device,))
            self.elsewhere(device, copy.wait_recv, pltpu.make_async_copy(source, target, token_sem).wait)

        def sent(chunk, device, at, part):
            block = self.chunk_rows(span_ref, chunk)
            copy = remote(block, block, span_sems.at[chunk], token_sems.at[0, 0, 0], (device,))
            self.elsewhere(device, copy.wait_send, None)

        self.each_own(wait)
        self.each_span(sent)

    def to_tokens(self, span_ref, landing, sems):
        token_sems, span_sems = sems

        def start(chunk, device, at, part):
            source = self.span_rows(span_ref, chunk)
            target = self.span_rows(landing.at[part, self.core], at)
            copy = remote(source, target, span_sems.at[chunk], token_sems.at[part, self.core, at], (device,))

            def here():
                target[...] = source[...]

            self.elsewhere(device, copy.start, here)

        self.each_span(start)

    def tokens_arrived(self, span_ref, landing, sems):
        token_sems, span_sems = sems

        def wait(part, side, chunk, device, at):
            block = self.span_rows(landing.at[part, side], chunk)
            copy = remote(block, block, span_sems.at[0], token_sems.at[part, side, chunk], (device,))
            self.elsewhere(device, copy.wait_recv, None)

        def sent(chunk, device, at, part):
            block = self.span_rows(span_ref, chunk)
            copy = remote(block, block, span_sems.at[chunk], token_sems.at[0, 0, 0], (device,))
            self.elsewhere(device, copy.wait_send, None)

        self.each_own(wait)
        self.each_span(sent)


def backward_kernel(
    counts, q_in, k_in, v_in, hidden_in, weight_in, att_ref, lse_ref, low_ref, high_ref, down_in, *rest
):
    pairs_in, rest = rest[:8], rest[8:]
    sums_ref, landing, down_total, up_total, out_total, qkv_total = rest[:6]
    (
        arrived, down_ref, up_ref, out_ref, qkv_ref, dq_acc, dk_acc, dv_acc, span, stt_ref,
        load_sems, token_sems, span_sems, back_token_sems, back_span_sems, swap_out, swap_in,
    ) = rest[6:23]
    scratch = rest[23:]
    place = position_of()
    rows = Rows(place)
    batches = span.shape[0]

    def loading(pairs):
        loads = [pltpu.make_async_copy(a, b, load_sems.at[n]) for n, (a, b) in enumerate(pairs)]
        for load in loads:
            load.start()
        return loads

    first_load = loading([(down_in, down_ref)])
    greet(pair_peers(*place) + line_peers(*place) + [(partner_of(*place), True)] + rows.peers())
    sems, sources = (token_sems, span_sems), (low_ref, high_ref)
    rows.to_images(sources, span, sems)
    count = Scatter.COUNT
    down, up, out, qkv = [
        Scatter(place, grad, total, split, scratch[n * count : (n + 1) * count])
        for n, (grad, total, split) in enumerate(
            zip((down_ref, up_ref, out_ref, qkv_ref), (down_total, up_total, out_total, qkv_total), BACK_SPLITS)
        )
    ]
    first_load[0].wait()
    each_turn(down.begin)

    def loop(action, first, last):
        def body(turn, carry):
            action(turn)
            return carry

        lax.fori_loop(first, last, body, 0)

    def rows_grad(left, right, grad_ref, blocks):
        for half in range(2):
            units = slice(half * CHIPS // 2, (half + 1) * CHIPS // 2)
            for first, end in blocks:
                width = end - first
                dq_acc[:HALF, :width] = mm(left[half * HALF : (half + 1) * HALF], right[:, first:end], NN)
                grad_ref[units, :, first:end] = dq_acc[:HALF, :width].reshape(CHIPS // 2, ROWS, width).astype(jnp.bfloat16)

    def weight_grads(left, turned, wide, narrow):
        own = pl.ds(0, SHARD * batches), pl.ds(SHARD * batches, SHARD * batches)
        h2, h2_swap, gu, gu_swap, att, att_swap, gb, gb_swap = pairs_in
        loads = loading(
            [(h2, left.at[own[0]]), (h2_swap, left.at[own[1]]), (gu, wide.at[own[0]]), (gu_swap, wide.at[own[1]])]
            + [(gb, narrow.at[own[0]]), (gb_swap, narrow.at[own[1]])]
        )
        for load in loads:
            load.wait()
        turned[...] = left[...].T
        loads = loading([(att, left.at[own[0]]), (att_swap, left.at[own[1]])])
        rows_grad(turned, wide, up_ref, [(0, 640), (640, 1280), (1280, 1920), (1920, FFH)])
        loop(down.pair, 0, 4)
        each_turn(up.begin)
        for load in loads:
            load.wait()
        turned[...] = left[...].T
        rows_grad(turned, narrow, out_ref, [(0, HALF)])

    tokens = 2 * SHARD * batches
    pl.run_scoped(
        weight_grads,
        pltpu.VMEM((tokens, D), jnp.bfloat16),
        pltpu.VMEM((D, tokens), jnp.bfloat16),
        pltpu.VMEM((tokens, FFH), jnp.bfloat16),
        pltpu.VMEM((tokens, HALF), jnp.bfloat16),
    )

    def attention(q_ref, k_ref, v_ref, hidden, weight):
        loads = loading([(q_in, q_ref), (k_in, k_ref), (v_in, v_ref), (hidden_in, hidden), (weight_in, weight)])
        each_turn(out.begin)
        rows.images_arrived(sources, span, sems)

        def prepare(batch, carry):
            there = in_image(rows.image, rows.has, rows.first, SPAN, 0)
            grads = jnp.where(there, span[batch], 0)
            span[batch] = grads
            lane = lax.broadcasted_iota(jnp.int32, (SPAN, 128), 1)
            stats = jnp.where(lane < CORE_HEADS, lse_ref[batch], 0.0)
            for head in range(CORE_HEADS):
                low, high, _ = head_lanes(head)
                product = grads[:, low:high].astype(jnp.float32) * att_ref[batch, :, low:high].astype(jnp.float32)
                total = jnp.sum(jnp.where(head_mask(head), product, 0.0), axis=1, keepdims=True)
                stats = jnp.where(lane == CORE_HEADS + head, total, stats)
            stt_ref[batch] = stats.T[: 2 * CORE_HEADS]
            return carry

        lax.fori_loop(0, batches, prepare, 0)
        for load in loads:
            load.wait()
        tiles = SPAN // TILE
        work = {
            1: [(down.join, 0, 1)],
            3: [(down.join, 1, 2), (up.pair, 0, 1)],
            5: [(down.join, 2, 3), (up.pair, 1, 2)],
            7: [(down.join, 3, 4), (up.pair, 2, 3)],
            9: [(up.pair, 3, 4)],
            11: [(out.pair, 0, 4), (up.join, 0, 1)],
        }

        def attend(index, carry):
            batch, tile = index // tiles, index % tiles
            attend_back_tile(
                rows.image, rows.has, rows.first, batch, tile, rows.image < counts[batch],
                q_ref, k_ref, v_ref, span, stt_ref, dq_acc, dk_acc, dv_acc,
            )
            for at, actions in work.items():
                @pl.when(index == at)
                def _():
                    for action, first, last in actions:
                        loop(action, first, last)
            return carry

        lax.fori_loop(0, batches * tiles, attend, 0)
        columns = lambda ref: sum(jnp.sum(ref[b].astype(jnp.float32), axis=0, keepdims=True) for b in range(batches))
        sums_ref[0:1] = columns(q_ref)
        sums_ref[1:2] = columns(v_ref)

        def weight_grad(first, end, grads):
            for half in range(2):
                units = slice(half * CHIPS // 2, (half + 1) * CHIPS // 2)
                for batch in range(batches):
                    part = mm(hidden[batch, :, half * HALF : (half + 1) * HALF], grads(batch), TN)
                    if batch == 0:
                        dq_acc[:HALF, : end - first] = part
                    else:
                        dq_acc[:HALF, : end - first] += part
                total = dq_acc[:HALF, : end - first].reshape(CHIPS // 2, ROWS, end - first)
                qkv_ref[units, :, first:end] = total.astype(jnp.bfloat16)

        weight_grad(0, 640, lambda batch: jnp.concatenate([q_ref[batch], k_ref[batch, :, :64]], axis=1))
        weight_grad(640, D, lambda batch: k_ref[batch, :, 64:])
        weight_grad(D, 3 * HALF, lambda batch: v_ref[batch])
        each_turn(qkv.begin)

        def token_grad(batch, others):
            def block(index, carry):
                here = pl.ds(pl.multiple_of(index * TILE, TILE), TILE)
                grads = jnp.concatenate([ref[batch, here] for ref in (q_ref, k_ref, v_ref)], axis=1)
                total = mm(grads, weight[...], NT)
                if others is not None:
                    total = total + others[here].astype(jnp.float32)
                hidden[batch, here] = total.astype(jnp.bfloat16)
                return carry

            lax.fori_loop(0, SPAN // TILE, block, 0)

        core = place[0]
        token_grad(1 - core, None)
        trade = remote(hidden.at[1 - core], arrived, swap_out, swap_in, partner_of(*place))
        trade.start()
        loop(up.join, 1, 2)
        trade.wait_recv()
        token_grad(core, arrived)
        back_sems = (back_token_sems, back_span_sems)
        rows.batch_to_tokens(hidden.at[core], landing, back_sems)
        loop(up.join, 2, 4)
        each_turn(qkv.pair)
        each_turn(out.join)
        each_turn(down.total, 3)
        each_turn(qkv.join)
        each_turn(up.total, 3)
        each_turn(out.total, 3)
        each_turn(qkv.total, 3)
        trade.wait_send()
        rows.batches_arrived(hidden.at[core], landing, back_sems)

    held = lambda *shape: pltpu.VMEM(shape, jnp.bfloat16)
    pl.run_scoped(
        attention, *[held(batches, SPAN, HALF)] * 3, held(batches, SPAN, D), held(D, 3 * HALF)
    )
    for scatter in (down, up, out, qkv):
        scatter.finish()


def backward(counts, query, keys, values, hidden, weight, attended, lse, low, high, down, pairs, collective_id):
    batches = query.shape[0]
    vmem, hbm = pl.BlockSpec(memory_space=pltpu.VMEM), pl.BlockSpec(memory_space=pl.ANY)
    shapes = [down.shape, (CHIPS, ROWS, FFH), (CHIPS, ROWS, HALF), (CHIPS, ROWS, 3 * HALF)]
    held = lambda *shape: pltpu.VMEM(shape, jnp.bfloat16)
    dma = pltpu.SemaphoreType.DMA
    return pl.pallas_call(
        backward_kernel,
        out_shape=[jax.ShapeDtypeStruct((2, HALF), jnp.float32)]
        + [jax.ShapeDtypeStruct((2, batches, SHARD, D), jnp.bfloat16)]
        + [jax.ShapeDtypeStruct(shape[1:], jnp.float32) for shape in shapes],
        in_specs=[pl.BlockSpec(memory_space=pltpu.SMEM)] + [hbm] * 5 + [vmem] * 2 + [hbm] * (3 + len(pairs)),
        out_specs=[vmem, hbm] + [vmem] * 4,
        scratch_shapes=[held(SPAN, D)]
        + [held(*shape) for shape in shapes]
        + [
            pltpu.VMEM((SPAN, HALF + 64), jnp.float32),
            pltpu.VMEM((TILE, HALF), jnp.float32),
            pltpu.VMEM((TILE, HALF), jnp.float32),
            held(batches, SPAN, HALF),
            pltpu.VMEM((batches, 2 * CORE_HEADS, SPAN), jnp.float32),
            dma((8,)),
        ]
        + Rows.scratch() * 2
        + [dma] * 2
        + sum([Scatter.scratch(shape, split) for shape, split in zip(shapes, BACK_SPLITS)], []),
        compiler_params=pltpu.CompilerParams(
            collective_id=collective_id, has_side_effects=True, vmem_limit_bytes=60 * 1024 * 1024
        ),
        cost_estimate=pl.CostEstimate(flops=0, bytes_accessed=500 * 10**6, transcendentals=0),
        name="backward",
    )(counts, query, keys, values, hidden, weight, attended, lse, low, high, down, *pairs)


def chip_unit(core, low, high):
    theirs = swap(by_core(core, high, low))
    return joined(core, by_core(core, low, high), theirs, 0)


def peer(x, y, z, core):
    return (((z * 2 + y) * 2 + x) * 2 + core,)


MESH_ID = pl.DeviceIdType.MESH


def position_of():
    device = lax.axis_index("dev")
    return device % 2, device // 2 % 2, device // 4 % 2, device // 8


def greet(targets):
    barrier = pltpu.get_barrier_semaphore()
    count = 0
    for target, there in targets:
        if there is True:
            pl.semaphore_signal(barrier, inc=1, device_id=target, device_id_type=MESH_ID)
            count = count + 1
        else:
            @pl.when(there)
            def _():
                pl.semaphore_signal(barrier, inc=1, device_id=target, device_id_type=MESH_ID)
            count = count + there.astype(jnp.int32)
    pl.semaphore_wait(barrier, count)


def pair_peers(core, x, y, z):
    return [(peer(1 - x, y, z, core), True), (peer(x, 1 - y, z, core), True)]


def next_peers(core, x, y, z):
    return [(peer(x, y, z - 1, core), z > 0), (peer(x, y, z + 1, core), z < 3)]


def line_peers(core, x, y, z):
    return [(peer(x, y, (z + step) % 4, core), True) for step in (1, 2, 3)]


def partner_of(core, x, y, z):
    return peer(x, y, z, 1 - core)


class Gather:
    def __init__(self, place, unit_ref, full_ref, other_ref, split, sems):
        self.core, self.x, self.y, self.z = place
        self.unit_ref, self.full_ref, self.other_ref, self.split = unit_ref, full_ref, other_ref, split
        (
            self.z_out,
            self.z_in,
            self.pair_out,
            self.pair_in,
            self.half_out,
            self.half_in,
            self.chain_out,
            self.chain_in,
            self.own_sem,
        ) = sems[:9]
        if other_ref is not None:
            self.swap_out, self.swap_in = sems[9:]
        self.sides = ((-1, self.z > 0), (1, self.z < 3))
        self.x_peer = peer(1 - self.x, self.y, self.z, self.core)
        self.y_peer = peer(self.x, 1 - self.y, self.z, self.core)

    @staticmethod
    def scratch(partner):
        dma = pltpu.SemaphoreType.DMA
        shapes = [(2, 4), (4,), (2, 4), (2, 4), (2, 4), (2, 4), (2, 4), (4,)]
        return [dma(shape) for shape in shapes] + [dma] + ([dma((CHIPS,))] * 2 if partner else [])

    def unit_index(self, at_x, at_y, at_z):
        return (at_z * 2 + at_y) * 2 + at_x

    def slot(self, at_x, at_y, at_z):
        return self.full_ref.at[self.unit_index(at_x, at_y, at_z)]

    def column(self, turn, at_z):
        at_x, at_y = [(self.x, self.y), (self.x, 1 - self.y), (1 - self.x, self.y), (1 - self.x, 1 - self.y)][turn]
        return self.slot(at_x, at_y, at_z)

    def copy(self, block, send_sem, recv_sem, target, source=None):
        return pltpu.make_async_remote_copy(
            src_ref=block if source is None else source,
            dst_ref=block,
            send_sem=send_sem,
            recv_sem=recv_sem,
            device_id=target,
            device_id_type=MESH_ID,
        )

    def along(self, at_z, side, source=None):
        index = 0 if side < 0 else 1
        target = peer(self.x, self.y, self.z + side, self.core)
        return self.copy(self.column(0, at_z), self.z_out.at[index, at_z], self.z_in.at[at_z], target, source)

    def chain(self, at_z, side):
        index = 0 if side < 0 else 1
        target = peer(self.x, self.y, self.z + side, self.core)
        return self.copy(self.column(3, at_z), self.chain_out.at[index, at_z], self.chain_in.at[at_z], target)

    def whole(self, at_z, axis, source=None):
        target = (self.x_peer, self.y_peer)[axis]
        return self.copy(self.column(0, at_z), self.pair_out.at[axis, at_z], self.pair_in.at[axis, at_z], target, source)

    def part(self, block, axis):
        width = self.full_ref.shape[2]
        return block.at[:, pl.ds(0, self.split) if axis == 0 else pl.ds(self.split, width - self.split)]

    def half(self, at_z, axis):
        block = self.part(self.column(1 + axis, at_z), axis)
        target = (self.x_peer, self.y_peer)[axis]
        return self.copy(block, self.half_out.at[axis, at_z], self.half_in.at[axis, at_z], target)

    def half_arrival(self, at_z, axis):
        block = self.part(self.column(3, at_z), axis)
        return self.copy(block, self.half_out.at[axis, at_z], self.half_in.at[axis, at_z], self.x_peer)

    def by_halves(self, at_z):
        near = jnp.logical_and(jnp.abs(at_z - self.z) == 1, jnp.logical_or(at_z == 1, at_z == 2))
        return jnp.logical_or(at_z == self.z, near)

    def trade(self, turn, at_z, source=None):
        at_x, at_y = [(self.x, self.y), (self.x, 1 - self.y), (1 - self.x, self.y), (1 - self.x, 1 - self.y)][turn]
        index = self.unit_index(at_x, at_y, at_z)
        block = self.full_ref.at[index] if source is None else source
        width = self.other_ref.shape[2]
        if width < self.full_ref.shape[2]:
            block = block.at[:, pl.ds(0, width)]
        return pltpu.make_async_remote_copy(
            src_ref=block,
            dst_ref=self.other_ref.at[index],
            send_sem=self.swap_out.at[index],
            recv_sem=self.swap_in.at[index],
            device_id=peer(self.x, self.y, self.z, 1 - self.core),
            device_id_type=MESH_ID,
        )

    def share(self, turn, at_z, source=None):
        if self.other_ref is not None:
            self.trade(turn, at_z, source).start()

    def each(self, distance, action):
        if distance == 0:
            action(self.z, 0)
            return
        for side in (-1, 1):
            at_z = self.z + side * distance
            @pl.when(jnp.logical_and(at_z >= 0, at_z <= 3))
            def _():
                action(at_z, side)

    def onwards(self, side, action):
        for to, there in self.sides:
            if side == 0 or to == -side:
                @pl.when(there)
                def _():
                    action(to)

    def arrive(self, at_z, side):
        source = None
        if side == 0:
            source = self.unit_ref
            pltpu.make_async_copy(self.unit_ref, self.column(0, at_z), self.own_sem).start()
        else:
            self.along(at_z, side).wait_recv()
        self.onwards(side, lambda to: self.along(at_z, to, source).start())
        self.whole(at_z, 0, source).start()
        self.whole(at_z, 1, source).start()
        self.share(0, at_z, source)

    def cross(self, at_z, side):
        for axis in (1, 0):
            arrived = self.column(2 - axis, at_z)
            self.copy(arrived, self.pair_out.at[axis, at_z], self.pair_in.at[axis, at_z], self.x_peer).wait_recv()
            @pl.when(self.by_halves(at_z))
            def _():
                self.half(at_z, 1 - axis).start()
            self.share(2 - axis, at_z)

    def far_chain(self, at_z, side):
        return jnp.logical_or(at_z == 0, at_z == 3) if side == 0 else True

    def diagonal(self, at_z, side):
        halves = self.by_halves(at_z)
        @pl.when(halves)
        def _():
            self.half_arrival(at_z, 0).wait_recv()
            self.half_arrival(at_z, 1).wait_recv()
        if side != 0:
            @pl.when(jnp.logical_not(halves))
            def _():
                self.chain(at_z, side).wait_recv()
        @pl.when(self.far_chain(at_z, side))
        def _():
            self.onwards(side, lambda to: self.chain(at_z, to).start())
        self.share(3, at_z)

    def steps(self):
        order = [
            (0, self.arrive),
            (1, self.arrive),
            (0, self.cross),
            (2, self.arrive),
            (0, self.diagonal),
            (1, self.cross),
            (3, self.arrive),
            (1, self.diagonal),
            (2, self.cross),
            (2, self.diagonal),
            (3, self.cross),
            (3, self.diagonal),
        ]
        return [partial(self.each, distance, action) for distance, action in order]

    def settle(self, at_z, side):
        self.onwards(side, lambda to: self.along(at_z, to).wait_send())
        @pl.when(self.far_chain(at_z, side))
        def _():
            self.onwards(side, lambda to: self.chain(at_z, to).wait_send())
        for axis in range(2):
            self.whole(at_z, axis).wait_send()
            @pl.when(self.by_halves(at_z))
            def _():
                self.half(at_z, axis).wait_send()

    def own_ready(self):
        pltpu.make_async_copy(self.unit_ref, self.column(0, self.z), self.own_sem).wait()

    def finish(self):
        for distance in range(4):
            self.each(distance, self.settle)
        if self.other_ref is not None:
            def traded(at_z, carry):
                for turn in range(4):
                    self.trade(turn, at_z).wait()
                return carry

            lax.fori_loop(0, 4, traded, 0)


def remote(source, target, send_sem, recv_sem, device):
    return pltpu.make_async_remote_copy(
        src_ref=source,
        dst_ref=target,
        send_sem=send_sem,
        recv_sem=recv_sem,
        device_id=device,
        device_id_type=MESH_ID,
    )


PADDED = 80
WIDE = CHIPS * PADDED
SHARE = 423


def vector_part(full_ref, start, length, width):
    lane = lax.broadcasted_iota(jnp.int32, (1, width), 1)
    total = jnp.zeros((1, width), jnp.float32)
    for device in range(start // SHARE, (start + length - 1) // SHARE + 1):
        base = 512 * (device % 2)
        tile = full_ref[device // 2, PADDED - 16 :, base : base + 512].astype(jnp.float32)
        row = tile[ROWS - PADDED + 16 : ROWS - PADDED + 17]
        if width > 512:
            row = jnp.concatenate([row, jnp.zeros((1, width - 512), jnp.float32)], axis=1)
        shift = device * SHARE - start
        row = pltpu.roll(row, shift % width, 1) if shift % width else row
        first, last = max(shift, 0), min(shift + SHARE, length)
        total = total + jnp.where((lane >= first) & (lane < last), row, 0.0)
    return total


FIRST_STEPS = (
    (0, 0), (3, 0), (0, 1), (0, 2), (3, 1), (0, 3), (0, 4), (0, 5), (0, 6), (3, 2), (0, 7), (0, 8), (0, 9), (0, 10), (0, 11),
    (1, 0), (2, 0),
)
PROJECT_STEPS = ((0, 0, 1, 2), (1, 0, 2, 3), (2, 1, 1, 2), (3, 0, 3, 4), (4, 1, 2, 3), (5, 0, 4, 6))
ATTEND_STEPS = (
    (1, 1, 3, 4), (3, 0, 6, 7), (5, 1, 4, 5), (6, 0, 7, 8), (7, 1, 5, 6), (8, 0, 8, 9), (9, 1, 6, 7), (10, 0, 9, 10), (11, 1, 7, 8),
)
LAST_STEPS = ((0, 10, 12), (1, 8, 12))


def forward_kernel(
    splits, counts, unit, up_unit, down_unit, tokens_ref, pad_ref,
    q_out, k_out, v_out, hidden_out, att_out, lse_out, full_out, landing, up_ref, up_other, down_ref, down_other,
    q_ref, k_ref, v_ref, hidden_ref, att_ref, lse_ref, full_ref, store_sems, span, padded, acc, token_sems, span_sems, trade_out, trade_in, back_token_sems, back_span_sems, *sems
):
    place = position_of()
    rows = Rows(place)
    greet(pair_peers(*place) + next_peers(*place) + [(partner_of(*place), True)] + rows.peers())
    plain, more = len(Gather.scratch(False)), len(Gather.scratch(True))
    first = Gather(place, unit, full_ref, None, splits[0], sems[:plain])
    second = Gather(place, up_unit, up_ref, up_other, splits[1], sems[plain : plain + more])
    third = Gather(place, down_unit, down_ref, down_other, splits[2], sems[plain + more :])
    held = (q_ref, k_ref, v_ref, hidden_ref, att_ref, lse_ref, full_ref)
    outs = (q_out, k_out, v_out, hidden_out, att_out, lse_out, full_out)
    stores = [pltpu.make_async_copy(a, b, store_sems.at[n]) for n, (a, b) in enumerate(zip(held, outs))]
    one, two, three = first.steps(), second.steps(), third.steps()
    row_sems = (token_sems, span_sems, trade_out, trade_in)

    def run(steps, start, stop):
        for step in steps[start:stop]:
            step()

    row_steps = (
        partial(rows.to_both, tokens_ref, span, row_sems),
        partial(rows.relay, span, row_sems),
        partial(rows.both_arrived, tokens_ref, span, row_sems),
    )

    def start(table):
        for which, step in table:
            if which == 3:
                row_steps[step]()
            else:
                run((one, two, three)[which], step, step + 1)

    start(FIRST_STEPS)
    first.own_ready()
    stores[6].start()
    batches = tokens_ref.shape[0]
    gain, bias = vector_part(full_ref, 0, D, WIDE)[:, :D], vector_part(full_ref, D, D, WIDE)[:, :D]
    core = place[0]
    half = lambda start: jnp.where(
        core == 0, vector_part(full_ref, start, HALF, 1024), vector_part(full_ref, start + HALF, HALF, 1024)
    )[:, :HALF]
    query_bias, value_bias = half(2 * D), half(3 * D)
    block = 256

    def between(table, index):
        for at, steps, begin, stop in table:
            @pl.when(index == at)
            def _():
                run((two, three)[steps], begin, stop)

    def project(index, carry):
        batch, at = index // (SPAN // block), index % (SPAN // block)
        here = pl.ds(pl.multiple_of(at * block, block), block)
        token = rows.first * CHUNK + at * block + lax.broadcasted_iota(jnp.int32, (block, 1), 0)
        there = (token >= rows.image * IMG_LEN) & (token < jnp.minimum((rows.image + 1) * IMG_LEN, TOKENS)) & rows.has
        value = jnp.where(there, span[batch, here], 0).astype(jnp.float32)
        centered = value - jnp.mean(value, axis=1, keepdims=True)
        inverse = lax.rsqrt(jnp.mean(centered * centered, axis=1, keepdims=True) + EPSILON)
        hidden = (centered * inverse * gain + bias).astype(jnp.bfloat16)
        hidden_ref[batch, here] = hidden
        padded[...] = mm(hidden, pad_ref[...], NN).astype(jnp.bfloat16)
        wide = mm(padded[...], full_ref[:, :, :D].reshape(WIDE, D), NN)
        q_ref[batch, here] = (wide[:, :HALF] + query_bias).astype(jnp.bfloat16)
        k_ref[batch, here] = wide[:, HALF:].astype(jnp.bfloat16)
        wide = mm(padded[...], full_ref[:, :, D:].reshape(WIDE, HALF), NN)
        v_ref[batch, here] = (wide + value_bias).astype(jnp.bfloat16)
        between(PROJECT_STEPS, index)
        return carry

    lax.fori_loop(0, batches * (SPAN // block), project, 0)
    for store in stores[:4]:
        store.start()
    tiles = SPAN // TILE

    def attend(index, carry):
        batch, tile = index // tiles, index % tiles
        attend_tile(
            rows.image, rows.has, rows.first, batch, tile, rows.image < counts[batch],
            q_ref, k_ref, v_ref, att_ref, lse_ref, acc,
        )
        between(ATTEND_STEPS, index)
        return carry

    lax.fori_loop(0, batches * tiles, attend, 0)
    for store in stores[4:6]:
        store.start()
    back_sems = (back_token_sems, back_span_sems)
    rows.to_tokens(att_ref, landing, back_sems)
    for steps, begin, stop in LAST_STEPS:
        run((two, three)[steps], begin, stop)
    rows.tokens_arrived(att_ref, landing, back_sems)
    second.own_ready()
    third.own_ready()
    for store in stores:
        store.wait()
    for gather in (first, second, third):
        gather.finish()


def forward(counts, unit, up_unit, down_unit, tokens, collective_id):
    batches = tokens.shape[0]
    full = lambda unit: jax.ShapeDtypeStruct((CHIPS,) + unit.shape, unit.dtype)
    low = lambda *shape: jax.ShapeDtypeStruct(shape, jnp.bfloat16)
    vmem, hbm = pl.BlockSpec(memory_space=pltpu.VMEM), pl.BlockSpec(memory_space=pl.ANY)
    dma = pltpu.SemaphoreType.DMA
    feature, lane = np.arange(D)[:, None], np.arange(WIDE)[None]
    pad = jnp.asarray(feature // ROWS * PADDED + feature % ROWS == lane, jnp.bfloat16)
    spans = [(batches, SPAN, HALF)] * 3 + [(batches, SPAN, D), (batches, SPAN, HALF)]
    outs = pl.pallas_call(
        partial(forward_kernel, (512, 896, 384)),
        out_shape=[low(*shape) for shape in spans]
        + [
            jax.ShapeDtypeStruct((batches, SPAN, 128), jnp.float32),
            full(unit),
            low(2, 2, batches, SHARD, HALF),
            full(up_unit),
            full(up_unit),
            full(down_unit),
            full(down_unit),
        ],
        in_specs=[pl.BlockSpec(memory_space=pltpu.SMEM)] + [vmem] * 5,
        out_specs=[hbm] * 7 + [vmem] + [hbm] * 4,
        scratch_shapes=[pltpu.VMEM(shape, jnp.bfloat16) for shape in spans]
        + [
            pltpu.VMEM((batches, SPAN, 128), jnp.float32),
            pltpu.VMEM((CHIPS,) + unit.shape, unit.dtype),
            dma((7,)),
            pltpu.VMEM((batches, SPAN, D), jnp.bfloat16),
            pltpu.VMEM((256, WIDE), jnp.bfloat16),
            pltpu.VMEM((TILE, HALF), jnp.float32),
        ]
        + Rows.scratch()
        + [dma((SPAN_CHUNKS,)), dma((SPAN_CHUNKS,))]
        + Rows.scratch()
        + Gather.scratch(False)
        + Gather.scratch(True) * 2,
        compiler_params=pltpu.CompilerParams(
            collective_id=collective_id, has_side_effects=True, vmem_limit_bytes=60 * 1024 * 1024
        ),
        cost_estimate=pl.CostEstimate(flops=0, bytes_accessed=500 * 10**6, transcendentals=0),
        name="forward",
    )(counts, unit, up_unit, down_unit, tokens, pad)
    return list(outs[:8]) + [w.reshape(-1, w.shape[2]) for w in outs[8:]]


def vector_kernel(sent_ref, total_ref, arrived, send_sems, recv_sems):
    device = lax.axis_index("dev")
    devices = 2 * CHIPS
    mesh_id = pl.DeviceIdType.MESH
    barrier = pltpu.get_barrier_semaphore()

    def greet(step, carry):
        pl.semaphore_signal(
            barrier, inc=1, device_id=(lax.rem(device + step, devices),), device_id_type=mesh_id
        )
        return carry

    lax.fori_loop(1, devices, greet, 0)
    pl.semaphore_wait(barrier, devices - 1)

    def copy(step):
        target = lax.rem(device + step, devices)
        return pltpu.make_async_remote_copy(
            src_ref=sent_ref.at[target],
            dst_ref=arrived.at[step],
            send_sem=send_sems.at[step],
            recv_sem=recv_sems.at[step],
            device_id=(target,),
            device_id_type=mesh_id,
        )

    def start(step, carry):
        copy(step).start()
        return carry

    lax.fori_loop(1, devices, start, 0)

    def add(step, total):
        copy(step).wait()
        return total + arrived[step]

    total_ref[...] = lax.fori_loop(1, devices, add, sent_ref[device])


def scatter_vector(vector, share, collective_id):
    rows = jnp.pad(vector.reshape(2 * CHIPS, share), ((0, 0), (0, 1024 - share)))
    dma = pltpu.SemaphoreType.DMA
    total = pl.pallas_call(
        vector_kernel,
        out_shape=jax.ShapeDtypeStruct((8, 128), jnp.float32),
        in_specs=[pl.BlockSpec(memory_space=pltpu.VMEM)],
        out_specs=pl.BlockSpec(memory_space=pltpu.VMEM),
        scratch_shapes=[
            pltpu.VMEM((2 * CHIPS, 8, 128), jnp.float32),
            dma((2 * CHIPS,)),
            dma((2 * CHIPS,)),
        ],
        compiler_params=pltpu.CompilerParams(collective_id=collective_id, has_side_effects=True),
        cost_estimate=pl.CostEstimate(flops=0, bytes_accessed=20 * 10**6, transcendentals=0),
        name="scatter_vector",
    )(rows.reshape(2 * CHIPS, 8, 128))
    return total.reshape(-1)[:share]


def later_image(device):
    start = device * SHARD
    at = start + lax.broadcasted_iota(jnp.int32, (SHARD, 1), 0)
    return at >= (start // IMG_LEN + 1) * IMG_LEN


MLP_ROWS = SHARD
GELU_A, GELU_B = 0.7978845608028654, 0.044715


def mlp_kernel(
    x_ref, landing, g_ref, up_a, up_b, down_a, down_b, vec_ref, bias_ref,
    att_ref, result_ref, act_a, act_b, gu_a, gu_b, h2_ref, gb_a, gb_b, gm_ref, go_a, go_b, sums_ref, bias_sums_ref,
    wo_a, wo_b, up_w, down_w, slope, sems,
):
    loads = [
        pltpu.make_async_copy(source, target, sems.at[n])
        for n, (source, target) in enumerate(
            [
                (up_a.at[:, pl.ds(0, FFH)], up_w.at[0]),
                (up_b.at[:, pl.ds(0, FFH)], up_w.at[1]),
                (down_a, down_w.at[0]),
                (down_b, down_w.at[1]),
                (up_a.at[:, pl.ds(FFH, HALF)], wo_a),
                (up_b.at[:, pl.ds(FFH, HALF)], wo_b),
            ]
        )
    ]
    for load in loads[4:] + loads[:4]:
        load.start()
    sums_ref[...] = jnp.zeros_like(sums_ref)
    bias_sums_ref[...] = jnp.zeros_like(bias_sums_ref)
    acts, grads_up = (act_a, act_b), (gu_a, gu_b)
    device = lax.axis_index("dev")
    core = device % 2
    later = later_image(device)
    mean = lambda value: jnp.mean(value, axis=1, keepdims=True)

    def tile(index, carry):
        rows = pl.ds(pl.multiple_of(index * MLP_ROWS, MLP_ROWS), MLP_ROWS)

        def ready(load):
            @pl.when(index == 0)
            def _():
                load.wait()

        ready(loads[4])
        ready(loads[5])
        atts = [jnp.where(later, landing[1, side, index], landing[0, side, index]) for side in range(2)]
        att_ref[rows] = jnp.concatenate(atts, axis=1)
        sides = [mm(atts[0], wo[:HALF], NN) + mm(atts[1], wo[HALF:], NN) for wo in (wo_a, wo_b)]
        branch = jnp.where(core == 0, jnp.concatenate(sides, axis=1), jnp.concatenate(sides[::-1], axis=1))
        middle = x_ref[rows].astype(jnp.float32) + (branch + vec_ref[0:1])
        centered = middle - mean(middle)
        inverse = lax.rsqrt(mean(centered * centered) + EPSILON)
        normed = centered * inverse
        gain = vec_ref[1:2]
        hidden = (normed * gain + vec_ref[2:3]).astype(jnp.bfloat16)
        h2_ref[rows] = hidden
        for half in range(2):
            ready(loads[half])
            upper = mm(hidden, up_w[half], NN) + bias_ref[half : half + 1]
            square = upper * upper
            tanh = jnp.tanh(GELU_A * (upper + GELU_B * (square * upper)))
            acts[half][rows] = (0.5 * upper * (1.0 + tanh)).astype(jnp.bfloat16)
            slope[half] = 0.5 * (1.0 + tanh) + (0.5 * GELU_A) * upper * (1.0 - tanh * tanh) * (
                1.0 + (3.0 * GELU_B) * square
            )
        for half in range(2):
            ready(loads[2 + half])
        lower = mm(act_a[rows], down_w[0], NN) + mm(act_b[rows], down_w[1], NN)
        result_ref[rows] = (middle + (lower + vec_ref[3:4])).astype(jnp.bfloat16)
        grad = g_ref[rows]
        for half in range(2):
            grad_upper = (mm(grad, down_w[half], NT) * slope[half]).astype(jnp.bfloat16)
            grads_up[half][rows] = grad_upper
            bias_sums_ref[half : half + 1] += jnp.sum(grad_upper.astype(jnp.float32), axis=0, keepdims=True)
        grad_hidden = mm(gu_a[rows], up_w[0], NT) + mm(gu_b[rows], up_w[1], NT)
        scaled = grad_hidden * gain
        wide = grad.astype(jnp.float32)
        grad_middle = wide + inverse * (scaled - mean(scaled) - normed * mean(scaled * normed))
        gm_ref[rows] = grad_middle
        branch = grad_middle.astype(jnp.bfloat16)
        low, high = branch[:, :HALF], branch[:, HALF:]
        branches = jnp.where(core == 0, low, high), jnp.where(core == 0, high, low)
        gb_a[rows], gb_b[rows] = branches
        for go_ref, heads in ((go_a, slice(0, HALF)), (go_b, slice(HALF, D))):
            total = mm(branches[0], wo_a[heads], NT) + mm(branches[1], wo_b[heads], NT)
            go_ref[rows] = total.astype(jnp.bfloat16)
        for n, value in enumerate([branch.astype(jnp.float32), grad_hidden * normed, grad_hidden, wide]):
            sums_ref[n : n + 1] += jnp.sum(value, axis=0, keepdims=True)
        return carry

    lax.fori_loop(0, x_ref.shape[0] // MLP_ROWS, tile, 0)


def mlp(x, landing, grad, ups, downs, vecs, biases):
    rows = x.shape[0]
    vmem, hbm = pl.BlockSpec(memory_space=pltpu.VMEM), pl.BlockSpec(memory_space=pl.ANY)
    low = lambda width: jax.ShapeDtypeStruct((rows, width), jnp.bfloat16)
    wide = lambda *shape: jax.ShapeDtypeStruct(shape, jnp.float32)
    return pl.pallas_call(
        mlp_kernel,
        out_shape=[low(D), low(D)] + [low(FFH)] * 4 + [low(D), low(HALF), low(HALF), wide(rows, D), low(HALF), low(HALF), wide(8, D), wide(8, FFH)],
        in_specs=[vmem] * 3 + [hbm] * 4 + [vmem] * 2,
        out_specs=[vmem] * 14,
        scratch_shapes=[
            pltpu.VMEM((D, HALF), jnp.bfloat16),
            pltpu.VMEM((D, HALF), jnp.bfloat16),
            pltpu.VMEM((2, D, FFH), jnp.bfloat16),
            pltpu.VMEM((2, FFH, D), jnp.bfloat16),
            pltpu.VMEM((2, MLP_ROWS, FFH), jnp.float32),
            pltpu.SemaphoreType.DMA((6,)),
        ],
        compiler_params=pltpu.CompilerParams(vmem_limit_bytes=62 * 1024 * 1024),
        cost_estimate=pl.CostEstimate(flops=0, bytes_accessed=130 * 10**6, transcendentals=0),
        name="mlp",
    )(x, landing, grad, *ups, *downs, vecs, biases)


def topo_local(tokens, counts, qkv_weight, out_weight, up_weight, down_weight, vectors, cotangent):
    device = lax.axis_index("dev")
    core, chip = device % 2, device // 2
    batches = tokens.shape[0]
    share = vectors.shape[0]
    own_rows = batches * SHARD

    qkv36 = qkv_weight.reshape(ROWS // 2, 3 * D)
    out36 = out_weight.reshape(ROWS // 2, D)
    side_qkv = [
        jnp.concatenate([qkv36[:, s * HALF + j * D :][:, :HALF] for j in range(3)], axis=1) for s in range(2)
    ]
    side_out = [out36[:, s * HALF :][:, :HALF] for s in range(2)]
    up36 = up_weight.reshape(ROWS // 2, CHIPS, UNIT)
    up_low = up36[:, :, :UNIT_HALF].reshape(ROWS // 2, FFH)
    up_high = jnp.pad(up36[:, :, UNIT_HALF:], ((0, 0), (0, 0), (0, 2 * UNIT_HALF - UNIT))).reshape(
        ROWS // 2, FFH
    )
    spill = UNIT_HALF * D - down_weight.shape[0]
    borrowed = lax.ppermute(
        down_weight[:spill], "dev", [(i + 1, i) for i in range(0, 2 * CHIPS, 2)]
    )
    down_unit = by_core(
        core,
        jnp.concatenate([down_weight, borrowed]),
        jnp.concatenate([down_weight[spill:], jnp.zeros((2 * spill,), jnp.bfloat16)]),
    ).reshape(UNIT_HALF, D)
    first_unit = chip_unit(
        core,
        jnp.concatenate([side_qkv[0], side_out[0], up_low], axis=1),
        jnp.concatenate([side_qkv[1], side_out[1], up_high], axis=1),
    )
    shares = jnp.pad(vectors, (0, 512 - share)).reshape(1, 512)
    shares = joined(core, shares, swap(shares), 0).reshape(1, 1024)
    extra = jnp.pad(shares, ((0, 7), (0, 3 * HALF - 1024)))
    up_unit = jnp.concatenate([first_unit[:, 4 * HALF :], first_unit[:, 3 * HALF : 4 * HALF]], axis=1)
    (
        query, keys, values, hidden_one, attended, log_sums, full, landing, up_mine, up_theirs, down_mine, down_theirs
    ) = forward(counts, jnp.concatenate([first_unit[:, : 3 * HALF], extra], axis=0), up_unit, down_unit, tokens, 1)
    qkv_w = full[:, :ROWS].reshape(D, 3 * HALF)
    packed = full[:, ROWS, :1024].reshape(2 * CHIPS, 512)[:, :share].reshape(-1).astype(jnp.float32)
    pieces = [packed[segment * D : (segment + 1) * D] for segment in range(8)]
    bias_units = packed[8 * D : 8 * D + FF].reshape(CHIPS, UNIT)
    bias_low = bias_units[:, :UNIT_HALF].reshape(-1)
    bias_high = jnp.pad(bias_units[:, UNIT_HALF:], ((0, 0), (0, 2 * UNIT_HALF - UNIT))).reshape(-1)
    up_bias_mine = by_core(core, bias_low, bias_high)
    up_bias_theirs = by_core(core, bias_high, bias_low)
    def dot_tn(left, right):
        return lax.dot_general(left, right, (((0,), (0,)), ((), ())), preferred_element_type=jnp.float32)

    inputs = tokens.reshape(own_rows, D).astype(jnp.float32)
    grad_output = cotangent.reshape(own_rows, D)
    eight = lambda rows: jnp.pad(jnp.stack(rows), ((0, 8 - len(rows)), (0, 0)))
    (
        att_own, result, active_mine, active_theirs, grad_upper_mine, grad_upper_theirs,
        hidden_two, branch_mine, branch_theirs, grad_middle, heads_low, heads_high, vec_sums, bias_sums,
    ) = mlp(
        tokens.reshape(own_rows, D), landing, grad_output, (up_mine, up_theirs), (down_mine, down_theirs),
        eight([pieces[4], pieces[5], pieces[6], pieces[7]]), eight([up_bias_mine, up_bias_theirs]),
    )

    pair = lambda mine, theirs: jnp.concatenate([mine, swap(theirs)], axis=0)
    grad_down = dot_tn(pair(active_mine, active_theirs), pair(grad_output, grad_output)).astype(jnp.bfloat16)
    both = lambda mine, theirs: [mine, swap(theirs)]
    pairs = (
        both(hidden_two, hidden_two) + both(grad_upper_mine, grad_upper_theirs) + both(att_own, att_own)
        + both(branch_mine, branch_theirs)
    )
    head_sums, landing, down_total, up_total, out_total, qkv_total = backward(
        counts, query, keys, values, hidden_one, qkv_w, attended, log_sums,
        heads_low.reshape(batches, SHARD, HALF), heads_high.reshape(batches, SHARD, HALF),
        grad_down.reshape(CHIPS, UNIT_HALF, D), pairs, 4,
    )
    attention_total = jnp.concatenate([qkv_total, out_total], axis=1)
    later = later_image(device)[None]
    grad_hidden_one = jnp.where(later, landing[1], landing[0]).astype(jnp.float32).reshape(own_rows, D)
    normed_one, inverse_one = layer_stats(inputs)
    grad_input = grad_middle + layer_back(grad_hidden_one, normed_one, inverse_one, pieces[0])

    sums = lambda values: jnp.sum(values.astype(jnp.float32), axis=0)
    at_heads = lambda vector: lax.dynamic_update_slice_in_dim(
        jnp.zeros((D,), jnp.float32), vector, core * HALF, 0
    )
    bias_mine, bias_theirs = bias_sums[0], bias_sums[1]
    bias_low = by_core(core, bias_mine, bias_theirs).reshape(CHIPS, UNIT_HALF)
    bias_high = by_core(core, bias_theirs, bias_mine).reshape(CHIPS, UNIT_HALF)
    grad_up_bias = jnp.concatenate([bias_low, bias_high[:, : UNIT - UNIT_HALF]], axis=1).reshape(-1)
    vector_grad = jnp.concatenate(
        [
            sums(grad_hidden_one * normed_one),
            sums(grad_hidden_one),
            at_heads(head_sums[0]),
            at_heads(head_sums[1]),
            *(vec_sums[n] for n in range(4)),
            grad_up_bias,
            jnp.zeros((32 * share - 8 * D - FF,), jnp.float32),
        ]
    )
    vector_grad = scatter_vector(vector_grad, share, 2)

    half_rows = ROWS // 2

    def whole_rows(total):
        kept = by_core(core, total[:half_rows], total[half_rows:])
        theirs = swap(by_core(core, total[half_rows:], total[:half_rows]))
        return by_core(core, kept, theirs), by_core(core, theirs, kept)

    low, high = whole_rows(attention_total)
    columns = [
        jnp.concatenate([low[:, j * HALF : (j + 1) * HALF], high[:, j * HALF : (j + 1) * HALF]], axis=1)
        for j in range(4)
    ]
    qkv_grad = jnp.concatenate(columns[:3], axis=1).reshape(-1)
    out_grad = columns[3].reshape(-1)
    low, high = whole_rows(up_total)
    up_grad = jnp.concatenate(
        [
            low.reshape(half_rows, CHIPS, UNIT_HALF),
            high.reshape(half_rows, CHIPS, UNIT_HALF)[:, :, : UNIT - UNIT_HALF],
        ],
        axis=2,
    ).reshape(-1)
    down_flat = down_total.reshape(-1)
    returned = lax.ppermute(
        down_flat[down_flat.shape[0] - spill :], "dev", [(i, i + 1) for i in range(0, 2 * CHIPS, 2)]
    )
    down_grad = by_core(
        core,
        down_flat[: down_weight.shape[0]],
        jnp.concatenate([returned, down_flat[: down_weight.shape[0] - spill]]),
    )
    return (
        result.reshape(tokens.shape),
        grad_input.astype(jnp.bfloat16).reshape(tokens.shape),
        qkv_grad,
        out_grad,
        up_grad,
        down_grad,
        vector_grad,
    )


def solution(mesh):
    local = topo_local if mesh.shape["dev"] == 32 else generic_local
    return jax.shard_map(
        local,
        mesh=mesh,
        in_specs=(
            P(None, "dev", None),
            P(),
            P("dev"),
            P("dev"),
            P("dev"),
            P("dev"),
            P("dev"),
            P(None, "dev", None),
        ),
        out_specs=(
            P(None, "dev", None),
            P(None, "dev", None),
            P("dev"),
            P("dev"),
            P("dev"),
            P("dev"),
            P("dev"),
        ),
        check_vma=False,
    )
```

```python
from functools import partial

import jax
import jax.numpy as jnp
import numpy as np
from jax import lax
from jax.experimental import pallas as pl
from jax.experimental.pallas import tpu as pltpu
from jax.sharding import PartitionSpec as P

D = 1152
HEADS = 16
FF = 4304
IMG_LEN = 729


heads_per_block = 4
EPSILON = 1e-06
MASKED = -1e30


def passed_along(block, axis, distance):
    devices = range(lax.axis_size(axis))
    route = [(i - distance, i) for i in devices if i - distance in devices]
    return lax.ppermute(block, axis, route)


def layer_stats(values):
    centered = values - jnp.mean(values, axis=-1, keepdims=True)
    inverse = lax.rsqrt(jnp.mean(centered * centered, axis=-1, keepdims=True) + EPSILON)
    return (centered * inverse, inverse)


def layer_back(grad_output, normed, inverse, gain):
    scaled = grad_output * gain
    return inverse * (
        scaled
        - jnp.mean(scaled, axis=-1, keepdims=True)
        - normed * jnp.mean(scaled * normed, axis=-1, keepdims=True)
    )


def image_of(positions, image_count):
    return jnp.where(positions < image_count * IMG_LEN, positions // IMG_LEN, -positions - 1)


def reach_sizes(shard_rows):
    rim_rows = IMG_LEN - 1
    reach_count = (rim_rows + shard_rows - 1) // shard_rows
    return [
        min(shard_rows, rim_rows - (distance - 1) * shard_rows)
        for distance in range(1, reach_count + 1)
    ]


def widen(key_value, shard_rows):
    edge_sizes = reach_sizes(shard_rows)
    arrived = {}
    for distance, amount in enumerate(edge_sizes, start=1):
        for direction in (1, -1):
            sent_rows = key_value[shard_rows - amount :] if direction > 0 else key_value[:amount]
            arrived[distance, direction] = passed_along(sent_rows, "dev", direction * distance)
    before = [arrived[distance, 1] for distance in range(len(edge_sizes), 0, -1)]
    after = [arrived[distance, -1] for distance in range(1, len(edge_sizes) + 1)]
    return jnp.concatenate(before + [key_value] + after, axis=0)


def return_edges(grad_extended, shard_rows):
    edge_sizes = reach_sizes(shard_rows)
    rim_rows = IMG_LEN - 1
    combined = grad_extended[rim_rows : rim_rows + shard_rows]
    for distance, amount in enumerate(edge_sizes, start=1):
        for direction in (1, -1):
            if direction > 0:
                begin_row = rim_rows - sum(edge_sizes[:distance])
            else:
                begin_row = rim_rows + shard_rows + sum(edge_sizes[: distance - 1])
            arrived = passed_along(
                grad_extended[begin_row : begin_row + amount].astype(jnp.bfloat16),
                "dev",
                -direction * distance,
            ).astype(jnp.float32)
            if direction > 0:
                combined = combined.at[shard_rows - amount :].add(arrived)
            else:
                combined = combined.at[:amount].add(arrived)
    return combined


def key_window(device_index, shard_rows, image_count):
    span_rows = ((shard_rows + IMG_LEN - 2) // IMG_LEN + 1) * IMG_LEN
    shard_start = device_index * shard_rows
    window_start = shard_start // IMG_LEN * IMG_LEN
    offset_rows = window_start - shard_start + IMG_LEN - 1
    query_images = image_of(shard_start + jnp.arange(shard_rows, dtype=jnp.int32), image_count)
    key_images = image_of(window_start + jnp.arange(span_rows, dtype=jnp.int32), image_count)
    return (span_rows, offset_rows, query_images[:, None] == key_images[None, :])


def head_slices(query, window_kv, block_index):
    head_dim = D // HEADS
    block_width = heads_per_block * head_dim
    first_column = block_index * block_width
    query_block = query[:, first_column : first_column + block_width].reshape(
        query.shape[0], heads_per_block, head_dim
    )
    key_block = window_kv[:, first_column : first_column + block_width].reshape(
        window_kv.shape[0], heads_per_block, head_dim
    )
    value_block = window_kv[:, D + first_column : D + first_column + block_width].reshape(
        window_kv.shape[0], heads_per_block, head_dim
    )
    return (query_block, key_block, value_block, first_column, block_width)


def attend(query, window_kv, visible):
    score_scale = (D // HEADS) ** (-0.5)
    outputs, log_sums = ([], [])
    for block_index in range(HEADS // heads_per_block):
        query_block, key_block, value_block, first_column, block_width = head_slices(
            query, window_kv, block_index
        )
        raw_scores = jnp.einsum(
            "qhd,khd->hqk", query_block, key_block, preferred_element_type=jnp.float32
        )
        scores = jnp.where(visible[None], raw_scores * score_scale, MASKED)
        largest = jnp.max(scores, axis=-1, keepdims=True)
        exponent = jnp.exp(scores - largest)
        row_totals = jnp.sum(exponent, axis=-1, keepdims=True)
        probabilities = (exponent / row_totals).astype(jnp.bfloat16)
        log_sums.append(largest + jnp.log(row_totals))
        attended = jnp.einsum(
            "hqk,khd->qhd", probabilities, value_block, preferred_element_type=jnp.float32
        )
        outputs.append(attended.reshape(query.shape[0], block_width))
    return (jnp.concatenate(outputs, axis=1), log_sums)


def attend_back(query, window_kv, visible, log_sums, grad_attended):
    score_scale = (D // HEADS) ** (-0.5)
    grad_queries, grad_keys, grad_values = ([], [], [])
    for block_index in range(HEADS // heads_per_block):
        query_block, key_block, value_block, first_column, block_width = head_slices(
            query, window_kv, block_index
        )
        grad_block = grad_attended[:, first_column : first_column + block_width].reshape(
            query.shape[0], heads_per_block, block_width // heads_per_block
        )
        raw_scores = jnp.einsum(
            "qhd,khd->hqk", query_block, key_block, preferred_element_type=jnp.float32
        )
        scores = jnp.where(visible[None], raw_scores * score_scale, MASKED)
        probabilities = jnp.exp(scores - log_sums[block_index])
        grad_values.append(
            jnp.einsum(
                "hqk,qhd->khd",
                probabilities.astype(jnp.bfloat16),
                grad_block,
                preferred_element_type=jnp.float32,
            ).reshape(window_kv.shape[0], block_width)
        )
        grad_probs = jnp.einsum(
            "qhd,khd->hqk", grad_block, value_block, preferred_element_type=jnp.float32
        )
        inner = jnp.sum(probabilities * grad_probs, axis=-1, keepdims=True)
        grad_raw = (probabilities * (grad_probs - inner) * score_scale).astype(jnp.bfloat16)
        grad_queries.append(
            jnp.einsum(
                "hqk,khd->qhd", grad_raw, key_block, preferred_element_type=jnp.float32
            ).reshape(query.shape[0], block_width)
        )
        grad_keys.append(
            jnp.einsum(
                "hqk,qhd->khd", grad_raw, query_block, preferred_element_type=jnp.float32
            ).reshape(window_kv.shape[0], block_width)
        )
    return (jnp.concatenate(grad_queries, axis=1), jnp.concatenate(grad_keys + grad_values, axis=1))


def unpack(gathered):
    qkv_flat, out_flat, up_flat, down_flat, packed = gathered
    packed = packed.astype(jnp.float32)
    pieces = [packed[segment * D : (segment + 1) * D] for segment in range(8)]
    up_bias = packed[8 * D : 8 * D + FF]
    return (
        qkv_flat.reshape(D, 3 * D),
        out_flat.reshape(D, D),
        up_flat.reshape(D, FF),
        down_flat.reshape(FF, D),
        pieces,
        up_bias,
    )


def forward_batch(tokens_batch, image_count, weights, device_index):
    qkv_w, out_w, up_w, down_w, pieces, up_bias = weights
    shard_rows = tokens_batch.shape[0]
    rim_rows = IMG_LEN - 1
    inputs = tokens_batch.astype(jnp.float32)
    normed_one, inverse_one = layer_stats(inputs)
    hidden_one = (normed_one * pieces[0] + pieces[1]).astype(jnp.bfloat16)
    projected = jnp.dot(hidden_one, qkv_w, preferred_element_type=jnp.float32)
    query = (projected[:, :D] + pieces[2]).astype(jnp.bfloat16)
    key_value = jnp.concatenate(
        [projected[:, D : 2 * D], projected[:, 2 * D :] + pieces[3]], axis=1
    ).astype(jnp.bfloat16)
    extended = widen(key_value, shard_rows)
    span_rows, offset_rows, visible = key_window(device_index, shard_rows, image_count)
    padded = jnp.pad(extended, ((0, rim_rows + span_rows - extended.shape[0]), (0, 0)))
    window_kv = lax.dynamic_slice_in_dim(padded, offset_rows, span_rows, 0)
    attended, log_sums = attend(query, window_kv, visible)
    attended_low = attended.astype(jnp.bfloat16)
    middle = inputs + (jnp.dot(attended_low, out_w, preferred_element_type=jnp.float32) + pieces[4])
    normed_two, inverse_two = layer_stats(middle)
    hidden_two = (normed_two * pieces[5] + pieces[6]).astype(jnp.bfloat16)
    upper = jnp.dot(hidden_two, up_w, preferred_element_type=jnp.float32) + up_bias
    active = jax.nn.gelu(upper, approximate=True).astype(jnp.bfloat16)
    output = middle + (jnp.dot(active, down_w, preferred_element_type=jnp.float32) + pieces[7])
    saved = (
        normed_one,
        inverse_one,
        hidden_one,
        query,
        window_kv,
        offset_rows,
        visible,
        log_sums,
        attended_low,
        normed_two,
        inverse_two,
        hidden_two,
        upper,
        active,
    )
    return (output.astype(jnp.bfloat16), saved)


def backward_batch(grad_output, saved, weights, vector_length):
    qkv_w, out_w, up_w, down_w, pieces, up_bias = weights
    (
        normed_one,
        inverse_one,
        hidden_one,
        query,
        window_kv,
        offset_rows,
        visible,
        log_sums,
        attended_low,
        normed_two,
        inverse_two,
        hidden_two,
        upper,
        active,
    ) = saved
    shard_rows = query.shape[0]
    span_rows = window_kv.shape[0]
    rim_rows = IMG_LEN - 1
    grad_wide = grad_output.astype(jnp.float32)
    grad_down = jnp.einsum("tf,td->fd", active, grad_output, preferred_element_type=jnp.float32)
    grad_down_bias = jnp.sum(grad_wide, axis=0)
    grad_active = jnp.einsum("td,fd->tf", grad_output, down_w, preferred_element_type=jnp.float32)
    gelu_back = jax.vjp(partial(jax.nn.gelu, approximate=True), upper)[1]
    grad_upper = gelu_back(grad_active)[0].astype(jnp.bfloat16)
    grad_up = jnp.einsum("td,tf->df", hidden_two, grad_upper, preferred_element_type=jnp.float32)
    grad_up_bias = jnp.sum(grad_upper.astype(jnp.float32), axis=0)
    grad_hidden_two = jnp.einsum("tf,df->td", grad_upper, up_w, preferred_element_type=jnp.float32)
    grad_gain_two = jnp.sum(grad_hidden_two * normed_two, axis=0)
    grad_bias_two = jnp.sum(grad_hidden_two, axis=0)
    grad_middle = grad_wide + layer_back(grad_hidden_two, normed_two, inverse_two, pieces[5])
    grad_branch = grad_middle.astype(jnp.bfloat16)
    grad_out = jnp.einsum(
        "td,te->de", attended_low, grad_branch, preferred_element_type=jnp.float32
    )
    grad_out_bias = jnp.sum(grad_branch.astype(jnp.float32), axis=0)
    grad_attended = jnp.einsum(
        "te,de->td", grad_branch, out_w, preferred_element_type=jnp.float32
    ).astype(jnp.bfloat16)
    grad_query, grad_window = attend_back(query, window_kv, visible, log_sums, grad_attended)
    grad_padded = lax.dynamic_update_slice_in_dim(
        jnp.zeros((rim_rows + span_rows, 2 * D), jnp.float32), grad_window, offset_rows, 0
    )
    grad_kv = return_edges(grad_padded[: shard_rows + 2 * rim_rows], shard_rows)
    grad_query_low = grad_query.astype(jnp.bfloat16)
    grad_kv_low = grad_kv.astype(jnp.bfloat16)
    grad_projected = jnp.concatenate([grad_query_low, grad_kv_low], axis=1)
    grad_qkv = jnp.einsum(
        "td,te->de", hidden_one, grad_projected, preferred_element_type=jnp.float32
    )
    grad_query_bias = jnp.sum(grad_query_low.astype(jnp.float32), axis=0)
    grad_value_bias = jnp.sum(grad_kv_low[:, D:].astype(jnp.float32), axis=0)
    grad_hidden_one = jnp.einsum(
        "te,de->td", grad_projected, qkv_w, preferred_element_type=jnp.float32
    )
    grad_gain_one = jnp.sum(grad_hidden_one * normed_one, axis=0)
    grad_bias_one = jnp.sum(grad_hidden_one, axis=0)
    grad_input = grad_middle + layer_back(grad_hidden_one, normed_one, inverse_one, pieces[0])
    vector_grad = jnp.concatenate(
        [
            grad_gain_one,
            grad_bias_one,
            grad_query_bias,
            grad_value_bias,
            grad_out_bias,
            grad_gain_two,
            grad_bias_two,
            grad_down_bias,
            grad_up_bias,
            jnp.zeros((vector_length - 8 * D - FF,), jnp.float32),
        ]
    )
    flat_grads = (
        grad_qkv.reshape(-1),
        grad_out.reshape(-1),
        grad_up.reshape(-1),
        grad_down.reshape(-1),
        vector_grad,
    )
    return (grad_input.astype(jnp.bfloat16), flat_grads)


def generic_local(tokens, counts, qkv_weight, out_weight, up_weight, down_weight, vectors, cotangent):
    device_index = lax.axis_index("dev")
    vector_length = vectors.shape[0] * lax.axis_size("dev")
    gathered = (
        lax.all_gather(qkv_weight, "dev", axis=0, tiled=True),
        lax.all_gather(out_weight, "dev", axis=0, tiled=True),
        lax.all_gather(up_weight, "dev", axis=0, tiled=True),
        lax.all_gather(down_weight, "dev", axis=0, tiled=True),
        lax.all_gather(vectors, "dev", axis=0, tiled=True),
    )
    weights = unpack(gathered)
    results, kept_state = ([], [])
    for batch_index in range(tokens.shape[0]):
        output, saved = forward_batch(
            tokens[batch_index], counts[batch_index], weights, device_index
        )
        results.append(output)
        kept_state.append(saved)
    weights = unpack(
        (
            lax.all_gather(qkv_weight, "dev", axis=0, tiled=True),
            lax.all_gather(out_weight, "dev", axis=0, tiled=True),
            lax.all_gather(up_weight, "dev", axis=0, tiled=True),
            lax.all_gather(down_weight, "dev", axis=0, tiled=True),
            lax.all_gather(vectors, "dev", axis=0, tiled=True),
        )
    )
    grad_inputs = []
    totals = None
    for batch_index in range(tokens.shape[0]):
        grad_input, flat_grads = backward_batch(
            cotangent[batch_index], kept_state[batch_index], weights, vector_length
        )
        grad_inputs.append(grad_input)
        totals = (
            flat_grads
            if totals is None
            else tuple((earlier + current for earlier, current in zip(totals, flat_grads)))
        )
    totals = lax.psum_scatter(totals, "dev", scatter_dimension=0, tiled=True)
    return (
        jnp.stack(results),
        jnp.stack(grad_inputs),
        totals[0],
        totals[1],
        totals[2],
        totals[3],
        totals[4],
    )


CHIPS = 16
HEAD = D // HEADS
HALF = D // 2
CORE_HEADS = HEADS // 2
ROWS = D // CHIPS
UNIT = FF // CHIPS
UNIT_HALF = 136
UNIT_SECOND = 134
FFH = CHIPS * UNIT_HALF
SHARD = 256
CHIP_ROWS = 2 * SHARD
TILE = 128
CHUNK = 16
SPAN = 768
SPAN_CHUNKS = SPAN // CHUNK
SHARD_CHUNKS = SHARD // CHUNK
SPAN_DEVICES = 4
TOKENS = 2 * CHIPS * SHARD
SCALE = HEAD**-0.5


def route(target):
    return [(i, target(i)) for i in range(2 * CHIPS)]


def swap(block):
    return lax.ppermute(block, "dev", route(lambda i: i ^ 1))


def by_core(core, first, second):
    return jnp.where(core == 0, first, second)


def joined(core, mine, theirs, axis):
    return by_core(
        core,
        jnp.concatenate([mine, theirs], axis=axis),
        jnp.concatenate([theirs, mine], axis=axis),
    )


def head_lanes(head):
    first = head * HEAD
    low = first // 128 * 128
    high = min((first + HEAD + 127) // 128 * 128, HALF)
    return low, high, first - low


def head_mask(head):
    low, high, skip = head_lanes(head)
    lanes = lax.broadcasted_iota(jnp.int32, (1, high - low), 1)
    return (lanes >= skip) & (lanes < skip + HEAD)


NT = (((1,), (1,)), ((), ()))
NN = (((1,), (0,)), ((), ()))
TN = (((0,), (0,)), ((), ()))


def mm(left, right, dims):
    return lax.dot_general(left, right, dims, preferred_element_type=jnp.float32)


def image_of_chip(chip):
    image = (CHIP_ROWS * chip + IMG_LEN // 2) // IMG_LEN
    has = owner_of_image(image) == chip
    first = image * IMG_LEN // CHUNK
    last = jnp.minimum((image * IMG_LEN + IMG_LEN - 1) // CHUNK, TOKENS // CHUNK - 1)
    return image, has, first, jnp.where(has, last - first + 1, 0)


def owner_of_image(image):
    return jnp.minimum((image * IMG_LEN + IMG_LEN // 2) // CHIP_ROWS, CHIPS - 1)


def in_image(image, has, first, rows, axis):
    shape = (rows, 1) if axis == 0 else (1, rows)
    at = first * CHUNK + lax.broadcasted_iota(jnp.int32, shape, axis)
    there = (at >= image * IMG_LEN) & (at < jnp.minimum((image + 1) * IMG_LEN, TOKENS))
    return there & has


def diagonal_tile(tile):
    row = tile * TILE + lax.broadcasted_iota(jnp.int32, (TILE, SPAN), 0)
    return row == lax.broadcasted_iota(jnp.int32, (TILE, SPAN), 1)


def attend_tile(image, has, first, batch, tile, live, q_ref, k_ref, v_ref, att_ref, lse_ref, acc):
    rows = pl.ds(pl.multiple_of(tile * TILE, TILE), TILE)
    visible = in_image(image, has, first, SPAN, 1) & (live | diagonal_tile(tile))
    stats = jnp.zeros((TILE, 128), jnp.float32)
    lane = lax.broadcasted_iota(jnp.int32, (TILE, 128), 1)
    acc[...] = jnp.zeros_like(acc)
    for head in range(CORE_HEADS):
        low, high, _ = head_lanes(head)
        mask = head_mask(head)
        query = jnp.where(mask, q_ref[batch, rows, low:high], 0)
        scores = jnp.where(visible, mm(query, k_ref[batch, :, low:high], NT) * SCALE, MASKED)
        largest = jnp.max(scores, axis=1, keepdims=True)
        exponent = jnp.exp(scores - largest)
        total = jnp.sum(exponent, axis=1, keepdims=True)
        probs = (exponent * (1.0 / total)).astype(jnp.bfloat16)
        part = mm(probs, v_ref[batch, :, low:high], NN)
        acc[:, low:high] += jnp.where(mask, part, 0.0)
        stats = jnp.where(lane == head, largest + jnp.log(total), stats)
    lse_ref[batch, rows] = stats
    att_ref[batch, rows] = acc[...].astype(jnp.bfloat16)


class Scatter:
    def __init__(self, place, grad_ref, total_ref, split, scratch):
        self.core, self.x, self.y, self.z = place
        self.grad_ref, self.total_ref, self.split = grad_ref, total_ref, split
        (self.half_x, self.half_y, self.whole_x, self.whole_y, self.from_z) = scratch[:5]
        (self.half_out, self.half_in, self.pair_out, self.pair_in, self.z_out, self.z_in) = scratch[5:]

    @staticmethod
    def scratch(shape, split):
        rows, columns = shape[1:]
        dma = pltpu.SemaphoreType.DMA
        block = lambda count, width: pltpu.VMEM((count, rows, width), jnp.bfloat16)
        return (
            [block(4, split), block(4, columns - split)]
            + [block(4, columns), block(4, columns), block(3, columns)]
            + [dma((2, 4)), dma((2, 4)), dma((2, 4)), dma((2, 4)), dma((3,)), dma((3,))]
        )

    COUNT = 11

    def unit(self, at_x, at_y, turn):
        at_z = (self.z + 1 + turn) % 4
        return self.grad_ref.at[(at_z * 2 + at_y) * 2 + at_x]

    def remote(self, source, target_ref, send_sem, recv_sem, device):
        return pltpu.make_async_remote_copy(
            src_ref=source,
            dst_ref=target_ref,
            send_sem=send_sem,
            recv_sem=recv_sem,
            device_id=device,
            device_id_type=MESH_ID,
        )

    def half(self, turn, axis):
        diagonal = self.unit(1 - self.x, 1 - self.y, turn)
        columns = self.grad_ref.shape[2]
        source = diagonal.at[:, pl.ds(0, self.split) if axis == 0 else pl.ds(self.split, columns - self.split)]
        device = (peer(1 - self.x, self.y, self.z, self.core), peer(self.x, 1 - self.y, self.z, self.core))[axis]
        target = (self.half_x, self.half_y)[axis].at[turn]
        return self.remote(source, target, self.half_out.at[axis, turn], self.half_in.at[axis, turn], device)

    def whole(self, turn, axis):
        device = (peer(1 - self.x, self.y, self.z, self.core), peer(self.x, 1 - self.y, self.z, self.core))[axis]
        source = (self.unit(1 - self.x, self.y, turn), self.unit(self.x, 1 - self.y, turn))[axis]
        target = (self.whole_x, self.whole_y)[axis]
        return self.remote(
            source, target.at[turn], self.pair_out.at[axis, turn], self.pair_in.at[axis, turn], device
        )

    def along(self, turn):
        device = peer(self.x, self.y, (self.z + 1 + turn) % 4, self.core)
        return self.remote(self.unit(self.x, self.y, turn), self.from_z.at[turn], self.z_out.at[turn], self.z_in.at[turn], device)

    def begin(self, turn):
        self.half(turn, 0).start()
        self.half(turn, 1).start()

    def pair(self, turn):
        split = self.split
        wide = lambda value: value.astype(jnp.float32)
        self.half(turn, 0).wait_recv()
        grad = self.unit(self.x, 1 - self.y, turn)
        grad[:, :split] = (wide(grad[:, :split]) + wide(self.half_x[turn])).astype(jnp.bfloat16)
        self.whole(turn, 1).start()
        self.half(turn, 1).wait_recv()
        grad = self.unit(1 - self.x, self.y, turn)
        grad[:, split:] = (wide(grad[:, split:]) + wide(self.half_y[turn])).astype(jnp.bfloat16)
        self.whole(turn, 0).start()

    def join(self, turn):
        wide = lambda value: value.astype(jnp.float32)
        self.whole(turn, 0).wait_recv()
        self.whole(turn, 1).wait_recv()
        own = self.unit(self.x, self.y, turn)
        total = wide(own[...]) + (wide(self.whole_x[turn]) + wide(self.whole_y[turn]))

        @pl.when(turn < 3)
        def _():
            own[...] = total.astype(jnp.bfloat16)
            self.along(turn).start()

        @pl.when(turn == 3)
        def _():
            self.total_ref[...] = total

    def total(self, turn):
        self.along(turn).wait_recv()
        self.total_ref[...] += self.from_z[turn].astype(jnp.float32)

    def finish(self):
        def pairs(turn, carry):
            for axis in range(2):
                self.half(turn, axis).wait_send()
                self.whole(turn, axis).wait_send()
            return carry

        def lines(turn, carry):
            self.along(turn).wait_send()
            return carry

        lax.fori_loop(0, 4, pairs, 0)
        lax.fori_loop(0, 3, lines, 0)


def each_turn(action, count=4):
    def body(turn, carry):
        action(turn)
        return carry

    lax.fori_loop(0, count, body, 0)


def attend_back_tile(
    image, has, first, batch, tile, live,
    q_ref, k_ref, v_ref, g_ref, stt_ref, dq_acc, dk_acc, dv_acc,
):
    rows = pl.ds(pl.multiple_of(tile * TILE, TILE), TILE)
    queries_there = in_image(image, has, first, SPAN, 1)
    at = first * CHUNK + tile * TILE + lax.broadcasted_iota(jnp.int32, (TILE, 1), 0)
    keys_there = (at >= image * IMG_LEN) & (at < jnp.minimum((image + 1) * IMG_LEN, TOKENS)) & has
    visible = queries_there & keys_there & (live | diagonal_tile(tile))
    dk_acc[...] = jnp.zeros_like(dk_acc)
    dv_acc[...] = jnp.zeros_like(dv_acc)

    @pl.when(tile == 0)
    def _():
        dq_acc[...] = jnp.zeros_like(dq_acc)

    for head in range(CORE_HEADS):
        low, high, _ = head_lanes(head)
        mask = head_mask(head)
        keys = jnp.where(mask, k_ref[batch, rows, low:high], 0)
        values = jnp.where(mask, v_ref[batch, rows, low:high], 0)
        queries = q_ref[batch, :, low:high]
        grads = g_ref[batch, :, low:high]
        lse = stt_ref[batch, head : head + 1]
        delta = stt_ref[batch, CORE_HEADS + head : CORE_HEADS + head + 1]
        probs = jnp.where(visible, jnp.exp(mm(keys, queries, NT) * SCALE - lse), 0.0)
        dv_acc[:, low:high] += jnp.where(mask, mm(probs.astype(jnp.bfloat16), grads, NN), 0.0)
        grad_probs = mm(values, grads, NT)
        grad_raw = (probs * (grad_probs - delta) * SCALE).astype(jnp.bfloat16)
        dk_acc[:, low:high] += jnp.where(mask, mm(grad_raw, queries, NN), 0.0)
        dq_acc[:, low:high] += mm(grad_raw, keys, TN)
    k_ref[batch, rows] = dk_acc[...].astype(jnp.bfloat16)
    v_ref[batch, rows] = dv_acc[...].astype(jnp.bfloat16)

    @pl.when(tile == SPAN // TILE - 1)
    def _():
        q_ref[batch] = dq_acc[:, :HALF].astype(jnp.bfloat16)


BACK_SPLITS = (384, 768, 128, 512)


class Rows:
    def __init__(self, place):
        core, x, y, z = place
        self.core = core
        self.chip = (z * 2 + y) * 2 + x
        self.device = self.chip * 2 + core
        self.image, self.has, self.first, self.count = image_of_chip(self.chip)
        start = self.device * SHARD
        images = [start // IMG_LEN, (start + SHARD - 1) // IMG_LEN]
        self.parts = []
        for part, image in enumerate(images):
            low = jnp.maximum(image * IMG_LEN - start, 0) // CHUNK
            high = jnp.minimum((image + 1) * IMG_LEN - 1 - start, SHARD - 1) // CHUNK + 1
            if part == 1:
                high = jnp.where(images[1] == images[0], low, high)
            self.parts.append((owner_of_image(image), image * IMG_LEN // CHUNK, low, high))

    def peers(self):
        holders = [
            ((self.first // SHARD_CHUNKS + n,), self.holds(n)) for n in range(SPAN_DEVICES)
        ]
        images = [
            ((owner * 2 + side,), jnp.logical_and(high > low, owner * 2 + side != self.device))
            for owner, _, low, high in self.parts
            for side in range(2)
        ]
        return holders + images

    def holds(self, n):
        device = self.first // SHARD_CHUNKS + n
        last = (self.first + self.count - 1) // SHARD_CHUNKS
        there = jnp.logical_and(self.count > 0, device <= last)
        return jnp.logical_and(there, device != self.device)

    @staticmethod
    def scratch():
        dma = pltpu.SemaphoreType.DMA
        return [dma((2, 2, SHARD_CHUNKS)), dma((SPAN_CHUNKS,))]

    def span_rows(self, ref, chunk):
        return ref.at[:, pl.ds(pl.multiple_of(chunk * CHUNK, CHUNK), CHUNK)]

    def chunk_rows(self, ref, chunk):
        return ref.at[pl.ds(pl.multiple_of(chunk * CHUNK, CHUNK), CHUNK)]

    def each_own(self, action):
        for part, (owner, first, low, high) in enumerate(self.parts):
            for side in range(2):
                def body(chunk, carry):
                    action(part, side, chunk, owner * 2 + side, self.device * SHARD_CHUNKS + chunk - first)
                    return carry

                lax.fori_loop(low, high, body, 0)

    def each_span(self, action):
        def body(chunk, carry):
            at = self.first + chunk
            device = at // SHARD_CHUNKS
            part = jnp.where(device * SHARD // IMG_LEN == self.image, 0, 1)
            action(chunk, device, at % SHARD_CHUNKS, part)
            return carry

        lax.fori_loop(0, self.count, body, 0)

    def elsewhere(self, device, action, here):
        @pl.when(device != self.device)
        def _():
            action()

        if here is not None:
            @pl.when(device == self.device)
            def _():
                here()

    def to_images(self, sources, span_ref, sems):
        token_sems, span_sems = sems

        def start(part, side, chunk, device, at):
            source, target = self.span_rows(sources[side], chunk), self.span_rows(span_ref, at)
            copy = remote(source, target, token_sems.at[part, side, chunk], span_sems.at[at], (device,))
            self.elsewhere(device, copy.start, pltpu.make_async_copy(source, target, span_sems.at[at]).start)

        self.each_own(start)

    def images_arrived(self, sources, span_ref, sems):
        token_sems, span_sems = sems

        def wait(chunk, device, at, part):
            block = self.span_rows(span_ref, chunk)
            span_sem = span_sems.at[chunk]
            copy = remote(block, block, token_sems.at[0, 0, 0], span_sem, (device,))
            local = pltpu.make_async_copy(self.span_rows(sources[0], at), block, span_sem)
            self.elsewhere(device, copy.wait_recv, local.wait)

        def sent(part, side, chunk, device, at):
            source = self.span_rows(sources[side], chunk)
            copy = remote(source, source, token_sems.at[part, side, chunk], span_sems.at[0], (device,))
            self.elsewhere(device, copy.wait_send, None)

        self.each_span(wait)
        self.each_own(sent)

    def to_both(self, own_ref, span_ref, sems):
        token_sems, span_sems, _, _ = sems

        def start(part, side, chunk, device, at):
            source, target = self.span_rows(own_ref, chunk), self.span_rows(span_ref, at)
            copy = remote(source, target, token_sems.at[part, 0, chunk], span_sems.at[at], (device,))

            def here():
                target[...] = source[...]

            @pl.when(side == self.core)
            def _():
                self.elsewhere(device, copy.start, here)

        self.each_own(start)

    def trade(self, span_ref, chunk, sems):
        block = self.span_rows(span_ref, chunk)
        return remote(block, block, sems[2].at[chunk], sems[3].at[chunk], (self.chip * 2 + 1 - self.core,))

    def relay(self, span_ref, sems):
        token_sems, span_sems, _, _ = sems

        def pass_on(chunk, device, at, part):
            block = self.span_rows(span_ref, chunk)
            copy = remote(block, block, token_sems.at[0, 0, 0], span_sems.at[chunk], (device,))

            @pl.when(device % 2 == self.core)
            def _():
                self.elsewhere(device, copy.wait_recv, None)
                self.trade(span_ref, chunk, sems).start()

        self.each_span(pass_on)

    def both_arrived(self, own_ref, span_ref, sems):
        token_sems, span_sems, _, _ = sems

        def traded(chunk, device, at, part):
            @pl.when(device % 2 == self.core)
            def _():
                self.trade(span_ref, chunk, sems).wait_send()

            @pl.when(device % 2 != self.core)
            def _():
                self.trade(span_ref, chunk, sems).wait_recv()

        def sent(part, side, chunk, device, at):
            source = self.span_rows(own_ref, chunk)
            copy = remote(source, source, token_sems.at[part, 0, chunk], span_sems.at[0], (device,))

            @pl.when(side == self.core)
            def _():
                self.elsewhere(device, copy.wait_send, None)

        self.each_span(traded)
        self.each_own(sent)

    def batch_to_tokens(self, span_ref, landing, sems):
        token_sems, span_sems = sems

        def start(chunk, device, at, part):
            source, target = self.chunk_rows(span_ref, chunk), self.chunk_rows(landing.at[part, self.core], at)
            token_sem = token_sems.at[part, self.core, at]
            copy = remote(source, target, span_sems.at[chunk], token_sem, (device,))
            self.elsewhere(device, copy.start, pltpu.make_async_copy(source, target, token_sem).start)

        self.each_span(start)

    def batches_arrived(self, span_ref, landing, sems):
        token_sems, span_sems = sems

        def wait(part, side, chunk, device, at):
            source, target = self.chunk_rows(span_ref, at), self.chunk_rows(landing.at[part, side], chunk)
            token_sem = token_sems.at[part, side, chunk]
            copy = remote(target, target, span_sems.at[0], token_sem, (device,))
            self.elsewhere(device, copy.wait_recv, pltpu.make_async_copy(source, target, token_sem).wait)

        def sent(chunk, device, at, part):
            block = self.chunk_rows(span_ref, chunk)
            copy = remote(block, block, span_sems.at[chunk], token_sems.at[0, 0, 0], (device,))
            self.elsewhere(device, copy.wait_send, None)

        self.each_own(wait)
        self.each_span(sent)

    def to_tokens(self, span_ref, landing, sems):
        token_sems, span_sems = sems

        def start(chunk, device, at, part):
            source = self.span_rows(span_ref, chunk)
            target = self.span_rows(landing.at[part, self.core], at)
            copy = remote(source, target, span_sems.at[chunk], token_sems.at[part, self.core, at], (device,))

            def here():
                target[...] = source[...]

            self.elsewhere(device, copy.start, here)

        self.each_span(start)

    def tokens_arrived(self, span_ref, landing, sems):
        token_sems, span_sems = sems

        def wait(part, side, chunk, device, at):
            block = self.span_rows(landing.at[part, side], chunk)
            copy = remote(block, block, span_sems.at[0], token_sems.at[part, side, chunk], (device,))
            self.elsewhere(device, copy.wait_recv, None)

        def sent(chunk, device, at, part):
            block = self.span_rows(span_ref, chunk)
            copy = remote(block, block, span_sems.at[chunk], token_sems.at[0, 0, 0], (device,))
            self.elsewhere(device, copy.wait_send, None)

        self.each_own(wait)
        self.each_span(sent)


def backward_kernel(
    counts, q_in, k_in, v_in, hidden_in, weight_in, att_ref, lse_ref, low_ref, high_ref, down_in, *rest
):
    pairs_in, rest = rest[:8], rest[8:]
    sums_ref, landing, down_total, up_total, out_total, qkv_total = rest[:6]
    (
        arrived, down_ref, up_ref, out_ref, qkv_ref, dq_acc, dk_acc, dv_acc, span, stt_ref,
        load_sems, token_sems, span_sems, back_token_sems, back_span_sems, swap_out, swap_in,
    ) = rest[6:23]
    scratch = rest[23:]
    place = position_of()
    rows = Rows(place)
    batches = span.shape[0]

    def loading(pairs):
        loads = [pltpu.make_async_copy(a, b, load_sems.at[n]) for n, (a, b) in enumerate(pairs)]
        for load in loads:
            load.start()
        return loads

    first_load = loading([(down_in, down_ref)])
    greet(pair_peers(*place) + line_peers(*place) + [(partner_of(*place), True)] + rows.peers())
    sems, sources = (token_sems, span_sems), (low_ref, high_ref)
    rows.to_images(sources, span, sems)
    count = Scatter.COUNT
    down, up, out, qkv = [
        Scatter(place, grad, total, split, scratch[n * count : (n + 1) * count])
        for n, (grad, total, split) in enumerate(
            zip((down_ref, up_ref, out_ref, qkv_ref), (down_total, up_total, out_total, qkv_total), BACK_SPLITS)
        )
    ]
    first_load[0].wait()
    each_turn(down.begin)

    def loop(action, first, last):
        def body(turn, carry):
            action(turn)
            return carry

        lax.fori_loop(first, last, body, 0)

    def rows_grad(left, right, grad_ref, blocks):
        for half in range(2):
            units = slice(half * CHIPS // 2, (half + 1) * CHIPS // 2)
            for first, end in blocks:
                width = end - first
                dq_acc[:HALF, :width] = mm(left[half * HALF : (half + 1) * HALF], right[:, first:end], NN)
                grad_ref[units, :, first:end] = dq_acc[:HALF, :width].reshape(CHIPS // 2, ROWS, width).astype(jnp.bfloat16)

    def weight_grads(left, turned, wide, narrow):
        own = pl.ds(0, SHARD * batches), pl.ds(SHARD * batches, SHARD * batches)
        h2, h2_swap, gu, gu_swap, att, att_swap, gb, gb_swap = pairs_in
        loads = loading(
            [(h2, left.at[own[0]]), (h2_swap, left.at[own[1]]), (gu, wide.at[own[0]]), (gu_swap, wide.at[own[1]])]
            + [(gb, narrow.at[own[0]]), (gb_swap, narrow.at[own[1]])]
        )
        for load in loads:
            load.wait()
        turned[...] = left[...].T
        loads = loading([(att, left.at[own[0]]), (att_swap, left.at[own[1]])])
        rows_grad(turned, wide, up_ref, [(0, 640), (640, 1280), (1280, 1920), (1920, FFH)])
        loop(down.pair, 0, 4)
        each_turn(up.begin)
        for load in loads:
            load.wait()
        turned[...] = left[...].T
        rows_grad(turned, narrow, out_ref, [(0, HALF)])

    tokens = 2 * SHARD * batches
    pl.run_scoped(
        weight_grads,
        pltpu.VMEM((tokens, D), jnp.bfloat16),
        pltpu.VMEM((D, tokens), jnp.bfloat16),
        pltpu.VMEM((tokens, FFH), jnp.bfloat16),
        pltpu.VMEM((tokens, HALF), jnp.bfloat16),
    )

    def attention(q_ref, k_ref, v_ref, hidden, weight):
        loads = loading([(q_in, q_ref), (k_in, k_ref), (v_in, v_ref), (hidden_in, hidden), (weight_in, weight)])
        each_turn(out.begin)
        rows.images_arrived(sources, span, sems)

        def prepare(batch, carry):
            there = in_image(rows.image, rows.has, rows.first, SPAN, 0)
            grads = jnp.where(there, span[batch], 0)
            span[batch] = grads
            lane = lax.broadcasted_iota(jnp.int32, (SPAN, 128), 1)
            stats = jnp.where(lane < CORE_HEADS, lse_ref[batch], 0.0)
            for head in range(CORE_HEADS):
                low, high, _ = head_lanes(head)
                product = grads[:, low:high].astype(jnp.float32) * att_ref[batch, :, low:high].astype(jnp.float32)
                total = jnp.sum(jnp.where(head_mask(head), product, 0.0), axis=1, keepdims=True)
                stats = jnp.where(lane == CORE_HEADS + head, total, stats)
            stt_ref[batch] = stats.T[: 2 * CORE_HEADS]
            return carry

        lax.fori_loop(0, batches, prepare, 0)
        for load in loads:
            load.wait()
        tiles = SPAN // TILE
        work = {
            1: [(down.join, 0, 1)],
            3: [(down.join, 1, 2), (up.pair, 0, 1)],
            5: [(down.join, 2, 3), (up.pair, 1, 2)],
            7: [(down.join, 3, 4), (up.pair, 2, 3)],
            9: [(up.pair, 3, 4)],
            11: [(out.pair, 0, 4), (up.join, 0, 1)],
        }

        def attend(index, carry):
            batch, tile = index // tiles, index % tiles
            attend_back_tile(
                rows.image, rows.has, rows.first, batch, tile, rows.image < counts[batch],
                q_ref, k_ref, v_ref, span, stt_ref, dq_acc, dk_acc, dv_acc,
            )
            for at, actions in work.items():
                @pl.when(index == at)
                def _():
                    for action, first, last in actions:
                        loop(action, first, last)
            return carry

        lax.fori_loop(0, batches * tiles, attend, 0)
        columns = lambda ref: sum(jnp.sum(ref[b].astype(jnp.float32), axis=0, keepdims=True) for b in range(batches))
        sums_ref[0:1] = columns(q_ref)
        sums_ref[1:2] = columns(v_ref)

        def weight_grad(first, end, grads):
            for half in range(2):
                units = slice(half * CHIPS // 2, (half + 1) * CHIPS // 2)
                for batch in range(batches):
                    part = mm(hidden[batch, :, half * HALF : (half + 1) * HALF], grads(batch), TN)
                    if batch == 0:
                        dq_acc[:HALF, : end - first] = part
                    else:
                        dq_acc[:HALF, : end - first] += part
                total = dq_acc[:HALF, : end - first].reshape(CHIPS // 2, ROWS, end - first)
                qkv_ref[units, :, first:end] = total.astype(jnp.bfloat16)

        weight_grad(0, 640, lambda batch: jnp.concatenate([q_ref[batch], k_ref[batch, :, :64]], axis=1))
        weight_grad(640, D, lambda batch: k_ref[batch, :, 64:])
        weight_grad(D, 3 * HALF, lambda batch: v_ref[batch])
        each_turn(qkv.begin)

        def token_grad(batch, others):
            def block(index, carry):
                here = pl.ds(pl.multiple_of(index * TILE, TILE), TILE)
                grads = jnp.concatenate([ref[batch, here] for ref in (q_ref, k_ref, v_ref)], axis=1)
                total = mm(grads, weight[...], NT)
                if others is not None:
                    total = total + others[here].astype(jnp.float32)
                hidden[batch, here] = total.astype(jnp.bfloat16)
                return carry

            lax.fori_loop(0, SPAN // TILE, block, 0)

        core = place[0]
        token_grad(1 - core, None)
        trade = remote(hidden.at[1 - core], arrived, swap_out, swap_in, partner_of(*place))
        trade.start()
        loop(up.join, 1, 2)
        trade.wait_recv()
        token_grad(core, arrived)
        back_sems = (back_token_sems, back_span_sems)
        rows.batch_to_tokens(hidden.at[core], landing, back_sems)
        loop(up.join, 2, 4)
        each_turn(qkv.pair)
        each_turn(out.join)
        each_turn(down.total, 3)
        each_turn(qkv.join)
        each_turn(up.total, 3)
        each_turn(out.total, 3)
        each_turn(qkv.total, 3)
        trade.wait_send()
        rows.batches_arrived(hidden.at[core], landing, back_sems)

    held = lambda *shape: pltpu.VMEM(shape, jnp.bfloat16)
    pl.run_scoped(
        attention, *[held(batches, SPAN, HALF)] * 3, held(batches, SPAN, D), held(D, 3 * HALF)
    )
    for scatter in (down, up, out, qkv):
        scatter.finish()


def backward(counts, query, keys, values, hidden, weight, attended, lse, low, high, down, pairs, collective_id):
    batches = query.shape[0]
    vmem, hbm = pl.BlockSpec(memory_space=pltpu.VMEM), pl.BlockSpec(memory_space=pl.ANY)
    shapes = [down.shape, (CHIPS, ROWS, FFH), (CHIPS, ROWS, HALF), (CHIPS, ROWS, 3 * HALF)]
    held = lambda *shape: pltpu.VMEM(shape, jnp.bfloat16)
    dma = pltpu.SemaphoreType.DMA
    return pl.pallas_call(
        backward_kernel,
        out_shape=[jax.ShapeDtypeStruct((2, HALF), jnp.float32)]
        + [jax.ShapeDtypeStruct((2, batches, SHARD, D), jnp.bfloat16)]
        + [jax.ShapeDtypeStruct(shape[1:], jnp.float32) for shape in shapes],
        in_specs=[pl.BlockSpec(memory_space=pltpu.SMEM)] + [hbm] * 5 + [vmem] * 2 + [hbm] * (3 + len(pairs)),
        out_specs=[vmem, hbm] + [vmem] * 4,
        scratch_shapes=[held(SPAN, D)]
        + [held(*shape) for shape in shapes]
        + [
            pltpu.VMEM((SPAN, HALF + 64), jnp.float32),
            pltpu.VMEM((TILE, HALF), jnp.float32),
            pltpu.VMEM((TILE, HALF), jnp.float32),
            held(batches, SPAN, HALF),
            pltpu.VMEM((batches, 2 * CORE_HEADS, SPAN), jnp.float32),
            dma((8,)),
        ]
        + Rows.scratch() * 2
        + [dma] * 2
        + sum([Scatter.scratch(shape, split) for shape, split in zip(shapes, BACK_SPLITS)], []),
        compiler_params=pltpu.CompilerParams(
            collective_id=collective_id, has_side_effects=True, vmem_limit_bytes=60 * 1024 * 1024
        ),
        cost_estimate=pl.CostEstimate(flops=0, bytes_accessed=500 * 10**6, transcendentals=0),
        name="backward",
    )(counts, query, keys, values, hidden, weight, attended, lse, low, high, down, *pairs)


def chip_unit(core, low, high):
    theirs = swap(by_core(core, high, low))
    return joined(core, by_core(core, low, high), theirs, 0)


def peer(x, y, z, core):
    return (((z * 2 + y) * 2 + x) * 2 + core,)


MESH_ID = pl.DeviceIdType.MESH


def position_of():
    device = lax.axis_index("dev")
    return device % 2, device // 2 % 2, device // 4 % 2, device // 8


def greet(targets):
    barrier = pltpu.get_barrier_semaphore()
    count = 0
    for target, there in targets:
        if there is True:
            pl.semaphore_signal(barrier, inc=1, device_id=target, device_id_type=MESH_ID)
            count = count + 1
        else:
            @pl.when(there)
            def _():
                pl.semaphore_signal(barrier, inc=1, device_id=target, device_id_type=MESH_ID)
            count = count + there.astype(jnp.int32)
    pl.semaphore_wait(barrier, count)


def pair_peers(core, x, y, z):
    return [(peer(1 - x, y, z, core), True), (peer(x, 1 - y, z, core), True)]


def next_peers(core, x, y, z):
    return [(peer(x, y, z - 1, core), z > 0), (peer(x, y, z + 1, core), z < 3)]


def line_peers(core, x, y, z):
    return [(peer(x, y, (z + step) % 4, core), True) for step in (1, 2, 3)]


def partner_of(core, x, y, z):
    return peer(x, y, z, 1 - core)


class Gather:
    def __init__(self, place, unit_ref, full_ref, other_ref, split, sems):
        self.core, self.x, self.y, self.z = place
        self.unit_ref, self.full_ref, self.other_ref, self.split = unit_ref, full_ref, other_ref, split
        (
            self.z_out,
            self.z_in,
            self.pair_out,
            self.pair_in,
            self.half_out,
            self.half_in,
            self.chain_out,
            self.chain_in,
            self.own_sem,
        ) = sems[:9]
        if other_ref is not None:
            self.swap_out, self.swap_in = sems[9:]
        self.sides = ((-1, self.z > 0), (1, self.z < 3))
        self.x_peer = peer(1 - self.x, self.y, self.z, self.core)
        self.y_peer = peer(self.x, 1 - self.y, self.z, self.core)

    @staticmethod
    def scratch(partner):
        dma = pltpu.SemaphoreType.DMA
        shapes = [(2, 4), (4,), (2, 4), (2, 4), (2, 4), (2, 4), (2, 4), (4,)]
        return [dma(shape) for shape in shapes] + [dma] + ([dma((CHIPS,))] * 2 if partner else [])

    def unit_index(self, at_x, at_y, at_z):
        return (at_z * 2 + at_y) * 2 + at_x

    def slot(self, at_x, at_y, at_z):
        return self.full_ref.at[self.unit_index(at_x, at_y, at_z)]

    def column(self, turn, at_z):
        at_x, at_y = [(self.x, self.y), (self.x, 1 - self.y), (1 - self.x, self.y), (1 - self.x, 1 - self.y)][turn]
        return self.slot(at_x, at_y, at_z)

    def copy(self, block, send_sem, recv_sem, target, source=None):
        return pltpu.make_async_remote_copy(
            src_ref=block if source is None else source,
            dst_ref=block,
            send_sem=send_sem,
            recv_sem=recv_sem,
            device_id=target,
            device_id_type=MESH_ID,
        )

    def along(self, at_z, side, source=None):
        index = 0 if side < 0 else 1
        target = peer(self.x, self.y, self.z + side, self.core)
        return self.copy(self.column(0, at_z), self.z_out.at[index, at_z], self.z_in.at[at_z], target, source)

    def chain(self, at_z, side):
        index = 0 if side < 0 else 1
        target = peer(self.x, self.y, self.z + side, self.core)
        return self.copy(self.column(3, at_z), self.chain_out.at[index, at_z], self.chain_in.at[at_z], target)

    def whole(self, at_z, axis, source=None):
        target = (self.x_peer, self.y_peer)[axis]
        return self.copy(self.column(0, at_z), self.pair_out.at[axis, at_z], self.pair_in.at[axis, at_z], target, source)

    def part(self, block, axis):
        width = self.full_ref.shape[2]
        return block.at[:, pl.ds(0, self.split) if axis == 0 else pl.ds(self.split, width - self.split)]

    def half(self, at_z, axis):
        block = self.part(self.column(1 + axis, at_z), axis)
        target = (self.x_peer, self.y_peer)[axis]
        return self.copy(block, self.half_out.at[axis, at_z], self.half_in.at[axis, at_z], target)

    def half_arrival(self, at_z, axis):
        block = self.part(self.column(3, at_z), axis)
        return self.copy(block, self.half_out.at[axis, at_z], self.half_in.at[axis, at_z], self.x_peer)

    def by_halves(self, at_z):
        near = jnp.logical_and(jnp.abs(at_z - self.z) == 1, jnp.logical_or(at_z == 1, at_z == 2))
        return jnp.logical_or(at_z == self.z, near)

    def trade(self, turn, at_z, source=None):
        at_x, at_y = [(self.x, self.y), (self.x, 1 - self.y), (1 - self.x, self.y), (1 - self.x, 1 - self.y)][turn]
        index = self.unit_index(at_x, at_y, at_z)
        block = self.full_ref.at[index] if source is None else source
        width = self.other_ref.shape[2]
        if width < self.full_ref.shape[2]:
            block = block.at[:, pl.ds(0, width)]
        return pltpu.make_async_remote_copy(
            src_ref=block,
            dst_ref=self.other_ref.at[index],
            send_sem=self.swap_out.at[index],
            recv_sem=self.swap_in.at[index],
            device_id=peer(self.x, self.y, self.z, 1 - self.core),
            device_id_type=MESH_ID,
        )

    def share(self, turn, at_z, source=None):
        if self.other_ref is not None:
            self.trade(turn, at_z, source).start()

    def each(self, distance, action):
        if distance == 0:
            action(self.z, 0)
            return
        for side in (-1, 1):
            at_z = self.z + side * distance
            @pl.when(jnp.logical_and(at_z >= 0, at_z <= 3))
            def _():
                action(at_z, side)

    def onwards(self, side, action):
        for to, there in self.sides:
            if side == 0 or to == -side:
                @pl.when(there)
                def _():
                    action(to)

    def arrive(self, at_z, side):
        source = None
        if side == 0:
            source = self.unit_ref
            pltpu.make_async_copy(self.unit_ref, self.column(0, at_z), self.own_sem).start()
        else:
            self.along(at_z, side).wait_recv()
        self.onwards(side, lambda to: self.along(at_z, to, source).start())
        self.whole(at_z, 0, source).start()
        self.whole(at_z, 1, source).start()
        self.share(0, at_z, source)

    def cross(self, at_z, side):
        for axis in (1, 0):
            arrived = self.column(2 - axis, at_z)
            self.copy(arrived, self.pair_out.at[axis, at_z], self.pair_in.at[axis, at_z], self.x_peer).wait_recv()
            @pl.when(self.by_halves(at_z))
            def _():
                self.half(at_z, 1 - axis).start()
            self.share(2 - axis, at_z)

    def far_chain(self, at_z, side):
        return jnp.logical_or(at_z == 0, at_z == 3) if side == 0 else True

    def diagonal(self, at_z, side):
        halves = self.by_halves(at_z)
        @pl.when(halves)
        def _():
            self.half_arrival(at_z, 0).wait_recv()
            self.half_arrival(at_z, 1).wait_recv()
        if side != 0:
            @pl.when(jnp.logical_not(halves))
            def _():
                self.chain(at_z, side).wait_recv()
        @pl.when(self.far_chain(at_z, side))
        def _():
            self.onwards(side, lambda to: self.chain(at_z, to).start())
        self.share(3, at_z)

    def steps(self):
        order = [
            (0, self.arrive),
            (1, self.arrive),
            (0, self.cross),
            (2, self.arrive),
            (0, self.diagonal),
            (1, self.cross),
            (3, self.arrive),
            (1, self.diagonal),
            (2, self.cross),
            (2, self.diagonal),
            (3, self.cross),
            (3, self.diagonal),
        ]
        return [partial(self.each, distance, action) for distance, action in order]

    def settle(self, at_z, side):
        self.onwards(side, lambda to: self.along(at_z, to).wait_send())
        @pl.when(self.far_chain(at_z, side))
        def _():
            self.onwards(side, lambda to: self.chain(at_z, to).wait_send())
        for axis in range(2):
            self.whole(at_z, axis).wait_send()
            @pl.when(self.by_halves(at_z))
            def _():
                self.half(at_z, axis).wait_send()

    def own_ready(self):
        pltpu.make_async_copy(self.unit_ref, self.column(0, self.z), self.own_sem).wait()

    def finish(self):
        for distance in range(4):
            self.each(distance, self.settle)
        if self.other_ref is not None:
            def traded(at_z, carry):
                for turn in range(4):
                    self.trade(turn, at_z).wait()
                return carry

            lax.fori_loop(0, 4, traded, 0)


def remote(source, target, send_sem, recv_sem, device):
    return pltpu.make_async_remote_copy(
        src_ref=source,
        dst_ref=target,
        send_sem=send_sem,
        recv_sem=recv_sem,
        device_id=device,
        device_id_type=MESH_ID,
    )


PADDED = 80
WIDE = CHIPS * PADDED
SHARE = 423


def vector_part(full_ref, start, length, width):
    lane = lax.broadcasted_iota(jnp.int32, (1, width), 1)
    total = jnp.zeros((1, width), jnp.float32)
    for device in range(start // SHARE, (start + length - 1) // SHARE + 1):
        base = 512 * (device % 2)
        tile = full_ref[device // 2, PADDED - 16 :, base : base + 512].astype(jnp.float32)
        row = tile[ROWS - PADDED + 16 : ROWS - PADDED + 17]
        if width > 512:
            row = jnp.concatenate([row, jnp.zeros((1, width - 512), jnp.float32)], axis=1)
        shift = device * SHARE - start
        row = pltpu.roll(row, shift % width, 1) if shift % width else row
        first, last = max(shift, 0), min(shift + SHARE, length)
        total = total + jnp.where((lane >= first) & (lane < last), row, 0.0)
    return total


FIRST_STEPS = (
    (0, 0), (3, 0), (0, 1), (0, 2), (3, 1), (0, 3), (0, 4), (0, 5), (0, 6), (3, 2), (0, 7), (0, 8), (0, 9), (0, 10), (0, 11),
    (1, 0), (2, 0),
)
PROJECT_STEPS = ((0, 0, 1, 2), (1, 0, 2, 3), (2, 1, 1, 2), (3, 0, 3, 4), (4, 1, 2, 3), (5, 0, 4, 6))
ATTEND_STEPS = (
    (1, 1, 3, 4), (3, 0, 6, 7), (5, 1, 4, 5), (6, 0, 7, 8), (7, 1, 5, 6), (8, 0, 8, 9), (9, 1, 6, 7), (10, 0, 9, 10), (11, 1, 7, 8),
)
LAST_STEPS = ((0, 10, 12), (1, 8, 12))


def forward_kernel(
    splits, counts, unit, up_unit, down_unit, tokens_ref, pad_ref,
    q_out, k_out, v_out, hidden_out, att_out, lse_out, full_out, landing, up_ref, up_other, down_ref, down_other,
    q_ref, k_ref, v_ref, hidden_ref, att_ref, lse_ref, full_ref, store_sems, span, padded, acc, token_sems, span_sems, trade_out, trade_in, back_token_sems, back_span_sems, *sems
):
    place = position_of()
    rows = Rows(place)
    greet(pair_peers(*place) + next_peers(*place) + [(partner_of(*place), True)] + rows.peers())
    plain, more = len(Gather.scratch(False)), len(Gather.scratch(True))
    first = Gather(place, unit, full_ref, None, splits[0], sems[:plain])
    second = Gather(place, up_unit, up_ref, up_other, splits[1], sems[plain : plain + more])
    third = Gather(place, down_unit, down_ref, down_other, splits[2], sems[plain + more :])
    held = (q_ref, k_ref, v_ref, hidden_ref, att_ref, lse_ref, full_ref)
    outs = (q_out, k_out, v_out, hidden_out, att_out, lse_out, full_out)
    stores = [pltpu.make_async_copy(a, b, store_sems.at[n]) for n, (a, b) in enumerate(zip(held, outs))]
    one, two, three = first.steps(), second.steps(), third.steps()
    row_sems = (token_sems, span_sems, trade_out, trade_in)

    def run(steps, start, stop):
        for step in steps[start:stop]:
            step()

    row_steps = (
        partial(rows.to_both, tokens_ref, span, row_sems),
        partial(rows.relay, span, row_sems),
        partial(rows.both_arrived, tokens_ref, span, row_sems),
    )

    def start(table):
        for which, step in table:
            if which == 3:
                row_steps[step]()
            else:
                run((one, two, three)[which], step, step + 1)

    start(FIRST_STEPS)
    first.own_ready()
    stores[6].start()
    batches = tokens_ref.shape[0]
    gain, bias = vector_part(full_ref, 0, D, WIDE)[:, :D], vector_part(full_ref, D, D, WIDE)[:, :D]
    core = place[0]
    half = lambda start: jnp.where(
        core == 0, vector_part(full_ref, start, HALF, 1024), vector_part(full_ref, start + HALF, HALF, 1024)
    )[:, :HALF]
    query_bias, value_bias = half(2 * D), half(3 * D)
    block = 256

    def between(table, index):
        for at, steps, begin, stop in table:
            @pl.when(index == at)
            def _():
                run((two, three)[steps], begin, stop)

    def project(index, carry):
        batch, at = index // (SPAN // block), index % (SPAN // block)
        here = pl.ds(pl.multiple_of(at * block, block), block)
        token = rows.first * CHUNK + at * block + lax.broadcasted_iota(jnp.int32, (block, 1), 0)
        there = (token >= rows.image * IMG_LEN) & (token < jnp.minimum((rows.image + 1) * IMG_LEN, TOKENS)) & rows.has
        value = jnp.where(there, span[batch, here], 0).astype(jnp.float32)
        centered = value - jnp.mean(value, axis=1, keepdims=True)
        inverse = lax.rsqrt(jnp.mean(centered * centered, axis=1, keepdims=True) + EPSILON)
        hidden = (centered * inverse * gain + bias).astype(jnp.bfloat16)
        hidden_ref[batch, here] = hidden
        padded[...] = mm(hidden, pad_ref[...], NN).astype(jnp.bfloat16)
        wide = mm(padded[...], full_ref[:, :, :D].reshape(WIDE, D), NN)
        q_ref[batch, here] = (wide[:, :HALF] + query_bias).astype(jnp.bfloat16)
        k_ref[batch, here] = wide[:, HALF:].astype(jnp.bfloat16)
        wide = mm(padded[...], full_ref[:, :, D:].reshape(WIDE, HALF), NN)
        v_ref[batch, here] = (wide + value_bias).astype(jnp.bfloat16)
        between(PROJECT_STEPS, index)
        return carry

    lax.fori_loop(0, batches * (SPAN // block), project, 0)
    for store in stores[:4]:
        store.start()
    tiles = SPAN // TILE

    def attend(index, carry):
        batch, tile = index // tiles, index % tiles
        attend_tile(
            rows.image, rows.has, rows.first, batch, tile, rows.image < counts[batch],
            q_ref, k_ref, v_ref, att_ref, lse_ref, acc,
        )
        between(ATTEND_STEPS, index)
        return carry

    lax.fori_loop(0, batches * tiles, attend, 0)
    for store in stores[4:6]:
        store.start()
    back_sems = (back_token_sems, back_span_sems)
    rows.to_tokens(att_ref, landing, back_sems)
    for steps, begin, stop in LAST_STEPS:
        run((two, three)[steps], begin, stop)
    rows.tokens_arrived(att_ref, landing, back_sems)
    second.own_ready()
    third.own_ready()
    for store in stores:
        store.wait()
    for gather in (first, second, third):
        gather.finish()


def forward(counts, unit, up_unit, down_unit, tokens, collective_id):
    batches = tokens.shape[0]
    full = lambda unit: jax.ShapeDtypeStruct((CHIPS,) + unit.shape, unit.dtype)
    low = lambda *shape: jax.ShapeDtypeStruct(shape, jnp.bfloat16)
    vmem, hbm = pl.BlockSpec(memory_space=pltpu.VMEM), pl.BlockSpec(memory_space=pl.ANY)
    dma = pltpu.SemaphoreType.DMA
    feature, lane = np.arange(D)[:, None], np.arange(WIDE)[None]
    pad = jnp.asarray(feature // ROWS * PADDED + feature % ROWS == lane, jnp.bfloat16)
    spans = [(batches, SPAN, HALF)] * 3 + [(batches, SPAN, D), (batches, SPAN, HALF)]
    outs = pl.pallas_call(
        partial(forward_kernel, (512, 896, 384)),
        out_shape=[low(*shape) for shape in spans]
        + [
            jax.ShapeDtypeStruct((batches, SPAN, 128), jnp.float32),
            full(unit),
            low(2, 2, batches, SHARD, HALF),
            full(up_unit),
            full(up_unit),
            full(down_unit),
            full(down_unit),
        ],
        in_specs=[pl.BlockSpec(memory_space=pltpu.SMEM)] + [vmem] * 5,
        out_specs=[hbm] * 7 + [vmem] + [hbm] * 4,
        scratch_shapes=[pltpu.VMEM(shape, jnp.bfloat16) for shape in spans]
        + [
            pltpu.VMEM((batches, SPAN, 128), jnp.float32),
            pltpu.VMEM((CHIPS,) + unit.shape, unit.dtype),
            dma((7,)),
            pltpu.VMEM((batches, SPAN, D), jnp.bfloat16),
            pltpu.VMEM((256, WIDE), jnp.bfloat16),
            pltpu.VMEM((TILE, HALF), jnp.float32),
        ]
        + Rows.scratch()
        + [dma((SPAN_CHUNKS,)), dma((SPAN_CHUNKS,))]
        + Rows.scratch()
        + Gather.scratch(False)
        + Gather.scratch(True) * 2,
        compiler_params=pltpu.CompilerParams(
            collective_id=collective_id, has_side_effects=True, vmem_limit_bytes=60 * 1024 * 1024
        ),
        cost_estimate=pl.CostEstimate(flops=0, bytes_accessed=500 * 10**6, transcendentals=0),
        name="forward",
    )(counts, unit, up_unit, down_unit, tokens, pad)
    return list(outs[:8]) + [w.reshape(-1, w.shape[2]) for w in outs[8:]]


def vector_kernel(sent_ref, total_ref, arrived, send_sems, recv_sems):
    device = lax.axis_index("dev")
    devices = 2 * CHIPS
    mesh_id = pl.DeviceIdType.MESH
    barrier = pltpu.get_barrier_semaphore()

    def greet(step, carry):
        pl.semaphore_signal(
            barrier, inc=1, device_id=(lax.rem(device + step, devices),), device_id_type=mesh_id
        )
        return carry

    lax.fori_loop(1, devices, greet, 0)
    pl.semaphore_wait(barrier, devices - 1)

    def copy(step):
        target = lax.rem(device + step, devices)
        return pltpu.make_async_remote_copy(
            src_ref=sent_ref.at[target],
            dst_ref=arrived.at[step],
            send_sem=send_sems.at[step],
            recv_sem=recv_sems.at[step],
            device_id=(target,),
            device_id_type=mesh_id,
        )

    def start(step, carry):
        copy(step).start()
        return carry

    lax.fori_loop(1, devices, start, 0)

    def add(step, total):
        copy(step).wait()
        return total + arrived[step]

    total_ref[...] = lax.fori_loop(1, devices, add, sent_ref[device])


def scatter_vector(vector, share, collective_id):
    rows = jnp.pad(vector.reshape(2 * CHIPS, share), ((0, 0), (0, 1024 - share)))
    dma = pltpu.SemaphoreType.DMA
    total = pl.pallas_call(
        vector_kernel,
        out_shape=jax.ShapeDtypeStruct((8, 128), jnp.float32),
        in_specs=[pl.BlockSpec(memory_space=pltpu.VMEM)],
        out_specs=pl.BlockSpec(memory_space=pltpu.VMEM),
        scratch_shapes=[
            pltpu.VMEM((2 * CHIPS, 8, 128), jnp.float32),
            dma((2 * CHIPS,)),
            dma((2 * CHIPS,)),
        ],
        compiler_params=pltpu.CompilerParams(collective_id=collective_id, has_side_effects=True),
        cost_estimate=pl.CostEstimate(flops=0, bytes_accessed=20 * 10**6, transcendentals=0),
        name="scatter_vector",
    )(rows.reshape(2 * CHIPS, 8, 128))
    return total.reshape(-1)[:share]


def later_image(device):
    start = device * SHARD
    at = start + lax.broadcasted_iota(jnp.int32, (SHARD, 1), 0)
    return at >= (start // IMG_LEN + 1) * IMG_LEN


MLP_ROWS = SHARD
GELU_A, GELU_B = 0.7978845608028654, 0.044715


def mlp_kernel(
    x_ref, landing, g_ref, up_a, up_b, down_a, down_b, vec_ref, bias_ref,
    att_ref, result_ref, act_a, act_b, gu_a, gu_b, h2_ref, gb_a, gb_b, gm_ref, go_a, go_b, sums_ref, bias_sums_ref,
    wo_a, wo_b, up_w, down_w, slope, sems,
):
    loads = [
        pltpu.make_async_copy(source, target, sems.at[n])
        for n, (source, target) in enumerate(
            [
                (up_a.at[:, pl.ds(0, FFH)], up_w.at[0]),
                (up_b.at[:, pl.ds(0, FFH)], up_w.at[1]),
                (down_a, down_w.at[0]),
                (down_b, down_w.at[1]),
                (up_a.at[:, pl.ds(FFH, HALF)], wo_a),
                (up_b.at[:, pl.ds(FFH, HALF)], wo_b),
            ]
        )
    ]
    for load in loads[4:] + loads[:4]:
        load.start()
    sums_ref[...] = jnp.zeros_like(sums_ref)
    bias_sums_ref[...] = jnp.zeros_like(bias_sums_ref)
    acts, grads_up = (act_a, act_b), (gu_a, gu_b)
    device = lax.axis_index("dev")
    core = device % 2
    later = later_image(device)
    mean = lambda value: jnp.mean(value, axis=1, keepdims=True)

    def tile(index, carry):
        rows = pl.ds(pl.multiple_of(index * MLP_ROWS, MLP_ROWS), MLP_ROWS)

        def ready(load):
            @pl.when(index == 0)
            def _():
                load.wait()

        ready(loads[4])
        ready(loads[5])
        atts = [jnp.where(later, landing[1, side, index], landing[0, side, index]) for side in range(2)]
        att_ref[rows] = jnp.concatenate(atts, axis=1)
        sides = [mm(atts[0], wo[:HALF], NN) + mm(atts[1], wo[HALF:], NN) for wo in (wo_a, wo_b)]
        branch = jnp.where(core == 0, jnp.concatenate(sides, axis=1), jnp.concatenate(sides[::-1], axis=1))
        middle = x_ref[rows].astype(jnp.float32) + (branch + vec_ref[0:1])
        centered = middle - mean(middle)
        inverse = lax.rsqrt(mean(centered * centered) + EPSILON)
        normed = centered * inverse
        gain = vec_ref[1:2]
        hidden = (normed * gain + vec_ref[2:3]).astype(jnp.bfloat16)
        h2_ref[rows] = hidden
        for half in range(2):
            ready(loads[half])
            upper = mm(hidden, up_w[half], NN) + bias_ref[half : half + 1]
            square = upper * upper
            tanh = jnp.tanh(GELU_A * (upper + GELU_B * (square * upper)))
            acts[half][rows] = (0.5 * upper * (1.0 + tanh)).astype(jnp.bfloat16)
            slope[half] = 0.5 * (1.0 + tanh) + (0.5 * GELU_A) * upper * (1.0 - tanh * tanh) * (
                1.0 + (3.0 * GELU_B) * square
            )
        for half in range(2):
            ready(loads[2 + half])
        lower = mm(act_a[rows], down_w[0], NN) + mm(act_b[rows], down_w[1], NN)
        result_ref[rows] = (middle + (lower + vec_ref[3:4])).astype(jnp.bfloat16)
        grad = g_ref[rows]
        for half in range(2):
            grad_upper = (mm(grad, down_w[half], NT) * slope[half]).astype(jnp.bfloat16)
            grads_up[half][rows] = grad_upper
            bias_sums_ref[half : half + 1] += jnp.sum(grad_upper.astype(jnp.float32), axis=0, keepdims=True)
        grad_hidden = mm(gu_a[rows], up_w[0], NT) + mm(gu_b[rows], up_w[1], NT)
        scaled = grad_hidden * gain
        wide = grad.astype(jnp.float32)
        grad_middle = wide + inverse * (scaled - mean(scaled) - normed * mean(scaled * normed))
        gm_ref[rows] = grad_middle
        branch = grad_middle.astype(jnp.bfloat16)
        low, high = branch[:, :HALF], branch[:, HALF:]
        branches = jnp.where(core == 0, low, high), jnp.where(core == 0, high, low)
        gb_a[rows], gb_b[rows] = branches
        for go_ref, heads in ((go_a, slice(0, HALF)), (go_b, slice(HALF, D))):
            total = mm(branches[0], wo_a[heads], NT) + mm(branches[1], wo_b[heads], NT)
            go_ref[rows] = total.astype(jnp.bfloat16)
        for n, value in enumerate([branch.astype(jnp.float32), grad_hidden * normed, grad_hidden, wide]):
            sums_ref[n : n + 1] += jnp.sum(value, axis=0, keepdims=True)
        return carry

    lax.fori_loop(0, x_ref.shape[0] // MLP_ROWS, tile, 0)


def mlp(x, landing, grad, ups, downs, vecs, biases):
    rows = x.shape[0]
    vmem, hbm = pl.BlockSpec(memory_space=pltpu.VMEM), pl.BlockSpec(memory_space=pl.ANY)
    low = lambda width: jax.ShapeDtypeStruct((rows, width), jnp.bfloat16)
    wide = lambda *shape: jax.ShapeDtypeStruct(shape, jnp.float32)
    return pl.pallas_call(
        mlp_kernel,
        out_shape=[low(D), low(D)] + [low(FFH)] * 4 + [low(D), low(HALF), low(HALF), wide(rows, D), low(HALF), low(HALF), wide(8, D), wide(8, FFH)],
        in_specs=[vmem] * 3 + [hbm] * 4 + [vmem] * 2,
        out_specs=[vmem] * 14,
        scratch_shapes=[
            pltpu.VMEM((D, HALF), jnp.bfloat16),
            pltpu.VMEM((D, HALF), jnp.bfloat16),
            pltpu.VMEM((2, D, FFH), jnp.bfloat16),
            pltpu.VMEM((2, FFH, D), jnp.bfloat16),
            pltpu.VMEM((2, MLP_ROWS, FFH), jnp.float32),
            pltpu.SemaphoreType.DMA((6,)),
        ],
        compiler_params=pltpu.CompilerParams(vmem_limit_bytes=62 * 1024 * 1024),
        cost_estimate=pl.CostEstimate(flops=0, bytes_accessed=130 * 10**6, transcendentals=0),
        name="mlp",
    )(x, landing, grad, *ups, *downs, vecs, biases)


def topo_local(tokens, counts, qkv_weight, out_weight, up_weight, down_weight, vectors, cotangent):
    device = lax.axis_index("dev")
    core, chip = device % 2, device // 2
    batches = tokens.shape[0]
    share = vectors.shape[0]
    own_rows = batches * SHARD

    qkv36 = qkv_weight.reshape(ROWS // 2, 3 * D)
    out36 = out_weight.reshape(ROWS // 2, D)
    side_qkv = [
        jnp.concatenate([qkv36[:, s * HALF + j * D :][:, :HALF] for j in range(3)], axis=1) for s in range(2)
    ]
    side_out = [out36[:, s * HALF :][:, :HALF] for s in range(2)]
    up36 = up_weight.reshape(ROWS // 2, CHIPS, UNIT)
    up_low = up36[:, :, :UNIT_HALF].reshape(ROWS // 2, FFH)
    filler = UNIT_SECOND + UNIT_HALF - UNIT
    up_high = jnp.pad(up36[:, :, UNIT_SECOND:], ((0, 0), (0, 0), (0, filler))).reshape(ROWS // 2, FFH)
    spill = UNIT_HALF * D - down_weight.shape[0]
    borrowed = lax.ppermute(
        down_weight[:spill], "dev", [(i + 1, i) for i in range(0, 2 * CHIPS, 2)]
    )
    down_unit = by_core(
        core,
        jnp.concatenate([down_weight, borrowed]),
        jnp.pad(down_weight[spill:], ((UNIT_HALF - UNIT_SECOND) * D, filler * D)),
    ).reshape(UNIT_HALF, D)
    first_unit = chip_unit(
        core,
        jnp.concatenate([side_qkv[0], side_out[0], up_low], axis=1),
        jnp.concatenate([side_qkv[1], side_out[1], up_high], axis=1),
    )
    shares = jnp.pad(vectors, (0, 512 - share)).reshape(1, 512)
    shares = joined(core, shares, swap(shares), 0).reshape(1, 1024)
    extra = jnp.pad(shares, ((0, 7), (0, 3 * HALF - 1024)))
    up_unit = jnp.concatenate([first_unit[:, 4 * HALF :], first_unit[:, 3 * HALF : 4 * HALF]], axis=1)
    (
        query, keys, values, hidden_one, attended, log_sums, full, landing, up_mine, up_theirs, down_mine, down_theirs
    ) = forward(counts, jnp.concatenate([first_unit[:, : 3 * HALF], extra], axis=0), up_unit, down_unit, tokens, 1)
    qkv_w = full[:, :ROWS].reshape(D, 3 * HALF)
    packed = full[:, ROWS, :1024].reshape(2 * CHIPS, 512)[:, :share].reshape(-1).astype(jnp.float32)
    pieces = [packed[segment * D : (segment + 1) * D] for segment in range(8)]
    bias_units = packed[8 * D : 8 * D + FF].reshape(CHIPS, UNIT)
    bias_low = bias_units[:, :UNIT_HALF].reshape(-1)
    bias_high = jnp.pad(bias_units[:, UNIT_SECOND:], ((0, 0), (0, filler))).reshape(-1)
    up_bias_mine = by_core(core, bias_low, bias_high)
    up_bias_theirs = by_core(core, bias_high, bias_low)
    def dot_tn(left, right):
        return lax.dot_general(left, right, (((0,), (0,)), ((), ())), preferred_element_type=jnp.float32)

    inputs = tokens.reshape(own_rows, D).astype(jnp.float32)
    grad_output = cotangent.reshape(own_rows, D)
    eight = lambda rows: jnp.pad(jnp.stack(rows), ((0, 8 - len(rows)), (0, 0)))
    (
        att_own, result, active_mine, active_theirs, grad_upper_mine, grad_upper_theirs,
        hidden_two, branch_mine, branch_theirs, grad_middle, heads_low, heads_high, vec_sums, bias_sums,
    ) = mlp(
        tokens.reshape(own_rows, D), landing, grad_output, (up_mine, up_theirs), (down_mine, down_theirs),
        eight([pieces[4], pieces[5], pieces[6], pieces[7]]), eight([up_bias_mine, up_bias_theirs]),
    )

    pair = lambda mine, theirs: jnp.concatenate([mine, swap(theirs)], axis=0)
    grad_down = dot_tn(pair(active_mine, active_theirs), pair(grad_output, grad_output)).astype(jnp.bfloat16)
    both = lambda mine, theirs: [mine, swap(theirs)]
    pairs = (
        both(hidden_two, hidden_two) + both(grad_upper_mine, grad_upper_theirs) + both(att_own, att_own)
        + both(branch_mine, branch_theirs)
    )
    head_sums, landing, down_total, up_total, out_total, qkv_total = backward(
        counts, query, keys, values, hidden_one, qkv_w, attended, log_sums,
        heads_low.reshape(batches, SHARD, HALF), heads_high.reshape(batches, SHARD, HALF),
        grad_down.reshape(CHIPS, UNIT_HALF, D), pairs, 4,
    )
    attention_total = jnp.concatenate([qkv_total, out_total], axis=1)
    later = later_image(device)[None]
    grad_hidden_one = jnp.where(later, landing[1], landing[0]).astype(jnp.float32).reshape(own_rows, D)
    normed_one, inverse_one = layer_stats(inputs)
    grad_input = grad_middle + layer_back(grad_hidden_one, normed_one, inverse_one, pieces[0])

    sums = lambda values: jnp.sum(values.astype(jnp.float32), axis=0)
    at_heads = lambda vector: lax.dynamic_update_slice_in_dim(
        jnp.zeros((D,), jnp.float32), vector, core * HALF, 0
    )
    bias_mine, bias_theirs = bias_sums[0], bias_sums[1]
    bias_low = by_core(core, bias_mine, bias_theirs).reshape(CHIPS, UNIT_HALF)
    bias_high = by_core(core, bias_theirs, bias_mine).reshape(CHIPS, UNIT_HALF)
    rest = slice(UNIT_HALF - UNIT_SECOND, UNIT - UNIT_SECOND)
    grad_up_bias = jnp.concatenate([bias_low, bias_high[:, rest]], axis=1).reshape(-1)
    vector_grad = jnp.concatenate(
        [
            sums(grad_hidden_one * normed_one),
            sums(grad_hidden_one),
            at_heads(head_sums[0]),
            at_heads(head_sums[1]),
            *(vec_sums[n] for n in range(4)),
            grad_up_bias,
            jnp.zeros((32 * share - 8 * D - FF,), jnp.float32),
        ]
    )
    vector_grad = scatter_vector(vector_grad, share, 2)

    half_rows = ROWS // 2

    def whole_rows(total):
        kept = by_core(core, total[:half_rows], total[half_rows:])
        theirs = swap(by_core(core, total[half_rows:], total[:half_rows]))
        return by_core(core, kept, theirs), by_core(core, theirs, kept)

    low, high = whole_rows(attention_total)
    columns = [
        jnp.concatenate([low[:, j * HALF : (j + 1) * HALF], high[:, j * HALF : (j + 1) * HALF]], axis=1)
        for j in range(4)
    ]
    qkv_grad = jnp.concatenate(columns[:3], axis=1).reshape(-1)
    out_grad = columns[3].reshape(-1)
    low, high = whole_rows(up_total)
    up_grad = jnp.concatenate(
        [
            low.reshape(half_rows, CHIPS, UNIT_HALF),
            high.reshape(half_rows, CHIPS, UNIT_HALF)[:, :, rest],
        ],
        axis=2,
    ).reshape(-1)
    down_flat = down_total.reshape(-1)
    size, lead = down_weight.shape[0], down_weight.shape[0] - UNIT_SECOND * D
    down_grad = by_core(core, down_flat[:size], down_flat[lead : lead + size])
    return (
        result.reshape(tokens.shape),
        grad_input.astype(jnp.bfloat16).reshape(tokens.shape),
        qkv_grad,
        out_grad,
        up_grad,
        down_grad,
        vector_grad,
    )


def solution(mesh):
    local = topo_local if mesh.shape["dev"] == 32 else generic_local
    return jax.shard_map(
        local,
        mesh=mesh,
        in_specs=(
            P(None, "dev", None),
            P(),
            P("dev"),
            P("dev"),
            P("dev"),
            P("dev"),
            P("dev"),
            P(None, "dev", None),
        ),
        out_specs=(
            P(None, "dev", None),
            P(None, "dev", None),
            P("dev"),
            P("dev"),
            P("dev"),
            P("dev"),
            P("dev"),
        ),
        check_vma=False,
    )
```

```python
from functools import partial

import jax
import jax.numpy as jnp
import numpy as np
from jax import lax
from jax.experimental import pallas as pl
from jax.experimental.pallas import tpu as pltpu
from jax.sharding import PartitionSpec as P

D = 1152
HEADS = 16
FF = 4304
IMG_LEN = 729


heads_per_block = 4
EPSILON = 1e-06
MASKED = -1e30


def passed_along(block, axis, distance):
    devices = range(lax.axis_size(axis))
    route = [(i - distance, i) for i in devices if i - distance in devices]
    return lax.ppermute(block, axis, route)


def layer_stats(values):
    centered = values - jnp.mean(values, axis=-1, keepdims=True)
    inverse = lax.rsqrt(jnp.mean(centered * centered, axis=-1, keepdims=True) + EPSILON)
    return (centered * inverse, inverse)


def layer_back(grad_output, normed, inverse, gain):
    scaled = grad_output * gain
    return inverse * (
        scaled
        - jnp.mean(scaled, axis=-1, keepdims=True)
        - normed * jnp.mean(scaled * normed, axis=-1, keepdims=True)
    )


def image_of(positions, image_count):
    return jnp.where(positions < image_count * IMG_LEN, positions // IMG_LEN, -positions - 1)


def reach_sizes(shard_rows):
    rim_rows = IMG_LEN - 1
    reach_count = (rim_rows + shard_rows - 1) // shard_rows
    return [
        min(shard_rows, rim_rows - (distance - 1) * shard_rows)
        for distance in range(1, reach_count + 1)
    ]


def widen(key_value, shard_rows):
    edge_sizes = reach_sizes(shard_rows)
    arrived = {}
    for distance, amount in enumerate(edge_sizes, start=1):
        for direction in (1, -1):
            sent_rows = key_value[shard_rows - amount :] if direction > 0 else key_value[:amount]
            arrived[distance, direction] = passed_along(sent_rows, "dev", direction * distance)
    before = [arrived[distance, 1] for distance in range(len(edge_sizes), 0, -1)]
    after = [arrived[distance, -1] for distance in range(1, len(edge_sizes) + 1)]
    return jnp.concatenate(before + [key_value] + after, axis=0)


def return_edges(grad_extended, shard_rows):
    edge_sizes = reach_sizes(shard_rows)
    rim_rows = IMG_LEN - 1
    combined = grad_extended[rim_rows : rim_rows + shard_rows]
    for distance, amount in enumerate(edge_sizes, start=1):
        for direction in (1, -1):
            if direction > 0:
                begin_row = rim_rows - sum(edge_sizes[:distance])
            else:
                begin_row = rim_rows + shard_rows + sum(edge_sizes[: distance - 1])
            arrived = passed_along(
                grad_extended[begin_row : begin_row + amount].astype(jnp.bfloat16),
                "dev",
                -direction * distance,
            ).astype(jnp.float32)
            if direction > 0:
                combined = combined.at[shard_rows - amount :].add(arrived)
            else:
                combined = combined.at[:amount].add(arrived)
    return combined


def key_window(device_index, shard_rows, image_count):
    span_rows = ((shard_rows + IMG_LEN - 2) // IMG_LEN + 1) * IMG_LEN
    shard_start = device_index * shard_rows
    window_start = shard_start // IMG_LEN * IMG_LEN
    offset_rows = window_start - shard_start + IMG_LEN - 1
    query_images = image_of(shard_start + jnp.arange(shard_rows, dtype=jnp.int32), image_count)
    key_images = image_of(window_start + jnp.arange(span_rows, dtype=jnp.int32), image_count)
    return (span_rows, offset_rows, query_images[:, None] == key_images[None, :])


def head_slices(query, window_kv, block_index):
    head_dim = D // HEADS
    block_width = heads_per_block * head_dim
    first_column = block_index * block_width
    query_block = query[:, first_column : first_column + block_width].reshape(
        query.shape[0], heads_per_block, head_dim
    )
    key_block = window_kv[:, first_column : first_column + block_width].reshape(
        window_kv.shape[0], heads_per_block, head_dim
    )
    value_block = window_kv[:, D + first_column : D + first_column + block_width].reshape(
        window_kv.shape[0], heads_per_block, head_dim
    )
    return (query_block, key_block, value_block, first_column, block_width)


def attend(query, window_kv, visible):
    score_scale = (D // HEADS) ** (-0.5)
    outputs, log_sums = ([], [])
    for block_index in range(HEADS // heads_per_block):
        query_block, key_block, value_block, first_column, block_width = head_slices(
            query, window_kv, block_index
        )
        raw_scores = jnp.einsum(
            "qhd,khd->hqk", query_block, key_block, preferred_element_type=jnp.float32
        )
        scores = jnp.where(visible[None], raw_scores * score_scale, MASKED)
        largest = jnp.max(scores, axis=-1, keepdims=True)
        exponent = jnp.exp(scores - largest)
        row_totals = jnp.sum(exponent, axis=-1, keepdims=True)
        probabilities = (exponent / row_totals).astype(jnp.bfloat16)
        log_sums.append(largest + jnp.log(row_totals))
        attended = jnp.einsum(
            "hqk,khd->qhd", probabilities, value_block, preferred_element_type=jnp.float32
        )
        outputs.append(attended.reshape(query.shape[0], block_width))
    return (jnp.concatenate(outputs, axis=1), log_sums)


def attend_back(query, window_kv, visible, log_sums, grad_attended):
    score_scale = (D // HEADS) ** (-0.5)
    grad_queries, grad_keys, grad_values = ([], [], [])
    for block_index in range(HEADS // heads_per_block):
        query_block, key_block, value_block, first_column, block_width = head_slices(
            query, window_kv, block_index
        )
        grad_block = grad_attended[:, first_column : first_column + block_width].reshape(
            query.shape[0], heads_per_block, block_width // heads_per_block
        )
        raw_scores = jnp.einsum(
            "qhd,khd->hqk", query_block, key_block, preferred_element_type=jnp.float32
        )
        scores = jnp.where(visible[None], raw_scores * score_scale, MASKED)
        probabilities = jnp.exp(scores - log_sums[block_index])
        grad_values.append(
            jnp.einsum(
                "hqk,qhd->khd",
                probabilities.astype(jnp.bfloat16),
                grad_block,
                preferred_element_type=jnp.float32,
            ).reshape(window_kv.shape[0], block_width)
        )
        grad_probs = jnp.einsum(
            "qhd,khd->hqk", grad_block, value_block, preferred_element_type=jnp.float32
        )
        inner = jnp.sum(probabilities * grad_probs, axis=-1, keepdims=True)
        grad_raw = (probabilities * (grad_probs - inner) * score_scale).astype(jnp.bfloat16)
        grad_queries.append(
            jnp.einsum(
                "hqk,khd->qhd", grad_raw, key_block, preferred_element_type=jnp.float32
            ).reshape(query.shape[0], block_width)
        )
        grad_keys.append(
            jnp.einsum(
                "hqk,qhd->khd", grad_raw, query_block, preferred_element_type=jnp.float32
            ).reshape(window_kv.shape[0], block_width)
        )
    return (jnp.concatenate(grad_queries, axis=1), jnp.concatenate(grad_keys + grad_values, axis=1))


def unpack(gathered):
    qkv_flat, out_flat, up_flat, down_flat, packed = gathered
    packed = packed.astype(jnp.float32)
    pieces = [packed[segment * D : (segment + 1) * D] for segment in range(8)]
    up_bias = packed[8 * D : 8 * D + FF]
    return (
        qkv_flat.reshape(D, 3 * D),
        out_flat.reshape(D, D),
        up_flat.reshape(D, FF),
        down_flat.reshape(FF, D),
        pieces,
        up_bias,
    )


def forward_batch(tokens_batch, image_count, weights, device_index):
    qkv_w, out_w, up_w, down_w, pieces, up_bias = weights
    shard_rows = tokens_batch.shape[0]
    rim_rows = IMG_LEN - 1
    inputs = tokens_batch.astype(jnp.float32)
    normed_one, inverse_one = layer_stats(inputs)
    hidden_one = (normed_one * pieces[0] + pieces[1]).astype(jnp.bfloat16)
    projected = jnp.dot(hidden_one, qkv_w, preferred_element_type=jnp.float32)
    query = (projected[:, :D] + pieces[2]).astype(jnp.bfloat16)
    key_value = jnp.concatenate(
        [projected[:, D : 2 * D], projected[:, 2 * D :] + pieces[3]], axis=1
    ).astype(jnp.bfloat16)
    extended = widen(key_value, shard_rows)
    span_rows, offset_rows, visible = key_window(device_index, shard_rows, image_count)
    padded = jnp.pad(extended, ((0, rim_rows + span_rows - extended.shape[0]), (0, 0)))
    window_kv = lax.dynamic_slice_in_dim(padded, offset_rows, span_rows, 0)
    attended, log_sums = attend(query, window_kv, visible)
    attended_low = attended.astype(jnp.bfloat16)
    middle = inputs + (jnp.dot(attended_low, out_w, preferred_element_type=jnp.float32) + pieces[4])
    normed_two, inverse_two = layer_stats(middle)
    hidden_two = (normed_two * pieces[5] + pieces[6]).astype(jnp.bfloat16)
    upper = jnp.dot(hidden_two, up_w, preferred_element_type=jnp.float32) + up_bias
    active = jax.nn.gelu(upper, approximate=True).astype(jnp.bfloat16)
    output = middle + (jnp.dot(active, down_w, preferred_element_type=jnp.float32) + pieces[7])
    saved = (
        normed_one,
        inverse_one,
        hidden_one,
        query,
        window_kv,
        offset_rows,
        visible,
        log_sums,
        attended_low,
        normed_two,
        inverse_two,
        hidden_two,
        upper,
        active,
    )
    return (output.astype(jnp.bfloat16), saved)


def backward_batch(grad_output, saved, weights, vector_length):
    qkv_w, out_w, up_w, down_w, pieces, up_bias = weights
    (
        normed_one,
        inverse_one,
        hidden_one,
        query,
        window_kv,
        offset_rows,
        visible,
        log_sums,
        attended_low,
        normed_two,
        inverse_two,
        hidden_two,
        upper,
        active,
    ) = saved
    shard_rows = query.shape[0]
    span_rows = window_kv.shape[0]
    rim_rows = IMG_LEN - 1
    grad_wide = grad_output.astype(jnp.float32)
    grad_down = jnp.einsum("tf,td->fd", active, grad_output, preferred_element_type=jnp.float32)
    grad_down_bias = jnp.sum(grad_wide, axis=0)
    grad_active = jnp.einsum("td,fd->tf", grad_output, down_w, preferred_element_type=jnp.float32)
    gelu_back = jax.vjp(partial(jax.nn.gelu, approximate=True), upper)[1]
    grad_upper = gelu_back(grad_active)[0].astype(jnp.bfloat16)
    grad_up = jnp.einsum("td,tf->df", hidden_two, grad_upper, preferred_element_type=jnp.float32)
    grad_up_bias = jnp.sum(grad_upper.astype(jnp.float32), axis=0)
    grad_hidden_two = jnp.einsum("tf,df->td", grad_upper, up_w, preferred_element_type=jnp.float32)
    grad_gain_two = jnp.sum(grad_hidden_two * normed_two, axis=0)
    grad_bias_two = jnp.sum(grad_hidden_two, axis=0)
    grad_middle = grad_wide + layer_back(grad_hidden_two, normed_two, inverse_two, pieces[5])
    grad_branch = grad_middle.astype(jnp.bfloat16)
    grad_out = jnp.einsum(
        "td,te->de", attended_low, grad_branch, preferred_element_type=jnp.float32
    )
    grad_out_bias = jnp.sum(grad_branch.astype(jnp.float32), axis=0)
    grad_attended = jnp.einsum(
        "te,de->td", grad_branch, out_w, preferred_element_type=jnp.float32
    ).astype(jnp.bfloat16)
    grad_query, grad_window = attend_back(query, window_kv, visible, log_sums, grad_attended)
    grad_padded = lax.dynamic_update_slice_in_dim(
        jnp.zeros((rim_rows + span_rows, 2 * D), jnp.float32), grad_window, offset_rows, 0
    )
    grad_kv = return_edges(grad_padded[: shard_rows + 2 * rim_rows], shard_rows)
    grad_query_low = grad_query.astype(jnp.bfloat16)
    grad_kv_low = grad_kv.astype(jnp.bfloat16)
    grad_projected = jnp.concatenate([grad_query_low, grad_kv_low], axis=1)
    grad_qkv = jnp.einsum(
        "td,te->de", hidden_one, grad_projected, preferred_element_type=jnp.float32
    )
    grad_query_bias = jnp.sum(grad_query_low.astype(jnp.float32), axis=0)
    grad_value_bias = jnp.sum(grad_kv_low[:, D:].astype(jnp.float32), axis=0)
    grad_hidden_one = jnp.einsum(
        "te,de->td", grad_projected, qkv_w, preferred_element_type=jnp.float32
    )
    grad_gain_one = jnp.sum(grad_hidden_one * normed_one, axis=0)
    grad_bias_one = jnp.sum(grad_hidden_one, axis=0)
    grad_input = grad_middle + layer_back(grad_hidden_one, normed_one, inverse_one, pieces[0])
    vector_grad = jnp.concatenate(
        [
            grad_gain_one,
            grad_bias_one,
            grad_query_bias,
            grad_value_bias,
            grad_out_bias,
            grad_gain_two,
            grad_bias_two,
            grad_down_bias,
            grad_up_bias,
            jnp.zeros((vector_length - 8 * D - FF,), jnp.float32),
        ]
    )
    flat_grads = (
        grad_qkv.reshape(-1),
        grad_out.reshape(-1),
        grad_up.reshape(-1),
        grad_down.reshape(-1),
        vector_grad,
    )
    return (grad_input.astype(jnp.bfloat16), flat_grads)


def generic_local(tokens, counts, qkv_weight, out_weight, up_weight, down_weight, vectors, cotangent):
    device_index = lax.axis_index("dev")
    vector_length = vectors.shape[0] * lax.axis_size("dev")
    gathered = (
        lax.all_gather(qkv_weight, "dev", axis=0, tiled=True),
        lax.all_gather(out_weight, "dev", axis=0, tiled=True),
        lax.all_gather(up_weight, "dev", axis=0, tiled=True),
        lax.all_gather(down_weight, "dev", axis=0, tiled=True),
        lax.all_gather(vectors, "dev", axis=0, tiled=True),
    )
    weights = unpack(gathered)
    results, kept_state = ([], [])
    for batch_index in range(tokens.shape[0]):
        output, saved = forward_batch(
            tokens[batch_index], counts[batch_index], weights, device_index
        )
        results.append(output)
        kept_state.append(saved)
    weights = unpack(
        (
            lax.all_gather(qkv_weight, "dev", axis=0, tiled=True),
            lax.all_gather(out_weight, "dev", axis=0, tiled=True),
            lax.all_gather(up_weight, "dev", axis=0, tiled=True),
            lax.all_gather(down_weight, "dev", axis=0, tiled=True),
            lax.all_gather(vectors, "dev", axis=0, tiled=True),
        )
    )
    grad_inputs = []
    totals = None
    for batch_index in range(tokens.shape[0]):
        grad_input, flat_grads = backward_batch(
            cotangent[batch_index], kept_state[batch_index], weights, vector_length
        )
        grad_inputs.append(grad_input)
        totals = (
            flat_grads
            if totals is None
            else tuple((earlier + current for earlier, current in zip(totals, flat_grads)))
        )
    totals = lax.psum_scatter(totals, "dev", scatter_dimension=0, tiled=True)
    return (
        jnp.stack(results),
        jnp.stack(grad_inputs),
        totals[0],
        totals[1],
        totals[2],
        totals[3],
        totals[4],
    )


CHIPS = 16
HEAD = D // HEADS
HALF = D // 2
CORE_HEADS = HEADS // 2
ROWS = D // CHIPS
UNIT = FF // CHIPS
UNIT_HALF = 136
UNIT_SECOND = 134
FFH = CHIPS * UNIT_HALF
SHARD = 256
CHIP_ROWS = 2 * SHARD
TILE = 128
CHUNK = 16
SPAN = 768
SPAN_CHUNKS = SPAN // CHUNK
SHARD_CHUNKS = SHARD // CHUNK
SPAN_DEVICES = 4
TOKENS = 2 * CHIPS * SHARD
SCALE = HEAD**-0.5


def route(target):
    return [(i, target(i)) for i in range(2 * CHIPS)]


def swap(block):
    return lax.ppermute(block, "dev", route(lambda i: i ^ 1))


def by_core(core, first, second):
    return jnp.where(core == 0, first, second)


def joined(core, mine, theirs, axis):
    return by_core(
        core,
        jnp.concatenate([mine, theirs], axis=axis),
        jnp.concatenate([theirs, mine], axis=axis),
    )


def head_lanes(head):
    first = head * HEAD
    low = first // 128 * 128
    high = min((first + HEAD + 127) // 128 * 128, HALF)
    return low, high, first - low


def head_mask(head):
    low, high, skip = head_lanes(head)
    lanes = lax.broadcasted_iota(jnp.int32, (1, high - low), 1)
    return (lanes >= skip) & (lanes < skip + HEAD)


NT = (((1,), (1,)), ((), ()))
NN = (((1,), (0,)), ((), ()))
TN = (((0,), (0,)), ((), ()))


def mm(left, right, dims):
    return lax.dot_general(left, right, dims, preferred_element_type=jnp.float32)


def image_of_chip(chip):
    image = (CHIP_ROWS * chip + IMG_LEN // 2) // IMG_LEN
    has = owner_of_image(image) == chip
    first = image * IMG_LEN // CHUNK
    last = jnp.minimum((image * IMG_LEN + IMG_LEN - 1) // CHUNK, TOKENS // CHUNK - 1)
    return image, has, first, jnp.where(has, last - first + 1, 0)


def owner_of_image(image):
    return jnp.minimum((image * IMG_LEN + IMG_LEN // 2) // CHIP_ROWS, CHIPS - 1)


def in_image(image, has, first, rows, axis):
    shape = (rows, 1) if axis == 0 else (1, rows)
    at = first * CHUNK + lax.broadcasted_iota(jnp.int32, shape, axis)
    there = (at >= image * IMG_LEN) & (at < jnp.minimum((image + 1) * IMG_LEN, TOKENS))
    return there & has


def diagonal_tile(tile):
    row = tile * TILE + lax.broadcasted_iota(jnp.int32, (TILE, SPAN), 0)
    return row == lax.broadcasted_iota(jnp.int32, (TILE, SPAN), 1)


def attend_tile(image, has, first, batch, tile, live, q_ref, k_ref, v_ref, att_ref, lse_ref, acc):
    rows = pl.ds(pl.multiple_of(tile * TILE, TILE), TILE)
    visible = in_image(image, has, first, SPAN, 1) & (live | diagonal_tile(tile))
    stats = jnp.zeros((TILE, 128), jnp.float32)
    lane = lax.broadcasted_iota(jnp.int32, (TILE, 128), 1)
    acc[...] = jnp.zeros_like(acc)
    for head in range(CORE_HEADS):
        low, high, _ = head_lanes(head)
        mask = head_mask(head)
        query = jnp.where(mask, q_ref[batch, rows, low:high], 0)
        scores = jnp.where(visible, mm(query, k_ref[batch, :, low:high], NT) * SCALE, MASKED)
        largest = jnp.max(scores, axis=1, keepdims=True)
        exponent = jnp.exp(scores - largest)
        total = jnp.sum(exponent, axis=1, keepdims=True)
        probs = (exponent * (1.0 / total)).astype(jnp.bfloat16)
        part = mm(probs, v_ref[batch, :, low:high], NN)
        acc[:, low:high] += jnp.where(mask, part, 0.0)
        stats = jnp.where(lane == head, largest + jnp.log(total), stats)
    lse_ref[batch, rows] = stats
    att_ref[batch, rows] = acc[...].astype(jnp.bfloat16)


class Scatter:
    def __init__(self, place, grad_ref, total_ref, split, scratch):
        self.core, self.x, self.y, self.z = place
        self.grad_ref, self.total_ref, self.split = grad_ref, total_ref, split
        (self.half_x, self.half_y, self.whole_x, self.whole_y, self.from_z) = scratch[:5]
        (self.half_out, self.half_in, self.pair_out, self.pair_in, self.z_out, self.z_in) = scratch[5:]

    @staticmethod
    def scratch(shape, split):
        rows, columns = shape[1:]
        dma = pltpu.SemaphoreType.DMA
        block = lambda count, width: pltpu.VMEM((count, rows, width), jnp.bfloat16)
        return (
            [block(4, split), block(4, columns - split)]
            + [block(4, columns), block(4, columns), block(3, columns)]
            + [dma((2, 4)), dma((2, 4)), dma((2, 4)), dma((2, 4)), dma((3,)), dma((3,))]
        )

    COUNT = 11

    def unit(self, at_x, at_y, turn):
        at_z = (self.z + 1 + turn) % 4
        return self.grad_ref.at[(at_z * 2 + at_y) * 2 + at_x]

    def remote(self, source, target_ref, send_sem, recv_sem, device):
        return pltpu.make_async_remote_copy(
            src_ref=source,
            dst_ref=target_ref,
            send_sem=send_sem,
            recv_sem=recv_sem,
            device_id=device,
            device_id_type=MESH_ID,
        )

    def half(self, turn, axis):
        diagonal = self.unit(1 - self.x, 1 - self.y, turn)
        columns = self.grad_ref.shape[2]
        source = diagonal.at[:, pl.ds(0, self.split) if axis == 0 else pl.ds(self.split, columns - self.split)]
        device = (peer(1 - self.x, self.y, self.z, self.core), peer(self.x, 1 - self.y, self.z, self.core))[axis]
        target = (self.half_x, self.half_y)[axis].at[turn]
        return self.remote(source, target, self.half_out.at[axis, turn], self.half_in.at[axis, turn], device)

    def whole(self, turn, axis):
        device = (peer(1 - self.x, self.y, self.z, self.core), peer(self.x, 1 - self.y, self.z, self.core))[axis]
        source = (self.unit(1 - self.x, self.y, turn), self.unit(self.x, 1 - self.y, turn))[axis]
        target = (self.whole_x, self.whole_y)[axis]
        return self.remote(
            source, target.at[turn], self.pair_out.at[axis, turn], self.pair_in.at[axis, turn], device
        )

    def along(self, turn):
        device = peer(self.x, self.y, (self.z + 1 + turn) % 4, self.core)
        return self.remote(self.unit(self.x, self.y, turn), self.from_z.at[turn], self.z_out.at[turn], self.z_in.at[turn], device)

    def begin(self, turn):
        self.half(turn, 0).start()
        self.half(turn, 1).start()

    def pair(self, turn):
        split = self.split
        wide = lambda value: value.astype(jnp.float32)
        self.half(turn, 0).wait_recv()
        grad = self.unit(self.x, 1 - self.y, turn)
        grad[:, :split] = (wide(grad[:, :split]) + wide(self.half_x[turn])).astype(jnp.bfloat16)
        self.whole(turn, 1).start()
        self.half(turn, 1).wait_recv()
        grad = self.unit(1 - self.x, self.y, turn)
        grad[:, split:] = (wide(grad[:, split:]) + wide(self.half_y[turn])).astype(jnp.bfloat16)
        self.whole(turn, 0).start()

    def join(self, turn):
        wide = lambda value: value.astype(jnp.float32)
        self.whole(turn, 0).wait_recv()
        self.whole(turn, 1).wait_recv()
        own = self.unit(self.x, self.y, turn)
        total = wide(own[...]) + (wide(self.whole_x[turn]) + wide(self.whole_y[turn]))

        @pl.when(turn < 3)
        def _():
            own[...] = total.astype(jnp.bfloat16)
            self.along(turn).start()

        @pl.when(turn == 3)
        def _():
            self.total_ref[...] = total

    def total(self, turn):
        self.along(turn).wait_recv()
        self.total_ref[...] += self.from_z[turn].astype(jnp.float32)

    def finish(self):
        def pairs(turn, carry):
            for axis in range(2):
                self.half(turn, axis).wait_send()
                self.whole(turn, axis).wait_send()
            return carry

        def lines(turn, carry):
            self.along(turn).wait_send()
            return carry

        lax.fori_loop(0, 4, pairs, 0)
        lax.fori_loop(0, 3, lines, 0)


def each_turn(action, count=4):
    def body(turn, carry):
        action(turn)
        return carry

    lax.fori_loop(0, count, body, 0)


def attend_back_tile(
    image, has, first, batch, tile, live,
    q_ref, k_ref, v_ref, g_ref, stt_ref, dq_acc, dk_acc, dv_acc,
):
    rows = pl.ds(pl.multiple_of(tile * TILE, TILE), TILE)
    queries_there = in_image(image, has, first, SPAN, 1)
    at = first * CHUNK + tile * TILE + lax.broadcasted_iota(jnp.int32, (TILE, 1), 0)
    keys_there = (at >= image * IMG_LEN) & (at < jnp.minimum((image + 1) * IMG_LEN, TOKENS)) & has
    visible = queries_there & keys_there & (live | diagonal_tile(tile))
    dk_acc[...] = jnp.zeros_like(dk_acc)
    dv_acc[...] = jnp.zeros_like(dv_acc)

    @pl.when(tile == 0)
    def _():
        dq_acc[...] = jnp.zeros_like(dq_acc)

    for head in range(CORE_HEADS):
        low, high, _ = head_lanes(head)
        mask = head_mask(head)
        keys = jnp.where(mask, k_ref[batch, rows, low:high], 0)
        values = jnp.where(mask, v_ref[batch, rows, low:high], 0)
        queries = q_ref[batch, :, low:high]
        grads = g_ref[batch, :, low:high]
        lse = stt_ref[batch, head : head + 1]
        delta = stt_ref[batch, CORE_HEADS + head : CORE_HEADS + head + 1]
        probs = jnp.where(visible, jnp.exp(mm(keys, queries, NT) * SCALE - lse), 0.0)
        dv_acc[:, low:high] += jnp.where(mask, mm(probs.astype(jnp.bfloat16), grads, NN), 0.0)
        grad_probs = mm(values, grads, NT)
        grad_raw = (probs * (grad_probs - delta) * SCALE).astype(jnp.bfloat16)
        dk_acc[:, low:high] += jnp.where(mask, mm(grad_raw, queries, NN), 0.0)
        dq_acc[:, low:high] += mm(grad_raw, keys, TN)
    k_ref[batch, rows] = dk_acc[...].astype(jnp.bfloat16)
    v_ref[batch, rows] = dv_acc[...].astype(jnp.bfloat16)

    @pl.when(tile == SPAN // TILE - 1)
    def _():
        q_ref[batch] = dq_acc[:, :HALF].astype(jnp.bfloat16)


BACK_SPLITS = (384, 768, 128, 512)


class Rows:
    def __init__(self, place):
        core, x, y, z = place
        self.core = core
        self.chip = (z * 2 + y) * 2 + x
        self.device = self.chip * 2 + core
        self.image, self.has, self.first, self.count = image_of_chip(self.chip)
        start = self.device * SHARD
        images = [start // IMG_LEN, (start + SHARD - 1) // IMG_LEN]
        self.parts = []
        for part, image in enumerate(images):
            low = jnp.maximum(image * IMG_LEN - start, 0) // CHUNK
            high = jnp.minimum((image + 1) * IMG_LEN - 1 - start, SHARD - 1) // CHUNK + 1
            if part == 1:
                high = jnp.where(images[1] == images[0], low, high)
            self.parts.append((owner_of_image(image), image * IMG_LEN // CHUNK, low, high))

    def peers(self):
        holders = [
            ((self.first // SHARD_CHUNKS + n,), self.holds(n)) for n in range(SPAN_DEVICES)
        ]
        images = [
            ((owner * 2 + side,), jnp.logical_and(high > low, owner * 2 + side != self.device))
            for owner, _, low, high in self.parts
            for side in range(2)
        ]
        return holders + images

    def holds(self, n):
        device = self.first // SHARD_CHUNKS + n
        last = (self.first + self.count - 1) // SHARD_CHUNKS
        there = jnp.logical_and(self.count > 0, device <= last)
        return jnp.logical_and(there, device != self.device)

    @staticmethod
    def scratch():
        dma = pltpu.SemaphoreType.DMA
        return [dma((2, 2, SHARD_CHUNKS)), dma((SPAN_CHUNKS,))]

    def span_rows(self, ref, chunk):
        return ref.at[:, pl.ds(pl.multiple_of(chunk * CHUNK, CHUNK), CHUNK)]

    def chunk_rows(self, ref, chunk):
        return ref.at[pl.ds(pl.multiple_of(chunk * CHUNK, CHUNK), CHUNK)]

    def each_own(self, action):
        for part, (owner, first, low, high) in enumerate(self.parts):
            for side in range(2):
                def body(chunk, carry):
                    action(part, side, chunk, owner * 2 + side, self.device * SHARD_CHUNKS + chunk - first)
                    return carry

                lax.fori_loop(low, high, body, 0)

    def each_span(self, action):
        def body(chunk, carry):
            at = self.first + chunk
            device = at // SHARD_CHUNKS
            part = jnp.where(device * SHARD // IMG_LEN == self.image, 0, 1)
            action(chunk, device, at % SHARD_CHUNKS, part)
            return carry

        lax.fori_loop(0, self.count, body, 0)

    def elsewhere(self, device, action, here):
        @pl.when(device != self.device)
        def _():
            action()

        if here is not None:
            @pl.when(device == self.device)
            def _():
                here()

    def to_images(self, sources, span_ref, sems):
        token_sems, span_sems = sems

        def start(part, side, chunk, device, at):
            source, target = self.span_rows(sources[side], chunk), self.span_rows(span_ref, at)
            copy = remote(source, target, token_sems.at[part, side, chunk], span_sems.at[at], (device,))
            self.elsewhere(device, copy.start, pltpu.make_async_copy(source, target, span_sems.at[at]).start)

        self.each_own(start)

    def images_arrived(self, sources, span_ref, sems):
        token_sems, span_sems = sems

        def wait(chunk, device, at, part):
            block = self.span_rows(span_ref, chunk)
            span_sem = span_sems.at[chunk]
            copy = remote(block, block, token_sems.at[0, 0, 0], span_sem, (device,))
            local = pltpu.make_async_copy(self.span_rows(sources[0], at), block, span_sem)
            self.elsewhere(device, copy.wait_recv, local.wait)

        def sent(part, side, chunk, device, at):
            source = self.span_rows(sources[side], chunk)
            copy = remote(source, source, token_sems.at[part, side, chunk], span_sems.at[0], (device,))
            self.elsewhere(device, copy.wait_send, None)

        self.each_span(wait)
        self.each_own(sent)

    def to_both(self, own_ref, span_ref, sems):
        token_sems, span_sems, _, _ = sems

        def start(part, side, chunk, device, at):
            source, target = self.span_rows(own_ref, chunk), self.span_rows(span_ref, at)
            copy = remote(source, target, token_sems.at[part, 0, chunk], span_sems.at[at], (device,))

            def here():
                target[...] = source[...]

            @pl.when(side == self.core)
            def _():
                self.elsewhere(device, copy.start, here)

        self.each_own(start)

    def trade(self, span_ref, chunk, sems):
        block = self.span_rows(span_ref, chunk)
        return remote(block, block, sems[2].at[chunk], sems[3].at[chunk], (self.chip * 2 + 1 - self.core,))

    def relay(self, span_ref, sems):
        token_sems, span_sems, _, _ = sems

        def pass_on(chunk, device, at, part):
            block = self.span_rows(span_ref, chunk)
            copy = remote(block, block, token_sems.at[0, 0, 0], span_sems.at[chunk], (device,))

            @pl.when(device % 2 == self.core)
            def _():
                self.elsewhere(device, copy.wait_recv, None)
                self.trade(span_ref, chunk, sems).start()

        self.each_span(pass_on)

    def both_arrived(self, own_ref, span_ref, sems):
        token_sems, span_sems, _, _ = sems

        def traded(chunk, device, at, part):
            @pl.when(device % 2 == self.core)
            def _():
                self.trade(span_ref, chunk, sems).wait_send()

            @pl.when(device % 2 != self.core)
            def _():
                self.trade(span_ref, chunk, sems).wait_recv()

        def sent(part, side, chunk, device, at):
            source = self.span_rows(own_ref, chunk)
            copy = remote(source, source, token_sems.at[part, 0, chunk], span_sems.at[0], (device,))

            @pl.when(side == self.core)
            def _():
                self.elsewhere(device, copy.wait_send, None)

        self.each_span(traded)
        self.each_own(sent)

    def batch_to_tokens(self, span_ref, landing, sems):
        token_sems, span_sems = sems

        def start(chunk, device, at, part):
            source, target = self.chunk_rows(span_ref, chunk), self.chunk_rows(landing.at[part, self.core], at)
            token_sem = token_sems.at[part, self.core, at]
            copy = remote(source, target, span_sems.at[chunk], token_sem, (device,))
            self.elsewhere(device, copy.start, pltpu.make_async_copy(source, target, token_sem).start)

        self.each_span(start)

    def batches_arrived(self, span_ref, landing, sems):
        token_sems, span_sems = sems

        def wait(part, side, chunk, device, at):
            source, target = self.chunk_rows(span_ref, at), self.chunk_rows(landing.at[part, side], chunk)
            token_sem = token_sems.at[part, side, chunk]
            copy = remote(target, target, span_sems.at[0], token_sem, (device,))
            self.elsewhere(device, copy.wait_recv, pltpu.make_async_copy(source, target, token_sem).wait)

        def sent(chunk, device, at, part):
            block = self.chunk_rows(span_ref, chunk)
            copy = remote(block, block, span_sems.at[chunk], token_sems.at[0, 0, 0], (device,))
            self.elsewhere(device, copy.wait_send, None)

        self.each_own(wait)
        self.each_span(sent)

    def to_tokens(self, span_ref, landing, sems):
        token_sems, span_sems = sems

        def start(chunk, device, at, part):
            source = self.span_rows(span_ref, chunk)
            target = self.span_rows(landing.at[part, self.core], at)
            copy = remote(source, target, span_sems.at[chunk], token_sems.at[part, self.core, at], (device,))

            def here():
                target[...] = source[...]

            self.elsewhere(device, copy.start, here)

        self.each_span(start)

    def tokens_arrived(self, span_ref, landing, sems):
        token_sems, span_sems = sems

        def wait(part, side, chunk, device, at):
            block = self.span_rows(landing.at[part, side], chunk)
            copy = remote(block, block, span_sems.at[0], token_sems.at[part, side, chunk], (device,))
            self.elsewhere(device, copy.wait_recv, None)

        def sent(chunk, device, at, part):
            block = self.span_rows(span_ref, chunk)
            copy = remote(block, block, span_sems.at[chunk], token_sems.at[0, 0, 0], (device,))
            self.elsewhere(device, copy.wait_send, None)

        self.each_own(wait)
        self.each_span(sent)


def backward_kernel(
    counts, q_in, k_in, v_in, hidden_in, weight_in, att_ref, lse_ref, low_ref, high_ref, down_in, *rest
):
    pairs_in, rest = rest[:8], rest[8:]
    sums_ref, landing, down_total, up_total, out_total, qkv_total = rest[:6]
    (
        arrived, down_ref, up_ref, out_ref, qkv_ref, dq_acc, dk_acc, dv_acc, span, stt_ref,
        load_sems, token_sems, span_sems, back_token_sems, back_span_sems, swap_out, swap_in,
    ) = rest[6:23]
    scratch = rest[23:]
    place = position_of()
    rows = Rows(place)
    batches = span.shape[0]

    def loading(pairs):
        loads = [pltpu.make_async_copy(a, b, load_sems.at[n]) for n, (a, b) in enumerate(pairs)]
        for load in loads:
            load.start()
        return loads

    first_load = loading([(down_in, down_ref)])
    greet(pair_peers(*place) + line_peers(*place) + [(partner_of(*place), True)] + rows.peers())
    sems, sources = (token_sems, span_sems), (low_ref, high_ref)
    rows.to_images(sources, span, sems)
    count = Scatter.COUNT
    down, up, out, qkv = [
        Scatter(place, grad, total, split, scratch[n * count : (n + 1) * count])
        for n, (grad, total, split) in enumerate(
            zip((down_ref, up_ref, out_ref, qkv_ref), (down_total, up_total, out_total, qkv_total), BACK_SPLITS)
        )
    ]
    first_load[0].wait()
    each_turn(down.begin)

    def loop(action, first, last):
        def body(turn, carry):
            action(turn)
            return carry

        lax.fori_loop(first, last, body, 0)

    def rows_grad(left, right, grad_ref, blocks):
        for half in range(2):
            units = slice(half * CHIPS // 2, (half + 1) * CHIPS // 2)
            for first, end in blocks:
                width = end - first
                dq_acc[:HALF, :width] = mm(left[half * HALF : (half + 1) * HALF], right[:, first:end], NN)
                grad_ref[units, :, first:end] = dq_acc[:HALF, :width].reshape(CHIPS // 2, ROWS, width).astype(jnp.bfloat16)

    def weight_grads(left, turned, wide, narrow):
        own = pl.ds(0, SHARD * batches), pl.ds(SHARD * batches, SHARD * batches)
        h2, h2_swap, gu, gu_swap, att, att_swap, gb, gb_swap = pairs_in
        loads = loading(
            [(h2, left.at[own[0]]), (h2_swap, left.at[own[1]]), (gu, wide.at[own[0]]), (gu_swap, wide.at[own[1]])]
            + [(gb, narrow.at[own[0]]), (gb_swap, narrow.at[own[1]])]
        )
        for load in loads:
            load.wait()
        turned[...] = left[...].T
        loads = loading([(att, left.at[own[0]]), (att_swap, left.at[own[1]])])
        rows_grad(turned, wide, up_ref, [(0, 640), (640, 1280), (1280, 1920), (1920, FFH)])
        loop(down.pair, 0, 4)
        each_turn(up.begin)
        for load in loads:
            load.wait()
        turned[...] = left[...].T
        rows_grad(turned, narrow, out_ref, [(0, HALF)])

    tokens = 2 * SHARD * batches
    pl.run_scoped(
        weight_grads,
        pltpu.VMEM((tokens, D), jnp.bfloat16),
        pltpu.VMEM((D, tokens), jnp.bfloat16),
        pltpu.VMEM((tokens, FFH), jnp.bfloat16),
        pltpu.VMEM((tokens, HALF + 64), jnp.bfloat16),
    )

    def attention(q_ref, k_ref, v_ref, hidden, weight):
        loads = loading([(q_in, q_ref), (k_in, k_ref), (v_in, v_ref), (hidden_in, hidden), (weight_in, weight)])
        each_turn(out.begin)
        rows.images_arrived(sources, span, sems)

        def prepare(batch, carry):
            there = in_image(rows.image, rows.has, rows.first, SPAN, 0)
            grads = jnp.where(there, span[batch], 0)
            span[batch] = grads
            lane = lax.broadcasted_iota(jnp.int32, (SPAN, 128), 1)
            stats = jnp.where(lane < CORE_HEADS, lse_ref[batch], 0.0)
            for head in range(CORE_HEADS):
                low, high, _ = head_lanes(head)
                product = grads[:, low:high].astype(jnp.float32) * att_ref[batch, :, low:high].astype(jnp.float32)
                total = jnp.sum(jnp.where(head_mask(head), product, 0.0), axis=1, keepdims=True)
                stats = jnp.where(lane == CORE_HEADS + head, total, stats)
            stt_ref[batch] = stats.T[: 2 * CORE_HEADS]
            return carry

        lax.fori_loop(0, batches, prepare, 0)
        for load in loads:
            load.wait()
        tiles = SPAN // TILE
        work = {
            1: [(down.join, 0, 1)],
            3: [(down.join, 1, 2), (up.pair, 0, 1)],
            5: [(down.join, 2, 3), (up.pair, 1, 2)],
            7: [(down.join, 3, 4), (up.pair, 2, 3)],
            9: [(up.pair, 3, 4)],
            11: [(out.pair, 0, 4), (up.join, 0, 1)],
        }

        def attend(index, carry):
            batch, tile = index // tiles, index % tiles
            attend_back_tile(
                rows.image, rows.has, rows.first, batch, tile, rows.image < counts[batch],
                q_ref, k_ref, v_ref, span, stt_ref, dq_acc, dk_acc, dv_acc,
            )
            for at, actions in work.items():
                @pl.when(index == at)
                def _():
                    for action, first, last in actions:
                        loop(action, first, last)
            return carry

        lax.fori_loop(0, batches * tiles, attend, 0)
        columns = lambda ref: sum(jnp.sum(ref[b].astype(jnp.float32), axis=0, keepdims=True) for b in range(batches))
        sums_ref[0:1] = columns(q_ref)
        sums_ref[1:2] = columns(v_ref)

        def weight_grad(first, end, grads):
            for half in range(2):
                units = slice(half * CHIPS // 2, (half + 1) * CHIPS // 2)
                for batch in range(batches):
                    part = mm(hidden[batch, :, half * HALF : (half + 1) * HALF], grads(batch), TN)
                    if batch == 0:
                        dq_acc[:HALF, : end - first] = part
                    else:
                        dq_acc[:HALF, : end - first] += part
                total = dq_acc[:HALF, : end - first].reshape(CHIPS // 2, ROWS, end - first)
                qkv_ref[units, :, first:end] = total.astype(jnp.bfloat16)

        weight_grad(0, 640, lambda batch: jnp.concatenate([q_ref[batch], k_ref[batch, :, :64]], axis=1))
        weight_grad(640, D, lambda batch: k_ref[batch, :, 64:])
        weight_grad(D, 3 * HALF, lambda batch: v_ref[batch])
        each_turn(qkv.begin)

        def token_grad(batch, others):
            def block(index, carry):
                here = pl.ds(pl.multiple_of(index * TILE, TILE), TILE)
                grads = jnp.concatenate([ref[batch, here] for ref in (q_ref, k_ref, v_ref)], axis=1)
                total = mm(grads, weight[...], NT)
                if others is not None:
                    total = total + others[here].astype(jnp.float32)
                hidden[batch, here] = total.astype(jnp.bfloat16)
                return carry

            lax.fori_loop(0, SPAN // TILE, block, 0)

        core = place[0]
        token_grad(1 - core, None)
        trade = remote(hidden.at[1 - core], arrived, swap_out, swap_in, partner_of(*place))
        trade.start()
        loop(up.join, 1, 2)
        trade.wait_recv()
        token_grad(core, arrived)
        back_sems = (back_token_sems, back_span_sems)
        rows.batch_to_tokens(hidden.at[core], landing, back_sems)
        loop(up.join, 2, 4)
        each_turn(qkv.pair)
        each_turn(out.join)
        each_turn(down.total, 3)
        each_turn(qkv.join)
        each_turn(up.total, 3)
        each_turn(out.total, 3)
        each_turn(qkv.total, 3)
        trade.wait_send()
        rows.batches_arrived(hidden.at[core], landing, back_sems)

    held = lambda *shape: pltpu.VMEM(shape, jnp.bfloat16)
    pl.run_scoped(
        attention, *[held(batches, SPAN, HALF)] * 3, held(batches, SPAN, D), held(D, 3 * HALF)
    )
    for scatter in (down, up, out, qkv):
        scatter.finish()


def backward(counts, query, keys, values, hidden, weight, attended, lse, low, high, down, pairs, collective_id):
    batches = query.shape[0]
    vmem, hbm = pl.BlockSpec(memory_space=pltpu.VMEM), pl.BlockSpec(memory_space=pl.ANY)
    shapes = [down.shape, (CHIPS, ROWS, FFH), (CHIPS, ROWS, HALF), (CHIPS, ROWS, 3 * HALF)]
    held = lambda *shape: pltpu.VMEM(shape, jnp.bfloat16)
    dma = pltpu.SemaphoreType.DMA
    return pl.pallas_call(
        backward_kernel,
        out_shape=[jax.ShapeDtypeStruct((2, HALF), jnp.float32)]
        + [jax.ShapeDtypeStruct((2, batches, SHARD, D), jnp.bfloat16)]
        + [jax.ShapeDtypeStruct(shape[1:], jnp.float32) for shape in shapes],
        in_specs=[pl.BlockSpec(memory_space=pltpu.SMEM)] + [hbm] * 5 + [vmem] * 2 + [hbm] * (3 + len(pairs)),
        out_specs=[vmem, hbm] + [vmem] * 4,
        scratch_shapes=[held(SPAN, D)]
        + [held(*shape) for shape in shapes]
        + [
            pltpu.VMEM((SPAN, HALF + 64), jnp.float32),
            pltpu.VMEM((TILE, HALF), jnp.float32),
            pltpu.VMEM((TILE, HALF), jnp.float32),
            held(batches, SPAN, HALF),
            pltpu.VMEM((batches, 2 * CORE_HEADS, SPAN), jnp.float32),
            dma((8,)),
        ]
        + Rows.scratch() * 2
        + [dma] * 2
        + sum([Scatter.scratch(shape, split) for shape, split in zip(shapes, BACK_SPLITS)], []),
        compiler_params=pltpu.CompilerParams(
            collective_id=collective_id, has_side_effects=True, vmem_limit_bytes=60 * 1024 * 1024
        ),
        cost_estimate=pl.CostEstimate(flops=0, bytes_accessed=500 * 10**6, transcendentals=0),
        name="backward",
    )(counts, query, keys, values, hidden, weight, attended, lse, low, high, down, *pairs)


def chip_unit(core, low, high):
    theirs = swap(by_core(core, high, low))
    return joined(core, by_core(core, low, high), theirs, 0)


def peer(x, y, z, core):
    return (((z * 2 + y) * 2 + x) * 2 + core,)


MESH_ID = pl.DeviceIdType.MESH


def position_of():
    device = lax.axis_index("dev")
    return device % 2, device // 2 % 2, device // 4 % 2, device // 8


def greet(targets):
    barrier = pltpu.get_barrier_semaphore()
    count = 0
    for target, there in targets:
        if there is True:
            pl.semaphore_signal(barrier, inc=1, device_id=target, device_id_type=MESH_ID)
            count = count + 1
        else:
            @pl.when(there)
            def _():
                pl.semaphore_signal(barrier, inc=1, device_id=target, device_id_type=MESH_ID)
            count = count + there.astype(jnp.int32)
    pl.semaphore_wait(barrier, count)


def pair_peers(core, x, y, z):
    return [(peer(1 - x, y, z, core), True), (peer(x, 1 - y, z, core), True)]


def next_peers(core, x, y, z):
    return [(peer(x, y, z - 1, core), z > 0), (peer(x, y, z + 1, core), z < 3)]


def line_peers(core, x, y, z):
    return [(peer(x, y, (z + step) % 4, core), True) for step in (1, 2, 3)]


def partner_of(core, x, y, z):
    return peer(x, y, z, 1 - core)


class Gather:
    def __init__(self, place, unit_ref, full_ref, other_ref, split, sems):
        self.core, self.x, self.y, self.z = place
        self.unit_ref, self.full_ref, self.other_ref, self.split = unit_ref, full_ref, other_ref, split
        (
            self.z_out,
            self.z_in,
            self.pair_out,
            self.pair_in,
            self.half_out,
            self.half_in,
            self.chain_out,
            self.chain_in,
            self.own_sem,
        ) = sems[:9]
        if other_ref is not None:
            self.swap_out, self.swap_in = sems[9:]
        self.sides = ((-1, self.z > 0), (1, self.z < 3))
        self.x_peer = peer(1 - self.x, self.y, self.z, self.core)
        self.y_peer = peer(self.x, 1 - self.y, self.z, self.core)

    @staticmethod
    def scratch(partner):
        dma = pltpu.SemaphoreType.DMA
        shapes = [(2, 4), (4,), (2, 4), (2, 4), (2, 4), (2, 4), (2, 4), (4,)]
        return [dma(shape) for shape in shapes] + [dma] + ([dma((CHIPS,))] * 2 if partner else [])

    def unit_index(self, at_x, at_y, at_z):
        return (at_z * 2 + at_y) * 2 + at_x

    def slot(self, at_x, at_y, at_z):
        return self.full_ref.at[self.unit_index(at_x, at_y, at_z)]

    def column(self, turn, at_z):
        at_x, at_y = [(self.x, self.y), (self.x, 1 - self.y), (1 - self.x, self.y), (1 - self.x, 1 - self.y)][turn]
        return self.slot(at_x, at_y, at_z)

    def copy(self, block, send_sem, recv_sem, target, source=None):
        return pltpu.make_async_remote_copy(
            src_ref=block if source is None else source,
            dst_ref=block,
            send_sem=send_sem,
            recv_sem=recv_sem,
            device_id=target,
            device_id_type=MESH_ID,
        )

    def along(self, at_z, side, source=None):
        index = 0 if side < 0 else 1
        target = peer(self.x, self.y, self.z + side, self.core)
        return self.copy(self.column(0, at_z), self.z_out.at[index, at_z], self.z_in.at[at_z], target, source)

    def chain(self, at_z, side):
        index = 0 if side < 0 else 1
        target = peer(self.x, self.y, self.z + side, self.core)
        return self.copy(self.column(3, at_z), self.chain_out.at[index, at_z], self.chain_in.at[at_z], target)

    def whole(self, at_z, axis, source=None):
        target = (self.x_peer, self.y_peer)[axis]
        return self.copy(self.column(0, at_z), self.pair_out.at[axis, at_z], self.pair_in.at[axis, at_z], target, source)

    def part(self, block, axis):
        width = self.full_ref.shape[2]
        return block.at[:, pl.ds(0, self.split) if axis == 0 else pl.ds(self.split, width - self.split)]

    def half(self, at_z, axis):
        block = self.part(self.column(1 + axis, at_z), axis)
        target = (self.x_peer, self.y_peer)[axis]
        return self.copy(block, self.half_out.at[axis, at_z], self.half_in.at[axis, at_z], target)

    def half_arrival(self, at_z, axis):
        block = self.part(self.column(3, at_z), axis)
        return self.copy(block, self.half_out.at[axis, at_z], self.half_in.at[axis, at_z], self.x_peer)

    def by_halves(self, at_z):
        near = jnp.logical_and(jnp.abs(at_z - self.z) == 1, jnp.logical_or(at_z == 1, at_z == 2))
        return jnp.logical_or(at_z == self.z, near)

    def trade(self, turn, at_z, source=None):
        at_x, at_y = [(self.x, self.y), (self.x, 1 - self.y), (1 - self.x, self.y), (1 - self.x, 1 - self.y)][turn]
        index = self.unit_index(at_x, at_y, at_z)
        block = self.full_ref.at[index] if source is None else source
        width = self.other_ref.shape[2]
        if width < self.full_ref.shape[2]:
            block = block.at[:, pl.ds(0, width)]
        return pltpu.make_async_remote_copy(
            src_ref=block,
            dst_ref=self.other_ref.at[index],
            send_sem=self.swap_out.at[index],
            recv_sem=self.swap_in.at[index],
            device_id=peer(self.x, self.y, self.z, 1 - self.core),
            device_id_type=MESH_ID,
        )

    def share(self, turn, at_z, source=None):
        if self.other_ref is not None:
            self.trade(turn, at_z, source).start()

    def each(self, distance, action):
        if distance == 0:
            action(self.z, 0)
            return
        for side in (-1, 1):
            at_z = self.z + side * distance
            @pl.when(jnp.logical_and(at_z >= 0, at_z <= 3))
            def _():
                action(at_z, side)

    def onwards(self, side, action):
        for to, there in self.sides:
            if side == 0 or to == -side:
                @pl.when(there)
                def _():
                    action(to)

    def arrive(self, at_z, side):
        source = None
        if side == 0:
            source = self.unit_ref
            pltpu.make_async_copy(self.unit_ref, self.column(0, at_z), self.own_sem).start()
        else:
            self.along(at_z, side).wait_recv()
        self.onwards(side, lambda to: self.along(at_z, to, source).start())
        self.whole(at_z, 0, source).start()
        self.whole(at_z, 1, source).start()
        self.share(0, at_z, source)

    def cross(self, at_z, side):
        for axis in (1, 0):
            arrived = self.column(2 - axis, at_z)
            self.copy(arrived, self.pair_out.at[axis, at_z], self.pair_in.at[axis, at_z], self.x_peer).wait_recv()
            @pl.when(self.by_halves(at_z))
            def _():
                self.half(at_z, 1 - axis).start()
            self.share(2 - axis, at_z)

    def far_chain(self, at_z, side):
        return jnp.logical_or(at_z == 0, at_z == 3) if side == 0 else True

    def diagonal(self, at_z, side):
        halves = self.by_halves(at_z)
        @pl.when(halves)
        def _():
            self.half_arrival(at_z, 0).wait_recv()
            self.half_arrival(at_z, 1).wait_recv()
        if side != 0:
            @pl.when(jnp.logical_not(halves))
            def _():
                self.chain(at_z, side).wait_recv()
        @pl.when(self.far_chain(at_z, side))
        def _():
            self.onwards(side, lambda to: self.chain(at_z, to).start())
        self.share(3, at_z)

    def steps(self):
        order = [
            (0, self.arrive),
            (1, self.arrive),
            (0, self.cross),
            (2, self.arrive),
            (0, self.diagonal),
            (1, self.cross),
            (3, self.arrive),
            (1, self.diagonal),
            (2, self.cross),
            (2, self.diagonal),
            (3, self.cross),
            (3, self.diagonal),
        ]
        return [partial(self.each, distance, action) for distance, action in order]

    def settle(self, at_z, side):
        self.onwards(side, lambda to: self.along(at_z, to).wait_send())
        @pl.when(self.far_chain(at_z, side))
        def _():
            self.onwards(side, lambda to: self.chain(at_z, to).wait_send())
        for axis in range(2):
            self.whole(at_z, axis).wait_send()
            @pl.when(self.by_halves(at_z))
            def _():
                self.half(at_z, axis).wait_send()

    def own_ready(self):
        pltpu.make_async_copy(self.unit_ref, self.column(0, self.z), self.own_sem).wait()

    def finish(self):
        for distance in range(4):
            self.each(distance, self.settle)
        if self.other_ref is not None:
            def traded(at_z, carry):
                for turn in range(4):
                    self.trade(turn, at_z).wait()
                return carry

            lax.fori_loop(0, 4, traded, 0)


def remote(source, target, send_sem, recv_sem, device):
    return pltpu.make_async_remote_copy(
        src_ref=source,
        dst_ref=target,
        send_sem=send_sem,
        recv_sem=recv_sem,
        device_id=device,
        device_id_type=MESH_ID,
    )


PADDED = 80
WIDE = CHIPS * PADDED
SHARE = 423


def vector_part(full_ref, start, length, width):
    lane = lax.broadcasted_iota(jnp.int32, (1, width), 1)
    total = jnp.zeros((1, width), jnp.float32)
    for device in range(start // SHARE, (start + length - 1) // SHARE + 1):
        base = 512 * (device % 2)
        tile = full_ref[device // 2, PADDED - 16 :, base : base + 512].astype(jnp.float32)
        row = tile[ROWS - PADDED + 16 : ROWS - PADDED + 17]
        if width > 512:
            row = jnp.concatenate([row, jnp.zeros((1, width - 512), jnp.float32)], axis=1)
        shift = device * SHARE - start
        row = pltpu.roll(row, shift % width, 1) if shift % width else row
        first, last = max(shift, 0), min(shift + SHARE, length)
        total = total + jnp.where((lane >= first) & (lane < last), row, 0.0)
    return total


FIRST_STEPS = (
    (0, 0), (3, 0), (0, 1), (0, 2), (3, 1), (0, 3), (0, 4), (0, 5), (0, 6), (3, 2), (0, 7), (0, 8), (0, 9), (0, 10), (0, 11),
    (1, 0), (2, 0),
)
PROJECT_STEPS = ((0, 0, 1, 2), (1, 0, 2, 3), (2, 1, 1, 2), (3, 0, 3, 4), (4, 1, 2, 3), (5, 0, 4, 6))
ATTEND_STEPS = (
    (1, 1, 3, 4), (3, 0, 6, 7), (5, 1, 4, 5), (6, 0, 7, 8), (7, 1, 5, 6), (8, 0, 8, 9), (9, 1, 6, 7), (10, 0, 9, 10), (11, 1, 7, 8),
)
LAST_STEPS = ((0, 10, 12), (1, 8, 12))


def forward_kernel(
    splits, counts, unit, up_unit, down_unit, tokens_ref, pad_ref,
    q_out, k_out, v_out, hidden_out, att_out, lse_out, full_out, landing, up_ref, up_other, down_ref, down_other,
    q_ref, k_ref, v_ref, hidden_ref, att_ref, lse_ref, full_ref, store_sems, span, padded, acc, token_sems, span_sems, trade_out, trade_in, back_token_sems, back_span_sems, *sems
):
    place = position_of()
    rows = Rows(place)
    greet(pair_peers(*place) + next_peers(*place) + [(partner_of(*place), True)] + rows.peers())
    plain, more = len(Gather.scratch(False)), len(Gather.scratch(True))
    first = Gather(place, unit, full_ref, None, splits[0], sems[:plain])
    second = Gather(place, up_unit, up_ref, up_other, splits[1], sems[plain : plain + more])
    third = Gather(place, down_unit, down_ref, down_other, splits[2], sems[plain + more :])
    held = (q_ref, k_ref, v_ref, hidden_ref, att_ref, lse_ref, full_ref)
    outs = (q_out, k_out, v_out, hidden_out, att_out, lse_out, full_out)
    stores = [pltpu.make_async_copy(a, b, store_sems.at[n]) for n, (a, b) in enumerate(zip(held, outs))]
    one, two, three = first.steps(), second.steps(), third.steps()
    row_sems = (token_sems, span_sems, trade_out, trade_in)

    def run(steps, start, stop):
        for step in steps[start:stop]:
            step()

    row_steps = (
        partial(rows.to_both, tokens_ref, span, row_sems),
        partial(rows.relay, span, row_sems),
        partial(rows.both_arrived, tokens_ref, span, row_sems),
    )

    def start(table):
        for which, step in table:
            if which == 3:
                row_steps[step]()
            else:
                run((one, two, three)[which], step, step + 1)

    start(FIRST_STEPS)
    first.own_ready()
    stores[6].start()
    batches = tokens_ref.shape[0]
    gain, bias = vector_part(full_ref, 0, D, WIDE)[:, :D], vector_part(full_ref, D, D, WIDE)[:, :D]
    core = place[0]
    half = lambda start: jnp.where(
        core == 0, vector_part(full_ref, start, HALF, 1024), vector_part(full_ref, start + HALF, HALF, 1024)
    )[:, :HALF]
    query_bias, value_bias = half(2 * D), half(3 * D)
    block = 256

    def between(table, index):
        for at, steps, begin, stop in table:
            @pl.when(index == at)
            def _():
                run((two, three)[steps], begin, stop)

    def project(index, carry):
        batch, at = index // (SPAN // block), index % (SPAN // block)
        here = pl.ds(pl.multiple_of(at * block, block), block)
        token = rows.first * CHUNK + at * block + lax.broadcasted_iota(jnp.int32, (block, 1), 0)
        there = (token >= rows.image * IMG_LEN) & (token < jnp.minimum((rows.image + 1) * IMG_LEN, TOKENS)) & rows.has
        value = jnp.where(there, span[batch, here], 0).astype(jnp.float32)
        centered = value - jnp.mean(value, axis=1, keepdims=True)
        inverse = lax.rsqrt(jnp.mean(centered * centered, axis=1, keepdims=True) + EPSILON)
        hidden = (centered * inverse * gain + bias).astype(jnp.bfloat16)
        hidden_ref[batch, here] = hidden
        padded[...] = mm(hidden, pad_ref[...], NN).astype(jnp.bfloat16)
        wide = mm(padded[...], full_ref[:, :, :D].reshape(WIDE, D), NN)
        q_ref[batch, here] = (wide[:, :HALF] + query_bias).astype(jnp.bfloat16)
        k_ref[batch, here] = wide[:, HALF:].astype(jnp.bfloat16)
        wide = mm(padded[...], full_ref[:, :, D:].reshape(WIDE, HALF), NN)
        v_ref[batch, here] = (wide + value_bias).astype(jnp.bfloat16)
        between(PROJECT_STEPS, index)
        return carry

    lax.fori_loop(0, batches * (SPAN // block), project, 0)
    for store in stores[:4]:
        store.start()
    tiles = SPAN // TILE

    def attend(index, carry):
        batch, tile = index // tiles, index % tiles
        attend_tile(
            rows.image, rows.has, rows.first, batch, tile, rows.image < counts[batch],
            q_ref, k_ref, v_ref, att_ref, lse_ref, acc,
        )
        between(ATTEND_STEPS, index)
        return carry

    lax.fori_loop(0, batches * tiles, attend, 0)
    for store in stores[4:6]:
        store.start()
    back_sems = (back_token_sems, back_span_sems)
    rows.to_tokens(att_ref, landing, back_sems)
    for steps, begin, stop in LAST_STEPS:
        run((two, three)[steps], begin, stop)
    rows.tokens_arrived(att_ref, landing, back_sems)
    second.own_ready()
    third.own_ready()
    for store in stores:
        store.wait()
    for gather in (first, second, third):
        gather.finish()


def forward(counts, unit, up_unit, down_unit, tokens, collective_id):
    batches = tokens.shape[0]
    full = lambda unit: jax.ShapeDtypeStruct((CHIPS,) + unit.shape, unit.dtype)
    low = lambda *shape: jax.ShapeDtypeStruct(shape, jnp.bfloat16)
    vmem, hbm = pl.BlockSpec(memory_space=pltpu.VMEM), pl.BlockSpec(memory_space=pl.ANY)
    dma = pltpu.SemaphoreType.DMA
    feature, lane = np.arange(D)[:, None], np.arange(WIDE)[None]
    pad = jnp.asarray(feature // ROWS * PADDED + feature % ROWS == lane, jnp.bfloat16)
    spans = [(batches, SPAN, HALF)] * 3 + [(batches, SPAN, D), (batches, SPAN, HALF)]
    outs = pl.pallas_call(
        partial(forward_kernel, (512, 896, 384)),
        out_shape=[low(*shape) for shape in spans]
        + [
            jax.ShapeDtypeStruct((batches, SPAN, 128), jnp.float32),
            full(unit),
            low(2, 2, batches, SHARD, HALF),
            full(up_unit),
            full(up_unit),
            full(down_unit),
            full(down_unit),
        ],
        in_specs=[pl.BlockSpec(memory_space=pltpu.SMEM)] + [vmem] * 5,
        out_specs=[hbm] * 7 + [vmem] + [hbm] * 4,
        scratch_shapes=[pltpu.VMEM(shape, jnp.bfloat16) for shape in spans]
        + [
            pltpu.VMEM((batches, SPAN, 128), jnp.float32),
            pltpu.VMEM((CHIPS,) + unit.shape, unit.dtype),
            dma((7,)),
            pltpu.VMEM((batches, SPAN, D), jnp.bfloat16),
            pltpu.VMEM((256, WIDE), jnp.bfloat16),
            pltpu.VMEM((TILE, HALF), jnp.float32),
        ]
        + Rows.scratch()
        + [dma((SPAN_CHUNKS,)), dma((SPAN_CHUNKS,))]
        + Rows.scratch()
        + Gather.scratch(False)
        + Gather.scratch(True) * 2,
        compiler_params=pltpu.CompilerParams(
            collective_id=collective_id, has_side_effects=True, vmem_limit_bytes=60 * 1024 * 1024
        ),
        cost_estimate=pl.CostEstimate(flops=0, bytes_accessed=500 * 10**6, transcendentals=0),
        name="forward",
    )(counts, unit, up_unit, down_unit, tokens, pad)
    return list(outs[:8]) + [w.reshape(-1, w.shape[2]) for w in outs[8:]]


def vector_kernel(sent_ref, total_ref, arrived, send_sems, recv_sems):
    device = lax.axis_index("dev")
    devices = 2 * CHIPS
    mesh_id = pl.DeviceIdType.MESH
    barrier = pltpu.get_barrier_semaphore()

    def greet(step, carry):
        pl.semaphore_signal(
            barrier, inc=1, device_id=(lax.rem(device + step, devices),), device_id_type=mesh_id
        )
        return carry

    lax.fori_loop(1, devices, greet, 0)
    pl.semaphore_wait(barrier, devices - 1)

    def copy(step):
        target = lax.rem(device + step, devices)
        return pltpu.make_async_remote_copy(
            src_ref=sent_ref.at[target],
            dst_ref=arrived.at[step],
            send_sem=send_sems.at[step],
            recv_sem=recv_sems.at[step],
            device_id=(target,),
            device_id_type=mesh_id,
        )

    def start(step, carry):
        copy(step).start()
        return carry

    lax.fori_loop(1, devices, start, 0)

    def add(step, total):
        copy(step).wait()
        return total + arrived[step]

    total_ref[...] = lax.fori_loop(1, devices, add, sent_ref[device])


def scatter_vector(vector, share, collective_id):
    rows = jnp.pad(vector.reshape(2 * CHIPS, share), ((0, 0), (0, 1024 - share)))
    dma = pltpu.SemaphoreType.DMA
    total = pl.pallas_call(
        vector_kernel,
        out_shape=jax.ShapeDtypeStruct((8, 128), jnp.float32),
        in_specs=[pl.BlockSpec(memory_space=pltpu.VMEM)],
        out_specs=pl.BlockSpec(memory_space=pltpu.VMEM),
        scratch_shapes=[
            pltpu.VMEM((2 * CHIPS, 8, 128), jnp.float32),
            dma((2 * CHIPS,)),
            dma((2 * CHIPS,)),
        ],
        compiler_params=pltpu.CompilerParams(collective_id=collective_id, has_side_effects=True),
        cost_estimate=pl.CostEstimate(flops=0, bytes_accessed=20 * 10**6, transcendentals=0),
        name="scatter_vector",
    )(rows.reshape(2 * CHIPS, 8, 128))
    return total.reshape(-1)[:share]


def later_image(device):
    start = device * SHARD
    at = start + lax.broadcasted_iota(jnp.int32, (SHARD, 1), 0)
    return at >= (start // IMG_LEN + 1) * IMG_LEN


MLP_ROWS = SHARD
GELU_A, GELU_B = 0.7978845608028654, 0.044715


def mlp_kernel(
    x_ref, landing, g_ref, up_a, up_b, down_a, down_b, vec_ref, bias_ref,
    att_ref, result_ref, act_a, act_b, gu_a, gu_b, h2_ref, gb_a, gb_b, gm_ref, go_a, go_b, sums_ref, bias_sums_ref,
    wo_a, wo_b, up_w, down_w, slope, sems,
):
    loads = [
        pltpu.make_async_copy(source, target, sems.at[n])
        for n, (source, target) in enumerate(
            [
                (up_a.at[:, pl.ds(0, FFH)], up_w.at[0]),
                (up_b.at[:, pl.ds(0, FFH)], up_w.at[1]),
                (down_a, down_w.at[0]),
                (down_b, down_w.at[1]),
                (up_a.at[:, pl.ds(FFH, HALF)], wo_a),
                (up_b.at[:, pl.ds(FFH, HALF)], wo_b),
            ]
        )
    ]
    for load in loads[4:] + loads[:4]:
        load.start()
    sums_ref[...] = jnp.zeros_like(sums_ref)
    bias_sums_ref[...] = jnp.zeros_like(bias_sums_ref)
    acts, grads_up = (act_a, act_b), (gu_a, gu_b)
    device = lax.axis_index("dev")
    core = device % 2
    later = later_image(device)
    mean = lambda value: jnp.mean(value, axis=1, keepdims=True)

    def tile(index, carry):
        rows = pl.ds(pl.multiple_of(index * MLP_ROWS, MLP_ROWS), MLP_ROWS)

        def ready(load):
            @pl.when(index == 0)
            def _():
                load.wait()

        ready(loads[4])
        ready(loads[5])
        atts = [jnp.where(later, landing[1, side, index], landing[0, side, index]) for side in range(2)]
        att_ref[rows] = jnp.concatenate(atts, axis=1)
        sides = [mm(atts[0], wo[:HALF], NN) + mm(atts[1], wo[HALF:], NN) for wo in (wo_a, wo_b)]
        branch = jnp.where(core == 0, jnp.concatenate(sides, axis=1), jnp.concatenate(sides[::-1], axis=1))
        middle = x_ref[rows].astype(jnp.float32) + (branch + vec_ref[0:1])
        centered = middle - mean(middle)
        inverse = lax.rsqrt(mean(centered * centered) + EPSILON)
        normed = centered * inverse
        gain = vec_ref[1:2]
        hidden = (normed * gain + vec_ref[2:3]).astype(jnp.bfloat16)
        h2_ref[rows] = hidden
        for half in range(2):
            ready(loads[half])
            upper = mm(hidden, up_w[half], NN) + bias_ref[half : half + 1]
            square = upper * upper
            tanh = jnp.tanh(GELU_A * (upper + GELU_B * (square * upper)))
            acts[half][rows] = (0.5 * upper * (1.0 + tanh)).astype(jnp.bfloat16)
            slope[half] = 0.5 * (1.0 + tanh) + (0.5 * GELU_A) * upper * (1.0 - tanh * tanh) * (
                1.0 + (3.0 * GELU_B) * square
            )
        for half in range(2):
            ready(loads[2 + half])
        lower = mm(act_a[rows], down_w[0], NN) + mm(act_b[rows], down_w[1], NN)
        result_ref[rows] = (middle + (lower + vec_ref[3:4])).astype(jnp.bfloat16)
        grad = g_ref[rows]
        for half in range(2):
            grad_upper = (mm(grad, down_w[half], NT) * slope[half]).astype(jnp.bfloat16)
            grads_up[half][rows] = grad_upper
            bias_sums_ref[half : half + 1] += jnp.sum(grad_upper.astype(jnp.float32), axis=0, keepdims=True)
        grad_hidden = mm(gu_a[rows], up_w[0], NT) + mm(gu_b[rows], up_w[1], NT)
        scaled = grad_hidden * gain
        wide = grad.astype(jnp.float32)
        grad_middle = wide + inverse * (scaled - mean(scaled) - normed * mean(scaled * normed))
        gm_ref[rows] = grad_middle
        branch = grad_middle.astype(jnp.bfloat16)
        low, high = branch[:, :HALF], branch[:, HALF:]
        branches = jnp.where(core == 0, low, high), jnp.where(core == 0, high, low)
        filler = jnp.zeros((MLP_ROWS, 64), jnp.bfloat16)
        gb_a[rows], gb_b[rows] = [jnp.concatenate([side, filler], axis=1) for side in branches]
        for go_ref, heads in ((go_a, slice(0, HALF)), (go_b, slice(HALF, D))):
            total = mm(branches[0], wo_a[heads], NT) + mm(branches[1], wo_b[heads], NT)
            go_ref[rows] = total.astype(jnp.bfloat16)
        for n, value in enumerate([branch.astype(jnp.float32), grad_hidden * normed, grad_hidden, wide]):
            sums_ref[n : n + 1] += jnp.sum(value, axis=0, keepdims=True)
        return carry

    lax.fori_loop(0, x_ref.shape[0] // MLP_ROWS, tile, 0)


def mlp(x, landing, grad, ups, downs, vecs, biases):
    rows = x.shape[0]
    vmem, hbm = pl.BlockSpec(memory_space=pltpu.VMEM), pl.BlockSpec(memory_space=pl.ANY)
    low = lambda width: jax.ShapeDtypeStruct((rows, width), jnp.bfloat16)
    wide = lambda *shape: jax.ShapeDtypeStruct(shape, jnp.float32)
    return pl.pallas_call(
        mlp_kernel,
        out_shape=[low(D), low(D)] + [low(FFH)] * 4 + [low(D), low(HALF + 64), low(HALF + 64), wide(rows, D), low(HALF), low(HALF), wide(8, D), wide(8, FFH)],
        in_specs=[vmem] * 3 + [hbm] * 4 + [vmem] * 2,
        out_specs=[vmem] * 14,
        scratch_shapes=[
            pltpu.VMEM((D, HALF), jnp.bfloat16),
            pltpu.VMEM((D, HALF), jnp.bfloat16),
            pltpu.VMEM((2, D, FFH), jnp.bfloat16),
            pltpu.VMEM((2, FFH, D), jnp.bfloat16),
            pltpu.VMEM((2, MLP_ROWS, FFH), jnp.float32),
            pltpu.SemaphoreType.DMA((6,)),
        ],
        compiler_params=pltpu.CompilerParams(vmem_limit_bytes=62 * 1024 * 1024),
        cost_estimate=pl.CostEstimate(flops=0, bytes_accessed=130 * 10**6, transcendentals=0),
        name="mlp",
    )(x, landing, grad, *ups, *downs, vecs, biases)


def topo_local(tokens, counts, qkv_weight, out_weight, up_weight, down_weight, vectors, cotangent):
    device = lax.axis_index("dev")
    core, chip = device % 2, device // 2
    batches = tokens.shape[0]
    share = vectors.shape[0]
    own_rows = batches * SHARD

    qkv36 = qkv_weight.reshape(ROWS // 2, 3 * D)
    out36 = out_weight.reshape(ROWS // 2, D)
    side_qkv = [
        jnp.concatenate([qkv36[:, s * HALF + j * D :][:, :HALF] for j in range(3)], axis=1) for s in range(2)
    ]
    side_out = [out36[:, s * HALF :][:, :HALF] for s in range(2)]
    up36 = up_weight.reshape(ROWS // 2, CHIPS, UNIT)
    up_low = up36[:, :, :UNIT_HALF].reshape(ROWS // 2, FFH)
    filler = UNIT_SECOND + UNIT_HALF - UNIT
    up_high = jnp.pad(up36[:, :, UNIT_SECOND:], ((0, 0), (0, 0), (0, filler))).reshape(ROWS // 2, FFH)
    spill = UNIT_HALF * D - down_weight.shape[0]
    borrowed = lax.ppermute(
        down_weight[:spill], "dev", [(i + 1, i) for i in range(0, 2 * CHIPS, 2)]
    )
    down_unit = by_core(
        core,
        jnp.concatenate([down_weight, borrowed]),
        jnp.pad(down_weight[spill:], ((UNIT_HALF - UNIT_SECOND) * D, filler * D)),
    ).reshape(UNIT_HALF, D)
    first_unit = chip_unit(
        core,
        jnp.concatenate([side_qkv[0], side_out[0], up_low], axis=1),
        jnp.concatenate([side_qkv[1], side_out[1], up_high], axis=1),
    )
    shares = jnp.pad(vectors, (0, 512 - share)).reshape(1, 512)
    shares = joined(core, shares, swap(shares), 0).reshape(1, 1024)
    extra = jnp.pad(shares, ((0, 7), (0, 3 * HALF - 1024)))
    up_unit = jnp.concatenate([first_unit[:, 4 * HALF :], first_unit[:, 3 * HALF : 4 * HALF]], axis=1)
    (
        query, keys, values, hidden_one, attended, log_sums, full, landing, up_mine, up_theirs, down_mine, down_theirs
    ) = forward(counts, jnp.concatenate([first_unit[:, : 3 * HALF], extra], axis=0), up_unit, down_unit, tokens, 1)
    qkv_w = full[:, :ROWS].reshape(D, 3 * HALF)
    packed = full[:, ROWS, :1024].reshape(2 * CHIPS, 512)[:, :share].reshape(-1).astype(jnp.float32)
    pieces = [packed[segment * D : (segment + 1) * D] for segment in range(8)]
    bias_units = packed[8 * D : 8 * D + FF].reshape(CHIPS, UNIT)
    bias_low = bias_units[:, :UNIT_HALF].reshape(-1)
    bias_high = jnp.pad(bias_units[:, UNIT_SECOND:], ((0, 0), (0, filler))).reshape(-1)
    up_bias_mine = by_core(core, bias_low, bias_high)
    up_bias_theirs = by_core(core, bias_high, bias_low)
    def dot_tn(left, right):
        return lax.dot_general(left, right, (((0,), (0,)), ((), ())), preferred_element_type=jnp.float32)

    inputs = tokens.reshape(own_rows, D).astype(jnp.float32)
    grad_output = cotangent.reshape(own_rows, D)
    eight = lambda rows: jnp.pad(jnp.stack(rows), ((0, 8 - len(rows)), (0, 0)))
    (
        att_own, result, active_mine, active_theirs, grad_upper_mine, grad_upper_theirs,
        hidden_two, branch_mine, branch_theirs, grad_middle, heads_low, heads_high, vec_sums, bias_sums,
    ) = mlp(
        tokens.reshape(own_rows, D), landing, grad_output, (up_mine, up_theirs), (down_mine, down_theirs),
        eight([pieces[4], pieces[5], pieces[6], pieces[7]]), eight([up_bias_mine, up_bias_theirs]),
    )

    pair = lambda mine, theirs: jnp.concatenate([mine, swap(theirs)], axis=0)
    grad_down = dot_tn(pair(active_mine, active_theirs), pair(grad_output, grad_output)).astype(jnp.bfloat16)
    both = lambda mine, theirs: [mine, swap(theirs)]
    pairs = (
        both(hidden_two, hidden_two) + both(grad_upper_mine, grad_upper_theirs) + both(att_own, att_own)
        + both(branch_mine, branch_theirs)
    )
    head_sums, landing, down_total, up_total, out_total, qkv_total = backward(
        counts, query, keys, values, hidden_one, qkv_w, attended, log_sums,
        heads_low.reshape(batches, SHARD, HALF), heads_high.reshape(batches, SHARD, HALF),
        grad_down.reshape(CHIPS, UNIT_HALF, D), pairs, 4,
    )
    attention_total = jnp.concatenate([qkv_total, out_total], axis=1)
    later = later_image(device)[None]
    grad_hidden_one = jnp.where(later, landing[1], landing[0]).astype(jnp.float32).reshape(own_rows, D)
    normed_one, inverse_one = layer_stats(inputs)
    grad_input = grad_middle + layer_back(grad_hidden_one, normed_one, inverse_one, pieces[0])

    sums = lambda values: jnp.sum(values.astype(jnp.float32), axis=0)
    at_heads = lambda vector: lax.dynamic_update_slice_in_dim(
        jnp.zeros((D,), jnp.float32), vector, core * HALF, 0
    )
    bias_mine, bias_theirs = bias_sums[0], bias_sums[1]
    bias_low = by_core(core, bias_mine, bias_theirs).reshape(CHIPS, UNIT_HALF)
    bias_high = by_core(core, bias_theirs, bias_mine).reshape(CHIPS, UNIT_HALF)
    rest = slice(UNIT_HALF - UNIT_SECOND, UNIT - UNIT_SECOND)
    grad_up_bias = jnp.concatenate([bias_low, bias_high[:, rest]], axis=1).reshape(-1)
    vector_grad = jnp.concatenate(
        [
            sums(grad_hidden_one * normed_one),
            sums(grad_hidden_one),
            at_heads(head_sums[0]),
            at_heads(head_sums[1]),
            *(vec_sums[n] for n in range(4)),
            grad_up_bias,
            jnp.zeros((32 * share - 8 * D - FF,), jnp.float32),
        ]
    )
    vector_grad = scatter_vector(vector_grad, share, 2)

    half_rows = ROWS // 2

    def whole_rows(total):
        kept = by_core(core, total[:half_rows], total[half_rows:])
        theirs = swap(by_core(core, total[half_rows:], total[:half_rows]))
        return by_core(core, kept, theirs), by_core(core, theirs, kept)

    low, high = whole_rows(attention_total)
    columns = [
        jnp.concatenate([low[:, j * HALF : (j + 1) * HALF], high[:, j * HALF : (j + 1) * HALF]], axis=1)
        for j in range(4)
    ]
    qkv_grad = jnp.concatenate(columns[:3], axis=1).reshape(-1)
    out_grad = columns[3].reshape(-1)
    low, high = whole_rows(up_total)
    up_grad = jnp.concatenate(
        [
            low.reshape(half_rows, CHIPS, UNIT_HALF),
            high.reshape(half_rows, CHIPS, UNIT_HALF)[:, :, rest],
        ],
        axis=2,
    ).reshape(-1)
    down_flat = down_total.reshape(-1)
    size, lead = down_weight.shape[0], down_weight.shape[0] - UNIT_SECOND * D
    down_grad = by_core(core, down_flat[:size], down_flat[lead : lead + size])
    return (
        result.reshape(tokens.shape),
        grad_input.astype(jnp.bfloat16).reshape(tokens.shape),
        qkv_grad,
        out_grad,
        up_grad,
        down_grad,
        vector_grad,
    )


def solution(mesh):
    local = topo_local if mesh.shape["dev"] == 32 else generic_local
    return jax.shard_map(
        local,
        mesh=mesh,
        in_specs=(
            P(None, "dev", None),
            P(),
            P("dev"),
            P("dev"),
            P("dev"),
            P("dev"),
            P("dev"),
            P(None, "dev", None),
        ),
        out_specs=(
            P(None, "dev", None),
            P(None, "dev", None),
            P("dev"),
            P("dev"),
            P("dev"),
            P("dev"),
            P("dev"),
        ),
        check_vma=False,
    )
```
